32 devices in a mesh: tm: 8 (over z, y), obs: 4 (over x, core).
Axes of the slice: x: 2, y: 2, z: 4, core: 2. Of those that a mesh axis runs over, the one named last changes fastest.
Arguments:
- records: bfloat16 [32768, 512], P(('tm', 'obs')), may hold values from -0.25 to 0.25
- obs_values: bfloat16 [32768], P(('tm', 'obs')), may hold values from -18 to 18
- block_day: int32 [256], P(('tm', 'obs')), may hold values from 0 to 1
- block_count: int32 [256], P(('tm', 'obs')), may hold values from 1 to 128
- propagator_matrix: float32 [512, 512], replicated, may hold values from -1 to 1
- analysis_cov: float32 [512, 512], replicated, may hold values from -0.05 to 0.1, as said below
- unattenuated_multiplier: float32 [512, 512], P('obs'), may hold values from -0.3 to 1
- damping: float32 [16, 512], P('tm'), may hold values from 0 to 1
- prior_mean: float32 [512], P('obs'), may hold values from -6 to 6
Outputs:
- filtered: float32 [16, 512], P('tm', 'obs')
- smoothed: float32 [16, 512], P('tm', 'obs')
The draws below stay inside these ranges and needn't reach their ends.
Inputs may be any that keep to these rules, and one draw needn't show every extreme that they name: `analysis_cov`: Symmetric.
All inputs are finite; a program needn't handle non-finite values.
Results may differ from the reference program's by a relative error of at most 0.0003.
Values may be sent and summed in bfloat16 or wider, within the bound.
No kernel may reach another device: no remote copies, remote signals or barrier semaphores. Data moves between devices by JAX's collectives and lax.ppermute only.
A program may use at most 192 MiB of HBM per device.

```python
import math
import jax
import jax.numpy as jnp
from jax import lax

S = 512
BLOCK = 128
DAYS_DEV = 2
WINDOW_DAYS = 16
BLOCKS = 256
N_TM = 8
N_OBS = 4


def draw_propagator_matrix(key, part):
    random_keys = jax.random.split(key, 2)
    noise = jax.random.normal(random_keys[0], (S, S), jnp.float32) * (0.02 / math.sqrt(S))
    diagonal = jax.random.uniform(random_keys[1], (S,), jnp.float32, 0.93, 1.0)
    return jnp.diag(diagonal) + (noise - noise.T)


def draw_analysis_cov(key, part):
    random_keys = jax.random.split(key, 2)
    lowest = 0.25 / WINDOW_DAYS
    variance = jnp.exp(jax.random.uniform(random_keys[0], (S,), jnp.float32, math.log(lowest), math.log(0.05)))
    noise = jax.random.normal(random_keys[1], (S, S), jnp.float32)
    mirror = 0.5 * (noise + noise.T)
    root = jnp.sqrt(variance)
    return jnp.diag(variance) + 0.3 * root[:, None] * root[None, :] * mirror / math.sqrt(S)


def draw_unattenuated_multiplier(key, part):
    random_keys = jax.random.split(key, 2)
    lowest, maximal_accuracy = (0.5 / WINDOW_DAYS, 1.0 / 30.0)
    rates = jnp.exp(jax.random.uniform(random_keys[0], (S,), jnp.float32, math.log(lowest), math.log(maximal_accuracy)))
    noise = jax.random.normal(random_keys[1], (S, S), jnp.float32) * (0.02 / math.sqrt(S))
    return jnp.diag(jnp.exp(-rates)) + (noise - noise.T)


def draw_damping(key, part):
    random_keys = jax.random.split(key, 4)
    spans = WINDOW_DAYS // DAYS_DEV
    lowest, maximal_accuracy = (0.25 / WINDOW_DAYS, 1.0 / 30.0)
    rates = jnp.exp(jax.random.uniform(random_keys[0], (1, 1, S), jnp.float32, math.log(lowest), math.log(maximal_accuracy)))
    spread = jnp.exp(jax.random.uniform(random_keys[1], (spans, 1, S), jnp.float32, math.log(0.5), 0.0))
    decay_factor = jnp.broadcast_to(rates * spread, (spans, DAYS_DEV, S)).reshape(WINDOW_DAYS, S)
    sudden_shock = jax.random.uniform(random_keys[2], (WINDOW_DAYS, 1), jnp.float32) < 3.0 / WINDOW_DAYS
    dropped_rows = jax.random.uniform(random_keys[3], (WINDOW_DAYS, S), jnp.float32, 0.5, 0.8)
    return jnp.exp(-decay_factor) * jnp.where(sudden_shock, dropped_rows, 1.0)


def set_ends(array, own_key, least, top_value):
    extent = array.shape
    index_at = [jax.random.randint(jax.random.fold_in(own_key, axis), (), 0, extent[axis]) for axis in range(len(extent))]
    array = array.at[tuple(index_at)].set(least)
    longest = extent.index(max(extent))
    index_at[longest] = (index_at[longest] + 1) % extent[longest]
    return array.at[tuple(index_at)].set(top_value)


def block_levels(key, dims, shards, low, top_value):
    def one(dim, blocks):
        steps = jax.random.uniform(jax.random.fold_in(jax.random.fold_in(key, 6), dim), (blocks,), jnp.float32, low / len(shards), top_value / len(shards))
        return jnp.repeat(jnp.exp(steps), dims[dim] // blocks).reshape((-1,) + (1,) * (len(dims) - dim - 1))

    level = one(*shards[0])
    for cut in shards[1:]:
        level = level * one(*cut)
    return level


def scatter_about(key, extent, scale, reach, cuts=(), kind=jnp.bfloat16):
    loudness = block_levels(key, extent, cuts, -0.22, 0.18) if cuts else 1.0
    result = jax.random.normal(key, extent, jnp.float32) * scale * loudness
    return jnp.minimum(jnp.maximum(result, -reach), reach).astype(kind)


def setup_inputs(seed: int = 0) -> dict:
    key_list = jax.random.split(jax.random.key(seed), 10)
    return {
        "records": scatter_about(key_list[0], (BLOCKS * BLOCK, S), S ** -0.5, 0.25, ((0, 32),)),
        "obs_values": scatter_about(key_list[1], (BLOCKS * BLOCK,), 3.0, 18.0, ((0, 32),)),
        "block_day": set_ends(jax.random.randint(key_list[2], (BLOCKS,), 0, DAYS_DEV), jax.random.fold_in(key_list[2], 1), 0, DAYS_DEV - 1).astype(jnp.int32),
        "block_count": set_ends(jax.random.randint(key_list[3], (BLOCKS,), 1, BLOCK + 1), jax.random.fold_in(key_list[3], 1), 1, BLOCK).astype(jnp.int32),
        "propagator_matrix": draw_propagator_matrix(jax.random.fold_in(key_list[9], 71), 0),
        "analysis_cov": draw_analysis_cov(jax.random.fold_in(key_list[9], 71), 0),
        "unattenuated_multiplier": draw_unattenuated_multiplier(jax.random.fold_in(key_list[9], 71), 0),
        "damping": draw_damping(jax.random.fold_in(key_list[9], 71), 0),
        "prior_mean": scatter_about(key_list[8], (S,), 1.0, 6.0, ((0, 4),), jnp.float32),
    }


def day_grams(rows_all, values_all, days_of_block, counts_of_block, day_total):
    maximal_accuracy = lax.Precision.HIGHEST
    block_total = days_of_block.shape[0]
    slot_total = rows_all.shape[0] // block_total
    width = rows_all.shape[1]
    group = math.gcd(block_total, 8)
    slot_index = lax.broadcasted_iota(jnp.int32, (block_total, slot_total), 1)
    valid_mask = slot_index < counts_of_block[:, None]
    held_rows = jnp.where(valid_mask[:, :, None], rows_all.reshape(block_total, slot_total, width).astype(jnp.float32), 0.0)
    held_values = jnp.where(valid_mask, values_all.reshape(block_total, slot_total).astype(jnp.float32), 0.0)
    day_mark = (days_of_block[:, None] == lax.broadcasted_iota(jnp.int32, (block_total, day_total), 1)).astype(jnp.float32)
    block_info = jnp.einsum('bk,bks->bs', held_values, held_rows, precision=maximal_accuracy)
    info = jnp.einsum('bd,bs->ds', day_mark, block_info, precision=maximal_accuracy)
    grouped_rows = held_rows.reshape(block_total // group, group, slot_total, width)
    grouped_mark = day_mark.reshape(block_total // group, group, day_total)

    def add_group(running, pieces):
        block_part, mark_part = pieces
        gram_blocks = jnp.einsum('bks,bkt->bst', block_part, block_part, precision=maximal_accuracy)
        return running + jnp.einsum('bd,bst->dst', mark_part, gram_blocks, precision=maximal_accuracy), None

    omega, _ = lax.scan(add_group, jnp.zeros((day_total, width, width), jnp.float32), (grouped_rows, grouped_mark))
    return omega, info


def reference(records, obs_values, block_day, block_count, propagator_matrix, analysis_cov, unattenuated_multiplier, damping, prior_mean):
    maximal_accuracy = lax.Precision.HIGHEST
    owners = N_TM * N_OBS
    span_rows = jnp.swapaxes(records.reshape(owners, N_TM, BLOCK, S), 0, 1)
    span_values = jnp.swapaxes(obs_values.reshape(owners, N_TM, BLOCK), 0, 1)
    span_days = jnp.swapaxes(block_day.reshape(owners, N_TM), 0, 1)
    span_counts = jnp.swapaxes(block_count.reshape(owners, N_TM), 0, 1)

    def per_span(pieces):
        rows_part, values_part, days_part, counts_part = pieces
        return day_grams(rows_part.reshape(owners * BLOCK, S), values_part.reshape(owners * BLOCK), days_part, counts_part, DAYS_DEV)

    omega, info = lax.map(per_span, (span_rows, span_values, span_days, span_counts))
    omega = omega.reshape(WINDOW_DAYS, S, S)
    info = info.reshape(WINDOW_DAYS, S)

    def forward(state, pieces):
        omega_day, info_day, attenuated_date = pieces
        moved = attenuated_date * jnp.dot(propagator_matrix, state, precision=maximal_accuracy)
        updated_vector = moved - jnp.dot(analysis_cov, jnp.dot(omega_day, moved, precision=maximal_accuracy) - info_day, precision=maximal_accuracy)
        return updated_vector, updated_vector

    _, filtered = lax.scan(forward, prior_mean, (omega, info, damping))
    attenuated_successor = jnp.concatenate([damping[1:], jnp.zeros((1, S), jnp.float32)], 0)

    def backward(subsequent_dates, pieces):
        assimilated_date, attenuated_date = pieces
        predicted_vector = attenuated_date * jnp.dot(propagator_matrix, assimilated_date, precision=maximal_accuracy)
        updated_vector = assimilated_date + jnp.dot(unattenuated_multiplier, attenuated_date * (subsequent_dates - predicted_vector), precision=maximal_accuracy)
        return updated_vector, updated_vector

    _, smoothed = lax.scan(backward, jnp.zeros((S,), jnp.float32), (filtered, attenuated_successor), reverse=True)
    return filtered, smoothed
```

```python
import functools

import jax
import jax.numpy as jnp
from jax import lax
from jax.experimental import pallas as pl
from jax.experimental.pallas import tpu as pltpu
from jax.sharding import PartitionSpec as P

LANES = 128
F32, BF16 = jnp.float32, jnp.bfloat16
VMEM = pl.BlockSpec(memory_space=pltpu.VMEM)
SMEM = pl.BlockSpec(memory_space=pltpu.SMEM)


def run(body, out, ins, scratch=(), limit=32, flops=0):
    specs = [x[1] if isinstance(x, tuple) else VMEM for x in ins]
    arrays = [x[0] if isinstance(x, tuple) else x for x in ins]
    moved = sum(a.size * a.dtype.itemsize for a in arrays)
    return pl.pallas_call(
        body,
        out_shape=[jax.ShapeDtypeStruct(s, d) for s, d in out],
        in_specs=specs,
        out_specs=[VMEM] * len(out),
        scratch_shapes=list(scratch),
        compiler_params=pltpu.CompilerParams(vmem_limit_bytes=limit * 1024 * 1024),
        cost_estimate=pl.CostEstimate(flops=flops, bytes_accessed=moved, transcendentals=0),
    )(*arrays)


def triangle(width):
    parts = width // LANES
    return [(i, j) for i in range(parts) for j in range(i + 1)]


def split(x):
    hi = x.astype(BF16)
    return hi, (x - hi.astype(F32)).astype(BF16)


def mm(x, hi, lo):
    xhi, xlo = split(x)
    dot = functools.partial(jnp.dot, preferred_element_type=F32)
    return dot(xhi, hi) + (dot(xlo, hi) + dot(xhi, lo))


def mv(x, hi, lo):
    wide = jnp.broadcast_to(x, (8, x.shape[1]))
    row = lax.broadcasted_iota(jnp.int32, wide.shape, 0)
    top = wide.astype(BF16).astype(F32)
    both = jnp.where(row == 0, top, jnp.where(row == 1, wide - top, 0.0)).astype(BF16)
    first = jnp.dot(both, hi, preferred_element_type=F32)
    second = jnp.dot(both, lo, preferred_element_type=F32)
    return first[0:1] + (first[1:2] + second[0:1])


def gram_kernel(ids, rows, meta, prior, keep, send, turned, marks):
    blocks, _, slots = meta.shape
    width = rows.shape[1]
    tiles = triangle(width)
    info_at = len(tiles)
    mine = (ids[1] % 2).astype(F32)
    group = min(blocks, 8)
    half = 2 * LANES

    def one(first, fresh):
        span = group * slots
        start = first * slots
        for k in range(group):
            at = slice(k * slots, (k + 1) * slots)
            valid = lax.broadcasted_iota(jnp.int32, (1, slots), 1).astype(F32) < meta[first + k, 2:3, :]
            here = meta[first + k, 1:2, :] == mine
            values = meta[first + k, 0:1, :]
            kept = jnp.where(valid & here, 1.0, 0.0)
            sent = jnp.where(valid & ~here, 1.0, 0.0)
            marks[:, at] = jnp.concatenate(
                [kept, sent, kept * values, sent * values, jnp.zeros((12, slots), F32)], 0
            ).astype(BF16)
        source = rows[pl.ds(start, span), :]
        turned[...] = source.T
        info = jnp.dot(marks[...], source, preferred_element_type=F32)
        for which, out in ((0, keep), (1, send)):
            for top in range(0, width, half):
                left = turned[top : top + half, :] * marks[which : which + 1, :]
                block = jnp.dot(left, source[:, : top + half], preferred_element_type=F32)
                for n, (i, j) in enumerate(tiles):
                    if top <= i * LANES < top + half:
                        r = i * LANES - top
                        piece = block[r : r + LANES, j * LANES : (j + 1) * LANES]
                        out[n] = piece if fresh else out[n] + piece
            for j in range(width // LANES):
                piece = info[2 + which : 3 + which, j * LANES : (j + 1) * LANES]
                out[info_at, j : j + 1, :] = piece if fresh else out[info_at, j : j + 1, :] + piece

    for out in (keep, send):
        out[info_at] = jnp.zeros((LANES, LANES), F32)
    if blocks == group:
        one(0, True)
    else:
        for out in (keep, send):
            out[...] = jnp.zeros(out.shape, F32)

        @pl.loop(0, blocks // group)
        def _(g):
            one(g * group, False)

    for out in (keep, send):
        for q in range(width // LANES):
            out[info_at, 4 + q : 5 + q, :] = jnp.where(ids[1] == q, prior[...], 0.0)


def chip_kernel(keep, got, chip, pay):
    last = keep.shape[0] - 1
    for n in range(last):
        total = keep[n] + got[n]
        chip[n] = total
        pay[n] = total.astype(BF16)
    small = keep[last, 0:16, :] + got[last, 0:16, :]
    chip[last] = jnp.zeros((LANES, LANES), F32)
    chip[last, 0:16, :] = small
    pay[last] = jnp.zeros((LANES, LANES), BF16)
    for part in range(3):
        piece = small.astype(BF16)
        pay[last, 16 * part : 16 * part + 16, :] = piece
        small = small - piece.astype(F32)


def day_kernel(chip, got, day):
    last = chip.shape[0] - 1
    for n in range(last):
        day[n] = chip[n] + got[n].astype(F32)
    day[last] = jnp.zeros((LANES, LANES), F32)
    small = [got[last, 16 * part : 16 * part + 16, :].astype(F32) for part in range(3)]
    day[last, 0:16, :] = chip[last, 0:16, :] + (small[0] + (small[1] + small[2]))


def prep_kernel(ids, m0, m1, m2, m3, trans, cov, pt, pthi, ptlo, mthi, mtlo, chi, clo):
    peers = 4
    rows = m0.shape[0]
    for step, part in enumerate((m0, m1, m2, m3)):
        owner = lax.rem(ids[1] - step + peers, peers)
        at = pl.ds(pl.multiple_of(owner * rows, rows), rows)
        hi, lo = split(part[...].T)
        mthi[:, at] = hi
        mtlo[:, at] = lo
    whole = trans[...].T
    pt[...] = whole
    pthi[...], ptlo[...] = split(whole)
    chi[...], clo[...] = split(cov[...])


def first_kernel(ids, own, other, damping, pthi, ptlo, chi, clo, omhi, omlo, info, start, y):
    width = pthi.shape[0]
    tiles = triangle(width)
    mine = ids[1] % 2
    for slot, src in ((mine, own), (1 - mine, other)):
        for n, (i, j) in enumerate(tiles):
            piece = src[n]
            hi, lo = split(piece)
            omhi[slot, i * LANES : (i + 1) * LANES, j * LANES : (j + 1) * LANES] = hi
            omlo[slot, i * LANES : (i + 1) * LANES, j * LANES : (j + 1) * LANES] = lo
            if i != j:
                hi, lo = split(piece.T)
                omhi[slot, j * LANES : (j + 1) * LANES, i * LANES : (i + 1) * LANES] = hi
                omlo[slot, j * LANES : (j + 1) * LANES, i * LANES : (i + 1) * LANES] = lo
        for j in range(width // LANES):
            info[slot, :, j * LANES : (j + 1) * LANES] = src[len(tiles), j : j + 1, :]
    state = jnp.concatenate(
        [own[len(tiles), 4 + q : 5 + q, :] for q in range(width // LANES)], 1
    )
    start[...] = jnp.where(ids[0] == 0, state, 0.0)
    for day in range(2):
        moved = mv(state, pthi[...], ptlo[...]) * damping[day : day + 1, :]
        gap = mv(moved, omhi[day], omlo[day]) - info[day]
        state = moved - mv(gap, chi[...], clo[...])
    y[...] = state


def maps_kernel(omhi, omlo, info, chi, clo, pt, damping, b1hi, b1lo, b2hi, b2lo, bchi, bclo, off):
    parts = ((b1hi, b1lo), (b2hi, b2lo))
    for day in range(2):
        moved = pt[...] * damping[day : day + 1, :]
        taken = mm(moved, omhi[day], omlo[day])
        step = moved - mm(taken, chi[...], clo[...])
        parts[day][0][...], parts[day][1][...] = split(step)
        off[day : day + 1, :] = mv(info[day], chi[...], clo[...])
    both = jnp.dot(b1hi[...], b2hi[...], preferred_element_type=F32) + (
        jnp.dot(b1lo[...], b2hi[...], preferred_element_type=F32)
        + jnp.dot(b1hi[...], b2lo[...], preferred_element_type=F32)
    )
    bchi[...], bclo[...] = split(both)
    off[2:3, :] = mv(off[0:1, :], b2hi[...], b2lo[...]) + off[1:2, :]


def hop_kernel(acc, got, bchi, bclo, off, total, y):
    state = acc[...] + got[...]
    total[...] = state
    y[...] = mv(state, bchi[...], bclo[...]) + off[2:3, :]


def last_kernel(acc, got, b1hi, b1lo, b2hi, b2lo, off, out):
    state = acc[...] + got[...]
    one = mv(state, b1hi[...], b1lo[...]) + off[0:1, :]
    two = mv(one, b2hi[...], b2lo[...]) + off[1:2, :]
    both = jnp.concatenate([one, two], 0)
    for c in range(out.shape[0]):
        out[c] = both


def back_kernel(ids, states, meta, pthi, ptlo, mthi, mtlo, filt, smooth, f, d, const):
    spans, days, width = states.shape
    total = spans * days
    parts = width // LANES
    for c in range(spans):
        f[c * days : (c + 1) * days, :] = states[c]
        for k in range(days):
            t = c * days + k - 1
            if t >= 0:
                for j in range(parts):
                    r = 8 + k * parts + j
                    d[t : t + 1, j * LANES : (j + 1) * LANES] = meta[c, r : r + 1, :]
    d[total - 1 : total, :] = jnp.zeros((1, width), F32)
    ahead = d[...] * mm(f[...], pthi[...], ptlo[...])
    const[...] = f[...] - mm(d[...] * ahead, mthi[...], mtlo[...])

    def step(k, state):
        t = total - 2 - k
        new = const[pl.ds(t, 1), :] + mv(d[pl.ds(t, 1), :] * state, mthi[...], mtlo[...])
        const[pl.ds(t, 1), :] = new
        return new

    lax.fori_loop(0, total - 1, step, const[total - 1 : total, :], unroll=total <= 16)
    for k in range(days):
        row = pl.ds(ids[0] * days + k, 1)
        for whole, out in ((f, filt), (const, smooth)):
            line = whole[row, :]
            mine = line[:, 0:LANES]
            for q in range(1, parts):
                mine = jnp.where(ids[1] == q, line[:, q * LANES : (q + 1) * LANES], mine)
            out[k : k + 1, :] = mine


def local(
    records,
    obs_values,
    block_day,
    block_count,
    propagator_matrix,
    analysis_cov,
    unattenuated_multiplier,
    damping,
    prior_mean,
):
    spans, peers = lax.axis_size("tm"), lax.axis_size("obs")
    blocks = block_day.shape[0]
    slots = records.shape[0] // blocks
    width = records.shape[1]
    days = damping.shape[0]
    assert peers == 4 and days == 2 and slots == LANES and blocks == spans
    ids = jnp.stack([lax.axis_index("tm"), lax.axis_index("obs")]).astype(jnp.int32)
    exchange = functools.partial(lax.all_to_all, axis_name="tm", split_axis=0, concat_axis=0, tiled=True)

    def swap(x, bit):
        return lax.ppermute(x, "obs", [(i, i ^ bit) for i in range(peers)])

    got_rows = exchange(records)
    lane = (blocks, 1, slots)
    meta = jnp.concatenate(
        [
            obs_values.reshape(lane).astype(F32),
            jnp.broadcast_to(block_day[:, None, None], lane).astype(F32),
            jnp.broadcast_to(block_count[:, None, None], lane).astype(F32),
            jnp.zeros((blocks, 5, slots), F32),
            jnp.broadcast_to(damping.reshape(1, days * width // LANES, LANES), (blocks, 8, LANES)),
        ],
        1,
    )
    got_meta = exchange(meta)
    gain = [unattenuated_multiplier] + [
        lax.ppermute(unattenuated_multiplier, "obs", [(i, (i + s) % peers) for i in range(peers)])
        for s in range(1, peers)
    ]
    full, parts = (width, width), len(triangle(width)) + 1
    pt, pthi, ptlo, mthi, mtlo, chi, clo = run(
        prep_kernel,
        [(full, F32)] + [(full, BF16)] * 6,
        [(ids, SMEM), *gain, propagator_matrix, analysis_cov],
    )
    packed = (parts, LANES, LANES)
    keep, send = run(
        gram_kernel,
        [(packed, F32)] * 2,
        [(ids, SMEM), got_rows, got_meta, prior_mean.reshape(1, -1)],
        [pltpu.VMEM((width, min(blocks, 8) * slots), BF16), pltpu.VMEM((16, min(blocks, 8) * slots), BF16)],
        flops=4 * width * width * blocks * slots,
    )
    chip, pay = run(chip_kernel, [(packed, F32), (packed, BF16)], [keep, swap(send, 1)])
    (own,) = run(day_kernel, [(packed, F32)], [chip, swap(pay, 2)])
    other = swap(own, 1)
    omhi, omlo, info, acc, y = run(
        first_kernel,
        [((days,) + full, BF16)] * 2 + [((days, 1, width), F32), ((1, width), F32), ((1, width), F32)],
        [(ids, SMEM), own, other, damping, pthi, ptlo, chi, clo],
    )
    b1hi, b1lo, b2hi, b2lo, bchi, bclo, off = run(
        maps_kernel,
        [(full, BF16)] * 6 + [((8, width), F32)],
        [omhi, omlo, info, chi, clo, pt, damping],
        flops=30 * width**3,
    )
    for k in range(spans - 1):
        got = lax.ppermute(y, "tm", [(k, k + 1)])
        if k < spans - 2:
            acc, y = run(hop_kernel, [((1, width), F32)] * 2, [acc, got, bchi, bclo, off])
    (sent,) = run(
        last_kernel, [((spans, days, width), F32)], [acc, got, b1hi, b1lo, b2hi, b2lo, off]
    )
    states = exchange(sent)
    total = spans * days
    out = ((days, LANES), F32)
    return run(
        back_kernel,
        [out, out],
        [(ids, SMEM), states, got_meta, pthi, ptlo, mthi, mtlo],
        [pltpu.VMEM((total, width), F32)] * 3,
    )


def solution(mesh):
    mapped = jax.shard_map(
        local,
        mesh=mesh,
        in_specs=(
            P(("tm", "obs"), None),
            P(("tm", "obs")),
            P(("tm", "obs")),
            P(("tm", "obs")),
            P(),
            P(),
            P("obs", None),
            P("tm", None),
            P("obs"),
        ),
        out_specs=(P("tm", "obs"), P("tm", "obs")),
        check_vma=False,
    )
    return lambda *args: tuple(mapped(*args))
```

```python
import functools

import jax
import jax.numpy as jnp
from jax import lax
from jax.experimental import pallas as pl
from jax.experimental.pallas import tpu as pltpu
from jax.sharding import PartitionSpec as P

LANES = 128
F32, BF16 = jnp.float32, jnp.bfloat16
VMEM = pl.BlockSpec(memory_space=pltpu.VMEM)
SMEM = pl.BlockSpec(memory_space=pltpu.SMEM)


def run(body, out, ins, scratch=(), limit=32, flops=0):
    specs = [x[1] if isinstance(x, tuple) else VMEM for x in ins]
    arrays = [x[0] if isinstance(x, tuple) else x for x in ins]
    moved = sum(a.size * a.dtype.itemsize for a in arrays)
    return pl.pallas_call(
        body,
        out_shape=[jax.ShapeDtypeStruct(s, d) for s, d in out],
        in_specs=specs,
        out_specs=[VMEM] * len(out),
        scratch_shapes=list(scratch),
        compiler_params=pltpu.CompilerParams(vmem_limit_bytes=limit * 1024 * 1024),
        cost_estimate=pl.CostEstimate(flops=flops, bytes_accessed=moved, transcendentals=0),
    )(*arrays)


def triangle(width):
    parts = width // LANES
    return [(i, j) for i in range(parts) for j in range(i + 1)]


def split(x):
    hi = x.astype(BF16)
    return hi, (x - hi.astype(F32)).astype(BF16)


def mm(x, hi, lo):
    xhi, xlo = split(x)
    dot = functools.partial(jnp.dot, preferred_element_type=F32)
    return dot(xhi, hi) + (dot(xlo, hi) + dot(xhi, lo))


def mv(x, hi, lo):
    wide = jnp.broadcast_to(x, (8, x.shape[1]))
    row = lax.broadcasted_iota(jnp.int32, wide.shape, 0)
    top = wide.astype(BF16).astype(F32)
    both = jnp.where(row == 0, top, jnp.where(row == 1, wide - top, 0.0)).astype(BF16)
    first = jnp.dot(both, hi, preferred_element_type=F32)
    second = jnp.dot(both, lo, preferred_element_type=F32)
    return first[0:1] + (first[1:2] + second[0:1])


def parts3(x):
    out = []
    for _ in range(3):
        piece = x.astype(BF16).astype(F32)
        out.append(piece)
        x = x - piece
    return out


def owner_plane(span):
    return 1 + span % 2


EXTRA = 16


def pack_kernel(day, count, rows, values, prior, damping, out):
    blocks = out.shape[0]
    slots = out.shape[1] - EXTRA
    width = out.shape[2]
    first, second, third = parts3(prior[...])
    below = jnp.concatenate(
        [jnp.concatenate([second, third, jnp.zeros((1, width - 2 * LANES), F32)], 1)]
        + parts3(damping[...])
        + [jnp.zeros((EXTRA - 8, width), F32)],
        0,
    )
    for k in range(blocks):
        out[k, 0:slots, :] = rows[k * slots : (k + 1) * slots, :]
        line = jnp.concatenate(
            [
                values[k : k + 1, :],
                jnp.full((1, LANES), day[k], jnp.int32).astype(F32),
                jnp.full((1, LANES), count[k], jnp.int32).astype(F32),
                first,
            ],
            1,
        )
        out[k, slots : slots + EXTRA, :] = jnp.concatenate([line, below], 0).astype(BF16)


def gram_kernel(got, gain, own, extra, pay, prior, gain_out, turned, marks):
    blocks = got.shape[0]
    slots = got.shape[1] - EXTRA
    width = got.shape[2]
    chunks = width // LANES
    tiles = triangle(width)
    group = min(blocks, 8)
    half = 2 * LANES
    gain_out[...] = gain[...]
    extra[...] = jnp.zeros(extra.shape, F32)

    def one(first, fresh):
        for k in range(group):
            at = slice(k * slots, (k + 1) * slots)
            line = got[first + k, slots : slots + EXTRA, :].astype(F32)
            valid = lax.broadcasted_iota(jnp.int32, (1, slots), 1).astype(F32) < line[0:1, 2 * LANES : 3 * LANES]
            day = line[0:1, LANES : 2 * LANES]
            values = line[0:1, 0:LANES]
            kept = [jnp.where(valid & (day == d), 1.0, 0.0) for d in (0.0, 1.0)]
            marks[:, at] = jnp.concatenate(
                kept + [kept[0] * values, kept[1] * values, jnp.zeros((12, slots), F32)], 0
            ).astype(BF16)
            turned[:, at] = got[first + k, 0:slots, :].T
        source = jnp.concatenate([got[first + k, 0:slots, :] for k in range(group)], 0)
        info = jnp.dot(marks[...], source, preferred_element_type=F32)
        for d in range(2):
            for top in range(0, width, half):
                left = turned[top : top + half, :] * marks[d : d + 1, :]
                block = jnp.dot(left, source[:, : top + half], preferred_element_type=F32)
                for n, (i, j) in enumerate(tiles):
                    if top <= i * LANES < top + half:
                        r = i * LANES - top
                        piece = block[r : r + LANES, j * LANES : (j + 1) * LANES]
                        at = d * len(tiles) + n
                        own[at] = piece if fresh else own[at] + piece
            for j in range(chunks):
                piece = info[2 + d : 3 + d, j * LANES : (j + 1) * LANES]
                r = 12 * d + j
                extra[r : r + 1, :] = piece if fresh else extra[r : r + 1, :] + piece

    if blocks == group:
        one(0, True)
    else:
        own[...] = jnp.zeros(own.shape, F32)

        @pl.loop(0, blocks // group)
        def _(g):
            one(g * group, False)

    for d in range(2):
        for part, piece in enumerate(parts3(extra[12 * d : 12 * d + chunks, :])):
            extra[12 * d + 4 * part : 12 * d + 4 * part + chunks, :] = piece
    for q in range(chunks):
        line = got[q, slots : slots + EXTRA, :].astype(F32)
        prior[:, q * LANES : (q + 1) * LANES] = line[0:1, 3 * LANES : 4 * LANES] + (
            line[1:2, 0:LANES] + line[1:2, LANES : 2 * LANES]
        )
    for y in range(blocks // 4):
        line = got[4 * y, slots : slots + EXTRA, :].astype(F32)
        for k in range(6):
            for j in range(chunks):
                r = 24 + 24 * y + 4 * k + j
                extra[r : r + 1, :] = line[2 + k : 3 + k, j * LANES : (j + 1) * LANES]
    for n in range(own.shape[0]):
        pay[n] = own[n].astype(BF16)
    for n in range(extra.shape[0] // LANES):
        pay[own.shape[0] + n] = extra[n * LANES : (n + 1) * LANES, :].astype(BF16)


def prep_kernel(ids, m0, m1, m2, m3, trans, cov, pt, pthi, ptlo, mthi, mtlo, chi, clo):
    peers = 4
    rows = m0.shape[0]
    for step, part in enumerate((m0, m1, m2, m3)):
        owner = lax.rem(ids[2] - step + peers, peers)
        at = pl.ds(pl.multiple_of(owner * rows, rows), rows)
        hi, lo = split(part[...].T)
        mthi[:, at] = hi
        mtlo[:, at] = lo
    whole = trans[...].T
    pt[...] = whole
    pthi[...], ptlo[...] = split(whole)
    chi[...], clo[...] = split(cov[...])


def two_days(state, damping, pthi, ptlo, omhi, omlo, info, chi, clo):
    for day in range(2):
        moved = mv(state, pthi[...], ptlo[...]) * damping[day : day + 1, :]
        gap = mv(moved, omhi[day], omlo[day]) - info[day]
        state = moved - mv(gap, chi[...], clo[...])
    return state


def owner_kernel(
    ids, own, extra, g1, g2, g3, prior, pthi, ptlo, chi, clo, omhi, omlo, info, mine, start, y, table, small
):
    planes = 4
    width = pthi.shape[0]
    chunks = width // LANES
    tiles = triangle(width)
    got = (g1, g2, g3)
    for day in range(2):
        for n, (i, j) in enumerate(tiles):
            at = day * len(tiles) + n
            piece = own[at] + (g1[at].astype(F32) + (g2[at].astype(F32) + g3[at].astype(F32)))
            hi, lo = split(piece)
            omhi[day, i * LANES : (i + 1) * LANES, j * LANES : (j + 1) * LANES] = hi
            omlo[day, i * LANES : (i + 1) * LANES, j * LANES : (j + 1) * LANES] = lo
            if i != j:
                hi, lo = split(piece.T)
                omhi[day, j * LANES : (j + 1) * LANES, i * LANES : (i + 1) * LANES] = hi
                omlo[day, j * LANES : (j + 1) * LANES, i * LANES : (i + 1) * LANES] = lo
    for s in range(planes):
        if s == 0:
            small[0] = extra[...]
        else:
            for n in range(extra.shape[0] // LANES):
                small[s, n * LANES : (n + 1) * LANES, :] = got[s - 1][own.shape[0] + n].astype(F32)

    def row(s, first, gap):
        return jnp.concatenate(
            [
                small[s, first + j : first + j + 1, :]
                + (
                    small[s, first + gap + j : first + gap + j + 1, :]
                    + small[s, first + 2 * gap + j : first + 2 * gap + j + 1, :]
                )
                for j in range(chunks)
            ],
            1,
        )

    for day in range(2):
        info[day] = row(0, 12 * day, 4) + (row(1, 12 * day, 4) + (row(2, 12 * day, 4) + row(3, 12 * day, 4)))
    held = table.shape[0] // 2 // planes
    for s in range(planes):
        plane = lax.rem(ids[0] + s, planes)
        for k in range(held):
            for day in range(2):
                table[pl.ds(2 * (plane * held + k) + day, 1), :] = row(s, 24 + 24 * k + 4 * day, 8)
    for day in range(2):
        mine[day : day + 1, :] = table[pl.ds(2 * ids[1] + day, 1), :]
    state = prior[...]
    start[...] = jnp.where((ids[1] == 0) & (ids[0] == owner_plane(0)), state, 0.0)
    y[...] = two_days(state, mine, pthi, ptlo, omhi, omlo, info, chi, clo)


def direct_kernel(acc, got, mine, pthi, ptlo, omhi, omlo, info, chi, clo, total, y):
    state = acc[...] + got[...]
    total[...] = state
    y[...] = two_days(state, mine, pthi, ptlo, omhi, omlo, info, chi, clo)


def maps_kernel(after, omhi, omlo, info, chi, clo, pt, damping, b1hi, b1lo, b2hi, b2lo, bchi, bclo, off):
    parts = ((b1hi, b1lo), (b2hi, b2lo))
    for day in range(2):
        moved = pt[...] * damping[day : day + 1, :]
        taken = mm(moved, omhi[day], omlo[day])
        step = moved - mm(taken, chi[...], clo[...])
        parts[day][0][...], parts[day][1][...] = split(step)
        off[day : day + 1, :] = mv(info[day], chi[...], clo[...])
    both = jnp.dot(b1hi[...], b2hi[...], preferred_element_type=F32) + (
        jnp.dot(b1lo[...], b2hi[...], preferred_element_type=F32)
        + jnp.dot(b1hi[...], b2lo[...], preferred_element_type=F32)
    )
    bchi[...], bclo[...] = split(both)
    off[2:3, :] = mv(off[0:1, :], b2hi[...], b2lo[...]) + off[1:2, :]


def hop_kernel(acc, got, bchi, bclo, off, total, y):
    state = acc[...] + got[...]
    total[...] = state
    y[...] = mv(state, bchi[...], bclo[...]) + off[2:3, :]


def last_kernel(acc, got, b1hi, b1lo, b2hi, b2lo, off, damping, out):
    state = acc[...] + got[...]
    one = mv(state, b1hi[...], b1lo[...]) + off[0:1, :]
    two = mv(one, b2hi[...], b2lo[...]) + off[1:2, :]
    both = jnp.concatenate([one, two, damping[...]], 0)
    for c in range(out.shape[0]):
        out[c] = both


def back_kernel(ids, states, pthi, ptlo, mthi, mtlo, filt, smooth, f, d, const):
    total, width = f.shape
    spans = total // 2
    chunks = width // LANES
    for c in range(spans):
        one = states[owner_plane(c) * spans + c]
        f[2 * c : 2 * c + 2, :] = one[0:2]
        if c:
            d[2 * c - 1 : 2 * c + 1, :] = one[2:4]
        else:
            d[0:1, :] = one[3:4]
    d[total - 1 : total, :] = jnp.zeros((1, width), F32)
    ahead = d[...] * mm(f[...], pthi[...], ptlo[...])
    const[...] = f[...] - mm(d[...] * ahead, mthi[...], mtlo[...])

    def step(k, state):
        t = total - 2 - k
        new = const[pl.ds(t, 1), :] + mv(d[pl.ds(t, 1), :] * state, mthi[...], mtlo[...])
        const[pl.ds(t, 1), :] = new
        return new

    lax.fori_loop(0, total - 1, step, const[total - 1 : total, :], unroll=total <= 16)
    for k in range(2):
        row = pl.ds(ids[3] * 2 + k, 1)
        for whole, out in ((f, filt), (const, smooth)):
            line = whole[row, :]
            mine = line[:, 0:LANES]
            for q in range(1, chunks):
                mine = jnp.where(ids[2] == q, line[:, q * LANES : (q + 1) * LANES], mine)
            out[k : k + 1, :] = mine


def local(
    records,
    obs_values,
    block_day,
    block_count,
    propagator_matrix,
    analysis_cov,
    unattenuated_multiplier,
    damping,
    prior_mean,
):
    planes, held, peers = (lax.axis_size(a) for a in ("z", "y", "obs"))
    spans = planes * held
    blocks = block_day.shape[0]
    slots = records.shape[0] // blocks
    width = records.shape[1]
    days = damping.shape[0]
    assert planes == peers == 4 and days == 2 and slots == LANES and blocks == spans
    z, y, o = (lax.axis_index(a) for a in ("z", "y", "obs"))
    ids = jnp.stack([z, y * peers + o, o, z * held + y]).astype(jnp.int32)
    everyone = ("z", "y", "obs")

    def owner(span):
        return owner_plane(span) * spans + span

    tiles = len(triangle(width))
    extras = -(-(24 + 24 * held) // LANES)
    full, row = (width, width), ((1, width), F32)
    (sent,) = run(
        pack_kernel,
        [((blocks, slots + EXTRA, width), BF16)],
        [
            (block_day, SMEM),
            (block_count, SMEM),
            records,
            obs_values.astype(F32).reshape(blocks, slots),
            prior_mean.reshape(1, -1),
            damping,
        ],
    )
    got = lax.all_to_all(sent, ("y", "obs"), split_axis=0, concat_axis=0, tiled=True)
    span_slots = min(blocks, 8) * slots
    own, extra, pay, prior, gain = run(
        gram_kernel,
        [
            ((2 * tiles, LANES, LANES), F32),
            ((extras * LANES, LANES), F32),
            ((2 * tiles + extras, LANES, LANES), BF16),
            row,
            (unattenuated_multiplier.shape, F32),
        ],
        [got, unattenuated_multiplier],
        [pltpu.VMEM((width, span_slots), BF16), pltpu.VMEM((16, span_slots), BF16)],
        flops=4 * width * width * blocks * slots,
    )
    plane_sums = [
        lax.ppermute(
            pay, everyone, [((owner_plane(p) + s) % planes * spans + p, owner(p)) for p in range(spans)]
        )
        for s in range(1, planes)
    ]
    gains = [gain] + [
        lax.ppermute(gain, "obs", [(i, (i + s) % peers) for i in range(peers)]) for s in range(1, peers)
    ]
    pt, pthi, ptlo, mthi, mtlo, chi, clo = run(
        prep_kernel,
        [(full, F32)] + [(full, BF16)] * 6,
        [(ids, SMEM), *gains, propagator_matrix, analysis_cov],
    )
    omhi, omlo, info, mine, acc, y = run(
        owner_kernel,
        [((days,) + full, BF16)] * 2 + [((days, 1, width), F32), ((days, width), F32), row, row],
        [(ids, SMEM), own, extra, *plane_sums, prior, pthi, ptlo, chi, clo],
        [pltpu.VMEM((spans * days, width), F32), pltpu.VMEM((planes, extras * LANES, LANES), F32)],
    )
    for k in range(spans - 1):
        received = lax.ppermute(y, everyone, [(owner(k), owner(k + 1))])
        if k == 0:
            acc, y = run(
                direct_kernel, [row, row], [acc, received, mine, pthi, ptlo, omhi, omlo, info, chi, clo]
            )
            b1hi, b1lo, b2hi, b2lo, bchi, bclo, off = run(
                maps_kernel,
                [(full, BF16)] * 6 + [((8, width), F32)],
                [y, omhi, omlo, info, chi, clo, pt, mine],
                flops=30 * width**3,
            )
        elif k < spans - 2:
            acc, y = run(hop_kernel, [row, row], [acc, received, bchi, bclo, off])
    (answer,) = run(
        last_kernel,
        [((spans * peers, 2 * days, width), F32)],
        [acc, received, b1hi, b1lo, b2hi, b2lo, off, mine],
    )
    states = lax.all_to_all(answer, everyone, split_axis=0, concat_axis=0, tiled=True)
    out = ((days, LANES), F32)
    return run(
        back_kernel,
        [out, out],
        [(ids, SMEM), states, pthi, ptlo, mthi, mtlo],
        [pltpu.VMEM((spans * days, width), F32)] * 3,
    )


def solution(mesh):
    spans, peers = mesh.devices.shape
    finer = jax.sharding.Mesh(mesh.devices.reshape(peers, spans // peers, peers), ("z", "y", "obs"))
    tm = ("z", "y")
    mapped = jax.shard_map(
        local,
        mesh=finer,
        in_specs=(
            P(("z", "y", "obs"), None),
            P(("z", "y", "obs")),
            P(("z", "y", "obs")),
            P(("z", "y", "obs")),
            P(),
            P(),
            P("obs", None),
            P(tm, None),
            P("obs"),
        ),
        out_specs=(P(tm, "obs"), P(tm, "obs")),
        check_vma=False,
    )
    return lambda *args: tuple(mapped(*args))
```

```python
import functools

import jax
import jax.numpy as jnp
from jax import lax
from jax.experimental import pallas as pl
from jax.experimental.pallas import tpu as pltpu
from jax.sharding import PartitionSpec as P

LANES = 128
F32, BF16 = jnp.float32, jnp.bfloat16
VMEM = pl.BlockSpec(memory_space=pltpu.VMEM)
SMEM = pl.BlockSpec(memory_space=pltpu.SMEM)
HBM = pl.BlockSpec(memory_space=pl.ANY)


def run(body, out, ins, scratch=(), limit=32, flops=0):
    specs = [x[1] if isinstance(x, tuple) else VMEM for x in ins]
    arrays = [x[0] if isinstance(x, tuple) else x for x in ins]
    moved = sum(a.size * a.dtype.itemsize for a in arrays)
    return pl.pallas_call(
        body,
        out_shape=[jax.ShapeDtypeStruct(s, d) for s, d in out],
        in_specs=specs,
        out_specs=[VMEM] * len(out),
        scratch_shapes=list(scratch),
        compiler_params=pltpu.CompilerParams(vmem_limit_bytes=limit * 1024 * 1024),
        cost_estimate=pl.CostEstimate(flops=flops, bytes_accessed=moved, transcendentals=0),
    )(*arrays)


def triangle(width):
    parts = width // LANES
    return [(i, j) for i in range(parts) for j in range(i + 1)]


def split(x):
    hi = x.astype(BF16)
    return hi, (x - hi.astype(F32)).astype(BF16)


def mm(x, hi, lo):
    xhi, xlo = split(x)
    dot = functools.partial(jnp.dot, preferred_element_type=F32)
    return dot(xhi, hi) + (dot(xlo, hi) + dot(xhi, lo))


def mv(x, hi, lo):
    wide = jnp.broadcast_to(x, (8, x.shape[1]))
    row = lax.broadcasted_iota(jnp.int32, wide.shape, 0)
    top = wide.astype(BF16).astype(F32)
    both = jnp.where(row == 0, top, jnp.where(row == 1, wide - top, 0.0)).astype(BF16)
    first = jnp.dot(both, hi, preferred_element_type=F32)
    second = jnp.dot(both, lo, preferred_element_type=F32)
    return first[0:1] + (first[1:2] + second[0:1])


def parts3(x):
    out = []
    for _ in range(3):
        piece = x.astype(BF16).astype(F32)
        out.append(piece)
        x = x - piece
    return out


def place(span):
    return span ^ (span >> 1)


def owner_plane(span):
    return 1 + place(span) % 2


EXTRA = 16


def pack_kernel(day, count, rows, values, prior, damping, out, day_s, count_s, values_v, prior_v, damping_v, sems):
    blocks = out.shape[0]
    slots = out.shape[1] - EXTRA
    width = out.shape[2]
    small = [(day, day_s), (count, count_s), (values, values_v), (prior, prior_v), (damping, damping_v)]
    copies = [pltpu.make_async_copy(src, dst, sems.at[n]) for n, (src, dst) in enumerate(small)]
    large = [
        pltpu.make_async_copy(
            rows.at[pl.ds(k * slots, slots)], out.at[place(k), pl.ds(0, slots)], sems.at[len(small) + k]
        )
        for k in range(blocks)
    ]
    for copy in copies + large:
        copy.start()
    for copy in copies:
        copy.wait()
    first, second, third = parts3(prior_v[...])
    below = jnp.concatenate(
        [jnp.concatenate([second, third, jnp.zeros((1, width - 2 * LANES), F32)], 1)]
        + parts3(damping_v[...])
        + [jnp.zeros((EXTRA - 8, width), F32)],
        0,
    )
    held = values_v[...].astype(F32)
    for k in range(blocks):
        line = jnp.concatenate(
            [
                held[k : k + 1, :],
                jnp.full((1, LANES), day_s[k], jnp.int32).astype(F32),
                jnp.full((1, LANES), count_s[k], jnp.int32).astype(F32),
                first,
            ],
            1,
        )
        out[place(k), slots : slots + EXTRA, :] = jnp.concatenate([line, below], 0).astype(BF16)
    for copy in large:
        copy.wait()


def gram_kernel(got, gain, own, extra, pay, prior, gain_out, turned, marks):
    blocks = got.shape[0]
    slots = got.shape[1] - EXTRA
    width = got.shape[2]
    chunks = width // LANES
    tiles = triangle(width)
    group = min(blocks, 8)
    half = 2 * LANES
    gain_out[...] = gain[...]

    def one(first, fresh):
        for k in range(group):
            at = slice(k * slots, (k + 1) * slots)
            line = got[first + k, slots : slots + EXTRA, :].astype(F32)
            valid = lax.broadcasted_iota(jnp.int32, (1, slots), 1).astype(F32) < line[0:1, 2 * LANES : 3 * LANES]
            day = line[0:1, LANES : 2 * LANES]
            values = line[0:1, 0:LANES]
            kept = [jnp.where(valid & (day == d), 1.0, 0.0) for d in (0.0, 1.0)]
            marks[:, at] = jnp.concatenate(
                kept + [kept[0] * values, kept[1] * values, jnp.zeros((12, slots), F32)], 0
            ).astype(BF16)
            turned[:, at] = got[first + k, 0:slots, :].T
        source = jnp.concatenate([got[first + k, 0:slots, :] for k in range(group)], 0)
        info = jnp.dot(marks[...], source, preferred_element_type=F32)
        for d in range(2):
            for top in range(0, width, half):
                left = turned[top : top + half, :] * marks[d : d + 1, :]
                block = jnp.dot(left, source[:, : top + half], preferred_element_type=F32)
                for n, (i, j) in enumerate(tiles):
                    if top <= i * LANES < top + half:
                        r = i * LANES - top
                        piece = block[r : r + LANES, j * LANES : (j + 1) * LANES]
                        at = d * len(tiles) + n
                        own[at] = piece if fresh else own[at] + piece
            for j in range(chunks):
                piece = info[2 + d : 3 + d, j * LANES : (j + 1) * LANES]
                r = 4 * d + j
                extra[r : r + 1, :] = piece if fresh else extra[r : r + 1, :] + piece

    if blocks == group:
        one(0, True)
    else:
        own[...] = jnp.zeros(own.shape, F32)
        extra[...] = jnp.zeros(extra.shape, F32)

        @pl.loop(0, blocks // group)
        def _(g):
            one(g * group, False)

    for n in range(own.shape[0]):
        pay[n] = own[n].astype(BF16)
    for q in range(chunks):
        line = got[q, slots : slots + EXTRA, :].astype(F32)
        prior[:, q * LANES : (q + 1) * LANES] = line[0:1, 3 * LANES : 4 * LANES] + (
            line[1:2, 0:LANES] + line[1:2, LANES : 2 * LANES]
        )
    for y in range(blocks // 4):
        line = got[4 * y, slots : slots + EXTRA, :].astype(F32)
        both = line[2:4] + (line[4:6] + line[6:8])
        for day in range(2):
            for j in range(chunks):
                r = 8 + 8 * y + 4 * day + j
                extra[r : r + 1, :] = both[day : day + 1, j * LANES : (j + 1) * LANES]


def prep_kernel(trans, cov, pt, pthi, ptlo, chi, clo):
    whole = trans[...].T
    pt[...] = whole
    pthi[...], ptlo[...] = split(whole)
    chi[...], clo[...] = split(cov[...])


def gain_kernel(after, ids, m0, m1, m2, m3, mthi, mtlo):
    rows = m0.shape[0]
    for step, part in enumerate((m0, m1, m2, m3)):
        holder = ids[2] ^ step
        at = pl.ds(pl.multiple_of(holder * rows, rows), rows)
        hi, lo = split(part[...].T)
        mthi[:, at] = hi
        mtlo[:, at] = lo


def two_days(state, damping, pthi, ptlo, omhi, omlo, info, chi, clo):
    for day in range(2):
        moved = mv(state, pthi[...], ptlo[...]) * damping[day : day + 1, :]
        gap = mv(moved, omhi[day], omlo[day]) - info[day]
        state = moved - mv(gap, chi[...], clo[...])
    return state


def owner_kernel(
    ids, own, g1, g2, g3, e0, e1, e2, e3, prior, pthi, ptlo, chi, clo, m1, m2, m3,
    omhi, omlo, info, mine, table, start, y,
):
    planes = 4
    width = pthi.shape[0]
    chunks = width // LANES
    tiles = triangle(width)
    for day in range(2):
        for n, (i, j) in enumerate(tiles):
            at = day * len(tiles) + n
            piece = own[at] + (g1[at].astype(F32) + (g2[at].astype(F32) + g3[at].astype(F32)))
            hi, lo = split(piece)
            omhi[day, i * LANES : (i + 1) * LANES, j * LANES : (j + 1) * LANES] = hi
            omlo[day, i * LANES : (i + 1) * LANES, j * LANES : (j + 1) * LANES] = lo
            if i != j:
                hi, lo = split(piece.T)
                omhi[day, j * LANES : (j + 1) * LANES, i * LANES : (i + 1) * LANES] = hi
                omlo[day, j * LANES : (j + 1) * LANES, i * LANES : (i + 1) * LANES] = lo

    def row(part, first):
        return jnp.concatenate([part[first + j : first + j + 1, :] for j in range(chunks)], 1)

    for day in range(2):
        info[day] = row(e0, 4 * day) + (row(e1, 4 * day) + (row(e2, 4 * day) + row(e3, 4 * day)))
    held = table.shape[0] // 2 // planes
    for s, part in enumerate((e0, e1, e2, e3)):
        plane = lax.rem(ids[0] + s, planes)
        for k in range(held):
            for day in range(2):
                table[pl.ds(2 * (plane * held + k) + day, 1), :] = row(part, 8 + 8 * k + 4 * day)
    for day in range(2):
        mine[day : day + 1, :] = table[pl.ds(2 * ids[1] + day, 1), :]
    state = prior[...]
    start[...] = jnp.where((ids[1] == 0) & (ids[0] == owner_plane(0)), state, 0.0)
    y[...] = two_days(state, mine, pthi, ptlo, omhi, omlo, info, chi, clo)


def direct_kernel(acc, got, mine, pthi, ptlo, omhi, omlo, info, chi, clo, total, y):
    state = acc[...] + got[...]
    total[...] = state
    y[...] = two_days(state, mine, pthi, ptlo, omhi, omlo, info, chi, clo)


def maps_kernel(after, omhi, omlo, info, chi, clo, pt, damping, b1hi, b1lo, b2hi, b2lo, bchi, bclo, off):
    parts = ((b1hi, b1lo), (b2hi, b2lo))
    for day in range(2):
        moved = pt[...] * damping[day : day + 1, :]
        taken = mm(moved, omhi[day], omlo[day])
        step = moved - mm(taken, chi[...], clo[...])
        parts[day][0][...], parts[day][1][...] = split(step)
        off[day : day + 1, :] = mv(info[day], chi[...], clo[...])
    both = jnp.dot(b1hi[...], b2hi[...], preferred_element_type=F32) + (
        jnp.dot(b1lo[...], b2hi[...], preferred_element_type=F32)
        + jnp.dot(b1hi[...], b2lo[...], preferred_element_type=F32)
    )
    bchi[...], bclo[...] = split(both)
    off[2:3, :] = mv(off[0:1, :], b2hi[...], b2lo[...]) + off[1:2, :]


def hop_kernel(after, acc, got, bchi, bclo, off, total, y):
    state = acc[...] + got[...]
    total[...] = state
    y[...] = mv(state, bchi[...], bclo[...]) + off[2:3, :]


def last_kernel(acc, got, b1hi, b1lo, b2hi, b2lo, off, out):
    state = acc[...] + got[...]
    one = mv(state, b1hi[...], b1lo[...]) + off[0:1, :]
    two = mv(one, b2hi[...], b2lo[...]) + off[1:2, :]
    both = jnp.concatenate([one, two], 0)
    for c in range(out.shape[0]):
        out[c] = both


def back_kernel(ids, states, table, pthi, ptlo, mthi, mtlo, filt, smooth, f, d, const):
    total, width = f.shape
    spans = total // 2
    chunks = width // LANES
    for c in range(spans):
        f[2 * c : 2 * c + 2, :] = states[owner_plane(c) * spans + place(c)]
    d[0 : total - 1, :] = table[1:total, :]
    d[total - 1 : total, :] = jnp.zeros((1, width), F32)
    ahead = d[...] * mm(f[...], pthi[...], ptlo[...])
    const[...] = f[...] - mm(d[...] * ahead, mthi[...], mtlo[...])

    def step(k, state):
        t = total - 2 - k
        new = const[pl.ds(t, 1), :] + mv(d[pl.ds(t, 1), :] * state, mthi[...], mtlo[...])
        const[pl.ds(t, 1), :] = new
        return new

    lax.fori_loop(0, total - 1, step, const[total - 1 : total, :], unroll=total <= 16)
    for k in range(2):
        row = pl.ds(ids[3] * 2 + k, 1)
        for whole, out in ((f, filt), (const, smooth)):
            line = whole[row, :]
            mine = line[:, 0:LANES]
            for q in range(1, chunks):
                mine = jnp.where(ids[2] == q, line[:, q * LANES : (q + 1) * LANES], mine)
            out[k : k + 1, :] = mine


def local(
    records,
    obs_values,
    block_day,
    block_count,
    propagator_matrix,
    analysis_cov,
    unattenuated_multiplier,
    damping,
    prior_mean,
):
    planes, held, peers = (lax.axis_size(a) for a in ("z", "y", "obs"))
    spans = planes * held
    blocks = block_day.shape[0]
    slots = records.shape[0] // blocks
    width = records.shape[1]
    days = damping.shape[0]
    assert planes == peers == 4 and days == 2 and slots == LANES and blocks == spans
    z, y, o = (lax.axis_index(a) for a in ("z", "y", "obs"))
    at = y * peers + o
    span = at
    for bit in range(1, spans.bit_length()):
        span = span ^ (at >> bit)
    ids = jnp.stack([z, span, o, z * held + y]).astype(jnp.int32)
    everyone = ("z", "y", "obs")

    def owner(span):
        return owner_plane(span) * spans + place(span)

    tiles = len(triangle(width))
    full, row = (width, width), ((1, width), F32)
    (sent,) = run(
        pack_kernel,
        [((blocks, slots + EXTRA, width), BF16)],
        [
            (x, HBM)
            for x in (
                block_day,
                block_count,
                records,
                obs_values.reshape(blocks, slots),
                prior_mean.reshape(1, -1),
                damping,
            )
        ],
        [
            pltpu.SMEM((blocks,), jnp.int32),
            pltpu.SMEM((blocks,), jnp.int32),
            pltpu.VMEM((blocks, slots), BF16),
            pltpu.VMEM((1, width // peers), F32),
            pltpu.VMEM((days, width), F32),
            pltpu.SemaphoreType.DMA((5 + blocks,)),
        ],
    )
    got = lax.all_to_all(sent, ("y", "obs"), split_axis=0, concat_axis=0, tiled=True)
    span_slots = min(blocks, 8) * slots
    own, extra, pay, prior, gain = run(
        gram_kernel,
        [
            ((2 * tiles, LANES, LANES), F32),
            ((8 + 8 * held, LANES), F32),
            ((2 * tiles, LANES, LANES), BF16),
            row,
            (unattenuated_multiplier.shape, F32),
        ],
        [got, unattenuated_multiplier],
        [pltpu.VMEM((width, span_slots), BF16), pltpu.VMEM((16, span_slots), BF16)],
        flops=4 * width * width * blocks * slots,
    )
    plane_sums = [
        lax.ppermute(
            pay, everyone, [((owner_plane(p) + s) % planes * spans + place(p), owner(p)) for p in range(spans)]
        )
        for s in range(1, planes)
    ]
    extras = [extra] + [
        lax.ppermute(extra, "z", [((i + s) % planes, i) for i in range(planes)]) for s in range(1, planes)
    ]

    def swap(x, bit):
        return lax.ppermute(x, "obs", [(i, i ^ bit) for i in range(peers)])

    across = swap(gain, 2)
    gains = [gain, swap(gain, 1), across, swap(across, 1)]
    pt, pthi, ptlo, chi, clo = run(
        prep_kernel, [(full, F32)] + [(full, BF16)] * 4, [propagator_matrix, analysis_cov]
    )
    omhi, omlo, info, mine, table, acc, y = run(
        owner_kernel,
        [((days,) + full, BF16)] * 2
        + [((days, 1, width), F32), ((days, width), F32), ((spans * days, width), F32), row, row],
        [(ids, SMEM), own, *plane_sums, *extras, prior, pthi, ptlo, chi, clo, *[(g, HBM) for g in gains[1:]]],
    )
    for k in range(spans - 1):
        received = lax.ppermute(y, everyone, [(owner(k), owner(k + 1))])
        if k == 0:
            acc, y = run(
                direct_kernel, [row, row], [acc, received, mine, pthi, ptlo, omhi, omlo, info, chi, clo]
            )
            b1hi, b1lo, b2hi, b2lo, bchi, bclo, off = run(
                maps_kernel,
                [(full, BF16)] * 6 + [((8, width), F32)],
                [y, omhi, omlo, info, chi, clo, pt, mine],
                flops=30 * width**3,
            )
            side = y
        elif k < spans - 2:
            acc, y = run(hop_kernel, [row, row], [(side, HBM), acc, received, bchi, bclo, off])
            if k == 2:
                mthi, mtlo = run(gain_kernel, [(full, BF16)] * 2, [(y, HBM), (ids, SMEM), *gains])
                side = mthi
    (answer,) = run(
        last_kernel,
        [((spans * peers, days, width), F32)],
        [acc, received, b1hi, b1lo, b2hi, b2lo, off],
    )
    states = lax.all_to_all(answer, everyone, split_axis=0, concat_axis=0, tiled=True)
    out = ((days, LANES), F32)
    return run(
        back_kernel,
        [out, out],
        [(ids, SMEM), states, table, pthi, ptlo, mthi, mtlo],
        [pltpu.VMEM((spans * days, width), F32)] * 3,
    )


def solution(mesh):
    spans, peers = mesh.devices.shape
    finer = jax.sharding.Mesh(mesh.devices.reshape(peers, spans // peers, peers), ("z", "y", "obs"))
    tm = ("z", "y")
    mapped = jax.shard_map(
        local,
        mesh=finer,
        in_specs=(
            P(("z", "y", "obs"), None),
            P(("z", "y", "obs")),
            P(("z", "y", "obs")),
            P(("z", "y", "obs")),
            P(),
            P(),
            P("obs", None),
            P(tm, None),
            P("obs"),
        ),
        out_specs=(P(tm, "obs"), P(tm, "obs")),
        check_vma=False,
    )
    return lambda *args: tuple(mapped(*args))
```

```python
import functools

import jax
import jax.numpy as jnp
from jax import lax
from jax.experimental import pallas as pl
from jax.experimental.pallas import tpu as pltpu
from jax.sharding import PartitionSpec as P

LANES = 128
F32, BF16 = jnp.float32, jnp.bfloat16
VMEM = pl.BlockSpec(memory_space=pltpu.VMEM)
SMEM = pl.BlockSpec(memory_space=pltpu.SMEM)
ANY = pl.BlockSpec(memory_space=pl.ANY)
HBM = pl.BlockSpec(memory_space=pltpu.HBM)


def run(body, out, ins, scratch=(), limit=32, flops=0):
    specs = [x[1] if isinstance(x, tuple) else VMEM for x in ins]
    arrays = [x[0] if isinstance(x, tuple) else x for x in ins]
    moved = sum(a.size * a.dtype.itemsize for a in arrays)
    return pl.pallas_call(
        body,
        out_shape=[jax.ShapeDtypeStruct(s, d) for s, d in out],
        in_specs=specs,
        out_specs=[VMEM] * len(out),
        scratch_shapes=list(scratch),
        compiler_params=pltpu.CompilerParams(vmem_limit_bytes=limit * 1024 * 1024),
        cost_estimate=pl.CostEstimate(flops=flops, bytes_accessed=moved, transcendentals=0),
    )(*arrays)


def triangle(width):
    parts = width // LANES
    return [(i, j) for i in range(parts) for j in range(i + 1)]


def split(x):
    hi = x.astype(BF16)
    return hi, (x - hi.astype(F32)).astype(BF16)


def mm(x, hi, lo):
    xhi, xlo = split(x)
    dot = functools.partial(jnp.dot, preferred_element_type=F32)
    return dot(xhi, hi) + (dot(xlo, hi) + dot(xhi, lo))


def mv(x, hi, lo):
    wide = jnp.broadcast_to(x, (8, x.shape[1]))
    row = lax.broadcasted_iota(jnp.int32, wide.shape, 0)
    top = wide.astype(BF16).astype(F32)
    both = jnp.where(row == 0, top, jnp.where(row == 1, wide - top, 0.0)).astype(BF16)
    first = jnp.dot(both, hi, preferred_element_type=F32)
    second = jnp.dot(both, lo, preferred_element_type=F32)
    return first[0:1] + (first[1:2] + second[0:1])


def parts3(x):
    out = []
    for _ in range(3):
        piece = x.astype(BF16).astype(F32)
        out.append(piece)
        x = x - piece
    return out


def place(span):
    return span ^ (span >> 1)


def owner_plane(span):
    return 1 + place(span) % 2


EXTRA = 16


def pack_kernel(day, count, rows, values, prior, damping, out, day_s, count_s, values_v, prior_v, damping_v, sems):
    blocks = out.shape[0]
    slots = out.shape[1] - EXTRA
    width = out.shape[2]
    small = [(day, day_s), (count, count_s), (values, values_v), (prior, prior_v), (damping, damping_v)]
    copies = [pltpu.make_async_copy(src, dst, sems.at[n]) for n, (src, dst) in enumerate(small)]
    large = [
        pltpu.make_async_copy(
            rows.at[pl.ds(k * slots, slots)], out.at[place(k), pl.ds(0, slots)], sems.at[len(small) + k]
        )
        for k in range(blocks)
    ]
    for copy in copies + large:
        copy.start()
    for copy in copies:
        copy.wait()
    first, second, third = parts3(prior_v[...])
    below = jnp.concatenate(
        [jnp.concatenate([second, third, jnp.zeros((1, width - 2 * LANES), F32)], 1)]
        + parts3(damping_v[...])
        + [jnp.zeros((EXTRA - 8, width), F32)],
        0,
    )
    held = values_v[...].astype(F32)
    for k in range(blocks):
        line = jnp.concatenate(
            [
                held[k : k + 1, :],
                jnp.full((1, LANES), day_s[k], jnp.int32).astype(F32),
                jnp.full((1, LANES), count_s[k], jnp.int32).astype(F32),
                first,
            ],
            1,
        )
        out[place(k), slots : slots + EXTRA, :] = jnp.concatenate([line, below], 0).astype(BF16)
    for copy in large:
        copy.wait()


def gram_kernel(got, gain, own, extra, pay, prior, gain_out, turned, marks):
    blocks = got.shape[0]
    slots = got.shape[1] - EXTRA
    width = got.shape[2]
    chunks = width // LANES
    tiles = triangle(width)
    group = min(blocks, 8)
    half = 2 * LANES
    gain_out[...] = gain[...]
    extra[...] = jnp.zeros(extra.shape, F32)

    def one(first, fresh):
        for k in range(group):
            at = slice(k * slots, (k + 1) * slots)
            line = got[first + k, slots : slots + EXTRA, :].astype(F32)
            valid = lax.broadcasted_iota(jnp.int32, (1, slots), 1).astype(F32) < line[0:1, 2 * LANES : 3 * LANES]
            day = line[0:1, LANES : 2 * LANES]
            values = line[0:1, 0:LANES]
            kept = [jnp.where(valid & (day == d), 1.0, 0.0) for d in (0.0, 1.0)]
            marks[:, at] = jnp.concatenate(
                kept + [kept[0] * values, kept[1] * values, jnp.zeros((12, slots), F32)], 0
            ).astype(BF16)
            turned[:, at] = got[first + k, 0:slots, :].T
        source = jnp.concatenate([got[first + k, 0:slots, :] for k in range(group)], 0)
        info = jnp.dot(marks[...], source, preferred_element_type=F32)
        for d in range(2):
            for top in range(0, width, half):
                left = turned[top : top + half, :] * marks[d : d + 1, :]
                block = jnp.dot(left, source[:, : top + half], preferred_element_type=F32)
                for n, (i, j) in enumerate(tiles):
                    if top <= i * LANES < top + half:
                        r = i * LANES - top
                        piece = block[r : r + LANES, j * LANES : (j + 1) * LANES]
                        at = d * len(tiles) + n
                        own[at] = piece if fresh else own[at] + piece
            for j in range(chunks):
                piece = info[2 + d : 3 + d, j * LANES : (j + 1) * LANES]
                r = 12 * d + j
                extra[r : r + 1, :] = piece if fresh else extra[r : r + 1, :] + piece

    if blocks == group:
        one(0, True)
    else:
        own[...] = jnp.zeros(own.shape, F32)

        @pl.loop(0, blocks // group)
        def _(g):
            one(g * group, False)

    for d in range(2):
        for part, piece in enumerate(parts3(extra[12 * d : 12 * d + chunks, :])):
            extra[12 * d + 4 * part : 12 * d + 4 * part + chunks, :] = piece
    for q in range(chunks):
        line = got[q, slots : slots + EXTRA, :].astype(F32)
        prior[:, q * LANES : (q + 1) * LANES] = line[0:1, 3 * LANES : 4 * LANES] + (
            line[1:2, 0:LANES] + line[1:2, LANES : 2 * LANES]
        )
    for y in range(blocks // 4):
        line = got[4 * y, slots : slots + EXTRA, :].astype(F32)
        for k in range(6):
            for j in range(chunks):
                r = 24 + 24 * y + 4 * k + j
                extra[r : r + 1, :] = line[2 + k : 3 + k, j * LANES : (j + 1) * LANES]
    for n in range(own.shape[0]):
        pay[n] = own[n].astype(BF16)
    for n in range(extra.shape[0] // LANES):
        pay[own.shape[0] + n] = extra[n * LANES : (n + 1) * LANES, :].astype(BF16)


def prep_kernel(trans, cov, pt, pthi, ptlo, chi, clo):
    whole = trans[...].T
    pt[...] = whole
    pthi[...], ptlo[...] = split(whole)
    chi[...], clo[...] = split(cov[...])


def gain_kernel(after, ids, m0, m1, m2, m3, mthi, mtlo):
    rows = m0.shape[0]
    for step, part in enumerate((m0, m1, m2, m3)):
        holder = ids[2] ^ step
        at = pl.ds(pl.multiple_of(holder * rows, rows), rows)
        hi, lo = split(part[...].T)
        mthi[:, at] = hi
        mtlo[:, at] = lo


def two_days(state, damping, pthi, ptlo, omhi, omlo, info, chi, clo):
    for day in range(2):
        moved = mv(state, pthi[...], ptlo[...]) * damping[day : day + 1, :]
        gap = mv(moved, omhi[day], omlo[day]) - info[day]
        state = moved - mv(gap, chi[...], clo[...])
    return state


def owner_kernel(
    ids, own, extra, g1, g2, g3, prior, pthi, ptlo, chi, clo, m1, m2, m3,
    omhi, omlo, info, mine, start, y, table, small,
):
    planes = 4
    width = pthi.shape[0]
    chunks = width // LANES
    tiles = triangle(width)
    got = (g1, g2, g3)
    for day in range(2):
        for n, (i, j) in enumerate(tiles):
            at = day * len(tiles) + n
            piece = own[at] + (g1[at].astype(F32) + (g2[at].astype(F32) + g3[at].astype(F32)))
            hi, lo = split(piece)
            omhi[day, i * LANES : (i + 1) * LANES, j * LANES : (j + 1) * LANES] = hi
            omlo[day, i * LANES : (i + 1) * LANES, j * LANES : (j + 1) * LANES] = lo
            if i != j:
                hi, lo = split(piece.T)
                omhi[day, j * LANES : (j + 1) * LANES, i * LANES : (i + 1) * LANES] = hi
                omlo[day, j * LANES : (j + 1) * LANES, i * LANES : (i + 1) * LANES] = lo
    for s in range(planes):
        if s == 0:
            small[0] = extra[...]
        else:
            for n in range(extra.shape[0] // LANES):
                small[s, n * LANES : (n + 1) * LANES, :] = got[s - 1][own.shape[0] + n].astype(F32)

    def row(s, first, gap):
        return jnp.concatenate(
            [
                small[s, first + j : first + j + 1, :]
                + (
                    small[s, first + gap + j : first + gap + j + 1, :]
                    + small[s, first + 2 * gap + j : first + 2 * gap + j + 1, :]
                )
                for j in range(chunks)
            ],
            1,
        )

    for day in range(2):
        info[day] = row(0, 12 * day, 4) + (row(1, 12 * day, 4) + (row(2, 12 * day, 4) + row(3, 12 * day, 4)))
    held = table.shape[0] // 2 // planes
    for s in range(planes):
        plane = lax.rem(ids[0] + s, planes)
        for k in range(held):
            for day in range(2):
                table[pl.ds(2 * (plane * held + k) + day, 1), :] = row(s, 24 + 24 * k + 4 * day, 8)
    for day in range(2):
        mine[day : day + 1, :] = table[pl.ds(2 * ids[1] + day, 1), :]
    state = prior[...]
    start[...] = jnp.where((ids[1] == 0) & (ids[0] == owner_plane(0)), state, 0.0)
    y[...] = two_days(state, mine, pthi, ptlo, omhi, omlo, info, chi, clo)


def direct_kernel(acc, got, mine, pthi, ptlo, omhi, omlo, info, chi, clo, total, y):
    state = acc[...] + got[...]
    total[...] = state
    y[...] = two_days(state, mine, pthi, ptlo, omhi, omlo, info, chi, clo)


def maps_kernel(after, omhi, omlo, info, chi, clo, pt, damping, b1hi, b1lo, b2hi, b2lo, bchi, bclo, off):
    parts = ((b1hi, b1lo), (b2hi, b2lo))
    for day in range(2):
        moved = pt[...] * damping[day : day + 1, :]
        taken = mm(moved, omhi[day], omlo[day])
        step = moved - mm(taken, chi[...], clo[...])
        parts[day][0][...], parts[day][1][...] = split(step)
        off[day : day + 1, :] = mv(info[day], chi[...], clo[...])
    both = jnp.dot(b1hi[...], b2hi[...], preferred_element_type=F32) + (
        jnp.dot(b1lo[...], b2hi[...], preferred_element_type=F32)
        + jnp.dot(b1hi[...], b2lo[...], preferred_element_type=F32)
    )
    bchi[...], bclo[...] = split(both)
    off[2:3, :] = mv(off[0:1, :], b2hi[...], b2lo[...]) + off[1:2, :]


def hop_kernel(after, acc, got, bchi, bclo, off, total, y):
    state = acc[...] + got[...]
    total[...] = state
    y[...] = mv(state, bchi[...], bclo[...]) + off[2:3, :]


def last_kernel(acc, got, b1hi, b1lo, b2hi, b2lo, off, damping, out):
    state = acc[...] + got[...]
    one = mv(state, b1hi[...], b1lo[...]) + off[0:1, :]
    two = mv(one, b2hi[...], b2lo[...]) + off[1:2, :]
    both = jnp.concatenate([one, two, damping[...]], 0)
    for c in range(out.shape[0]):
        out[c] = both


def back_kernel(ids, states, pthi, ptlo, mthi, mtlo, filt, smooth, f, d, const):
    total, width = f.shape
    spans = total // 2
    chunks = width // LANES
    for c in range(spans):
        one = states[owner_plane(c) * spans + place(c)]
        f[2 * c : 2 * c + 2, :] = one[0:2]
        if c:
            d[2 * c - 1 : 2 * c + 1, :] = one[2:4]
        else:
            d[0:1, :] = one[3:4]
    d[total - 1 : total, :] = jnp.zeros((1, width), F32)
    ahead = d[...] * mm(f[...], pthi[...], ptlo[...])
    const[...] = f[...] - mm(d[...] * ahead, mthi[...], mtlo[...])

    def step(k, state):
        t = total - 2 - k
        new = const[pl.ds(t, 1), :] + mv(d[pl.ds(t, 1), :] * state, mthi[...], mtlo[...])
        const[pl.ds(t, 1), :] = new
        return new

    lax.fori_loop(0, total - 1, step, const[total - 1 : total, :], unroll=total <= 16)
    for k in range(2):
        row = pl.ds(ids[3] * 2 + k, 1)
        for whole, out in ((f, filt), (const, smooth)):
            line = whole[row, :]
            mine = line[:, 0:LANES]
            for q in range(1, chunks):
                mine = jnp.where(ids[2] == q, line[:, q * LANES : (q + 1) * LANES], mine)
            out[k : k + 1, :] = mine


def local(
    records,
    obs_values,
    block_day,
    block_count,
    propagator_matrix,
    analysis_cov,
    unattenuated_multiplier,
    damping,
    prior_mean,
):
    planes, held, peers = (lax.axis_size(a) for a in ("z", "y", "obs"))
    spans = planes * held
    blocks = block_day.shape[0]
    slots = records.shape[0] // blocks
    width = records.shape[1]
    days = damping.shape[0]
    assert planes == peers == 4 and days == 2 and slots == LANES and blocks == spans
    z, y, o = (lax.axis_index(a) for a in ("z", "y", "obs"))
    at = y * peers + o
    span = at
    for bit in range(1, spans.bit_length()):
        span = span ^ (at >> bit)
    ids = jnp.stack([z, span, o, z * held + y]).astype(jnp.int32)
    everyone = ("z", "y", "obs")

    def owner(span):
        return owner_plane(span) * spans + place(span)

    tiles = len(triangle(width))
    extra_tiles = -(-(24 + 24 * held) // LANES)
    full, row = (width, width), ((1, width), F32)
    (sent,) = run(
        pack_kernel,
        [((blocks, slots + EXTRA, width), BF16)],
        [
            (x, HBM)
            for x in (
                block_day,
                block_count,
                records,
                obs_values.reshape(blocks, slots),
                prior_mean.reshape(1, -1),
                damping,
            )
        ],
        [
            pltpu.SMEM((blocks,), jnp.int32),
            pltpu.SMEM((blocks,), jnp.int32),
            pltpu.VMEM((blocks, slots), BF16),
            pltpu.VMEM((1, width // peers), F32),
            pltpu.VMEM((days, width), F32),
            pltpu.SemaphoreType.DMA((5 + blocks,)),
        ],
        limit=60,
    )
    got = lax.all_to_all(sent, ("y", "obs"), split_axis=0, concat_axis=0, tiled=True)
    span_slots = min(blocks, 8) * slots
    own, extra, pay, prior, gain = run(
        gram_kernel,
        [
            ((2 * tiles, LANES, LANES), F32),
            ((extra_tiles * LANES, LANES), F32),
            ((2 * tiles + extra_tiles, LANES, LANES), BF16),
            row,
            (unattenuated_multiplier.shape, F32),
        ],
        [got, unattenuated_multiplier],
        [pltpu.VMEM((width, span_slots), BF16), pltpu.VMEM((16, span_slots), BF16)],
        flops=4 * width * width * blocks * slots,
    )
    plane_sums = [
        lax.ppermute(
            pay, everyone, [((owner_plane(p) + s) % planes * spans + place(p), owner(p)) for p in range(spans)]
        )
        for s in range(1, planes)
    ]
    def swap(x, bit):
        return lax.ppermute(x, "obs", [(i, i ^ bit) for i in range(peers)])

    across = swap(gain, 2)
    gains = [gain, swap(gain, 1), across, swap(across, 1)]
    pt, pthi, ptlo, chi, clo = run(
        prep_kernel, [(full, F32)] + [(full, BF16)] * 4, [propagator_matrix, analysis_cov]
    )
    omhi, omlo, info, mine, acc, y = run(
        owner_kernel,
        [((days,) + full, BF16)] * 2
        + [((days, 1, width), F32), ((days, width), F32), row, row],
        [(ids, SMEM), own, extra, *plane_sums, prior, pthi, ptlo, chi, clo, *[(g, ANY) for g in gains[1:]]],
        [pltpu.VMEM((spans * days, width), F32), pltpu.VMEM((planes, extra_tiles * LANES, LANES), F32)],
    )
    for k in range(spans - 1):
        received = lax.ppermute(y, everyone, [(owner(k), owner(k + 1))])
        if k == 0:
            acc, y = run(
                direct_kernel, [row, row], [acc, received, mine, pthi, ptlo, omhi, omlo, info, chi, clo]
            )
            b1hi, b1lo, b2hi, b2lo, bchi, bclo, off = run(
                maps_kernel,
                [(full, BF16)] * 6 + [((8, width), F32)],
                [y, omhi, omlo, info, chi, clo, pt, mine],
                flops=30 * width**3,
            )
            side = y
        elif k < spans - 2:
            acc, y = run(hop_kernel, [row, row], [(side, ANY), acc, received, bchi, bclo, off])
            if k == 2:
                mthi, mtlo = run(gain_kernel, [(full, BF16)] * 2, [(y, ANY), (ids, SMEM), *gains])
                side = mthi
    (answer,) = run(
        last_kernel,
        [((spans * peers, 2 * days, width), F32)],
        [acc, received, b1hi, b1lo, b2hi, b2lo, off, mine],
    )
    states = lax.all_to_all(answer, everyone, split_axis=0, concat_axis=0, tiled=True)
    out = ((days, LANES), F32)
    return run(
        back_kernel,
        [out, out],
        [(ids, SMEM), states, pthi, ptlo, mthi, mtlo],
        [pltpu.VMEM((spans * days, width), F32)] * 3,
    )


def solution(mesh):
    spans, peers = mesh.devices.shape
    finer = jax.sharding.Mesh(mesh.devices.reshape(peers, spans // peers, peers), ("z", "y", "obs"))
    tm = ("z", "y")
    mapped = jax.shard_map(
        local,
        mesh=finer,
        in_specs=(
            P(("z", "y", "obs"), None),
            P(("z", "y", "obs")),
            P(("z", "y", "obs")),
            P(("z", "y", "obs")),
            P(),
            P(),
            P("obs", None),
            P(tm, None),
            P("obs"),
        ),
        out_specs=(P(tm, "obs"), P(tm, "obs")),
        check_vma=False,
    )
    return lambda *args: tuple(mapped(*args))
```

```python
import functools

import jax
import jax.numpy as jnp
from jax import lax
from jax.experimental import pallas as pl
from jax.experimental.pallas import tpu as pltpu
from jax.sharding import PartitionSpec as P

LANES = 128
F32, BF16 = jnp.float32, jnp.bfloat16
VMEM = pl.BlockSpec(memory_space=pltpu.VMEM)
SMEM = pl.BlockSpec(memory_space=pltpu.SMEM)
ANY = pl.BlockSpec(memory_space=pl.ANY)
HBM = pl.BlockSpec(memory_space=pltpu.HBM)


def run(body, out, ins, scratch=(), limit=32, flops=0, outs=VMEM):
    specs = [x[1] if isinstance(x, tuple) else VMEM for x in ins]
    arrays = [x[0] if isinstance(x, tuple) else x for x in ins]
    moved = sum(a.size * a.dtype.itemsize for a in arrays)
    return pl.pallas_call(
        body,
        out_shape=[jax.ShapeDtypeStruct(s, d) for s, d in out],
        in_specs=specs,
        out_specs=[outs] * len(out),
        scratch_shapes=list(scratch),
        compiler_params=pltpu.CompilerParams(vmem_limit_bytes=limit * 1024 * 1024),
        cost_estimate=pl.CostEstimate(flops=flops, bytes_accessed=moved, transcendentals=0),
    )(*arrays)


def triangle(width):
    parts = width // LANES
    return [(i, j) for i in range(parts) for j in range(i + 1)]


def split(x):
    hi = x.astype(BF16)
    return hi, (x - hi.astype(F32)).astype(BF16)


def mm(x, hi, lo):
    xhi, xlo = split(x)
    dot = functools.partial(jnp.dot, preferred_element_type=F32)
    return dot(xhi, hi) + (dot(xlo, hi) + dot(xhi, lo))


def mv(x, hi, lo):
    wide = jnp.broadcast_to(x, (8, x.shape[1]))
    row = lax.broadcasted_iota(jnp.int32, wide.shape, 0)
    top = wide.astype(BF16).astype(F32)
    both = jnp.where(row == 0, top, jnp.where(row == 1, wide - top, 0.0)).astype(BF16)
    first = jnp.dot(both, hi, preferred_element_type=F32)
    second = jnp.dot(both, lo, preferred_element_type=F32)
    return first[0:1] + (first[1:2] + second[0:1])


def parts3(x):
    out = []
    for _ in range(3):
        piece = x.astype(BF16).astype(F32)
        out.append(piece)
        x = x - piece
    return out


def place(span):
    return span ^ (span >> 1)


def owner_plane(span):
    return 1 + place(span) % 2


EXTRA = 8
DIAG, DAMP = 24, 48


def pack_kernel(
    day, count, rows, values, prior, damping, out, day_s, count_s, values_v, prior_v, damping_v, meta, sems
):
    blocks = out.shape[0]
    slots = out.shape[1] - EXTRA
    width = out.shape[2]
    small = [(day, day_s), (count, count_s), (values, values_v), (prior, prior_v), (damping, damping_v)]
    copies = [pltpu.make_async_copy(src, dst, sems.at[n]) for n, (src, dst) in enumerate(small)]
    large = [
        pltpu.make_async_copy(
            rows.at[pl.ds(k * slots, slots)], out.at[place(k), pl.ds(0, slots)], sems.at[len(small) + k]
        )
        for k in range(blocks)
    ]
    for copy in copies + large:
        copy.start()
    for copy in copies:
        copy.wait()
    first, second, third = parts3(prior_v[...])
    below = jnp.concatenate(
        [jnp.concatenate([second, third, jnp.zeros((1, width - 2 * LANES), F32)], 1)] + parts3(damping_v[...]), 0
    )
    held = values_v[...].astype(F32)
    for k in range(blocks):
        line = jnp.concatenate(
            [
                held[k : k + 1, :],
                jnp.full((1, LANES), day_s[k], jnp.int32).astype(F32),
                jnp.full((1, LANES), count_s[k], jnp.int32).astype(F32),
                first,
            ],
            1,
        )
        meta[place(k)] = jnp.concatenate([line, below], 0).astype(BF16)
    tail = pltpu.make_async_copy(meta, out.at[:, pl.ds(slots, EXTRA)], sems.at[len(small) + blocks])
    tail.start()
    for copy in large + [tail]:
        copy.wait()


def gram_kernel(got, gain, own, extra, pay, prior, gain_out, turned, marks):
    blocks = got.shape[0]
    slots = got.shape[1] - EXTRA
    width = got.shape[2]
    chunks = width // LANES
    tiles = triangle(width)
    group = min(blocks, 8)
    half = 2 * LANES
    gain_out[...] = gain[...]
    extra[...] = jnp.zeros(extra.shape, F32)

    def one(first, fresh):
        for k in range(group):
            at = slice(k * slots, (k + 1) * slots)
            line = got[first + k, slots : slots + EXTRA, :].astype(F32)
            valid = lax.broadcasted_iota(jnp.int32, (1, slots), 1).astype(F32) < line[0:1, 2 * LANES : 3 * LANES]
            day = line[0:1, LANES : 2 * LANES]
            values = line[0:1, 0:LANES]
            kept = [jnp.where(valid & (day == d), 1.0, 0.0) for d in (0.0, 1.0)]
            marks[:, at] = jnp.concatenate(
                kept + [kept[0] * values, kept[1] * values, jnp.zeros((12, slots), F32)], 0
            ).astype(BF16)
            turned[:, at] = got[first + k, 0:slots, :].T
        source = jnp.concatenate([got[first + k, 0:slots, :] for k in range(group)], 0)
        info = jnp.dot(marks[...], source, preferred_element_type=F32)
        for d in range(2):
            for top in range(0, width, half):
                left = turned[top : top + half, :] * marks[d : d + 1, :]
                block = jnp.dot(left, source[:, : top + half], preferred_element_type=F32)
                for n, (i, j) in enumerate(tiles):
                    if top <= i * LANES < top + half:
                        r = i * LANES - top
                        piece = block[r : r + LANES, j * LANES : (j + 1) * LANES]
                        at = d * len(tiles) + n
                        own[at] = piece if fresh else own[at] + piece
            for j in range(chunks):
                piece = info[2 + d : 3 + d, j * LANES : (j + 1) * LANES]
                r = 12 * d + j
                extra[r : r + 1, :] = piece if fresh else extra[r : r + 1, :] + piece

    if blocks == group:
        one(0, True)
    else:
        own[...] = jnp.zeros(own.shape, F32)

        @pl.loop(0, blocks // group)
        def _(g):
            one(g * group, False)

    row = lax.broadcasted_iota(jnp.int32, (LANES, LANES), 0)
    column = lax.broadcasted_iota(jnp.int32, (LANES, LANES), 1)
    sides = [n for n, (i, j) in enumerate(tiles) if i != j]
    middles = [n for n, (i, j) in enumerate(tiles) if i == j]
    for d in range(2):
        for part, piece in enumerate(parts3(extra[12 * d : 12 * d + chunks, :])):
            extra[12 * d + 4 * part : 12 * d + 4 * part + chunks, :] = piece
        for m, n in enumerate(sides):
            pay[d * len(sides) + m] = own[d * len(tiles) + n].astype(BF16)
    for i, n in enumerate(middles):
        squares = [own[d * len(tiles) + n] for d in range(2)]
        pay[2 * len(sides) + i] = jnp.where(row >= column, squares[0], squares[1]).astype(BF16)
        for d in range(2):
            line = jnp.sum(jnp.where(row == column, squares[d], 0.0), axis=0, keepdims=True)
            for part, piece in enumerate(parts3(line)):
                r = DIAG + 12 * d + 4 * part + i
                extra[r : r + 1, :] = piece
    for q in range(chunks):
        line = got[q, slots : slots + EXTRA, :].astype(F32)
        prior[:, q * LANES : (q + 1) * LANES] = line[0:1, 3 * LANES : 4 * LANES] + (
            line[1:2, 0:LANES] + line[1:2, LANES : 2 * LANES]
        )
    for y in range(blocks // 4):
        line = got[4 * y, slots : slots + EXTRA, :].astype(F32)
        for k in range(6):
            for j in range(chunks):
                r = DAMP + 24 * y + 4 * k + j
                extra[r : r + 1, :] = line[2 + k : 3 + k, j * LANES : (j + 1) * LANES]
    small_at = pay.shape[0] - extra.shape[0] // LANES
    for n in range(extra.shape[0] // LANES):
        pay[small_at + n] = extra[n * LANES : (n + 1) * LANES, :].astype(BF16)


def prep_kernel(trans, cov, pt, pthi, ptlo, chi, clo):
    whole = trans[...].T
    pt[...] = whole
    pthi[...], ptlo[...] = split(whole)
    chi[...], clo[...] = split(cov[...])


def gain_kernel(after, ids, m0, m1, m2, m3, mthi, mtlo):
    rows = m0.shape[0]
    for step, part in enumerate((m0, m1, m2, m3)):
        holder = ids[2] ^ step
        at = pl.ds(pl.multiple_of(holder * rows, rows), rows)
        hi, lo = split(part[...].T)
        mthi[:, at] = hi
        mtlo[:, at] = lo


def two_days(state, damping, pthi, ptlo, omhi, omlo, info, chi, clo):
    for day in range(2):
        moved = mv(state, pthi[...], ptlo[...]) * damping[day : day + 1, :]
        gap = mv(moved, omhi[day], omlo[day]) - info[day]
        state = moved - mv(gap, chi[...], clo[...])
    return state


def owner_kernel(
    ids, own, extra, g1, g2, g3, g4, prior, pthi, ptlo, chi, clo, m1, m2, m3,
    omhi, omlo, info, mine, start, y, table, small,
):
    planes = 4
    width = pthi.shape[0]
    chunks = width // LANES
    tiles = triangle(width)
    got = (g1, g2, g3, g4)
    share = jnp.where(ids[0] == 2, 1.0, 0.0)
    row = lax.broadcasted_iota(jnp.int32, (LANES, LANES), 0)
    column = lax.broadcasted_iota(jnp.int32, (LANES, LANES), 1)
    small_at = g1.shape[0] - extra.shape[0] // LANES
    small[0] = extra[...]
    for s, part in enumerate(got):
        for n in range(extra.shape[0] // LANES):
            small[s + 1, n * LANES : (n + 1) * LANES, :] = part[small_at + n].astype(F32)

    def line(s, first, gap):
        return small[s, first : first + 1, :] + (
            small[s, first + gap : first + gap + 1, :] + small[s, first + 2 * gap : first + 2 * gap + 1, :]
        )

    def summed(first, gap):
        others = line(1, first, gap) + (line(2, first, gap) + (line(3, first, gap) + line(4, first, gap)))
        return line(0, first, gap) * share + others

    def added(at):
        return (g1[at].astype(F32) + g2[at].astype(F32)) + (g3[at].astype(F32) + g4[at].astype(F32))

    def put(day, i, j, piece):
        hi, lo = split(piece)
        omhi[day, i * LANES : (i + 1) * LANES, j * LANES : (j + 1) * LANES] = hi
        omlo[day, i * LANES : (i + 1) * LANES, j * LANES : (j + 1) * LANES] = lo

    sides = [n for n, (i, j) in enumerate(tiles) if i != j]
    middles = [n for n, (i, j) in enumerate(tiles) if i == j]
    for i, n in enumerate(middles):
        both = added(2 * len(sides) + i)
        for day, part in enumerate((jnp.where(row > column, both, 0.0), jnp.where(row < column, both, 0.0))):
            others = sum(line(s, DIAG + 12 * day + i, 4) for s in range(1, 5))
            piece = own[day * len(tiles) + n] * share + (part + part.T)
            put(day, i, i, piece + jnp.where(row == column, others, 0.0))
    for day in range(2):
        for m, n in enumerate(sides):
            i, j = tiles[n]
            piece = own[day * len(tiles) + n] * share + added(day * len(sides) + m)
            put(day, i, j, piece)
            put(day, j, i, piece.T)
        info[day] = jnp.concatenate([summed(12 * day + j, 4) for j in range(chunks)], 1)
    held = table.shape[0] // 2 // planes
    for s in range(planes):
        plane = lax.rem(ids[0] + s, planes)
        for k in range(held):
            for day in range(2):
                table[pl.ds(2 * (plane * held + k) + day, 1), :] = jnp.concatenate(
                    [line(s, DAMP + 24 * k + 4 * day + j, 8) for j in range(chunks)], 1
                )
    for day in range(2):
        mine[day : day + 1, :] = table[pl.ds(2 * ids[1] + day, 1), :]
    state = prior[...]
    start[...] = jnp.where((ids[1] == 0) & (ids[0] == owner_plane(0)), state, 0.0)
    y[...] = two_days(state, mine, pthi, ptlo, omhi, omlo, info, chi, clo)


def direct_kernel(acc, got, mine, pthi, ptlo, omhi, omlo, info, chi, clo, total, y):
    state = acc[...] + got[...]
    total[...] = state
    y[...] = two_days(state, mine, pthi, ptlo, omhi, omlo, info, chi, clo)


def maps_kernel(after, omhi, omlo, info, chi, clo, pt, damping, b1hi, b1lo, b2hi, b2lo, bchi, bclo, off):
    parts = ((b1hi, b1lo), (b2hi, b2lo))
    for day in range(2):
        moved = pt[...] * damping[day : day + 1, :]
        taken = mm(moved, omhi[day], omlo[day])
        step = moved - mm(taken, chi[...], clo[...])
        parts[day][0][...], parts[day][1][...] = split(step)
        off[day : day + 1, :] = mv(info[day], chi[...], clo[...])
    both = jnp.dot(b1hi[...], b2hi[...], preferred_element_type=F32) + (
        jnp.dot(b1lo[...], b2hi[...], preferred_element_type=F32)
        + jnp.dot(b1hi[...], b2lo[...], preferred_element_type=F32)
    )
    bchi[...], bclo[...] = split(both)
    off[2:3, :] = mv(off[0:1, :], b2hi[...], b2lo[...]) + off[1:2, :]


def hop_kernel(after, acc, got, bchi, bclo, off, total, y):
    state = acc[...] + got[...]
    total[...] = state
    y[...] = mv(state, bchi[...], bclo[...]) + off[2:3, :]


def last_kernel(acc, got, b1hi, b1lo, b2hi, b2lo, off, damping, out):
    state = acc[...] + got[...]
    one = mv(state, b1hi[...], b1lo[...]) + off[0:1, :]
    two = mv(one, b2hi[...], b2lo[...]) + off[1:2, :]
    both = jnp.concatenate([one, two, damping[...]], 0)
    for c in range(out.shape[0]):
        out[c] = both


def back_kernel(ids, states, pthi, ptlo, mthi, mtlo, filt, smooth, f, d, const):
    total, width = f.shape
    spans = total // 2
    chunks = width // LANES
    for c in range(spans):
        one = states[owner_plane(c) * spans + (place(c) | 1)]
        f[2 * c : 2 * c + 2, :] = one[0:2]
        if c:
            d[2 * c - 1 : 2 * c + 1, :] = one[2:4]
        else:
            d[0:1, :] = one[3:4]
    d[total - 1 : total, :] = jnp.zeros((1, width), F32)
    ahead = d[...] * mm(f[...], pthi[...], ptlo[...])
    const[...] = f[...] - mm(d[...] * ahead, mthi[...], mtlo[...])

    def step(k, state):
        t = total - 2 - k
        new = const[pl.ds(t, 1), :] + mv(d[pl.ds(t, 1), :] * state, mthi[...], mtlo[...])
        const[pl.ds(t, 1), :] = new
        return new

    lax.fori_loop(0, total - 1, step, const[total - 1 : total, :], unroll=total <= 16)
    for k in range(2):
        row = pl.ds(ids[3] * 2 + k, 1)
        for whole, out in ((f, filt), (const, smooth)):
            line = whole[row, :]
            mine = line[:, 0:LANES]
            for q in range(1, chunks):
                mine = jnp.where(ids[2] == q, line[:, q * LANES : (q + 1) * LANES], mine)
            out[k : k + 1, :] = mine


def local(
    records,
    obs_values,
    block_day,
    block_count,
    propagator_matrix,
    analysis_cov,
    unattenuated_multiplier,
    damping,
    prior_mean,
):
    planes, held, peers = (lax.axis_size(a) for a in ("z", "y", "obs"))
    spans = planes * held
    blocks = block_day.shape[0]
    slots = records.shape[0] // blocks
    width = records.shape[1]
    days = damping.shape[0]
    assert planes == peers == 4 and days == 2 and slots == LANES and blocks == spans
    z, y, o = (lax.axis_index(a) for a in ("z", "y", "obs"))
    at = y * peers + o
    span = seat = jnp.where(z == 1, at - at % 2, at)
    for bit in range(1, spans.bit_length()):
        span = span ^ (seat >> bit)
    ids = jnp.stack([z, span, o, z * held + y]).astype(jnp.int32)
    everyone = ("z", "y", "obs")

    def owner(span):
        return owner_plane(span) * spans + (place(span) | 1)

    tiles = len(triangle(width))
    extra_tiles = -(-(DAMP + 24 * held) // LANES)
    full, row = (width, width), ((1, width), F32)
    sent = run(
        pack_kernel,
        [((blocks, slots + EXTRA, width), BF16)],
        [
            (x, HBM)
            for x in (
                block_day,
                block_count,
                records,
                obs_values.reshape(blocks, slots),
                prior_mean.reshape(1, -1),
                damping,
            )
        ],
        [
            pltpu.SMEM((blocks,), jnp.int32),
            pltpu.SMEM((blocks,), jnp.int32),
            pltpu.VMEM((blocks, slots), BF16),
            pltpu.VMEM((1, width // peers), F32),
            pltpu.VMEM((days, width), F32),
            pltpu.VMEM((blocks, EXTRA, width), BF16),
            pltpu.SemaphoreType.DMA((6 + blocks,)),
        ],
        limit=60,
        outs=HBM,
    )[0]
    got = lax.all_to_all(sent, ("y", "obs"), split_axis=0, concat_axis=0, tiled=True)
    span_slots = min(blocks, 8) * slots
    own, extra, pay, prior, gain = run(
        gram_kernel,
        [
            ((2 * tiles, LANES, LANES), F32),
            ((extra_tiles * LANES, LANES), F32),
            ((2 * tiles - width // LANES + extra_tiles, LANES, LANES), BF16),
            row,
            (unattenuated_multiplier.shape, F32),
        ],
        [got, unattenuated_multiplier],
        [pltpu.VMEM((width, span_slots), BF16), pltpu.VMEM((16, span_slots), BF16)],
        flops=4 * width * width * blocks * slots,
    )
    plane_sums = [
        lax.ppermute(
            pay, everyone, [((owner_plane(p) + s) % planes * spans + place(p), owner(p)) for p in range(spans)]
        )
        for s in range(1, planes)
    ]
    plane_sums.append(
        lax.ppermute(
            pay, everyone, [(spans + place(p), owner(p)) for p in range(spans) if place(p) % 2 == 0]
        )
    )

    def swap(x, bit):
        return lax.ppermute(x, "obs", [(i, i ^ bit) for i in range(peers)])

    across = swap(gain, 2)
    gains = [gain, swap(gain, 1), across, swap(across, 1)]
    pt, pthi, ptlo, chi, clo = run(
        prep_kernel, [(full, F32)] + [(full, BF16)] * 4, [propagator_matrix, analysis_cov]
    )
    omhi, omlo, info, mine, acc, y = run(
        owner_kernel,
        [((days,) + full, BF16)] * 2
        + [((days, 1, width), F32), ((days, width), F32), row, row],
        [(ids, SMEM), own, extra, *plane_sums, prior, pthi, ptlo, chi, clo, *[(g, ANY) for g in gains[1:]]],
        [pltpu.VMEM((spans * days, width), F32), pltpu.VMEM((planes + 1, extra_tiles * LANES, LANES), F32)],
    )
    for k in range(spans - 1):
        received = lax.ppermute(y, everyone, [(owner(k), owner(k + 1))])
        if k == 0:
            acc, y = run(
                direct_kernel, [row, row], [acc, received, mine, pthi, ptlo, omhi, omlo, info, chi, clo]
            )
            b1hi, b1lo, b2hi, b2lo, bchi, bclo, off = run(
                maps_kernel,
                [(full, BF16)] * 6 + [((8, width), F32)],
                [y, omhi, omlo, info, chi, clo, pt, mine],
                flops=30 * width**3,
            )
            side = y
        elif k < spans - 2:
            acc, y = run(hop_kernel, [row, row], [(side, ANY), acc, received, bchi, bclo, off])
            if k == 2:
                mthi, mtlo = run(gain_kernel, [(full, BF16)] * 2, [(y, ANY), (ids, SMEM), *gains])
                side = mthi
    (answer,) = run(
        last_kernel,
        [((spans * peers, 2 * days, width), F32)],
        [acc, received, b1hi, b1lo, b2hi, b2lo, off, mine],
    )
    states = lax.all_to_all(answer, everyone, split_axis=0, concat_axis=0, tiled=True)
    out = ((days, LANES), F32)
    return run(
        back_kernel,
        [out, out],
        [(ids, SMEM), states, pthi, ptlo, mthi, mtlo],
        [pltpu.VMEM((spans * days, width), F32)] * 3,
    )


def solution(mesh):
    spans, peers = mesh.devices.shape
    finer = jax.sharding.Mesh(mesh.devices.reshape(peers, spans // peers, peers), ("z", "y", "obs"))
    tm = ("z", "y")
    mapped = jax.shard_map(
        local,
        mesh=finer,
        in_specs=(
            P(("z", "y", "obs"), None),
            P(("z", "y", "obs")),
            P(("z", "y", "obs")),
            P(("z", "y", "obs")),
            P(),
            P(),
            P("obs", None),
            P(tm, None),
            P("obs"),
        ),
        out_specs=(P(tm, "obs"), P(tm, "obs")),
        check_vma=False,
    )
    return lambda *args: tuple(mapped(*args))
```

```python
import functools

import jax
import jax.numpy as jnp
from jax import lax
from jax.experimental import pallas as pl
from jax.experimental.pallas import tpu as pltpu
from jax.sharding import PartitionSpec as P

LANES = 128
F32, BF16 = jnp.float32, jnp.bfloat16
VMEM = pl.BlockSpec(memory_space=pltpu.VMEM)
SMEM = pl.BlockSpec(memory_space=pltpu.SMEM)
ANY = pl.BlockSpec(memory_space=pl.ANY)
HBM = pl.BlockSpec(memory_space=pltpu.HBM)


def run(body, out, ins, scratch=(), limit=32, flops=0, outs=VMEM):
    specs = [x[1] if isinstance(x, tuple) else VMEM for x in ins]
    arrays = [x[0] if isinstance(x, tuple) else x for x in ins]
    moved = sum(a.size * a.dtype.itemsize for a in arrays)
    return pl.pallas_call(
        body,
        out_shape=[jax.ShapeDtypeStruct(s, d) for s, d in out],
        in_specs=specs,
        out_specs=[outs] * len(out),
        scratch_shapes=list(scratch),
        compiler_params=pltpu.CompilerParams(vmem_limit_bytes=limit * 1024 * 1024),
        cost_estimate=pl.CostEstimate(flops=flops, bytes_accessed=moved, transcendentals=0),
    )(*arrays)


def triangle(width):
    parts = width // LANES
    return [(i, j) for i in range(parts) for j in range(i + 1)]


def split(x):
    hi = x.astype(BF16)
    return hi, (x - hi.astype(F32)).astype(BF16)


def mm(x, hi, lo):
    xhi, xlo = split(x)
    dot = functools.partial(jnp.dot, preferred_element_type=F32)
    return dot(xhi, hi) + (dot(xlo, hi) + dot(xhi, lo))


def mv(x, hi, lo):
    wide = jnp.broadcast_to(x, (8, x.shape[1]))
    row = lax.broadcasted_iota(jnp.int32, wide.shape, 0)
    top = wide.astype(BF16).astype(F32)
    both = jnp.where(row == 0, top, jnp.where(row == 1, wide - top, 0.0)).astype(BF16)
    first = jnp.dot(both, hi, preferred_element_type=F32)
    second = jnp.dot(both, lo, preferred_element_type=F32)
    return first[0:1] + (first[1:2] + second[0:1])


def parts3(x):
    out = []
    for _ in range(3):
        piece = x.astype(BF16).astype(F32)
        out.append(piece)
        x = x - piece
    return out


def place(span):
    return span ^ (span >> 1)


def owner_plane(span):
    return 1 + place(span) % 2


EXTRA = 8
DIAG, DAMP = 24, 48


def pack_kernel(
    day, count, rows, values, prior, damping, out, day_s, count_s, values_v, prior_v, damping_v, stage, sems
):
    blocks = out.shape[0]
    slots = out.shape[1] - EXTRA
    width = out.shape[2]
    small = [(day, day_s), (count, count_s), (values, values_v), (prior, prior_v), (damping, damping_v)]
    copies = [pltpu.make_async_copy(src, dst, sems.at[n]) for n, (src, dst) in enumerate(small)]
    large = [
        pltpu.make_async_copy(
            rows.at[pl.ds(k * slots, slots)], stage.at[place(k), pl.ds(0, slots)], sems.at[len(small) + k]
        )
        for k in range(blocks)
    ]
    for copy in copies + large:
        copy.start()
    for copy in copies:
        copy.wait()
    first, second, third = parts3(prior_v[...])
    below = jnp.concatenate(
        [jnp.concatenate([second, third, jnp.zeros((1, width - 2 * LANES), F32)], 1)] + parts3(damping_v[...]), 0
    )
    held = values_v[...].astype(F32)
    for k in range(blocks):
        line = jnp.concatenate(
            [
                held[k : k + 1, :],
                jnp.full((1, LANES), day_s[k], jnp.int32).astype(F32),
                jnp.full((1, LANES), count_s[k], jnp.int32).astype(F32),
                first,
            ],
            1,
        )
        stage[place(k), slots : slots + EXTRA, :] = jnp.concatenate([line, below], 0).astype(BF16)
    sends = [
        pltpu.make_async_copy(stage.at[place(k)], out.at[place(k)], sems.at[len(small) + blocks + k])
        for k in range(blocks)
    ]
    for k in range(blocks):
        large[k].wait()
        sends[k].start()
    for copy in sends:
        copy.wait()


def gram_kernel(got, gain, own, extra, pay, prior, gain_out, turned, marks):
    blocks = got.shape[0]
    slots = got.shape[1] - EXTRA
    width = got.shape[2]
    chunks = width // LANES
    tiles = triangle(width)
    group = min(blocks, 8)
    half = 2 * LANES
    gain_out[...] = gain[...]
    extra[...] = jnp.zeros(extra.shape, F32)

    def one(first, fresh):
        for k in range(group):
            at = slice(k * slots, (k + 1) * slots)
            line = got[first + k, slots : slots + EXTRA, :].astype(F32)
            valid = lax.broadcasted_iota(jnp.int32, (1, slots), 1).astype(F32) < line[0:1, 2 * LANES : 3 * LANES]
            day = line[0:1, LANES : 2 * LANES]
            values = line[0:1, 0:LANES]
            kept = [jnp.where(valid & (day == d), 1.0, 0.0) for d in (0.0, 1.0)]
            marks[:, at] = jnp.concatenate(
                kept + [kept[0] * values, kept[1] * values, jnp.zeros((12, slots), F32)], 0
            ).astype(BF16)
            turned[:, at] = got[first + k, 0:slots, :].T
        source = jnp.concatenate([got[first + k, 0:slots, :] for k in range(group)], 0)
        info = jnp.dot(marks[...], source, preferred_element_type=F32)
        for d in range(2):
            for top in range(0, width, half):
                left = turned[top : top + half, :] * marks[d : d + 1, :]
                block = jnp.dot(left, source[:, : top + half], preferred_element_type=F32)
                for n, (i, j) in enumerate(tiles):
                    if top <= i * LANES < top + half:
                        r = i * LANES - top
                        piece = block[r : r + LANES, j * LANES : (j + 1) * LANES]
                        at = d * len(tiles) + n
                        own[at] = piece if fresh else own[at] + piece
            for j in range(chunks):
                piece = info[2 + d : 3 + d, j * LANES : (j + 1) * LANES]
                r = 12 * d + j
                extra[r : r + 1, :] = piece if fresh else extra[r : r + 1, :] + piece

    if blocks == group:
        one(0, True)
    else:
        own[...] = jnp.zeros(own.shape, F32)

        @pl.loop(0, blocks // group)
        def _(g):
            one(g * group, False)

    row = lax.broadcasted_iota(jnp.int32, (LANES, LANES), 0)
    column = lax.broadcasted_iota(jnp.int32, (LANES, LANES), 1)
    sides = [n for n, (i, j) in enumerate(tiles) if i != j]
    middles = [n for n, (i, j) in enumerate(tiles) if i == j]
    for d in range(2):
        for part, piece in enumerate(parts3(extra[12 * d : 12 * d + chunks, :])):
            extra[12 * d + 4 * part : 12 * d + 4 * part + chunks, :] = piece
        for m, n in enumerate(sides):
            pay[d * len(sides) + m] = own[d * len(tiles) + n].astype(BF16)
    for i, n in enumerate(middles):
        squares = [own[d * len(tiles) + n] for d in range(2)]
        pay[2 * len(sides) + i] = jnp.where(row >= column, squares[0], squares[1]).astype(BF16)
        for d in range(2):
            line = jnp.sum(jnp.where(row == column, squares[d], 0.0), axis=0, keepdims=True)
            for part, piece in enumerate(parts3(line)):
                r = DIAG + 12 * d + 4 * part + i
                extra[r : r + 1, :] = piece
    for q in range(chunks):
        line = got[q, slots : slots + EXTRA, :].astype(F32)
        prior[:, q * LANES : (q + 1) * LANES] = line[0:1, 3 * LANES : 4 * LANES] + (
            line[1:2, 0:LANES] + line[1:2, LANES : 2 * LANES]
        )
    for y in range(blocks // 4):
        line = got[4 * y, slots : slots + EXTRA, :].astype(F32)
        for k in range(6):
            for j in range(chunks):
                r = DAMP + 24 * y + 4 * k + j
                extra[r : r + 1, :] = line[2 + k : 3 + k, j * LANES : (j + 1) * LANES]
    small_at = pay.shape[0] - extra.shape[0] // LANES
    for n in range(extra.shape[0] // LANES):
        pay[small_at + n] = extra[n * LANES : (n + 1) * LANES, :].astype(BF16)


def prep_kernel(trans, cov, pt, pthi, ptlo, chi, clo):
    whole = trans[...].T
    pt[...] = whole
    pthi[...], ptlo[...] = split(whole)
    chi[...], clo[...] = split(cov[...])


def gain_kernel(after, ids, m0, m1, m2, m3, mthi, mtlo):
    rows = m0.shape[0]
    for step, part in enumerate((m0, m1, m2, m3)):
        holder = ids[2] ^ step
        at = pl.ds(pl.multiple_of(holder * rows, rows), rows)
        hi, lo = split(part[...].T)
        mthi[:, at] = hi
        mtlo[:, at] = lo


def two_days(state, damping, pthi, ptlo, omhi, omlo, info, chi, clo):
    for day in range(2):
        moved = mv(state, pthi[...], ptlo[...]) * damping[day : day + 1, :]
        gap = mv(moved, omhi[day], omlo[day]) - info[day]
        state = moved - mv(gap, chi[...], clo[...])
    return state


def owner_kernel(
    ids, own, extra, g4, g3, g2, g1, prior, pthi, ptlo, chi, clo, m1, m2, m3,
    omhi, omlo, info, mine, start, y, table, small,
):
    planes = 4
    width = pthi.shape[0]
    chunks = width // LANES
    tiles = triangle(width)
    got = (g1, g2, g3, g4)
    share = jnp.where(ids[0] == 2, 1.0, 0.0)
    row = lax.broadcasted_iota(jnp.int32, (LANES, LANES), 0)
    column = lax.broadcasted_iota(jnp.int32, (LANES, LANES), 1)
    small_at = g1.shape[0] - extra.shape[0] // LANES
    small[0] = extra[...]
    for s, part in enumerate(got):
        for n in range(extra.shape[0] // LANES):
            small[s + 1, n * LANES : (n + 1) * LANES, :] = part[small_at + n].astype(F32)

    def line(s, first, gap):
        return small[s, first : first + 1, :] + (
            small[s, first + gap : first + gap + 1, :] + small[s, first + 2 * gap : first + 2 * gap + 1, :]
        )

    def summed(first, gap):
        others = line(1, first, gap) + (line(2, first, gap) + (line(3, first, gap) + line(4, first, gap)))
        return line(0, first, gap) * share + others

    def added(at):
        return (g1[at].astype(F32) + g2[at].astype(F32)) + (g3[at].astype(F32) + g4[at].astype(F32))

    def put(day, i, j, piece):
        hi, lo = split(piece)
        omhi[day, i * LANES : (i + 1) * LANES, j * LANES : (j + 1) * LANES] = hi
        omlo[day, i * LANES : (i + 1) * LANES, j * LANES : (j + 1) * LANES] = lo

    sides = [n for n, (i, j) in enumerate(tiles) if i != j]
    middles = [n for n, (i, j) in enumerate(tiles) if i == j]
    for i, n in enumerate(middles):
        both = added(2 * len(sides) + i)
        for day, part in enumerate((jnp.where(row > column, both, 0.0), jnp.where(row < column, both, 0.0))):
            others = sum(line(s, DIAG + 12 * day + i, 4) for s in range(1, 5))
            piece = own[day * len(tiles) + n] * share + (part + part.T)
            put(day, i, i, piece + jnp.where(row == column, others, 0.0))
    for day in range(2):
        for m, n in enumerate(sides):
            i, j = tiles[n]
            piece = own[day * len(tiles) + n] * share + added(day * len(sides) + m)
            put(day, i, j, piece)
            put(day, j, i, piece.T)
        info[day] = jnp.concatenate([summed(12 * day + j, 4) for j in range(chunks)], 1)
    held = table.shape[0] // 2 // planes
    for s in range(planes):
        plane = lax.rem(ids[0] + s, planes)
        for k in range(held):
            for day in range(2):
                table[pl.ds(2 * (plane * held + k) + day, 1), :] = jnp.concatenate(
                    [line(s, DAMP + 24 * k + 4 * day + j, 8) for j in range(chunks)], 1
                )
    for day in range(2):
        mine[day : day + 1, :] = table[pl.ds(2 * ids[1] + day, 1), :]
    state = prior[...]
    start[...] = jnp.where((ids[1] == 0) & (ids[0] == owner_plane(0)), state, 0.0)
    y[...] = two_days(state, mine, pthi, ptlo, omhi, omlo, info, chi, clo)


def direct_kernel(acc, got, mine, pthi, ptlo, omhi, omlo, info, chi, clo, total, y):
    state = acc[...] + got[...]
    total[...] = state
    y[...] = two_days(state, mine, pthi, ptlo, omhi, omlo, info, chi, clo)


def maps_kernel(after, omhi, omlo, info, chi, clo, pt, damping, b1hi, b1lo, b2hi, b2lo, bchi, bclo, off):
    parts = ((b1hi, b1lo), (b2hi, b2lo))
    for day in range(2):
        moved = pt[...] * damping[day : day + 1, :]
        taken = mm(moved, omhi[day], omlo[day])
        step = moved - mm(taken, chi[...], clo[...])
        parts[day][0][...], parts[day][1][...] = split(step)
        off[day : day + 1, :] = mv(info[day], chi[...], clo[...])
    both = jnp.dot(b1hi[...], b2hi[...], preferred_element_type=F32) + (
        jnp.dot(b1lo[...], b2hi[...], preferred_element_type=F32)
        + jnp.dot(b1hi[...], b2lo[...], preferred_element_type=F32)
    )
    bchi[...], bclo[...] = split(both)
    off[2:3, :] = mv(off[0:1, :], b2hi[...], b2lo[...]) + off[1:2, :]


def hop_kernel(after, acc, got, bchi, bclo, off, total, y):
    state = acc[...] + got[...]
    total[...] = state
    y[...] = mv(state, bchi[...], bclo[...]) + off[2:3, :]


def last_kernel(acc, got, b1hi, b1lo, b2hi, b2lo, off, damping, out):
    state = acc[...] + got[...]
    one = mv(state, b1hi[...], b1lo[...]) + off[0:1, :]
    two = mv(one, b2hi[...], b2lo[...]) + off[1:2, :]
    both = jnp.concatenate([one, two, damping[...]], 0)
    for c in range(out.shape[0]):
        out[c] = both


def back_kernel(ids, states, pthi, ptlo, mthi, mtlo, filt, smooth, f, d, const):
    total, width = f.shape
    spans = total // 2
    chunks = width // LANES
    for c in range(spans):
        one = states[owner_plane(c) * spans + (place(c) | 1)]
        f[2 * c : 2 * c + 2, :] = one[0:2]
        if c:
            d[2 * c - 1 : 2 * c + 1, :] = one[2:4]
        else:
            d[0:1, :] = one[3:4]
    d[total - 1 : total, :] = jnp.zeros((1, width), F32)
    ahead = d[...] * mm(f[...], pthi[...], ptlo[...])
    const[...] = f[...] - mm(d[...] * ahead, mthi[...], mtlo[...])

    def step(k, state):
        t = total - 2 - k
        new = const[pl.ds(t, 1), :] + mv(d[pl.ds(t, 1), :] * state, mthi[...], mtlo[...])
        const[pl.ds(t, 1), :] = new
        return new

    lax.fori_loop(0, total - 1, step, const[total - 1 : total, :], unroll=total <= 16)
    for k in range(2):
        row = pl.ds(ids[3] * 2 + k, 1)
        for whole, out in ((f, filt), (const, smooth)):
            line = whole[row, :]
            mine = line[:, 0:LANES]
            for q in range(1, chunks):
                mine = jnp.where(ids[2] == q, line[:, q * LANES : (q + 1) * LANES], mine)
            out[k : k + 1, :] = mine


def local(
    records,
    obs_values,
    block_day,
    block_count,
    propagator_matrix,
    analysis_cov,
    unattenuated_multiplier,
    damping,
    prior_mean,
):
    planes, held, peers = (lax.axis_size(a) for a in ("z", "y", "obs"))
    spans = planes * held
    blocks = block_day.shape[0]
    slots = records.shape[0] // blocks
    width = records.shape[1]
    days = damping.shape[0]
    assert planes == peers == 4 and days == 2 and slots == LANES and blocks == spans
    z, y, o = (lax.axis_index(a) for a in ("z", "y", "obs"))
    at = y * peers + o
    span = seat = jnp.where(z == 1, at - at % 2, at)
    for bit in range(1, spans.bit_length()):
        span = span ^ (seat >> bit)
    ids = jnp.stack([z, span, o, z * held + y]).astype(jnp.int32)
    everyone = ("z", "y", "obs")

    def owner(span):
        return owner_plane(span) * spans + (place(span) | 1)

    tiles = len(triangle(width))
    extra_tiles = -(-(DAMP + 24 * held) // LANES)
    full, row = (width, width), ((1, width), F32)
    sent = run(
        pack_kernel,
        [((blocks, slots + EXTRA, width), BF16)],
        [
            (x, HBM)
            for x in (
                block_day,
                block_count,
                records,
                obs_values.reshape(blocks, slots),
                prior_mean.reshape(1, -1),
                damping,
            )
        ],
        [
            pltpu.SMEM((blocks,), jnp.int32),
            pltpu.SMEM((blocks,), jnp.int32),
            pltpu.VMEM((blocks, slots), BF16),
            pltpu.VMEM((1, width // peers), F32),
            pltpu.VMEM((days, width), F32),
            pltpu.VMEM((blocks, slots + EXTRA, width), BF16),
            pltpu.SemaphoreType.DMA((5 + 2 * blocks,)),
        ],
        limit=60,
        outs=HBM,
    )[0]
    got = lax.all_to_all(sent, ("y", "obs"), split_axis=0, concat_axis=0, tiled=True)
    span_slots = min(blocks, 8) * slots
    own, extra, pay, prior, gain = run(
        gram_kernel,
        [
            ((2 * tiles, LANES, LANES), F32),
            ((extra_tiles * LANES, LANES), F32),
            ((2 * tiles - width // LANES + extra_tiles, LANES, LANES), BF16),
            row,
            (unattenuated_multiplier.shape, F32),
        ],
        [got, unattenuated_multiplier],
        [pltpu.VMEM((width, span_slots), BF16), pltpu.VMEM((16, span_slots), BF16)],
        flops=4 * width * width * blocks * slots,
    )
    plane_sums = [
        lax.ppermute(
            pay, everyone, [(spans + place(p), owner(p)) for p in range(spans) if place(p) % 2 == 0]
        )
    ] + [
        lax.ppermute(
            pay, everyone, [((owner_plane(p) + s) % planes * spans + place(p), owner(p)) for p in range(spans)]
        )
        for s in range(planes - 1, 0, -1)
    ]

    def swap(x, bit):
        return lax.ppermute(x, "obs", [(i, i ^ bit) for i in range(peers)])

    across = swap(gain, 2)
    gains = [gain, swap(gain, 1), across, swap(across, 1)]
    pt, pthi, ptlo, chi, clo = run(
        prep_kernel, [(full, F32)] + [(full, BF16)] * 4, [propagator_matrix, analysis_cov]
    )
    omhi, omlo, info, mine, acc, y = run(
        owner_kernel,
        [((days,) + full, BF16)] * 2
        + [((days, 1, width), F32), ((days, width), F32), row, row],
        [(ids, SMEM), own, extra, *plane_sums, prior, pthi, ptlo, chi, clo, *[(g, ANY) for g in gains[1:]]],
        [pltpu.VMEM((spans * days, width), F32), pltpu.VMEM((planes + 1, extra_tiles * LANES, LANES), F32)],
    )
    for k in range(spans - 1):
        received = lax.ppermute(y, everyone, [(owner(k), owner(k + 1))])
        if k == 0:
            acc, y = run(
                direct_kernel, [row, row], [acc, received, mine, pthi, ptlo, omhi, omlo, info, chi, clo]
            )
            b1hi, b1lo, b2hi, b2lo, bchi, bclo, off = run(
                maps_kernel,
                [(full, BF16)] * 6 + [((8, width), F32)],
                [y, omhi, omlo, info, chi, clo, pt, mine],
                flops=30 * width**3,
            )
            side = y
        elif k < spans - 2:
            acc, y = run(hop_kernel, [row, row], [(side, ANY), acc, received, bchi, bclo, off])
            if k == 2:
                mthi, mtlo = run(gain_kernel, [(full, BF16)] * 2, [(y, ANY), (ids, SMEM), *gains])
                side = mthi
    (answer,) = run(
        last_kernel,
        [((spans * peers, 2 * days, width), F32)],
        [acc, received, b1hi, b1lo, b2hi, b2lo, off, mine],
    )
    states = lax.all_to_all(answer, everyone, split_axis=0, concat_axis=0, tiled=True)
    out = ((days, LANES), F32)
    return run(
        back_kernel,
        [out, out],
        [(ids, SMEM), states, pthi, ptlo, mthi, mtlo],
        [pltpu.VMEM((spans * days, width), F32)] * 3,
    )


def solution(mesh):
    spans, peers = mesh.devices.shape
    finer = jax.sharding.Mesh(mesh.devices.reshape(peers, spans // peers, peers), ("z", "y", "obs"))
    tm = ("z", "y")
    mapped = jax.shard_map(
        local,
        mesh=finer,
        in_specs=(
            P(("z", "y", "obs"), None),
            P(("z", "y", "obs")),
            P(("z", "y", "obs")),
            P(("z", "y", "obs")),
            P(),
            P(),
            P("obs", None),
            P(tm, None),
            P("obs"),
        ),
        out_specs=(P(tm, "obs"), P(tm, "obs")),
        check_vma=False,
    )
    return lambda *args: tuple(mapped(*args))
```

```python
import functools

import jax
import jax.numpy as jnp
from jax import lax
from jax.experimental import pallas as pl
from jax.experimental.pallas import tpu as pltpu
from jax.sharding import PartitionSpec as P

LANES = 128
F32, BF16 = jnp.float32, jnp.bfloat16
VMEM = pl.BlockSpec(memory_space=pltpu.VMEM)
SMEM = pl.BlockSpec(memory_space=pltpu.SMEM)
ANY = pl.BlockSpec(memory_space=pl.ANY)
HBM = pl.BlockSpec(memory_space=pltpu.HBM)


def run(body, out, ins, scratch=(), limit=32, flops=0, outs=VMEM):
    specs = [x[1] if isinstance(x, tuple) else VMEM for x in ins]
    arrays = [x[0] if isinstance(x, tuple) else x for x in ins]
    moved = sum(a.size * a.dtype.itemsize for a in arrays)
    return pl.pallas_call(
        body,
        out_shape=[jax.ShapeDtypeStruct(s, d) for s, d in out],
        in_specs=specs,
        out_specs=[outs] * len(out),
        scratch_shapes=list(scratch),
        compiler_params=pltpu.CompilerParams(vmem_limit_bytes=limit * 1024 * 1024),
        cost_estimate=pl.CostEstimate(flops=flops, bytes_accessed=moved, transcendentals=0),
    )(*arrays)


def triangle(width):
    parts = width // LANES
    return [(i, j) for i in range(parts) for j in range(i + 1)]


def split(x):
    hi = x.astype(BF16)
    return hi, (x - hi.astype(F32)).astype(BF16)


def mm(x, hi, lo):
    xhi, xlo = split(x)
    dot = functools.partial(jnp.dot, preferred_element_type=F32)
    return dot(xhi, hi) + (dot(xlo, hi) + dot(xhi, lo))


def mv(x, hi, lo):
    wide = jnp.broadcast_to(x, (8, x.shape[1]))
    row = lax.broadcasted_iota(jnp.int32, wide.shape, 0)
    top = wide.astype(BF16).astype(F32)
    both = jnp.where(row == 0, top, jnp.where(row == 1, wide - top, 0.0)).astype(BF16)
    first = jnp.dot(both, hi, preferred_element_type=F32)
    second = jnp.dot(both, lo, preferred_element_type=F32)
    return first[0:1] + (first[1:2] + second[0:1])


def parts3(x):
    out = []
    for _ in range(3):
        piece = x.astype(BF16).astype(F32)
        out.append(piece)
        x = x - piece
    return out


def place(span):
    return span ^ (span >> 1)


def owner_plane(span):
    return 1 + place(span) % 2


EXTRA = 8
DIAG, DAMP = 24, 48


def pack_kernel(
    day, count, rows, values, prior, damping, out, day_s, count_s, values_v, prior_v, damping_v, stage, sems
):
    blocks = out.shape[0]
    slots = out.shape[1] - EXTRA
    width = out.shape[2]
    small = [(day, day_s), (count, count_s), (values, values_v), (prior, prior_v), (damping, damping_v)]
    copies = [pltpu.make_async_copy(src, dst, sems.at[n]) for n, (src, dst) in enumerate(small)]
    large = [
        pltpu.make_async_copy(
            rows.at[pl.ds(k * slots, slots)], stage.at[place(k), pl.ds(0, slots)], sems.at[len(small) + k]
        )
        for k in range(blocks)
    ]
    for copy in copies + large:
        copy.start()
    for copy in copies:
        copy.wait()
    first, second, third = parts3(prior_v[...])
    below = jnp.concatenate(
        [jnp.concatenate([second, third, jnp.zeros((1, width - 2 * LANES), F32)], 1)] + parts3(damping_v[...]), 0
    )
    held = values_v[...].astype(F32)
    for k in range(blocks):
        line = jnp.concatenate(
            [
                held[k : k + 1, :],
                jnp.full((1, LANES), day_s[k], jnp.int32).astype(F32),
                jnp.full((1, LANES), count_s[k], jnp.int32).astype(F32),
                first,
            ],
            1,
        )
        stage[place(k), slots : slots + EXTRA, :] = jnp.concatenate([line, below], 0).astype(BF16)
    sends = [
        pltpu.make_async_copy(stage.at[place(k)], out.at[place(k)], sems.at[len(small) + blocks + k])
        for k in range(blocks)
    ]
    for k in range(blocks):
        large[k].wait()
        sends[k].start()
    for copy in sends:
        copy.wait()


def gram_kernel(got, gain, own, extra, pay, prior, gain_out, turned, marks):
    blocks = got.shape[0]
    slots = got.shape[1] - EXTRA
    width = got.shape[2]
    chunks = width // LANES
    tiles = triangle(width)
    group = min(blocks, 8)
    half = 2 * LANES
    gain_out[...] = gain[...]
    extra[...] = jnp.zeros(extra.shape, F32)

    def one(first, fresh):
        for k in range(group):
            at = slice(k * slots, (k + 1) * slots)
            line = got[first + k, slots : slots + EXTRA, :].astype(F32)
            valid = lax.broadcasted_iota(jnp.int32, (1, slots), 1).astype(F32) < line[0:1, 2 * LANES : 3 * LANES]
            day = line[0:1, LANES : 2 * LANES]
            values = line[0:1, 0:LANES]
            kept = [jnp.where(valid & (day == d), 1.0, 0.0) for d in (0.0, 1.0)]
            marks[:, at] = jnp.concatenate(
                kept + [kept[0] * values, kept[1] * values, jnp.zeros((12, slots), F32)], 0
            ).astype(BF16)
            turned[:, at] = got[first + k, 0:slots, :].T
        source = jnp.concatenate([got[first + k, 0:slots, :] for k in range(group)], 0)
        info = jnp.dot(marks[...], source, preferred_element_type=F32)
        for d in range(2):
            for top in range(0, width, half):
                left = turned[top : top + half, :] * marks[d : d + 1, :]
                block = jnp.dot(left, source[:, : top + half], preferred_element_type=F32)
                for n, (i, j) in enumerate(tiles):
                    if top <= i * LANES < top + half:
                        r = i * LANES - top
                        piece = block[r : r + LANES, j * LANES : (j + 1) * LANES]
                        at = d * len(tiles) + n
                        own[at] = piece if fresh else own[at] + piece
            for j in range(chunks):
                piece = info[2 + d : 3 + d, j * LANES : (j + 1) * LANES]
                r = 12 * d + j
                extra[r : r + 1, :] = piece if fresh else extra[r : r + 1, :] + piece

    if blocks == group:
        one(0, True)
    else:
        own[...] = jnp.zeros(own.shape, F32)

        @pl.loop(0, blocks // group)
        def _(g):
            one(g * group, False)

    row = lax.broadcasted_iota(jnp.int32, (LANES, LANES), 0)
    column = lax.broadcasted_iota(jnp.int32, (LANES, LANES), 1)
    sides = [n for n, (i, j) in enumerate(tiles) if i != j]
    middles = [n for n, (i, j) in enumerate(tiles) if i == j]
    for d in range(2):
        for part, piece in enumerate(parts3(extra[12 * d : 12 * d + chunks, :])):
            extra[12 * d + 4 * part : 12 * d + 4 * part + chunks, :] = piece
        for m, n in enumerate(sides):
            pay[d * len(sides) + m] = own[d * len(tiles) + n].astype(BF16)
    for i, n in enumerate(middles):
        squares = [own[d * len(tiles) + n] for d in range(2)]
        pay[2 * len(sides) + i] = jnp.where(row >= column, squares[0], squares[1]).astype(BF16)
        for d in range(2):
            line = jnp.sum(jnp.where(row == column, squares[d], 0.0), axis=0, keepdims=True)
            for part, piece in enumerate(parts3(line)):
                r = DIAG + 12 * d + 4 * part + i
                extra[r : r + 1, :] = piece
    for q in range(chunks):
        line = got[q, slots : slots + EXTRA, :].astype(F32)
        prior[:, q * LANES : (q + 1) * LANES] = line[0:1, 3 * LANES : 4 * LANES] + (
            line[1:2, 0:LANES] + line[1:2, LANES : 2 * LANES]
        )
    for y in range(blocks // 4):
        line = got[4 * y, slots : slots + EXTRA, :].astype(F32)
        for k in range(6):
            for j in range(chunks):
                r = DAMP + 24 * y + 4 * k + j
                extra[r : r + 1, :] = line[2 + k : 3 + k, j * LANES : (j + 1) * LANES]
    small_at = pay.shape[0] - extra.shape[0] // LANES
    for n in range(extra.shape[0] // LANES):
        pay[small_at + n] = extra[n * LANES : (n + 1) * LANES, :].astype(BF16)


def prep_kernel(trans, cov, pt, pthi, ptlo, chi, clo):
    whole = trans[...].T
    pt[...] = whole
    pthi[...], ptlo[...] = split(whole)
    chi[...], clo[...] = split(cov[...])


def gain_kernel(after, ids, m0, m1, m2, m3, mthi, mtlo):
    rows = m0.shape[0]
    for step, part in enumerate((m0, m1, m2, m3)):
        holder = ids[2] ^ step
        at = pl.ds(pl.multiple_of(holder * rows, rows), rows)
        hi, lo = split(part[...].T)
        mthi[:, at] = hi
        mtlo[:, at] = lo


def few(x, hi, lo):
    top = x.astype(BF16).astype(F32)
    both = jnp.concatenate([top, x - top, jnp.zeros((4, x.shape[1]), F32)], 0).astype(BF16)
    first = jnp.dot(both, hi, preferred_element_type=F32)
    second = jnp.dot(both, lo, preferred_element_type=F32)
    return first[0:2] + (first[2:4] + second[0:2])


def one_day(day, state, damping, pthi, ptlo, omhi, omlo, info, chi, clo):
    moved = mv(state, pthi[...], ptlo[...]) * damping[day : day + 1, :]
    gap = mv(moved, omhi[day], omlo[day]) - info[day]
    return moved - mv(gap, chi[...], clo[...])


def owner_kernel(
    ids, own, extra, g4, g3, g2, g1, prior, pthi, ptlo, chi, clo, m1, m2, m3,
    omhi, omlo, info, mine, table, start, y, small,
):
    planes = 4
    width = pthi.shape[0]
    chunks = width // LANES
    tiles = triangle(width)
    got = (g1, g2, g3, g4)
    share = jnp.where(ids[0] == 2, 1.0, 0.0)
    row = lax.broadcasted_iota(jnp.int32, (LANES, LANES), 0)
    column = lax.broadcasted_iota(jnp.int32, (LANES, LANES), 1)
    small_at = g1.shape[0] - extra.shape[0] // LANES
    small[0] = extra[...]
    for s, part in enumerate(got):
        for n in range(extra.shape[0] // LANES):
            small[s + 1, n * LANES : (n + 1) * LANES, :] = part[small_at + n].astype(F32)

    def line(s, first, gap):
        return small[s, first : first + 1, :] + (
            small[s, first + gap : first + gap + 1, :] + small[s, first + 2 * gap : first + 2 * gap + 1, :]
        )

    def summed(first, gap):
        others = line(1, first, gap) + (line(2, first, gap) + (line(3, first, gap) + line(4, first, gap)))
        return line(0, first, gap) * share + others

    def added(at):
        return (g1[at].astype(F32) + g2[at].astype(F32)) + (g3[at].astype(F32) + g4[at].astype(F32))

    def put(day, i, j, piece):
        hi, lo = split(piece)
        omhi[day, i * LANES : (i + 1) * LANES, j * LANES : (j + 1) * LANES] = hi
        omlo[day, i * LANES : (i + 1) * LANES, j * LANES : (j + 1) * LANES] = lo

    sides = [n for n, (i, j) in enumerate(tiles) if i != j]
    middles = [n for n, (i, j) in enumerate(tiles) if i == j]

    def unpack(day):
        for i, n in enumerate(middles):
            both = added(2 * len(sides) + i)
            part = jnp.where(row < column if day else row > column, both, 0.0)
            others = sum(line(s, DIAG + 12 * day + i, 4) for s in range(1, 5))
            piece = own[day * len(tiles) + n] * share + (part + part.T)
            put(day, i, i, piece + jnp.where(row == column, others, 0.0))
        for m, n in enumerate(sides):
            i, j = tiles[n]
            piece = own[day * len(tiles) + n] * share + added(day * len(sides) + m)
            put(day, i, j, piece)
            put(day, j, i, piece.T)

    for day in range(2):
        info[day] = jnp.concatenate([summed(12 * day + j, 4) for j in range(chunks)], 1)
    held = table.shape[0] // 2 // planes
    for s in range(planes):
        plane = lax.rem(ids[0] + s, planes)
        for k in range(held):
            for day in range(2):
                table[pl.ds(2 * (plane * held + k) + day, 1), :] = jnp.concatenate(
                    [line(s, DAMP + 24 * k + 4 * day + j, 8) for j in range(chunks)], 1
                )
    for day in range(2):
        mine[day : day + 1, :] = table[pl.ds(2 * ids[1] + day, 1), :]
    first = (ids[1] == 0) & (ids[0] == owner_plane(0))
    start[...] = jnp.where(first, prior[...], 0.0)

    @pl.when(first)
    def _():
        state = prior[...]
        for day in range(2):
            unpack(day)
            state = one_day(day, state, mine, pthi, ptlo, omhi, omlo, info, chi, clo)
        y[...] = state

    @pl.when(jnp.logical_not(first))
    def _():
        for day in range(2):
            unpack(day)
        y[...] = jnp.zeros(y.shape, F32)


def direct_kernel(ids, acc, got, mine, pthi, ptlo, omhi, omlo, info, chi, clo, total, y):
    total[...] = acc[...] + got[...]
    y[...] = jnp.zeros(y.shape, F32)

    @pl.when(ids[1] == 1)
    def _():
        state = total[...]
        for day in range(2):
            state = one_day(day, state, mine, pthi, ptlo, omhi, omlo, info, chi, clo)
        y[...] = state


def maps_kernel(after, omhi, omlo, info, chi, clo, pt, damping, b1hi, b1lo, b2hi, b2lo, bchi, bclo, off):
    parts = ((b1hi, b1lo), (b2hi, b2lo))
    for day in range(2):
        moved = pt[...] * damping[day : day + 1, :]
        taken = mm(moved, omhi[day], omlo[day])
        step = moved - mm(taken, chi[...], clo[...])
        parts[day][0][...], parts[day][1][...] = split(step)
        off[day : day + 1, :] = mv(info[day], chi[...], clo[...])
    both = jnp.dot(b1hi[...], b2hi[...], preferred_element_type=F32) + (
        jnp.dot(b1lo[...], b2hi[...], preferred_element_type=F32)
        + jnp.dot(b1hi[...], b2lo[...], preferred_element_type=F32)
    )
    bchi[...], bclo[...] = split(both)
    off[2:3, :] = mv(off[0:1, :], b2hi[...], b2lo[...]) + off[1:2, :]


def hop_kernel(after, acc, got, bchi, bclo, off, total, y):
    state = acc[...] + got[...]
    total[...] = state
    y[...] = mv(state, bchi[...], bclo[...]) + off[2:3, :]


def pairs_kernel(ids, table, mthi, mtlo, khi, klo):
    spans = table.shape[0] // 2

    @pl.when(ids[1] == spans - 1)
    def _():
        whole = mthi[...].astype(F32) + mtlo[...].astype(F32)

        @pl.loop(0, khi.shape[0])
        def _(k):
            scaled = whole * table[pl.ds(2 * (spans - 2 - k) + 1, 1), :]
            khi[k], klo[k] = split(mm(scaled, mthi[...], mtlo[...]))


def last_kernel(
    ids, acc, got, b1hi, b1lo, b2hi, b2lo, off, table, pthi, ptlo, mthi, mtlo, khi, klo, out, shares
):
    total, width = shares.shape
    spans = total // 2
    chunks = width // LANES
    span = ids[1]
    state = acc[...] + got[...]
    one = mv(state, b1hi[...], b1lo[...]) + off[0:1, :]
    two = mv(one, b2hi[...], b2lo[...]) + off[1:2, :]
    within = table[pl.ds(2 * span + 1, 1), :]
    after = table[pl.ds(jnp.minimum(2 * span + 2, total - 1), 1), :] * jnp.where(span == spans - 1, 0.0, 1.0)
    damped = jnp.concatenate([within, after], 0)
    both = jnp.concatenate([one, two], 0)
    const = both - few(few(both, pthi[...], ptlo[...]) * damped * damped, mthi[...], mtlo[...])
    even = const[0:1] + mv(const[1:2] * within, mthi[...], mtlo[...])
    shares[...] = jnp.zeros(shares.shape, F32)
    shares[pl.ds(2 * span + 1, 1), :] = const[1:2]
    shares[pl.ds(2 * span, 1), :] = even

    def step(k, v):
        t = 2 * span - 1 - k
        v = mv(v * table[pl.ds(t + 1, 1), :], mthi[...], mtlo[...])
        shares[pl.ds(t, 1), :] = v
        return v

    @pl.when(span < spans - 1)
    def _():
        lax.fori_loop(0, 2 * span, step, even)

    @pl.when(span == spans - 1)
    def _():
        v, damped_rows = even, []
        for k in range(khi.shape[0]):
            t = 2 * (spans - 1 - k)
            v = v * table[t : t + 1, :]
            damped_rows.append(v)
            v = mv(v, khi[k], klo[k])
            shares[t - 2 : t - 1, :] = v
        batch = jnp.concatenate(damped_rows + [jnp.zeros((1, width), F32)] * (-len(damped_rows) % 8), 0)
        odd = mm(batch, mthi[...], mtlo[...])
        for k in range(khi.shape[0]):
            t = 2 * (spans - 1 - k)
            shares[t - 1 : t, :] = odd[k : k + 1]
        lax.fori_loop(2 * khi.shape[0], 2 * span, step, v)

    for c in range(spans):
        for q in range(chunks):
            out[c * chunks + q, 0:2, :] = shares[2 * c : 2 * c + 2, q * LANES : (q + 1) * LANES]
    for q in range(chunks):
        out[span * chunks + q, 2:4, :] = both[:, q * LANES : (q + 1) * LANES]


def add_kernel(ids, parts, filt, smooth):
    spans = parts.shape[0] // 4
    filt[...] = parts[ids[4], 2:4, :]
    smooth[...] = sum(parts[owner_plane(c) * spans + (place(c) | 1), 0:2, :] for c in range(spans))


def local(
    records,
    obs_values,
    block_day,
    block_count,
    propagator_matrix,
    analysis_cov,
    unattenuated_multiplier,
    damping,
    prior_mean,
):
    planes, held, peers = (lax.axis_size(a) for a in ("z", "y", "obs"))
    spans = planes * held
    blocks = block_day.shape[0]
    slots = records.shape[0] // blocks
    width = records.shape[1]
    days = damping.shape[0]
    assert planes == peers == 4 and days == 2 and slots == LANES and blocks == spans
    z, y, o = (lax.axis_index(a) for a in ("z", "y", "obs"))
    at = y * peers + o
    span = seat = jnp.where(z == 1, at - at % 2, at)
    for bit in range(1, spans.bit_length()):
        span = span ^ (seat >> bit)
    c = z * held + y
    seat = c ^ (c >> 1)
    ids = jnp.stack([z, span, o, c, (1 + seat % 2) * spans + (seat | 1)]).astype(jnp.int32)
    everyone = ("z", "y", "obs")

    def owner(span):
        return owner_plane(span) * spans + (place(span) | 1)

    tiles = len(triangle(width))
    extra_tiles = -(-(DAMP + 24 * held) // LANES)
    full, row = (width, width), ((1, width), F32)
    sent = run(
        pack_kernel,
        [((blocks, slots + EXTRA, width), BF16)],
        [
            (x, HBM)
            for x in (
                block_day,
                block_count,
                records,
                obs_values.reshape(blocks, slots),
                prior_mean.reshape(1, -1),
                damping,
            )
        ],
        [
            pltpu.SMEM((blocks,), jnp.int32),
            pltpu.SMEM((blocks,), jnp.int32),
            pltpu.VMEM((blocks, slots), BF16),
            pltpu.VMEM((1, width // peers), F32),
            pltpu.VMEM((days, width), F32),
            pltpu.VMEM((blocks, slots + EXTRA, width), BF16),
            pltpu.SemaphoreType.DMA((5 + 2 * blocks,)),
        ],
        limit=60,
        outs=HBM,
    )[0]
    got = lax.all_to_all(sent, ("y", "obs"), split_axis=0, concat_axis=0, tiled=True)
    span_slots = min(blocks, 8) * slots
    own, extra, pay, prior, gain = run(
        gram_kernel,
        [
            ((2 * tiles, LANES, LANES), F32),
            ((extra_tiles * LANES, LANES), F32),
            ((2 * tiles - width // LANES + extra_tiles, LANES, LANES), BF16),
            row,
            (unattenuated_multiplier.shape, F32),
        ],
        [got, unattenuated_multiplier],
        [pltpu.VMEM((width, span_slots), BF16), pltpu.VMEM((16, span_slots), BF16)],
        flops=4 * width * width * blocks * slots,
    )
    plane_sums = [
        lax.ppermute(
            pay, everyone, [(spans + place(p), owner(p)) for p in range(spans) if place(p) % 2 == 0]
        )
    ] + [
        lax.ppermute(
            pay, everyone, [((owner_plane(p) + s) % planes * spans + place(p), owner(p)) for p in range(spans)]
        )
        for s in range(planes - 1, 0, -1)
    ]

    def swap(x, bit):
        return lax.ppermute(x, "obs", [(i, i ^ bit) for i in range(peers)])

    across = swap(gain, 2)
    gains = [gain, swap(gain, 1), across, swap(across, 1)]
    pt, pthi, ptlo, chi, clo = run(
        prep_kernel, [(full, F32)] + [(full, BF16)] * 4, [propagator_matrix, analysis_cov]
    )
    omhi, omlo, info, mine, table, acc, y = run(
        owner_kernel,
        [((days,) + full, BF16)] * 2
        + [((days, 1, width), F32), ((days, width), F32), ((spans * days, width), F32), row, row],
        [(ids, SMEM), own, extra, *plane_sums, prior, pthi, ptlo, chi, clo, *[(g, ANY) for g in gains[1:]]],
        [pltpu.VMEM((planes + 1, extra_tiles * LANES, LANES), F32)],
    )
    for k in range(spans - 1):
        received = lax.ppermute(y, everyone, [(owner(k), owner(k + 1))])
        if k == 0:
            acc, y = run(
                direct_kernel,
                [row, row],
                [(ids, SMEM), acc, received, mine, pthi, ptlo, omhi, omlo, info, chi, clo],
            )
            b1hi, b1lo, b2hi, b2lo, bchi, bclo, off = run(
                maps_kernel,
                [(full, BF16)] * 6 + [((8, width), F32)],
                [y, omhi, omlo, info, chi, clo, pt, mine],
                flops=30 * width**3,
            )
            side = y
        elif k < spans - 2:
            acc, y = run(hop_kernel, [row, row], [(side, ANY), acc, received, bchi, bclo, off])
            if k == 2:
                mthi, mtlo = run(gain_kernel, [(full, BF16)] * 2, [(y, ANY), (ids, SMEM), *gains])
                khi, klo = run(
                    pairs_kernel,
                    [((min(spans - 1, 7),) + full, BF16)] * 2,
                    [(ids, SMEM), table, mthi, mtlo],
                )
                side = khi
    (answer,) = run(
        last_kernel,
        [((spans * peers, 8, LANES), F32)],
        [
            (ids, SMEM), acc, received, b1hi, b1lo, b2hi, b2lo, off, table, pthi, ptlo, mthi, mtlo, khi, klo
        ],
        [pltpu.VMEM((spans * days, width), F32)],
    )
    parts = lax.all_to_all(answer, everyone, split_axis=0, concat_axis=0, tiled=True)
    out = ((days, LANES), F32)
    return run(add_kernel, [out, out], [(ids, SMEM), parts])


def solution(mesh):
    spans, peers = mesh.devices.shape
    finer = jax.sharding.Mesh(mesh.devices.reshape(peers, spans // peers, peers), ("z", "y", "obs"))
    tm = ("z", "y")
    mapped = jax.shard_map(
        local,
        mesh=finer,
        in_specs=(
            P(("z", "y", "obs"), None),
            P(("z", "y", "obs")),
            P(("z", "y", "obs")),
            P(("z", "y", "obs")),
            P(),
            P(),
            P("obs", None),
            P(tm, None),
            P("obs"),
        ),
        out_specs=(P(tm, "obs"), P(tm, "obs")),
        check_vma=False,
    )
    return lambda *args: tuple(mapped(*args))
```

```python
import functools

import jax
import jax.numpy as jnp
from jax import lax
from jax.experimental import pallas as pl
from jax.experimental.pallas import tpu as pltpu
from jax.sharding import PartitionSpec as P

LANES = 128
F32, BF16 = jnp.float32, jnp.bfloat16
VMEM = pl.BlockSpec(memory_space=pltpu.VMEM)
SMEM = pl.BlockSpec(memory_space=pltpu.SMEM)
ANY = pl.BlockSpec(memory_space=pl.ANY)
HBM = pl.BlockSpec(memory_space=pltpu.HBM)


def run(body, out, ins, scratch=(), limit=16, flops=0, outs=VMEM):
    specs = [x[1] if isinstance(x, tuple) else VMEM for x in ins]
    arrays = [x[0] if isinstance(x, tuple) else x for x in ins]
    moved = sum(a.size * a.dtype.itemsize for a in arrays)
    return pl.pallas_call(
        body,
        out_shape=[jax.ShapeDtypeStruct(s, d) for s, d in out],
        in_specs=specs,
        out_specs=[outs] * len(out),
        scratch_shapes=list(scratch),
        compiler_params=pltpu.CompilerParams(vmem_limit_bytes=limit * 1024 * 1024),
        cost_estimate=pl.CostEstimate(flops=flops, bytes_accessed=moved, transcendentals=0),
    )(*arrays)


def triangle(width):
    parts = width // LANES
    return [(i, j) for i in range(parts) for j in range(i + 1)]


def split(x):
    hi = x.astype(BF16)
    return hi, (x - hi.astype(F32)).astype(BF16)


def mm(x, hi, lo):
    xhi, xlo = split(x)
    dot = functools.partial(jnp.dot, preferred_element_type=F32)
    return dot(xhi, hi) + (dot(xlo, hi) + dot(xhi, lo))


def mv(x, hi, lo):
    wide = jnp.broadcast_to(x, (8, x.shape[1]))
    row = lax.broadcasted_iota(jnp.int32, wide.shape, 0)
    top = wide.astype(BF16).astype(F32)
    both = jnp.where(row == 0, top, jnp.where(row == 1, wide - top, 0.0)).astype(BF16)
    first = jnp.dot(both, hi, preferred_element_type=F32)
    second = jnp.dot(both, lo, preferred_element_type=F32)
    return first[0:1] + (first[1:2] + second[0:1])


def parts3(x):
    out = []
    for _ in range(3):
        piece = x.astype(BF16).astype(F32)
        out.append(piece)
        x = x - piece
    return out


def place(span):
    return span ^ (span >> 1)


def owner_plane(span):
    return 1 + place(span) % 2


EXTRA = 8
DIAG, DAMP = 24, 48


def pack_kernel(
    day, count, rows, values, prior, damping, out, day_s, count_s, values_v, prior_v, damping_v, stage, sems
):
    blocks = out.shape[0]
    slots = out.shape[1] - EXTRA
    width = out.shape[2]
    small = [(day, day_s), (count, count_s), (values, values_v), (prior, prior_v), (damping, damping_v)]
    copies = [pltpu.make_async_copy(src, dst, sems.at[n]) for n, (src, dst) in enumerate(small)]
    large = [
        pltpu.make_async_copy(
            rows.at[pl.ds(k * slots, slots)], stage.at[place(k), pl.ds(0, slots)], sems.at[len(small) + k]
        )
        for k in range(blocks)
    ]
    for copy in copies + large:
        copy.start()
    for copy in copies:
        copy.wait()
    first, second, third = parts3(prior_v[...])
    below = jnp.concatenate(
        [jnp.concatenate([second, third, jnp.zeros((1, width - 2 * LANES), F32)], 1)] + parts3(damping_v[...]), 0
    )
    held = values_v[...].astype(F32)
    for k in range(blocks):
        line = jnp.concatenate(
            [
                held[k : k + 1, :],
                jnp.full((1, LANES), day_s[k], jnp.int32).astype(F32),
                jnp.full((1, LANES), count_s[k], jnp.int32).astype(F32),
                first,
            ],
            1,
        )
        stage[place(k), slots : slots + EXTRA, :] = jnp.concatenate([line, below], 0).astype(BF16)
    sends = [
        pltpu.make_async_copy(stage.at[place(k)], out.at[place(k)], sems.at[len(small) + blocks + k])
        for k in range(blocks)
    ]
    for k in range(blocks):
        large[k].wait()
        sends[k].start()
    for copy in sends:
        copy.wait()


def gram_kernel(got, gain, own, extra, pay, prior, gain_out, turned, marks):
    blocks = got.shape[0]
    slots = got.shape[1] - EXTRA
    width = got.shape[2]
    chunks = width // LANES
    tiles = triangle(width)
    group = min(blocks, 8)
    half = 2 * LANES
    gain_out[...] = gain[...]
    extra[...] = jnp.zeros(extra.shape, F32)

    def one(first, fresh):
        for k in range(group):
            at = slice(k * slots, (k + 1) * slots)
            line = got[first + k, slots : slots + EXTRA, :].astype(F32)
            valid = lax.broadcasted_iota(jnp.int32, (1, slots), 1).astype(F32) < line[0:1, 2 * LANES : 3 * LANES]
            day = line[0:1, LANES : 2 * LANES]
            values = line[0:1, 0:LANES]
            kept = [jnp.where(valid & (day == d), 1.0, 0.0) for d in (0.0, 1.0)]
            marks[:, at] = jnp.concatenate(
                kept + [kept[0] * values, kept[1] * values, jnp.zeros((12, slots), F32)], 0
            ).astype(BF16)
            turned[:, at] = got[first + k, 0:slots, :].T
        source = jnp.concatenate([got[first + k, 0:slots, :] for k in range(group)], 0)
        info = jnp.dot(marks[...], source, preferred_element_type=F32)
        for d in range(2):
            for top in range(0, width, half):
                left = turned[top : top + half, :] * marks[d : d + 1, :]
                block = jnp.dot(left, source[:, : top + half], preferred_element_type=F32)
                for n, (i, j) in enumerate(tiles):
                    if top <= i * LANES < top + half:
                        r = i * LANES - top
                        piece = block[r : r + LANES, j * LANES : (j + 1) * LANES]
                        at = d * len(tiles) + n
                        own[at] = piece if fresh else own[at] + piece
            for j in range(chunks):
                piece = info[2 + d : 3 + d, j * LANES : (j + 1) * LANES]
                r = 12 * d + j
                extra[r : r + 1, :] = piece if fresh else extra[r : r + 1, :] + piece

    if blocks == group:
        one(0, True)
    else:
        own[...] = jnp.zeros(own.shape, F32)

        @pl.loop(0, blocks // group)
        def _(g):
            one(g * group, False)

    row = lax.broadcasted_iota(jnp.int32, (LANES, LANES), 0)
    column = lax.broadcasted_iota(jnp.int32, (LANES, LANES), 1)
    sides = [n for n, (i, j) in enumerate(tiles) if i != j]
    middles = [n for n, (i, j) in enumerate(tiles) if i == j]
    for d in range(2):
        for part, piece in enumerate(parts3(extra[12 * d : 12 * d + chunks, :])):
            extra[12 * d + 4 * part : 12 * d + 4 * part + chunks, :] = piece
        for m, n in enumerate(sides):
            pay[d * len(sides) + m] = own[d * len(tiles) + n].astype(BF16)
    for i, n in enumerate(middles):
        squares = [own[d * len(tiles) + n] for d in range(2)]
        pay[2 * len(sides) + i] = jnp.where(row >= column, squares[0], squares[1]).astype(BF16)
        for d in range(2):
            line = jnp.sum(jnp.where(row == column, squares[d], 0.0), axis=0, keepdims=True)
            for part, piece in enumerate(parts3(line)):
                r = DIAG + 12 * d + 4 * part + i
                extra[r : r + 1, :] = piece
    for q in range(chunks):
        line = got[q, slots : slots + EXTRA, :].astype(F32)
        prior[:, q * LANES : (q + 1) * LANES] = line[0:1, 3 * LANES : 4 * LANES] + (
            line[1:2, 0:LANES] + line[1:2, LANES : 2 * LANES]
        )
    for y in range(blocks // 4):
        line = got[4 * y, slots : slots + EXTRA, :].astype(F32)
        for k in range(6):
            for j in range(chunks):
                r = DAMP + 24 * y + 4 * k + j
                extra[r : r + 1, :] = line[2 + k : 3 + k, j * LANES : (j + 1) * LANES]
    small_at = pay.shape[0] - extra.shape[0] // LANES
    for n in range(extra.shape[0] // LANES):
        pay[small_at + n] = extra[n * LANES : (n + 1) * LANES, :].astype(BF16)


def prep_kernel(trans, cov, pt, pthi, ptlo, chi, clo):
    whole = trans[...].T
    pt[...] = whole
    pthi[...], ptlo[...] = split(whole)
    chi[...], clo[...] = split(cov[...])


def gain_kernel(ids, m0, m1, m2, m3, mthi, mtlo):
    rows = m0.shape[0]
    for step, part in enumerate((m0, m1, m2, m3)):
        holder = ids[2] ^ step
        at = pl.ds(pl.multiple_of(holder * rows, rows), rows)
        hi, lo = split(part[...].T)
        mthi[:, at] = hi
        mtlo[:, at] = lo


def few(x, hi, lo):
    top = x.astype(BF16).astype(F32)
    both = jnp.concatenate([top, x - top, jnp.zeros((4, x.shape[1]), F32)], 0).astype(BF16)
    first = jnp.dot(both, hi, preferred_element_type=F32)
    second = jnp.dot(both, lo, preferred_element_type=F32)
    return first[0:2] + (first[2:4] + second[0:2])


def one_day(day, state, damping, pthi, ptlo, omhi, omlo, info, chi, clo):
    moved = mv(state, pthi[...], ptlo[...]) * damping[day : day + 1, :]
    gap = mv(moved, omhi[day], omlo[day]) - info[day]
    return moved - mv(gap, chi[...], clo[...])


def spread(extra, got, small):
    small_at = got[0].shape[0] - extra.shape[0] // LANES
    small[0] = extra[...]
    for s, part in enumerate(got):
        for n in range(extra.shape[0] // LANES):
            small[s + 1, n * LANES : (n + 1) * LANES, :] = part[small_at + n].astype(F32)


def line_of(small, s, first, gap):
    return small[s, first : first + 1, :] + (
        small[s, first + gap : first + gap + 1, :] + small[s, first + 2 * gap : first + 2 * gap + 1, :]
    )


def table_kernel(after, ids, extra, g1, g2, g3, table, small):
    planes = 4
    chunks = table.shape[1] // LANES
    held = table.shape[0] // 2 // planes
    spread(extra, (g1, g2, g3), small)
    for s in range(planes):
        plane = lax.rem(ids[0] + s, planes)
        for k in range(held):
            for day in range(2):
                table[pl.ds(2 * (plane * held + k) + day, 1), :] = jnp.concatenate(
                    [line_of(small, s, DAMP + 24 * k + 4 * day + j, 8) for j in range(chunks)], 1
                )


def owner_kernel(
    ids, own, extra, g4, g3, g1, g2, prior, pthi, ptlo, chi, clo, after, omhi, omlo, info, mine, start, y, small
):
    planes = 4
    width = pthi.shape[0]
    chunks = width // LANES
    tiles = triangle(width)
    got = (g1, g2, g3, g4)
    share = jnp.where(ids[0] == 2, 1.0, 0.0)
    row = lax.broadcasted_iota(jnp.int32, (LANES, LANES), 0)
    column = lax.broadcasted_iota(jnp.int32, (LANES, LANES), 1)
    spread(extra, got, small)

    def line(s, first, gap):
        return line_of(small, s, first, gap)

    def summed(first, gap):
        others = line(1, first, gap) + (line(2, first, gap) + (line(3, first, gap) + line(4, first, gap)))
        return line(0, first, gap) * share + others

    def added(at):
        return (g1[at].astype(F32) + g2[at].astype(F32)) + (g3[at].astype(F32) + g4[at].astype(F32))

    def put(day, i, j, piece):
        hi, lo = split(piece)
        omhi[day, i * LANES : (i + 1) * LANES, j * LANES : (j + 1) * LANES] = hi
        omlo[day, i * LANES : (i + 1) * LANES, j * LANES : (j + 1) * LANES] = lo

    sides = [n for n, (i, j) in enumerate(tiles) if i != j]
    middles = [n for n, (i, j) in enumerate(tiles) if i == j]

    def unpack(day):
        for i, n in enumerate(middles):
            both = added(2 * len(sides) + i)
            part = jnp.where(row < column if day else row > column, both, 0.0)
            others = sum(line(s, DIAG + 12 * day + i, 4) for s in range(1, 5))
            piece = own[day * len(tiles) + n] * share + (part + part.T)
            put(day, i, i, piece + jnp.where(row == column, others, 0.0))
        for m, n in enumerate(sides):
            i, j = tiles[n]
            piece = own[day * len(tiles) + n] * share + added(day * len(sides) + m)
            put(day, i, j, piece)
            put(day, j, i, piece.T)

    for day in range(2):
        info[day] = jnp.concatenate([summed(12 * day + j, 4) for j in range(chunks)], 1)
    held = ids[5]
    source = lax.rem(ids[1] // held - ids[0] + planes, planes)
    for day in range(2):
        for j in range(chunks):
            r = DAMP + 24 * lax.rem(ids[1], held) + 4 * day + j
            mine[day : day + 1, j * LANES : (j + 1) * LANES] = small[source, pl.ds(r, 1), :] + (
                small[source, pl.ds(r + 8, 1), :] + small[source, pl.ds(r + 16, 1), :]
            )
    first = (ids[1] == 0) & (ids[0] == owner_plane(0))
    start[...] = jnp.where(first, prior[...], 0.0)

    @pl.when(first)
    def _():
        state = prior[...]
        for day in range(2):
            unpack(day)
            state = one_day(day, state, mine, pthi, ptlo, omhi, omlo, info, chi, clo)
        y[...] = state

    @pl.when(jnp.logical_not(first))
    def _():
        for day in range(2):
            unpack(day)
        y[...] = jnp.zeros(y.shape, F32)


def second_kernel(acc, got, b1hi, b1lo, b2hi, b2lo, off, total, y):
    state = acc[...] + got[...]
    total[...] = state
    state = mv(state, b1hi[...], b1lo[...]) + off[0:1, :]
    y[...] = mv(state, b2hi[...], b2lo[...]) + off[1:2, :]


def maps_kernel(after, omhi, omlo, info, chi, clo, pt, damping, b1hi, b1lo, b2hi, b2lo, off):
    parts = ((b1hi, b1lo), (b2hi, b2lo))
    for day in range(2):
        moved = pt[...] * damping[day : day + 1, :]
        taken = mm(moved, omhi[day], omlo[day])
        step = moved - mm(taken, chi[...], clo[...])
        parts[day][0][...], parts[day][1][...] = split(step)
        off[day : day + 1, :] = mv(info[day], chi[...], clo[...])


def both_kernel(after, b1hi, b1lo, b2hi, b2lo, off, bchi, bclo, offset):
    both = jnp.dot(b1hi[...], b2hi[...], preferred_element_type=F32) + (
        jnp.dot(b1lo[...], b2hi[...], preferred_element_type=F32)
        + jnp.dot(b1hi[...], b2lo[...], preferred_element_type=F32)
    )
    bchi[...], bclo[...] = split(both)
    offset[...] = mv(off[0:1, :], b2hi[...], b2lo[...]) + off[1:2, :]


def hop_kernel(after, acc, got, bchi, bclo, offset, total, y):
    state = acc[...] + got[...]
    total[...] = state
    y[...] = mv(state, bchi[...], bclo[...]) + offset[...]


def pairs_kernel(after, ids, table, mthi, mtlo, khi, klo):
    spans = table.shape[0] // 2

    @pl.when(ids[1] == spans - 1)
    def _():
        whole = mthi[...].astype(F32) + mtlo[...].astype(F32)

        @pl.loop(0, khi.shape[0])
        def _(k):
            scaled = whole * table[pl.ds(2 * (spans - 2 - k) + 1, 1), :]
            khi[k], klo[k] = split(mm(scaled, mthi[...], mtlo[...]))


def last_kernel(
    ids, acc, got, b1hi, b1lo, b2hi, b2lo, off, table, pthi, ptlo, mthi, mtlo, khi, klo, out, shares
):
    total, width = shares.shape
    spans = total // 2
    chunks = width // LANES
    span = ids[1]
    state = acc[...] + got[...]
    one = mv(state, b1hi[...], b1lo[...]) + off[0:1, :]
    two = mv(one, b2hi[...], b2lo[...]) + off[1:2, :]
    within = table[pl.ds(2 * span + 1, 1), :]
    after = table[pl.ds(jnp.minimum(2 * span + 2, total - 1), 1), :] * jnp.where(span == spans - 1, 0.0, 1.0)
    damped = jnp.concatenate([within, after], 0)
    both = jnp.concatenate([one, two], 0)
    const = both - few(few(both, pthi[...], ptlo[...]) * damped * damped, mthi[...], mtlo[...])
    even = const[0:1] + mv(const[1:2] * within, mthi[...], mtlo[...])
    shares[...] = jnp.zeros(shares.shape, F32)
    shares[pl.ds(2 * span + 1, 1), :] = const[1:2]
    shares[pl.ds(2 * span, 1), :] = even

    def step(k, v):
        t = 2 * span - 1 - k
        v = mv(v * table[pl.ds(t + 1, 1), :], mthi[...], mtlo[...])
        shares[pl.ds(t, 1), :] = v
        return v

    @pl.when(span < spans - 1)
    def _():
        lax.fori_loop(0, 2 * span, step, even)

    @pl.when(span == spans - 1)
    def _():
        v, damped_rows = even, []
        for k in range(khi.shape[0]):
            t = 2 * (spans - 1 - k)
            v = v * table[t : t + 1, :]
            damped_rows.append(v)
            v = mv(v, khi[k], klo[k])
            shares[t - 2 : t - 1, :] = v
        batch = jnp.concatenate(damped_rows + [jnp.zeros((1, width), F32)] * (-len(damped_rows) % 8), 0)
        odd = mm(batch, mthi[...], mtlo[...])
        for k in range(khi.shape[0]):
            t = 2 * (spans - 1 - k)
            shares[t - 1 : t, :] = odd[k : k + 1]
        lax.fori_loop(2 * khi.shape[0], 2 * span, step, v)

    for c in range(spans):
        for q in range(chunks):
            out[c * chunks + q, 0:2, :] = shares[2 * c : 2 * c + 2, q * LANES : (q + 1) * LANES]
    for q in range(chunks):
        out[span * chunks + q, 2:4, :] = both[:, q * LANES : (q + 1) * LANES]


def add_kernel(ids, parts, filt, smooth):
    spans = parts.shape[0] // 4
    filt[...] = parts[ids[4], 2:4, :]
    smooth[...] = sum(parts[owner_plane(c) * spans + (place(c) | 1), 0:2, :] for c in range(spans))


def local(
    records,
    obs_values,
    block_day,
    block_count,
    propagator_matrix,
    analysis_cov,
    unattenuated_multiplier,
    damping,
    prior_mean,
):
    planes, held, peers = (lax.axis_size(a) for a in ("z", "y", "obs"))
    spans = planes * held
    blocks = block_day.shape[0]
    slots = records.shape[0] // blocks
    width = records.shape[1]
    days = damping.shape[0]
    assert planes == peers == 4 and days == 2 and slots == LANES and blocks == spans
    z, y, o = (lax.axis_index(a) for a in ("z", "y", "obs"))
    at = y * peers + o
    span = seat = jnp.where(z == 1, at - at % 2, at)
    for bit in range(1, spans.bit_length()):
        span = span ^ (seat >> bit)
    c = z * held + y
    seat = c ^ (c >> 1)
    ids = jnp.stack([z, span, o, c, (1 + seat % 2) * spans + (seat | 1), held]).astype(jnp.int32)
    everyone = ("z", "y", "obs")

    def owner(span):
        return owner_plane(span) * spans + (place(span) | 1)

    tiles = len(triangle(width))
    extra_tiles = -(-(DAMP + 24 * held) // LANES)
    full, row = (width, width), ((1, width), F32)
    sent = run(
        pack_kernel,
        [((blocks, slots + EXTRA, width), BF16)],
        [
            (x, HBM)
            for x in (
                block_day,
                block_count,
                records,
                obs_values.reshape(blocks, slots),
                prior_mean.reshape(1, -1),
                damping,
            )
        ],
        [
            pltpu.SMEM((blocks,), jnp.int32),
            pltpu.SMEM((blocks,), jnp.int32),
            pltpu.VMEM((blocks, slots), BF16),
            pltpu.VMEM((1, width // peers), F32),
            pltpu.VMEM((days, width), F32),
            pltpu.VMEM((blocks, slots + EXTRA, width), BF16),
            pltpu.SemaphoreType.DMA((5 + 2 * blocks,)),
        ],
        limit=60,
        outs=HBM,
    )[0]
    got = lax.all_to_all(sent, ("y", "obs"), split_axis=0, concat_axis=0, tiled=True)
    span_slots = min(blocks, 8) * slots
    own, extra, pay, prior, gain = run(
        gram_kernel,
        [
            ((2 * tiles, LANES, LANES), F32),
            ((extra_tiles * LANES, LANES), F32),
            ((2 * tiles - width // LANES + extra_tiles, LANES, LANES), BF16),
            row,
            (unattenuated_multiplier.shape, F32),
        ],
        [got, unattenuated_multiplier],
        [pltpu.VMEM((width, span_slots), BF16), pltpu.VMEM((16, span_slots), BF16)],
        flops=4 * width * width * blocks * slots,
    )
    def swap(x, bit):
        return lax.ppermute(x, "obs", [(i, i ^ bit) for i in range(peers)])

    def plane_sum(s):
        return lax.ppermute(
            pay, everyone, [((owner_plane(p) + s) % planes * spans + place(p), owner(p)) for p in range(spans)]
        )

    across = swap(gain, 2)
    beside = swap(gain, 1)
    fourth = lax.ppermute(
        pay, everyone, [(spans + place(p), owner(p)) for p in range(spans) if place(p) % 2 == 0]
    )
    third, first, second = plane_sum(3), plane_sum(1), plane_sum(2)
    mthi, mtlo = run(
        gain_kernel, [(full, BF16)] * 2, [(ids, SMEM), gain, beside, across, swap(across, 1)]
    )
    pt, pthi, ptlo, chi, clo = run(
        prep_kernel, [(full, F32)] + [(full, BF16)] * 4, [propagator_matrix, analysis_cov]
    )
    smalls = pltpu.VMEM((planes + 1, extra_tiles * LANES, LANES), F32)
    omhi, omlo, info, mine, acc, y = run(
        owner_kernel,
        [((days,) + full, BF16)] * 2 + [((days, 1, width), F32), ((days, width), F32), row, row],
        [
            (ids, SMEM), own, extra, fourth, third, first, second, prior, pthi, ptlo, chi, clo, (mthi, ANY)
        ],
        [smalls],
    )
    for k in range(spans - 1):
        received = lax.ppermute(y, everyone, [(owner(k), owner(k + 1))])
        if k == 0:
            b1hi, b1lo, b2hi, b2lo, off = run(
                maps_kernel,
                [(full, BF16)] * 4 + [((8, width), F32)],
                [(y, ANY), omhi, omlo, info, chi, clo, pt, mine],
                flops=24 * width**3,
            )
            acc, y = run(second_kernel, [row, row], [acc, received, b1hi, b1lo, b2hi, b2lo, off])
            bchi, bclo, offset = run(
                both_kernel, [(full, BF16)] * 2 + [row], [(y, ANY), b1hi, b1lo, b2hi, b2lo, off]
            )
            (table,) = run(
                table_kernel,
                [((spans * days, width), F32)],
                [(offset, ANY), (ids, SMEM), extra, first, second, third],
                [smalls],
            )
            side = table
        elif k < spans - 2:
            acc, y = run(hop_kernel, [row, row], [(side, ANY), acc, received, bchi, bclo, offset])
            if k == 2:
                khi, klo = run(
                    pairs_kernel,
                    [((min(spans - 1, 7),) + full, BF16)] * 2,
                    [(y, ANY), (ids, SMEM), table, mthi, mtlo],
                )
                side = khi
    (answer,) = run(
        last_kernel,
        [((spans * peers, 8, LANES), F32)],
        [
            (ids, SMEM), acc, received, b1hi, b1lo, b2hi, b2lo, off, table, pthi, ptlo, mthi, mtlo, khi, klo
        ],
        [pltpu.VMEM((spans * days, width), F32)],
    )
    parts = lax.all_to_all(answer, everyone, split_axis=0, concat_axis=0, tiled=True)
    out = ((days, LANES), F32)
    return run(add_kernel, [out, out], [(ids, SMEM), parts])


def solution(mesh):
    spans, peers = mesh.devices.shape
    finer = jax.sharding.Mesh(mesh.devices.reshape(peers, spans // peers, peers), ("z", "y", "obs"))
    tm = ("z", "y")
    mapped = jax.shard_map(
        local,
        mesh=finer,
        in_specs=(
            P(("z", "y", "obs"), None),
            P(("z", "y", "obs")),
            P(("z", "y", "obs")),
            P(("z", "y", "obs")),
            P(),
            P(),
            P("obs", None),
            P(tm, None),
            P("obs"),
        ),
        out_specs=(P(tm, "obs"), P(tm, "obs")),
        check_vma=False,
    )
    return lambda *args: tuple(mapped(*args))
```

```python
import functools

import jax
import jax.numpy as jnp
from jax import lax
from jax.experimental import pallas as pl
from jax.experimental.pallas import tpu as pltpu
from jax.sharding import PartitionSpec as P

LANES = 128
F32, BF16 = jnp.float32, jnp.bfloat16
VMEM = pl.BlockSpec(memory_space=pltpu.VMEM)
SMEM = pl.BlockSpec(memory_space=pltpu.SMEM)
ANY = pl.BlockSpec(memory_space=pl.ANY)
HBM = pl.BlockSpec(memory_space=pltpu.HBM)


def run(body, out, ins, scratch=(), limit=16, flops=0, outs=VMEM):
    specs = [x[1] if isinstance(x, tuple) else VMEM for x in ins]
    arrays = [x[0] if isinstance(x, tuple) else x for x in ins]
    moved = sum(a.size * a.dtype.itemsize for a in arrays)
    return pl.pallas_call(
        body,
        out_shape=[jax.ShapeDtypeStruct(s, d) for s, d in out],
        in_specs=specs,
        out_specs=[outs] * len(out),
        scratch_shapes=list(scratch),
        compiler_params=pltpu.CompilerParams(vmem_limit_bytes=limit * 1024 * 1024),
        cost_estimate=pl.CostEstimate(flops=flops, bytes_accessed=moved, transcendentals=0),
    )(*arrays)


def here():
    z, y, o = (lax.axis_index(a) for a in ("z", "y", "obs"))
    held, peers = lax.axis_size("y"), lax.axis_size("obs")
    spans = held * peers
    at = y * peers + o
    seat = jnp.where(z == 1, at - lax.rem(at, 2), at)
    span = seat
    for bit in range(1, spans.bit_length()):
        span = span ^ (seat >> bit)
    c = z * held + y
    seat = c ^ (c >> 1)
    return z, span, o, c, (1 + (seat & 1)) * spans + (seat | 1), held


def triangle(width):
    parts = width // LANES
    return [(i, j) for i in range(parts) for j in range(i + 1)]


def split(x):
    hi = x.astype(BF16)
    return hi, (x - hi.astype(F32)).astype(BF16)


def mm(x, hi, lo):
    xhi, xlo = split(x)
    dot = functools.partial(jnp.dot, preferred_element_type=F32)
    return dot(xhi, hi) + (dot(xlo, hi) + dot(xhi, lo))


def mv(x, hi, lo):
    wide = jnp.broadcast_to(x, (8, x.shape[1]))
    row = lax.broadcasted_iota(jnp.int32, wide.shape, 0)
    top = wide.astype(BF16).astype(F32)
    both = jnp.where(row == 0, top, jnp.where(row == 1, wide - top, 0.0)).astype(BF16)
    first = jnp.dot(both, hi, preferred_element_type=F32)
    second = jnp.dot(both, lo, preferred_element_type=F32)
    return first[0:1] + (first[1:2] + second[0:1])


def parts3(x):
    out = []
    for _ in range(3):
        piece = x.astype(BF16).astype(F32)
        out.append(piece)
        x = x - piece
    return out


def place(span):
    return span ^ (span >> 1)


def owner_plane(span):
    return 1 + place(span) % 2


EXTRA = 8
DIAG, DAMP = 24, 48


def pack_kernel(
    day, count, rows, values, prior, damping, out, day_s, count_s, values_v, prior_v, damping_v, stage, sems
):
    blocks = out.shape[0]
    slots = out.shape[1] - EXTRA
    width = out.shape[2]
    small = [(day, day_s), (count, count_s), (values, values_v), (prior, prior_v), (damping, damping_v)]
    copies = [pltpu.make_async_copy(src, dst, sems.at[n]) for n, (src, dst) in enumerate(small)]
    large = [
        pltpu.make_async_copy(
            rows.at[pl.ds(k * slots, slots)], stage.at[place(k), pl.ds(0, slots)], sems.at[len(small) + k]
        )
        for k in range(blocks)
    ]
    for copy in copies + large:
        copy.start()
    for copy in copies:
        copy.wait()
    first, second, third = parts3(prior_v[...])
    below = jnp.concatenate(
        [jnp.concatenate([second, third, jnp.zeros((1, width - 2 * LANES), F32)], 1)] + parts3(damping_v[...]), 0
    )
    held = values_v[...].astype(F32)
    for k in range(blocks):
        line = jnp.concatenate(
            [
                held[k : k + 1, :],
                jnp.full((1, LANES), day_s[k], jnp.int32).astype(F32),
                jnp.full((1, LANES), count_s[k], jnp.int32).astype(F32),
                first,
            ],
            1,
        )
        stage[place(k), slots : slots + EXTRA, :] = jnp.concatenate([line, below], 0).astype(BF16)
    sends = [
        pltpu.make_async_copy(stage.at[place(k)], out.at[place(k)], sems.at[len(small) + blocks + k])
        for k in range(blocks)
    ]
    for k in range(blocks):
        large[k].wait()
        sends[k].start()
    for copy in sends:
        copy.wait()


def gram_kernel(got, gain, own, extra, pay, prior, gain_out, turned, marks):
    blocks = got.shape[0]
    slots = got.shape[1] - EXTRA
    width = got.shape[2]
    chunks = width // LANES
    tiles = triangle(width)
    group = min(blocks, 8)
    half = 2 * LANES
    gain_out[...] = gain[...]
    extra[...] = jnp.zeros(extra.shape, F32)

    def one(first, fresh):
        for k in range(group):
            at = slice(k * slots, (k + 1) * slots)
            line = got[first + k, slots : slots + EXTRA, :].astype(F32)
            valid = lax.broadcasted_iota(jnp.int32, (1, slots), 1).astype(F32) < line[0:1, 2 * LANES : 3 * LANES]
            day = line[0:1, LANES : 2 * LANES]
            values = line[0:1, 0:LANES]
            kept = [jnp.where(valid & (day == d), 1.0, 0.0) for d in (0.0, 1.0)]
            marks[:, at] = jnp.concatenate(
                kept + [kept[0] * values, kept[1] * values, jnp.zeros((12, slots), F32)], 0
            ).astype(BF16)
            turned[:, at] = got[first + k, 0:slots, :].T
        source = jnp.concatenate([got[first + k, 0:slots, :] for k in range(group)], 0)
        info = jnp.dot(marks[...], source, preferred_element_type=F32)
        for d in range(2):
            for top in range(0, width, half):
                left = turned[top : top + half, :] * marks[d : d + 1, :]
                block = jnp.dot(left, source[:, : top + half], preferred_element_type=F32)
                for n, (i, j) in enumerate(tiles):
                    if top <= i * LANES < top + half:
                        r = i * LANES - top
                        piece = block[r : r + LANES, j * LANES : (j + 1) * LANES]
                        at = d * len(tiles) + n
                        own[at] = piece if fresh else own[at] + piece
            for j in range(chunks):
                piece = info[2 + d : 3 + d, j * LANES : (j + 1) * LANES]
                r = 12 * d + j
                extra[r : r + 1, :] = piece if fresh else extra[r : r + 1, :] + piece

    if blocks == group:
        one(0, True)
    else:
        own[...] = jnp.zeros(own.shape, F32)

        @pl.loop(0, blocks // group)
        def _(g):
            one(g * group, False)

    row = lax.broadcasted_iota(jnp.int32, (LANES, LANES), 0)
    column = lax.broadcasted_iota(jnp.int32, (LANES, LANES), 1)
    sides = [n for n, (i, j) in enumerate(tiles) if i != j]
    middles = [n for n, (i, j) in enumerate(tiles) if i == j]
    for d in range(2):
        for part, piece in enumerate(parts3(extra[12 * d : 12 * d + chunks, :])):
            extra[12 * d + 4 * part : 12 * d + 4 * part + chunks, :] = piece
        for m, n in enumerate(sides):
            pay[d * len(sides) + m] = own[d * len(tiles) + n].astype(BF16)
    for i, n in enumerate(middles):
        squares = [own[d * len(tiles) + n] for d in range(2)]
        pay[2 * len(sides) + i] = jnp.where(row >= column, squares[0], squares[1]).astype(BF16)
        for d in range(2):
            line = jnp.sum(jnp.where(row == column, squares[d], 0.0), axis=0, keepdims=True)
            for part, piece in enumerate(parts3(line)):
                r = DIAG + 12 * d + 4 * part + i
                extra[r : r + 1, :] = piece
    for q in range(chunks):
        line = got[q, slots : slots + EXTRA, :].astype(F32)
        prior[:, q * LANES : (q + 1) * LANES] = line[0:1, 3 * LANES : 4 * LANES] + (
            line[1:2, 0:LANES] + line[1:2, LANES : 2 * LANES]
        )
    for y in range(blocks // 4):
        line = got[4 * y, slots : slots + EXTRA, :].astype(F32)
        for k in range(6):
            for j in range(chunks):
                r = DAMP + 24 * y + 4 * k + j
                extra[r : r + 1, :] = line[2 + k : 3 + k, j * LANES : (j + 1) * LANES]
    small_at = pay.shape[0] - extra.shape[0] // LANES
    for n in range(extra.shape[0] // LANES):
        pay[small_at + n] = extra[n * LANES : (n + 1) * LANES, :].astype(BF16)


def prep_kernel(trans, cov, pt, pthi, ptlo, chi, clo):
    whole = trans[...].T
    pt[...] = whole
    pthi[...], ptlo[...] = split(whole)
    chi[...], clo[...] = split(cov[...])


def gain_kernel(m0, m1, m2, m3, mthi, mtlo):
    ids = here()
    rows = m0.shape[0]
    for step, part in enumerate((m0, m1, m2, m3)):
        holder = ids[2] ^ step
        at = pl.ds(pl.multiple_of(holder * rows, rows), rows)
        hi, lo = split(part[...].T)
        mthi[:, at] = hi
        mtlo[:, at] = lo


def few(x, hi, lo):
    top = x.astype(BF16).astype(F32)
    both = jnp.concatenate([top, x - top, jnp.zeros((4, x.shape[1]), F32)], 0).astype(BF16)
    first = jnp.dot(both, hi, preferred_element_type=F32)
    second = jnp.dot(both, lo, preferred_element_type=F32)
    return first[0:2] + (first[2:4] + second[0:2])


def one_day(day, state, damping, pthi, ptlo, omhi, omlo, info, chi, clo):
    moved = mv(state, pthi[...], ptlo[...]) * damping[day : day + 1, :]
    gap = mv(moved, omhi[day], omlo[day]) - info[day]
    return moved - mv(gap, chi[...], clo[...])


def spread(extra, got, small):
    small_at = got[0].shape[0] - extra.shape[0] // LANES
    small[0] = extra[...]
    for s, part in enumerate(got):
        for n in range(extra.shape[0] // LANES):
            small[s + 1, n * LANES : (n + 1) * LANES, :] = part[small_at + n].astype(F32)


def line_of(small, s, first, gap):
    return small[s, first : first + 1, :] + (
        small[s, first + gap : first + gap + 1, :] + small[s, first + 2 * gap : first + 2 * gap + 1, :]
    )


def table_kernel(after, extra, g1, g2, g3, table, small):
    ids = here()
    planes = 4
    chunks = table.shape[1] // LANES
    held = table.shape[0] // 2 // planes
    spread(extra, (g1, g2, g3), small)
    for s in range(planes):
        plane = lax.rem(ids[0] + s, planes)
        for k in range(held):
            for day in range(2):
                table[pl.ds(2 * (plane * held + k) + day, 1), :] = jnp.concatenate(
                    [line_of(small, s, DAMP + 24 * k + 4 * day + j, 8) for j in range(chunks)], 1
                )


def owner_kernel(
    own, extra, g4, g3, g1, g2, prior, pthi, ptlo, chi, clo, after, omhi, omlo, info, mine, start, y, small
):
    ids = here()
    planes = 4
    width = pthi.shape[0]
    chunks = width // LANES
    tiles = triangle(width)
    got = (g1, g2, g3, g4)
    share = jnp.where(ids[0] == 2, 1.0, 0.0)
    row = lax.broadcasted_iota(jnp.int32, (LANES, LANES), 0)
    column = lax.broadcasted_iota(jnp.int32, (LANES, LANES), 1)
    spread(extra, got, small)

    def line(s, first, gap):
        return line_of(small, s, first, gap)

    def summed(first, gap):
        others = line(1, first, gap) + (line(2, first, gap) + (line(3, first, gap) + line(4, first, gap)))
        return line(0, first, gap) * share + others

    def added(at):
        return (g1[at].astype(F32) + g2[at].astype(F32)) + (g3[at].astype(F32) + g4[at].astype(F32))

    def put(day, i, j, piece):
        hi, lo = split(piece)
        omhi[day, i * LANES : (i + 1) * LANES, j * LANES : (j + 1) * LANES] = hi
        omlo[day, i * LANES : (i + 1) * LANES, j * LANES : (j + 1) * LANES] = lo

    sides = [n for n, (i, j) in enumerate(tiles) if i != j]
    middles = [n for n, (i, j) in enumerate(tiles) if i == j]

    def unpack(day):
        for i, n in enumerate(middles):
            both = added(2 * len(sides) + i)
            part = jnp.where(row < column if day else row > column, both, 0.0)
            others = sum(line(s, DIAG + 12 * day + i, 4) for s in range(1, 5))
            piece = own[day * len(tiles) + n] * share + (part + part.T)
            put(day, i, i, piece + jnp.where(row == column, others, 0.0))
        for m, n in enumerate(sides):
            i, j = tiles[n]
            piece = own[day * len(tiles) + n] * share + added(day * len(sides) + m)
            put(day, i, j, piece)
            put(day, j, i, piece.T)

    for day in range(2):
        info[day] = jnp.concatenate([summed(12 * day + j, 4) for j in range(chunks)], 1)
    held = ids[5]
    source = lax.rem(ids[1] // held - ids[0] + planes, planes)
    for day in range(2):
        for j in range(chunks):
            r = DAMP + 24 * lax.rem(ids[1], held) + 4 * day + j
            mine[day : day + 1, j * LANES : (j + 1) * LANES] = small[source, pl.ds(r, 1), :] + (
                small[source, pl.ds(r + 8, 1), :] + small[source, pl.ds(r + 16, 1), :]
            )
    first = (ids[1] == 0) & (ids[0] == owner_plane(0))
    start[...] = jnp.where(first, prior[...], 0.0)

    @pl.when(first)
    def _():
        state = prior[...]
        for day in range(2):
            unpack(day)
            state = one_day(day, state, mine, pthi, ptlo, omhi, omlo, info, chi, clo)
        y[...] = state

    @pl.when(jnp.logical_not(first))
    def _():
        for day in range(2):
            unpack(day)
        y[...] = jnp.zeros(y.shape, F32)


def second_kernel(acc, got, b1hi, b1lo, b2hi, b2lo, off, total, y):
    state = acc[...] + got[...]
    total[...] = state
    state = mv(state, b1hi[...], b1lo[...]) + off[0:1, :]
    y[...] = mv(state, b2hi[...], b2lo[...]) + off[1:2, :]


def maps_kernel(after, omhi, omlo, info, chi, clo, pt, damping, b1hi, b1lo, b2hi, b2lo, off):
    parts = ((b1hi, b1lo), (b2hi, b2lo))
    for day in range(2):
        moved = pt[...] * damping[day : day + 1, :]
        taken = mm(moved, omhi[day], omlo[day])
        step = moved - mm(taken, chi[...], clo[...])
        parts[day][0][...], parts[day][1][...] = split(step)
        off[day : day + 1, :] = mv(info[day], chi[...], clo[...])


def both_kernel(after, b1hi, b1lo, b2hi, b2lo, off, bchi, bclo, offset):
    both = jnp.dot(b1hi[...], b2hi[...], preferred_element_type=F32) + (
        jnp.dot(b1lo[...], b2hi[...], preferred_element_type=F32)
        + jnp.dot(b1hi[...], b2lo[...], preferred_element_type=F32)
    )
    bchi[...], bclo[...] = split(both)
    offset[...] = mv(off[0:1, :], b2hi[...], b2lo[...]) + off[1:2, :]


def hop_kernel(after, acc, got, bchi, bclo, offset, total, y):
    state = acc[...] + got[...]
    total[...] = state
    y[...] = mv(state, bchi[...], bclo[...]) + offset[...]


def pairs_kernel(after, table, mthi, mtlo, khi, klo):
    ids = here()
    spans = table.shape[0] // 2

    @pl.when(ids[1] == spans - 1)
    def _():
        whole = mthi[...].astype(F32) + mtlo[...].astype(F32)

        @pl.loop(0, khi.shape[0])
        def _(k):
            scaled = whole * table[pl.ds(2 * (spans - 2 - k) + 1, 1), :]
            khi[k], klo[k] = split(mm(scaled, mthi[...], mtlo[...]))


def last_kernel(
    acc, got, b1hi, b1lo, b2hi, b2lo, off, table, pthi, ptlo, mthi, mtlo, khi, klo, out, shares
):
    ids = here()
    total, width = shares.shape
    spans = total // 2
    chunks = width // LANES
    span = ids[1]
    state = acc[...] + got[...]
    one = mv(state, b1hi[...], b1lo[...]) + off[0:1, :]
    two = mv(one, b2hi[...], b2lo[...]) + off[1:2, :]
    within = table[pl.ds(2 * span + 1, 1), :]
    after = table[pl.ds(jnp.minimum(2 * span + 2, total - 1), 1), :] * jnp.where(span == spans - 1, 0.0, 1.0)
    damped = jnp.concatenate([within, after], 0)
    both = jnp.concatenate([one, two], 0)
    const = both - few(few(both, pthi[...], ptlo[...]) * damped * damped, mthi[...], mtlo[...])
    even = const[0:1] + mv(const[1:2] * within, mthi[...], mtlo[...])
    shares[...] = jnp.zeros(shares.shape, F32)
    shares[pl.ds(2 * span + 1, 1), :] = const[1:2]
    shares[pl.ds(2 * span, 1), :] = even

    def step(k, v):
        t = 2 * span - 1 - k
        v = mv(v * table[pl.ds(t + 1, 1), :], mthi[...], mtlo[...])
        shares[pl.ds(t, 1), :] = v
        return v

    @pl.when(span < spans - 1)
    def _():
        lax.fori_loop(0, 2 * span, step, even)

    @pl.when(span == spans - 1)
    def _():
        v, damped_rows = even, []
        for k in range(khi.shape[0]):
            t = 2 * (spans - 1 - k)
            v = v * table[t : t + 1, :]
            damped_rows.append(v)
            v = mv(v, khi[k], klo[k])
            shares[t - 2 : t - 1, :] = v
        batch = jnp.concatenate(damped_rows + [jnp.zeros((1, width), F32)] * (-len(damped_rows) % 8), 0)
        odd = mm(batch, mthi[...], mtlo[...])
        for k in range(khi.shape[0]):
            t = 2 * (spans - 1 - k)
            shares[t - 1 : t, :] = odd[k : k + 1]
        lax.fori_loop(2 * khi.shape[0], 2 * span, step, v)

    for c in range(spans):
        for q in range(chunks):
            out[c * chunks + q, 0:2, :] = shares[2 * c : 2 * c + 2, q * LANES : (q + 1) * LANES]
    for q in range(chunks):
        out[span * chunks + q, 2:4, :] = both[:, q * LANES : (q + 1) * LANES]


def add_kernel(parts, filt, smooth):
    ids = here()
    spans = parts.shape[0] // 4
    filt[...] = parts[ids[4], 2:4, :]
    smooth[...] = sum(parts[owner_plane(c) * spans + (place(c) | 1), 0:2, :] for c in range(spans))


def local(
    records,
    obs_values,
    block_day,
    block_count,
    propagator_matrix,
    analysis_cov,
    unattenuated_multiplier,
    damping,
    prior_mean,
):
    planes, held, peers = (lax.axis_size(a) for a in ("z", "y", "obs"))
    spans = planes * held
    blocks = block_day.shape[0]
    slots = records.shape[0] // blocks
    width = records.shape[1]
    days = damping.shape[0]
    assert planes == peers == 4 and days == 2 and slots == LANES and blocks == spans
    everyone = ("z", "y", "obs")

    def owner(span):
        return owner_plane(span) * spans + (place(span) | 1)

    tiles = len(triangle(width))
    extra_tiles = -(-(DAMP + 24 * held) // LANES)
    full, row = (width, width), ((1, width), F32)
    sent = run(
        pack_kernel,
        [((blocks, slots + EXTRA, width), BF16)],
        [
            (x, HBM)
            for x in (
                block_day,
                block_count,
                records,
                obs_values.reshape(blocks, slots),
                prior_mean.reshape(1, -1),
                damping,
            )
        ],
        [
            pltpu.SMEM((blocks,), jnp.int32),
            pltpu.SMEM((blocks,), jnp.int32),
            pltpu.VMEM((blocks, slots), BF16),
            pltpu.VMEM((1, width // peers), F32),
            pltpu.VMEM((days, width), F32),
            pltpu.VMEM((blocks, slots + EXTRA, width), BF16),
            pltpu.SemaphoreType.DMA((5 + 2 * blocks,)),
        ],
        limit=60,
        outs=HBM,
    )[0]
    got = lax.all_to_all(sent, ("y", "obs"), split_axis=0, concat_axis=0, tiled=True)
    span_slots = min(blocks, 8) * slots
    own, extra, pay, prior, gain = run(
        gram_kernel,
        [
            ((2 * tiles, LANES, LANES), F32),
            ((extra_tiles * LANES, LANES), F32),
            ((2 * tiles - width // LANES + extra_tiles, LANES, LANES), BF16),
            row,
            (unattenuated_multiplier.shape, F32),
        ],
        [got, unattenuated_multiplier],
        [pltpu.VMEM((width, span_slots), BF16), pltpu.VMEM((16, span_slots), BF16)],
        flops=4 * width * width * blocks * slots,
    )
    def swap(x, bit):
        return lax.ppermute(x, "obs", [(i, i ^ bit) for i in range(peers)])

    def plane_sum(s):
        return lax.ppermute(
            pay, everyone, [((owner_plane(p) + s) % planes * spans + place(p), owner(p)) for p in range(spans)]
        )

    across = swap(gain, 2)
    beside = swap(gain, 1)
    fourth = lax.ppermute(
        pay, everyone, [(spans + place(p), owner(p)) for p in range(spans) if place(p) % 2 == 0]
    )
    third, first, second = plane_sum(3), plane_sum(1), plane_sum(2)
    mthi, mtlo = run(
        gain_kernel, [(full, BF16)] * 2, [gain, beside, across, swap(across, 1)]
    )
    pt, pthi, ptlo, chi, clo = run(
        prep_kernel, [(full, F32)] + [(full, BF16)] * 4, [propagator_matrix, analysis_cov]
    )
    smalls = pltpu.VMEM((planes + 1, extra_tiles * LANES, LANES), F32)
    omhi, omlo, info, mine, acc, y = run(
        owner_kernel,
        [((days,) + full, BF16)] * 2 + [((days, 1, width), F32), ((days, width), F32), row, row],
        [
            own, extra, fourth, third, first, second, prior, pthi, ptlo, chi, clo, (mthi, ANY)
        ],
        [smalls],
    )
    for k in range(spans - 1):
        received = lax.ppermute(y, everyone, [(owner(k), owner(k + 1))])
        if k == 0:
            b1hi, b1lo, b2hi, b2lo, off = run(
                maps_kernel,
                [(full, BF16)] * 4 + [((8, width), F32)],
                [(y, ANY), omhi, omlo, info, chi, clo, pt, mine],
                flops=24 * width**3,
            )
            acc, y = run(second_kernel, [row, row], [acc, received, b1hi, b1lo, b2hi, b2lo, off])
            bchi, bclo, offset = run(
                both_kernel, [(full, BF16)] * 2 + [row], [(y, ANY), b1hi, b1lo, b2hi, b2lo, off]
            )
            (table,) = run(
                table_kernel,
                [((spans * days, width), F32)],
                [(offset, ANY), extra, first, second, third],
                [smalls],
            )
            side = table
        elif k < spans - 2:
            acc, y = run(hop_kernel, [row, row], [(side, ANY), acc, received, bchi, bclo, offset])
            if k == 2:
                khi, klo = run(
                    pairs_kernel,
                    [((min(spans - 1, 7),) + full, BF16)] * 2,
                    [(y, ANY), table, mthi, mtlo],
                )
                side = khi
    (answer,) = run(
        last_kernel,
        [((spans * peers, 8, LANES), F32)],
        [
            acc, received, b1hi, b1lo, b2hi, b2lo, off, table, pthi, ptlo, mthi, mtlo, khi, klo
        ],
        [pltpu.VMEM((spans * days, width), F32)],
    )
    parts = lax.all_to_all(answer, everyone, split_axis=0, concat_axis=0, tiled=True)
    out = ((days, LANES), F32)
    return run(add_kernel, [out, out], [parts])


def solution(mesh):
    spans, peers = mesh.devices.shape
    finer = jax.sharding.Mesh(mesh.devices.reshape(peers, spans // peers, peers), ("z", "y", "obs"))
    tm = ("z", "y")
    mapped = jax.shard_map(
        local,
        mesh=finer,
        in_specs=(
            P(("z", "y", "obs"), None),
            P(("z", "y", "obs")),
            P(("z", "y", "obs")),
            P(("z", "y", "obs")),
            P(),
            P(),
            P("obs", None),
            P(tm, None),
            P("obs"),
        ),
        out_specs=(P(tm, "obs"), P(tm, "obs")),
        check_vma=False,
    )
    return lambda *args: tuple(mapped(*args))
```

```python
import functools

import jax
import jax.numpy as jnp
from jax import lax
from jax.experimental import pallas as pl
from jax.experimental.pallas import tpu as pltpu
from jax.sharding import PartitionSpec as P

LANES = 128
F32, BF16 = jnp.float32, jnp.bfloat16
VMEM = pl.BlockSpec(memory_space=pltpu.VMEM)
SMEM = pl.BlockSpec(memory_space=pltpu.SMEM)
ANY = pl.BlockSpec(memory_space=pl.ANY)
HBM = pl.BlockSpec(memory_space=pltpu.HBM)


def run(body, out, ins, scratch=(), limit=16, flops=0, outs=VMEM, same=None):
    specs = [x[1] if isinstance(x, tuple) else VMEM for x in ins]
    arrays = [x[0] if isinstance(x, tuple) else x for x in ins]
    moved = sum(a.size * a.dtype.itemsize for a in arrays)
    return pl.pallas_call(
        body,
        out_shape=[jax.ShapeDtypeStruct(s, d) for s, d in out],
        in_specs=specs,
        out_specs=[outs] * len(out),
        scratch_shapes=list(scratch),
        input_output_aliases=same or {},
        compiler_params=pltpu.CompilerParams(vmem_limit_bytes=limit * 1024 * 1024),
        cost_estimate=pl.CostEstimate(flops=flops, bytes_accessed=moved, transcendentals=0),
    )(*arrays)


def here():
    z, y, o = (lax.axis_index(a) for a in ("z", "y", "obs"))
    held, peers = lax.axis_size("y"), lax.axis_size("obs")
    spans = held * peers
    at = y * peers + o
    seat = jnp.where(z == 1, at - lax.rem(at, 2), at)
    span = seat
    for bit in range(1, spans.bit_length()):
        span = span ^ (seat >> bit)
    c = z * held + y
    seat = c ^ (c >> 1)
    return z, span, o, c, (1 + (seat & 1)) * spans + (seat | 1), held


def triangle(width):
    parts = width // LANES
    return [(i, j) for i in range(parts) for j in range(i + 1)]


def split(x):
    hi = x.astype(BF16)
    return hi, (x - hi.astype(F32)).astype(BF16)


def mm(x, hi, lo):
    xhi, xlo = split(x)
    dot = functools.partial(jnp.dot, preferred_element_type=F32)
    return dot(xhi, hi) + (dot(xlo, hi) + dot(xhi, lo))


def mv(x, hi, lo):
    wide = jnp.broadcast_to(x, (8, x.shape[1]))
    row = lax.broadcasted_iota(jnp.int32, wide.shape, 0)
    top = wide.astype(BF16).astype(F32)
    both = jnp.where(row == 0, top, jnp.where(row == 1, wide - top, 0.0)).astype(BF16)
    first = jnp.dot(both, hi, preferred_element_type=F32)
    second = jnp.dot(both, lo, preferred_element_type=F32)
    return first[0:1] + (first[1:2] + second[0:1])


def parts3(x):
    out = []
    for _ in range(3):
        piece = x.astype(BF16).astype(F32)
        out.append(piece)
        x = x - piece
    return out


def place(span):
    return span ^ (span >> 1)


def owner_plane(span):
    return 1 + place(span) % 2


EXTRA = 8
DIAG, DAMP = 24, 48


def pack_kernel(
    day, count, rows, values, prior, damping, out, day_s, count_s, values_v, prior_v, damping_v, stage, sems
):
    blocks = out.shape[0]
    slots = out.shape[1] - EXTRA
    width = out.shape[2]
    small = [(day, day_s), (count, count_s), (values, values_v), (prior, prior_v), (damping, damping_v)]
    copies = [pltpu.make_async_copy(src, dst, sems.at[n]) for n, (src, dst) in enumerate(small)]
    large = [
        pltpu.make_async_copy(
            rows.at[pl.ds(k * slots, slots)], stage.at[place(k), pl.ds(0, slots)], sems.at[len(small) + k]
        )
        for k in range(blocks)
    ]
    for copy in copies + large:
        copy.start()
    for copy in copies:
        copy.wait()
    first, second, third = parts3(prior_v[...])
    below = jnp.concatenate(
        [jnp.concatenate([second, third, jnp.zeros((1, width - 2 * LANES), F32)], 1)] + parts3(damping_v[...]), 0
    )
    held = values_v[...].astype(F32)
    for k in range(blocks):
        line = jnp.concatenate(
            [
                held[k : k + 1, :],
                jnp.full((1, LANES), day_s[k], jnp.int32).astype(F32),
                jnp.full((1, LANES), count_s[k], jnp.int32).astype(F32),
                first,
            ],
            1,
        )
        stage[place(k), slots : slots + EXTRA, :] = jnp.concatenate([line, below], 0).astype(BF16)
    sends = [
        pltpu.make_async_copy(stage.at[place(k)], out.at[place(k)], sems.at[len(small) + blocks + k])
        for k in range(blocks)
    ]
    for k in range(blocks):
        large[k].wait()
        sends[k].start()
    for copy in sends:
        copy.wait()


def gram_kernel(got, gain, own, extra, pay, prior, gain_out, turned, marks):
    blocks = got.shape[0]
    slots = got.shape[1] - EXTRA
    width = got.shape[2]
    chunks = width // LANES
    tiles = triangle(width)
    group = min(blocks, 8)
    half = 2 * LANES
    gain_out[...] = gain[...]
    extra[...] = jnp.zeros(extra.shape, F32)

    def one(first, fresh):
        for k in range(group):
            at = slice(k * slots, (k + 1) * slots)
            line = got[first + k, slots : slots + EXTRA, :].astype(F32)
            valid = lax.broadcasted_iota(jnp.int32, (1, slots), 1).astype(F32) < line[0:1, 2 * LANES : 3 * LANES]
            day = line[0:1, LANES : 2 * LANES]
            values = line[0:1, 0:LANES]
            kept = [jnp.where(valid & (day == d), 1.0, 0.0) for d in (0.0, 1.0)]
            marks[:, at] = jnp.concatenate(
                kept + [kept[0] * values, kept[1] * values, jnp.zeros((12, slots), F32)], 0
            ).astype(BF16)
            turned[:, at] = got[first + k, 0:slots, :].T
        source = jnp.concatenate([got[first + k, 0:slots, :] for k in range(group)], 0)
        info = jnp.dot(marks[...], source, preferred_element_type=F32)
        for d in range(2):
            for top in range(0, width, half):
                left = turned[top : top + half, :] * marks[d : d + 1, :]
                block = jnp.dot(left, source[:, : top + half], preferred_element_type=F32)
                for n, (i, j) in enumerate(tiles):
                    if top <= i * LANES < top + half:
                        r = i * LANES - top
                        piece = block[r : r + LANES, j * LANES : (j + 1) * LANES]
                        at = d * len(tiles) + n
                        own[at] = piece if fresh else own[at] + piece
            for j in range(chunks):
                piece = info[2 + d : 3 + d, j * LANES : (j + 1) * LANES]
                r = 12 * d + j
                extra[r : r + 1, :] = piece if fresh else extra[r : r + 1, :] + piece

    if blocks == group:
        one(0, True)
    else:
        own[...] = jnp.zeros(own.shape, F32)

        @pl.loop(0, blocks // group)
        def _(g):
            one(g * group, False)

    row = lax.broadcasted_iota(jnp.int32, (LANES, LANES), 0)
    column = lax.broadcasted_iota(jnp.int32, (LANES, LANES), 1)
    sides = [n for n, (i, j) in enumerate(tiles) if i != j]
    middles = [n for n, (i, j) in enumerate(tiles) if i == j]
    for d in range(2):
        for part, piece in enumerate(parts3(extra[12 * d : 12 * d + chunks, :])):
            extra[12 * d + 4 * part : 12 * d + 4 * part + chunks, :] = piece
        for m, n in enumerate(sides):
            pay[d * len(sides) + m] = own[d * len(tiles) + n].astype(BF16)
    for i, n in enumerate(middles):
        squares = [own[d * len(tiles) + n] for d in range(2)]
        pay[2 * len(sides) + i] = jnp.where(row >= column, squares[0], squares[1]).astype(BF16)
        for d in range(2):
            line = jnp.sum(jnp.where(row == column, squares[d], 0.0), axis=0, keepdims=True)
            for part, piece in enumerate(parts3(line)):
                r = DIAG + 12 * d + 4 * part + i
                extra[r : r + 1, :] = piece
    for q in range(chunks):
        line = got[q, slots : slots + EXTRA, :].astype(F32)
        prior[:, q * LANES : (q + 1) * LANES] = line[0:1, 3 * LANES : 4 * LANES] + (
            line[1:2, 0:LANES] + line[1:2, LANES : 2 * LANES]
        )
    for y in range(blocks // 4):
        line = got[4 * y, slots : slots + EXTRA, :].astype(F32)
        for k in range(6):
            for j in range(chunks):
                r = DAMP + 24 * y + 4 * k + j
                extra[r : r + 1, :] = line[2 + k : 3 + k, j * LANES : (j + 1) * LANES]
    small_at = pay.shape[0] - extra.shape[0] // LANES
    for n in range(extra.shape[0] // LANES):
        pay[small_at + n] = extra[n * LANES : (n + 1) * LANES, :].astype(BF16)


def prep_kernel(trans, cov, pt, pthi, ptlo, chi, clo):
    whole = trans[...].T
    pt[...] = whole
    pthi[...], ptlo[...] = split(whole)
    chi[...], clo[...] = split(cov[...])


def stack_kernel(one, two, out):
    out[0] = one[...]
    out[1] = two[...]


def gain_kernel(held, got, mthi, mtlo):
    ids = here()
    rows = held.shape[1]
    for step, part in enumerate((held.at[0], got.at[0], held.at[1], got.at[1])):
        holder = ids[2] ^ step
        at = pl.ds(pl.multiple_of(holder * rows, rows), rows)
        hi, lo = split(part[...].T)
        mthi[:, at] = hi
        mtlo[:, at] = lo


def few(x, hi, lo):
    top = x.astype(BF16).astype(F32)
    both = jnp.concatenate([top, x - top, jnp.zeros((4, x.shape[1]), F32)], 0).astype(BF16)
    first = jnp.dot(both, hi, preferred_element_type=F32)
    second = jnp.dot(both, lo, preferred_element_type=F32)
    return first[0:2] + (first[2:4] + second[0:2])


def one_day(day, state, damping, pthi, ptlo, omhi, omlo, info, chi, clo):
    moved = mv(state, pthi[...], ptlo[...]) * damping[day : day + 1, :]
    gap = mv(moved, omhi[day], omlo[day]) - info[day]
    return moved - mv(gap, chi[...], clo[...])


def spread(extra, got, small):
    small_at = got[0].shape[0] - extra.shape[0] // LANES
    small[0] = extra[...]
    for s, part in enumerate(got):
        for n in range(extra.shape[0] // LANES):
            small[s + 1, n * LANES : (n + 1) * LANES, :] = part[small_at + n].astype(F32)


def line_of(small, s, first, gap):
    return small[s, first : first + 1, :] + (
        small[s, first + gap : first + gap + 1, :] + small[s, first + 2 * gap : first + 2 * gap + 1, :]
    )


def table_kernel(after, extra, g1, g2, g3, table, small):
    ids = here()
    planes = 4
    chunks = table.shape[1] // LANES
    held = table.shape[0] // 2 // planes
    spread(extra, (g1, g2, g3), small)
    for s in range(planes):
        plane = lax.rem(ids[0] + s, planes)
        for k in range(held):
            for day in range(2):
                table[pl.ds(2 * (plane * held + k) + day, 1), :] = jnp.concatenate(
                    [line_of(small, s, DAMP + 24 * k + 4 * day + j, 8) for j in range(chunks)], 1
                )


def owner_kernel(
    own, extra, g4, g3, g1, g2, prior, pthi, ptlo, chi, clo, after, omhi, omlo, info, mine, start, y, small
):
    ids = here()
    planes = 4
    width = pthi.shape[0]
    chunks = width // LANES
    tiles = triangle(width)
    got = (g1, g2, g3, g4)
    share = jnp.where(ids[0] == 2, 1.0, 0.0)
    row = lax.broadcasted_iota(jnp.int32, (LANES, LANES), 0)
    column = lax.broadcasted_iota(jnp.int32, (LANES, LANES), 1)
    spread(extra, got, small)

    def line(s, first, gap):
        return line_of(small, s, first, gap)

    def summed(first, gap):
        others = line(1, first, gap) + (line(2, first, gap) + (line(3, first, gap) + line(4, first, gap)))
        return line(0, first, gap) * share + others

    def added(at):
        return (g1[at].astype(F32) + g2[at].astype(F32)) + (g3[at].astype(F32) + g4[at].astype(F32))

    def put(day, i, j, piece):
        hi, lo = split(piece)
        omhi[day, i * LANES : (i + 1) * LANES, j * LANES : (j + 1) * LANES] = hi
        omlo[day, i * LANES : (i + 1) * LANES, j * LANES : (j + 1) * LANES] = lo

    sides = [n for n, (i, j) in enumerate(tiles) if i != j]
    middles = [n for n, (i, j) in enumerate(tiles) if i == j]

    def unpack(day):
        for i, n in enumerate(middles):
            both = added(2 * len(sides) + i)
            part = jnp.where(row < column if day else row > column, both, 0.0)
            others = sum(line(s, DIAG + 12 * day + i, 4) for s in range(1, 5))
            piece = own[day * len(tiles) + n] * share + (part + part.T)
            put(day, i, i, piece + jnp.where(row == column, others, 0.0))
        for m, n in enumerate(sides):
            i, j = tiles[n]
            piece = own[day * len(tiles) + n] * share + added(day * len(sides) + m)
            put(day, i, j, piece)
            put(day, j, i, piece.T)

    for day in range(2):
        info[day] = jnp.concatenate([summed(12 * day + j, 4) for j in range(chunks)], 1)
    held = ids[5]
    source = lax.rem(ids[1] // held - ids[0] + planes, planes)
    for day in range(2):
        for j in range(chunks):
            r = DAMP + 24 * lax.rem(ids[1], held) + 4 * day + j
            mine[day : day + 1, j * LANES : (j + 1) * LANES] = small[source, pl.ds(r, 1), :] + (
                small[source, pl.ds(r + 8, 1), :] + small[source, pl.ds(r + 16, 1), :]
            )
    first = (ids[1] == 0) & (ids[0] == owner_plane(0))
    start[...] = jnp.where(first, prior[...], 0.0)

    @pl.when(first)
    def _():
        state = prior[...]
        for day in range(2):
            unpack(day)
            state = one_day(day, state, mine, pthi, ptlo, omhi, omlo, info, chi, clo)
        y[...] = state

    @pl.when(jnp.logical_not(first))
    def _():
        for day in range(2):
            unpack(day)
        y[...] = jnp.zeros(y.shape, F32)


def second_kernel(acc, got, mine, pthi, ptlo, omhi, omlo, info, chi, clo, total, y):
    total[...] = acc[...] + got[...]
    y[...] = jnp.zeros(y.shape, F32)

    @pl.when(here()[1] == 1)
    def _():
        state = acc[...] + got[...]
        for day in range(2):
            state = one_day(day, state, mine, pthi, ptlo, omhi, omlo, info, chi, clo)
        y[...] = state


def maps_kernel(after, omhi, omlo, info, chi, clo, pt, damping, *rest):
    late = len(rest) == 10
    b1hi, b1lo, b2hi, b2lo, off = rest[-5:]
    parts = ((b1hi, b1lo), (b2hi, b2lo))

    @pl.when((here()[1] == 1) == late)
    def _():
        for day in range(2):
            moved = pt[...] * damping[day : day + 1, :]
            taken = mm(moved, omhi[day], omlo[day])
            step = moved - mm(taken, chi[...], clo[...])
            parts[day][0][...], parts[day][1][...] = split(step)
            off[day : day + 1, :] = mv(info[day], chi[...], clo[...])


def both_kernel(after, b1hi, b1lo, b2hi, b2lo, off, bchi, bclo, offset):
    both = jnp.dot(b1hi[...], b2hi[...], preferred_element_type=F32) + (
        jnp.dot(b1lo[...], b2hi[...], preferred_element_type=F32)
        + jnp.dot(b1hi[...], b2lo[...], preferred_element_type=F32)
    )
    bchi[...], bclo[...] = split(both)
    offset[...] = mv(off[0:1, :], b2hi[...], b2lo[...]) + off[1:2, :]


def hop_kernel(after, acc, got, bchi, bclo, offset, total, y):
    state = acc[...] + got[...]
    total[...] = state
    y[...] = mv(state, bchi[...], bclo[...]) + offset[...]


def whole_of(hi, lo):
    return hi[...].astype(F32) + lo[...].astype(F32)


def pairs_kernel(
    after, b1hi, b1lo, bchi, bclo, off, offset, table, pthi, ptlo, mthi, mtlo,
    khi, klo, ohi, olo, ehi, elo, shift, held,
):
    span = here()[1]
    total = table.shape[0]
    spans = total // 2

    @pl.when(span >= spans - 2)
    def _():
        @pl.loop(0, khi.shape[0])
        def _(k):
            scaled = whole_of(mthi, mtlo) * table[pl.ds(2 * (spans - 2 - k) + 1, 1), :]
            khi[k], klo[k] = split(mm(scaled, mthi[...], mtlo[...]))

        within = table[pl.ds(2 * span + 1, 1), :]
        after_d = table[pl.ds(jnp.minimum(2 * span + 2, total - 1), 1), :] * jnp.where(span == spans - 1, 0.0, 1.0)
        one, two = off[0:1, :], offset[...]
        odd = two - mv(mv(two, pthi[...], ptlo[...]) * (after_d * after_d), mthi[...], mtlo[...])
        even = one + mv(
            odd * within - mv(one, pthi[...], ptlo[...]) * (within * within), mthi[...], mtlo[...]
        )
        shift[0:1, :] = odd
        shift[1:2, :] = even
        moved = mm(whole_of(bchi, bclo), pthi[...], ptlo[...]) * (after_d * after_d)
        held[...] = whole_of(bchi, bclo) - mm(moved, mthi[...], mtlo[...])
        ohi[...], olo[...] = split(held[...])
        moved = mm(whole_of(b1hi, b1lo), pthi[...], ptlo[...]) * (within * within)
        moved = held[...] * within - moved
        ehi[...], elo[...] = split(whole_of(b1hi, b1lo) + mm(moved, mthi[...], mtlo[...]))


def last_kernel(
    acc, got, b1hi, b1lo, b2hi, b2lo, bchi, bclo, off, offset, table, pthi, ptlo, mthi, mtlo,
    khi, klo, ohi, olo, ehi, elo, shift, out, shares, means,
):
    span = here()[1]
    total, width = shares.shape
    spans = total // 2
    chunks = width // LANES
    shares[...] = jnp.zeros(shares.shape, F32)

    def step(k, v):
        t = 2 * span - 1 - k
        v = mv(v * table[pl.ds(t + 1, 1), :], mthi[...], mtlo[...])
        shares[pl.ds(t, 1), :] = v
        return v

    @pl.when(span < spans - 2)
    def _():
        state = acc[...] + got[...]
        one = mv(state, b1hi[...], b1lo[...]) + off[0:1, :]
        two = mv(one, b2hi[...], b2lo[...]) + off[1:2, :]
        both = jnp.concatenate([one, two], 0)
        within = table[pl.ds(2 * span + 1, 1), :]
        damped = jnp.concatenate([within, table[pl.ds(2 * span + 2, 1), :]], 0)
        const = both - few(few(both, pthi[...], ptlo[...]) * damped * damped, mthi[...], mtlo[...])
        even = const[0:1] + mv(const[1:2] * within, mthi[...], mtlo[...])
        shares[pl.ds(2 * span + 1, 1), :] = const[1:2]
        shares[pl.ds(2 * span, 1), :] = even
        means[0:2, :] = both
        lax.fori_loop(0, 2 * span, step, even)

    @pl.when(span >= spans - 2)
    def _():
        state = acc[...] + got[...]
        even = mv(state, ehi[...], elo[...]) + shift[1:2, :]
        v, damped_rows = even, []
        for k in range(khi.shape[0]):
            t = 2 * (spans - 1 - k)
            damped = v * table[t : t + 1, :]
            damped_rows.append(damped)
            reached = mv(damped, khi[k], klo[k])
            v = reached if k else jnp.where(span == spans - 1, reached, v)
            shares[t - 2 : t - 1, :] = v
        odd = mv(state, ohi[...], olo[...]) + shift[0:1, :]
        means[0:1, :] = mv(state, b1hi[...], b1lo[...]) + off[0:1, :]
        means[1:2, :] = mv(state, bchi[...], bclo[...]) + offset[...]
        batch = jnp.concatenate(damped_rows + [jnp.zeros((1, width), F32)] * (-len(damped_rows) % 8), 0)
        batch = mm(batch, mthi[...], mtlo[...])
        for k in range(khi.shape[0]):
            t = 2 * (spans - 1 - k)
            shares[t - 1 : t, :] = batch[k : k + 1]
        shares[pl.ds(2 * span + 1, 1), :] = odd
        shares[pl.ds(2 * span, 1), :] = even
        lax.fori_loop(2 * khi.shape[0] - 2 * (spans - 1 - span), 2 * span, step, v)

    for c in range(spans):
        for q in range(chunks):
            out[c * chunks + q, 0:2, :] = shares[2 * c : 2 * c + 2, q * LANES : (q + 1) * LANES]
    for q in range(chunks):
        out[span * chunks + q, 2:4, :] = means[0:2, q * LANES : (q + 1) * LANES]


def add_kernel(parts, filt, smooth):
    ids = here()
    spans = parts.shape[0] // 4
    filt[...] = parts[ids[4], 2:4, :]
    smooth[...] = sum(parts[owner_plane(c) * spans + (place(c) | 1), 0:2, :] for c in range(spans))


def local(
    records,
    obs_values,
    block_day,
    block_count,
    propagator_matrix,
    analysis_cov,
    unattenuated_multiplier,
    damping,
    prior_mean,
):
    planes, held, peers = (lax.axis_size(a) for a in ("z", "y", "obs"))
    spans = planes * held
    blocks = block_day.shape[0]
    slots = records.shape[0] // blocks
    width = records.shape[1]
    days = damping.shape[0]
    assert planes == peers == 4 and days == 2 and slots == LANES and blocks == spans
    everyone = ("z", "y", "obs")

    def owner(span):
        return owner_plane(span) * spans + (place(span) | 1)

    tiles = len(triangle(width))
    extra_tiles = -(-(DAMP + 24 * held) // LANES)
    full, row = (width, width), ((1, width), F32)
    sent = run(
        pack_kernel,
        [((blocks, slots + EXTRA, width), BF16)],
        [
            (x, HBM)
            for x in (
                block_day,
                block_count,
                records,
                obs_values.reshape(blocks, slots),
                prior_mean.reshape(1, -1),
                damping,
            )
        ],
        [
            pltpu.SMEM((blocks,), jnp.int32),
            pltpu.SMEM((blocks,), jnp.int32),
            pltpu.VMEM((blocks, slots), BF16),
            pltpu.VMEM((1, width // peers), F32),
            pltpu.VMEM((days, width), F32),
            pltpu.VMEM((blocks, slots + EXTRA, width), BF16),
            pltpu.SemaphoreType.DMA((5 + 2 * blocks,)),
        ],
        limit=60,
        outs=HBM,
    )[0]
    got = lax.all_to_all(sent, ("y", "obs"), split_axis=0, concat_axis=0, tiled=True)
    span_slots = min(blocks, 8) * slots
    own, extra, pay, prior, gain = run(
        gram_kernel,
        [
            ((2 * tiles, LANES, LANES), F32),
            ((extra_tiles * LANES, LANES), F32),
            ((2 * tiles - width // LANES + extra_tiles, LANES, LANES), BF16),
            row,
            (unattenuated_multiplier.shape, F32),
        ],
        [got, unattenuated_multiplier],
        [pltpu.VMEM((width, span_slots), BF16), pltpu.VMEM((16, span_slots), BF16)],
        flops=4 * width * width * blocks * slots,
    )
    def swap(x, bit):
        return lax.ppermute(x, "obs", [(i, i ^ bit) for i in range(peers)])

    def plane_sum(s):
        return lax.ppermute(
            pay, everyone, [((owner_plane(p) + s) % planes * spans + place(p), owner(p)) for p in range(spans)]
        )

    fourth = lax.ppermute(
        pay, everyone, [(spans + place(p), owner(p)) for p in range(spans) if place(p) % 2 == 0]
    )
    third, first, second = plane_sum(3), plane_sum(1), plane_sum(2)
    (gains,) = run(stack_kernel, [((2,) + gain.shape, F32)], [gain, swap(gain, 2)])
    mthi, mtlo = run(gain_kernel, [(full, BF16)] * 2, [gains, swap(gains, 1)])
    pt, pthi, ptlo, chi, clo = run(
        prep_kernel, [(full, F32)] + [(full, BF16)] * 4, [propagator_matrix, analysis_cov]
    )
    smalls = pltpu.VMEM((planes + 1, extra_tiles * LANES, LANES), F32)
    omhi, omlo, info, mine, acc, y = run(
        owner_kernel,
        [((days,) + full, BF16)] * 2 + [((days, 1, width), F32), ((days, width), F32), row, row],
        [
            own, extra, fourth, third, first, second, prior, pthi, ptlo, chi, clo, (mthi, ANY)
        ],
        [smalls],
    )
    for k in range(spans - 1):
        received = lax.ppermute(y, everyone, [(owner(k), owner(k + 1))])
        if k == 0:
            maps = [(full, BF16)] * 4 + [((8, width), F32)]
            given = [omhi, omlo, info, chi, clo, pt, mine]
            flops = 24 * width**3
            days_maps = run(maps_kernel, maps, [(y, ANY), *given], flops=flops)
            acc, y = run(
                second_kernel, [row, row], [acc, received, mine, pthi, ptlo, omhi, omlo, info, chi, clo]
            )
            b1hi, b1lo, b2hi, b2lo, off = run(
                maps_kernel,
                maps,
                [(y, ANY), *given, *days_maps],
                flops=flops,
                same={8 + n: n for n in range(5)},
            )
            bchi, bclo, offset = run(
                both_kernel, [(full, BF16)] * 2 + [row], [(y, ANY), b1hi, b1lo, b2hi, b2lo, off]
            )
            (table,) = run(
                table_kernel,
                [((spans * days, width), F32)],
                [(offset, ANY), extra, first, second, third],
                [smalls],
            )
            side = table
        elif k < spans - 2:
            acc, y = run(hop_kernel, [row, row], [(side, ANY), acc, received, bchi, bclo, offset])
            if k == 2:
                ahead = run(
                    pairs_kernel,
                    [((min(spans - 1, 7),) + full, BF16)] * 2 + [(full, BF16)] * 4 + [((8, width), F32)],
                    [
                        (y, ANY), b1hi, b1lo, bchi, bclo, off, offset, table, pthi, ptlo, mthi, mtlo
                    ],
                    [pltpu.VMEM(full, F32)],
                )
                side = ahead[0]

    (answer,) = run(
        last_kernel,
        [((spans * peers, 8, LANES), F32)],
        [
            acc, received, b1hi, b1lo, b2hi, b2lo, bchi, bclo, off, offset, table, pthi, ptlo, mthi, mtlo,
            *ahead,
        ],
        [pltpu.VMEM((spans * days, width), F32), pltpu.VMEM((8, width), F32)],
    )
    parts = lax.all_to_all(answer, everyone, split_axis=0, concat_axis=0, tiled=True)
    out = ((days, LANES), F32)
    return run(add_kernel, [out, out], [parts])


def solution(mesh):
    spans, peers = mesh.devices.shape
    finer = jax.sharding.Mesh(mesh.devices.reshape(peers, spans // peers, peers), ("z", "y", "obs"))
    tm = ("z", "y")
    mapped = jax.shard_map(
        local,
        mesh=finer,
        in_specs=(
            P(("z", "y", "obs"), None),
            P(("z", "y", "obs")),
            P(("z", "y", "obs")),
            P(("z", "y", "obs")),
            P(),
            P(),
            P("obs", None),
            P(tm, None),
            P("obs"),
        ),
        out_specs=(P(tm, "obs"), P(tm, "obs")),
        check_vma=False,
    )
    return lambda *args: tuple(mapped(*args))
```

```python
import functools

import jax
import jax.numpy as jnp
from jax import lax
from jax.experimental import pallas as pl
from jax.experimental.pallas import tpu as pltpu
from jax.sharding import PartitionSpec as P

LANES = 128
F32, BF16 = jnp.float32, jnp.bfloat16
VMEM = pl.BlockSpec(memory_space=pltpu.VMEM)
SMEM = pl.BlockSpec(memory_space=pltpu.SMEM)
ANY = pl.BlockSpec(memory_space=pl.ANY)
HBM = pl.BlockSpec(memory_space=pltpu.HBM)


def run(body, out, ins, scratch=(), limit=16, flops=0, outs=VMEM, same=None):
    specs = [x[1] if isinstance(x, tuple) else VMEM for x in ins]
    arrays = [x[0] if isinstance(x, tuple) else x for x in ins]
    moved = sum(a.size * a.dtype.itemsize for a in arrays)
    return pl.pallas_call(
        body,
        out_shape=[jax.ShapeDtypeStruct(s, d) for s, d in out],
        in_specs=specs,
        out_specs=[outs] * len(out),
        scratch_shapes=list(scratch),
        input_output_aliases=same or {},
        compiler_params=pltpu.CompilerParams(vmem_limit_bytes=limit * 1024 * 1024),
        cost_estimate=pl.CostEstimate(flops=flops, bytes_accessed=moved, transcendentals=0),
    )(*arrays)


def here():
    z, y, o = (lax.axis_index(a) for a in ("z", "y", "obs"))
    held, peers = lax.axis_size("y"), lax.axis_size("obs")
    spans = held * peers
    at = y * peers + o
    seat = jnp.where(z == 1, at - lax.rem(at, 2), at)
    span = seat
    for bit in range(1, spans.bit_length()):
        span = span ^ (seat >> bit)
    c = z * held + y
    seat = c ^ (c >> 1)
    return z, span, o, c, (1 + (seat & 1)) * spans + (seat | 1), held


def triangle(width):
    parts = width // LANES
    return [(i, j) for i in range(parts) for j in range(i + 1)]


def split(x):
    hi = x.astype(BF16)
    return hi, (x - hi.astype(F32)).astype(BF16)


def mm(x, hi, lo):
    xhi, xlo = split(x)
    dot = functools.partial(jnp.dot, preferred_element_type=F32)
    return dot(xhi, hi) + (dot(xlo, hi) + dot(xhi, lo))


def mv(x, hi, lo):
    wide = jnp.broadcast_to(x, (8, x.shape[1]))
    row = lax.broadcasted_iota(jnp.int32, wide.shape, 0)
    top = wide.astype(BF16).astype(F32)
    both = jnp.where(row == 0, top, jnp.where(row == 1, wide - top, 0.0)).astype(BF16)
    first = jnp.dot(both, hi, preferred_element_type=F32)
    second = jnp.dot(both, lo, preferred_element_type=F32)
    return first[0:1] + (first[1:2] + second[0:1])


def parts3(x):
    out = []
    for _ in range(3):
        piece = x.astype(BF16).astype(F32)
        out.append(piece)
        x = x - piece
    return out


def place(span):
    return span ^ (span >> 1)


def owner_plane(span):
    return 1 + place(span) % 2


EXTRA = 8
DIAG, DAMP = 24, 48


def pack_kernel(
    day, count, rows, values, prior, damping, out, day_s, count_s, values_v, prior_v, damping_v, stage, sems
):
    blocks = out.shape[0]
    slots = out.shape[1] - EXTRA
    width = out.shape[2]
    small = [(day, day_s), (count, count_s), (values, values_v), (prior, prior_v), (damping, damping_v)]
    copies = [pltpu.make_async_copy(src, dst, sems.at[n]) for n, (src, dst) in enumerate(small)]
    large = [
        pltpu.make_async_copy(
            rows.at[pl.ds(k * slots, slots)], stage.at[place(k), pl.ds(0, slots)], sems.at[len(small) + k]
        )
        for k in range(blocks)
    ]
    for copy in copies + large:
        copy.start()
    for copy in copies:
        copy.wait()
    first, second, third = parts3(prior_v[...])
    below = jnp.concatenate(
        [jnp.concatenate([second, third, jnp.zeros((1, width - 2 * LANES), F32)], 1)] + parts3(damping_v[...]), 0
    )
    held = values_v[...].astype(F32)
    for k in range(blocks):
        line = jnp.concatenate(
            [
                held[k : k + 1, :],
                jnp.full((1, LANES), day_s[k], jnp.int32).astype(F32),
                jnp.full((1, LANES), count_s[k], jnp.int32).astype(F32),
                first,
            ],
            1,
        )
        stage[place(k), slots : slots + EXTRA, :] = jnp.concatenate([line, below], 0).astype(BF16)
    sends = [
        pltpu.make_async_copy(stage.at[place(k)], out.at[place(k)], sems.at[len(small) + blocks + k])
        for k in range(blocks)
    ]
    for k in range(blocks):
        large[k].wait()
        sends[k].start()
    for copy in sends:
        copy.wait()


def gram_kernel(got, gain, own, extra, pay, prior, gain_out, turned, marks):
    blocks = got.shape[0]
    slots = got.shape[1] - EXTRA
    width = got.shape[2]
    chunks = width // LANES
    tiles = triangle(width)
    group = min(blocks, 8)
    half = 2 * LANES
    gain_out[...] = gain[...]
    extra[...] = jnp.zeros(extra.shape, F32)

    def one(first, fresh):
        for k in range(group):
            at = slice(k * slots, (k + 1) * slots)
            line = got[first + k, slots : slots + EXTRA, :].astype(F32)
            valid = lax.broadcasted_iota(jnp.int32, (1, slots), 1).astype(F32) < line[0:1, 2 * LANES : 3 * LANES]
            day = line[0:1, LANES : 2 * LANES]
            values = line[0:1, 0:LANES]
            kept = [jnp.where(valid & (day == d), 1.0, 0.0) for d in (0.0, 1.0)]
            marks[:, at] = jnp.concatenate(
                kept + [kept[0] * values, kept[1] * values, jnp.zeros((12, slots), F32)], 0
            ).astype(BF16)
            turned[:, at] = got[first + k, 0:slots, :].T
        source = jnp.concatenate([got[first + k, 0:slots, :] for k in range(group)], 0)
        info = jnp.dot(marks[...], source, preferred_element_type=F32)
        for d in range(2):
            for top in range(0, width, half):
                left = turned[top : top + half, :] * marks[d : d + 1, :]
                block = jnp.dot(left, source[:, : top + half], preferred_element_type=F32)
                for n, (i, j) in enumerate(tiles):
                    if top <= i * LANES < top + half:
                        r = i * LANES - top
                        piece = block[r : r + LANES, j * LANES : (j + 1) * LANES]
                        at = d * len(tiles) + n
                        own[at] = piece if fresh else own[at] + piece
            for j in range(chunks):
                piece = info[2 + d : 3 + d, j * LANES : (j + 1) * LANES]
                r = 12 * d + j
                extra[r : r + 1, :] = piece if fresh else extra[r : r + 1, :] + piece

    if blocks == group:
        one(0, True)
    else:
        own[...] = jnp.zeros(own.shape, F32)

        @pl.loop(0, blocks // group)
        def _(g):
            one(g * group, False)

    row = lax.broadcasted_iota(jnp.int32, (LANES, LANES), 0)
    column = lax.broadcasted_iota(jnp.int32, (LANES, LANES), 1)
    sides = [n for n, (i, j) in enumerate(tiles) if i != j]
    middles = [n for n, (i, j) in enumerate(tiles) if i == j]
    for d in range(2):
        for part, piece in enumerate(parts3(extra[12 * d : 12 * d + chunks, :])):
            extra[12 * d + 4 * part : 12 * d + 4 * part + chunks, :] = piece
        for m, n in enumerate(sides):
            pay[d * len(sides) + m] = own[d * len(tiles) + n].astype(BF16)
    for i, n in enumerate(middles):
        squares = [own[d * len(tiles) + n] for d in range(2)]
        pay[2 * len(sides) + i] = jnp.where(row >= column, squares[0], squares[1]).astype(BF16)
        for d in range(2):
            line = jnp.sum(jnp.where(row == column, squares[d], 0.0), axis=0, keepdims=True)
            for part, piece in enumerate(parts3(line)):
                r = DIAG + 12 * d + 4 * part + i
                extra[r : r + 1, :] = piece
    for q in range(chunks):
        line = got[q, slots : slots + EXTRA, :].astype(F32)
        prior[:, q * LANES : (q + 1) * LANES] = line[0:1, 3 * LANES : 4 * LANES] + (
            line[1:2, 0:LANES] + line[1:2, LANES : 2 * LANES]
        )
    for y in range(blocks // 4):
        line = got[4 * y, slots : slots + EXTRA, :].astype(F32)
        for k in range(6):
            for j in range(chunks):
                r = DAMP + 24 * y + 4 * k + j
                extra[r : r + 1, :] = line[2 + k : 3 + k, j * LANES : (j + 1) * LANES]
    small_at = pay.shape[0] - extra.shape[0] // LANES
    for n in range(extra.shape[0] // LANES):
        pay[small_at + n] = extra[n * LANES : (n + 1) * LANES, :].astype(BF16)


def prep_kernel(trans, cov, pt, pthi, ptlo, chi, clo):
    whole = trans[...].T
    pt[...] = whole
    pthi[...], ptlo[...] = split(whole)
    chi[...], clo[...] = split(cov[...])


def stack_kernel(one, two, out):
    out[0] = one[...]
    out[1] = two[...]


def gain_kernel(held, got, mthi, mtlo):
    ids = here()
    rows = held.shape[1]
    for step, part in enumerate((held.at[0], got.at[0], held.at[1], got.at[1])):
        holder = ids[2] ^ step
        at = pl.ds(pl.multiple_of(holder * rows, rows), rows)
        hi, lo = split(part[...].T)
        mthi[:, at] = hi
        mtlo[:, at] = lo


def few(x, hi, lo):
    top = x.astype(BF16).astype(F32)
    both = jnp.concatenate([top, x - top, jnp.zeros((4, x.shape[1]), F32)], 0).astype(BF16)
    first = jnp.dot(both, hi, preferred_element_type=F32)
    second = jnp.dot(both, lo, preferred_element_type=F32)
    return first[0:2] + (first[2:4] + second[0:2])


def one_day(day, state, damping, pthi, ptlo, omhi, omlo, info, chi, clo):
    moved = mv(state, pthi[...], ptlo[...]) * damping[day : day + 1, :]
    gap = mv(moved, omhi[day], omlo[day]) - info[day]
    return moved - mv(gap, chi[...], clo[...])


def spread(extra, got, small):
    small_at = got[0].shape[0] - extra.shape[0] // LANES
    small[0] = extra[...]
    for s, part in enumerate(got):
        for n in range(extra.shape[0] // LANES):
            small[s + 1, n * LANES : (n + 1) * LANES, :] = part[small_at + n].astype(F32)


def line_of(small, s, first, gap):
    return small[s, first : first + 1, :] + (
        small[s, first + gap : first + gap + 1, :] + small[s, first + 2 * gap : first + 2 * gap + 1, :]
    )


def table_kernel(after, extra, g1, g2, g3, table, small):
    ids = here()
    planes = 4
    chunks = table.shape[1] // LANES
    held = table.shape[0] // 2 // planes
    spread(extra, (g1, g2, g3), small)
    for s in range(planes):
        plane = lax.rem(ids[0] + s, planes)
        for k in range(held):
            for day in range(2):
                table[pl.ds(2 * (plane * held + k) + day, 1), :] = jnp.concatenate(
                    [line_of(small, s, DAMP + 24 * k + 4 * day + j, 8) for j in range(chunks)], 1
                )


def owner_kernel(
    own, extra, g4, g3, g1, g2, prior, pthi, ptlo, chi, clo, after, omhi, omlo, info, mine, start, y, small
):
    ids = here()
    planes = 4
    width = pthi.shape[0]
    chunks = width // LANES
    tiles = triangle(width)
    got = (g1, g2, g3, g4)
    share = jnp.where(ids[0] == 2, 1.0, 0.0)
    row = lax.broadcasted_iota(jnp.int32, (LANES, LANES), 0)
    column = lax.broadcasted_iota(jnp.int32, (LANES, LANES), 1)
    spread(extra, got, small)

    def line(s, first, gap):
        return line_of(small, s, first, gap)

    def summed(first, gap):
        others = line(1, first, gap) + (line(2, first, gap) + (line(3, first, gap) + line(4, first, gap)))
        return line(0, first, gap) * share + others

    def added(at):
        return (g1[at].astype(F32) + g2[at].astype(F32)) + (g3[at].astype(F32) + g4[at].astype(F32))

    def put(day, i, j, piece):
        hi, lo = split(piece)
        omhi[day, i * LANES : (i + 1) * LANES, j * LANES : (j + 1) * LANES] = hi
        omlo[day, i * LANES : (i + 1) * LANES, j * LANES : (j + 1) * LANES] = lo

    sides = [n for n, (i, j) in enumerate(tiles) if i != j]
    middles = [n for n, (i, j) in enumerate(tiles) if i == j]

    def unpack(day):
        for i, n in enumerate(middles):
            both = added(2 * len(sides) + i)
            part = jnp.where(row < column if day else row > column, both, 0.0)
            others = sum(line(s, DIAG + 12 * day + i, 4) for s in range(1, 5))
            piece = own[day * len(tiles) + n] * share + (part + part.T)
            put(day, i, i, piece + jnp.where(row == column, others, 0.0))
        for m, n in enumerate(sides):
            i, j = tiles[n]
            piece = own[day * len(tiles) + n] * share + added(day * len(sides) + m)
            put(day, i, j, piece)
            put(day, j, i, piece.T)

    for day in range(2):
        info[day] = jnp.concatenate([summed(12 * day + j, 4) for j in range(chunks)], 1)
    held = ids[5]
    source = lax.rem(ids[1] // held - ids[0] + planes, planes)
    for day in range(2):
        for j in range(chunks):
            r = DAMP + 24 * lax.rem(ids[1], held) + 4 * day + j
            mine[day : day + 1, j * LANES : (j + 1) * LANES] = small[source, pl.ds(r, 1), :] + (
                small[source, pl.ds(r + 8, 1), :] + small[source, pl.ds(r + 16, 1), :]
            )
    first = (ids[1] == 0) & (ids[0] == owner_plane(0))
    start[...] = jnp.where(first, prior[...], 0.0)

    @pl.when(first)
    def _():
        state = prior[...]
        for day in range(2):
            unpack(day)
            state = one_day(day, state, mine, pthi, ptlo, omhi, omlo, info, chi, clo)
        y[...] = state

    @pl.when(jnp.logical_not(first))
    def _():
        for day in range(2):
            unpack(day)
        y[...] = jnp.zeros(y.shape, F32)


def second_kernel(acc, got, mine, pthi, ptlo, omhi, omlo, info, chi, clo, total, y):
    total[...] = acc[...] + got[...]
    y[...] = jnp.zeros(y.shape, F32)

    @pl.when(here()[1] == 1)
    def _():
        state = acc[...] + got[...]
        for day in range(2):
            state = one_day(day, state, mine, pthi, ptlo, omhi, omlo, info, chi, clo)
        y[...] = state


def maps_kernel(after, omhi, omlo, info, chi, clo, pt, damping, *rest):
    late = len(rest) == 10
    b1hi, b1lo, b2hi, b2lo, off = rest[-5:]
    parts = ((b1hi, b1lo), (b2hi, b2lo))

    @pl.when((here()[1] == 1) == late)
    def _():
        for day in range(2):
            moved = pt[...] * damping[day : day + 1, :]
            taken = mm(moved, omhi[day], omlo[day])
            step = moved - mm(taken, chi[...], clo[...])
            parts[day][0][...], parts[day][1][...] = split(step)
            off[day : day + 1, :] = mv(info[day], chi[...], clo[...])


def both_kernel(after, b1hi, b1lo, b2hi, b2lo, off, bchi, bclo, offset):
    both = jnp.dot(b1hi[...], b2hi[...], preferred_element_type=F32) + (
        jnp.dot(b1lo[...], b2hi[...], preferred_element_type=F32)
        + jnp.dot(b1hi[...], b2lo[...], preferred_element_type=F32)
    )
    bchi[...], bclo[...] = split(both)
    offset[...] = mv(off[0:1, :], b2hi[...], b2lo[...]) + off[1:2, :]


def hop_kernel(after, acc, got, bchi, bclo, offset, total, y):
    state = acc[...] + got[...]
    total[...] = state
    y[...] = mv(state, bchi[...], bclo[...]) + offset[...]


def whole_of(hi, lo):
    return hi[...].astype(F32) + lo[...].astype(F32)


def pairs_kernel(
    after, b1hi, b1lo, bchi, bclo, off, offset, table, pthi, ptlo, mthi, mtlo,
    khi, klo, ohi, olo, ehi, elo, shift, held,
):
    span = here()[1]
    total = table.shape[0]
    spans = total // 2

    @pl.when(span >= spans - 2)
    def _():
        @pl.loop(spans - 1 - span, khi.shape[0])
        def _(k):
            scaled = whole_of(mthi, mtlo) * table[pl.ds(2 * (spans - 2 - k) + 1, 1), :]
            khi[k], klo[k] = split(mm(scaled, mthi[...], mtlo[...]))

        within = table[pl.ds(2 * span + 1, 1), :]
        after_d = table[pl.ds(jnp.minimum(2 * span + 2, total - 1), 1), :] * jnp.where(span == spans - 1, 0.0, 1.0)
        one, two = off[0:1, :], offset[...]
        odd = two - mv(mv(two, pthi[...], ptlo[...]) * (after_d * after_d), mthi[...], mtlo[...])
        even = one + mv(
            odd * within - mv(one, pthi[...], ptlo[...]) * (within * within), mthi[...], mtlo[...]
        )
        shift[0:1, :] = odd
        shift[1:2, :] = even
        moved = mm(whole_of(bchi, bclo), pthi[...], ptlo[...]) * (after_d * after_d)
        held[...] = whole_of(bchi, bclo) - mm(moved, mthi[...], mtlo[...])
        ohi[...], olo[...] = split(held[...])
        moved = mm(whole_of(b1hi, b1lo), pthi[...], ptlo[...]) * (within * within)
        moved = held[...] * within - moved
        ehi[...], elo[...] = split(whole_of(b1hi, b1lo) + mm(moved, mthi[...], mtlo[...]))


def last_kernel(
    acc, got, b1hi, b1lo, b2hi, b2lo, bchi, bclo, off, offset, table, pthi, ptlo, mthi, mtlo,
    khi, klo, ohi, olo, ehi, elo, shift, out, shares, means,
):
    span = here()[1]
    total, width = shares.shape
    spans = total // 2
    chunks = width // LANES
    shares[...] = jnp.zeros(shares.shape, F32)

    def step(k, v):
        t = 2 * span - 1 - k
        v = mv(v * table[pl.ds(t + 1, 1), :], mthi[...], mtlo[...])
        shares[pl.ds(t, 1), :] = v
        return v

    @pl.when(span < spans - 2)
    def _():
        state = acc[...] + got[...]
        one = mv(state, b1hi[...], b1lo[...]) + off[0:1, :]
        two = mv(one, b2hi[...], b2lo[...]) + off[1:2, :]
        both = jnp.concatenate([one, two], 0)
        within = table[pl.ds(2 * span + 1, 1), :]
        damped = jnp.concatenate([within, table[pl.ds(2 * span + 2, 1), :]], 0)
        const = both - few(few(both, pthi[...], ptlo[...]) * damped * damped, mthi[...], mtlo[...])
        even = const[0:1] + mv(const[1:2] * within, mthi[...], mtlo[...])
        shares[pl.ds(2 * span + 1, 1), :] = const[1:2]
        shares[pl.ds(2 * span, 1), :] = even
        means[0:2, :] = both
        lax.fori_loop(0, 2 * span, step, even)

    @pl.when(span >= spans - 2)
    def _():
        state = acc[...] + got[...]
        even = mv(state, ehi[...], elo[...]) + shift[1:2, :]
        v, damped_rows = even, []
        for k in range(khi.shape[0]):
            t = 2 * (spans - 1 - k)
            damped = v * table[t : t + 1, :]
            damped_rows.append(damped)
            reached = mv(damped, khi[k], klo[k])
            v = reached if k else jnp.where(span == spans - 1, reached, v)
            shares[t - 2 : t - 1, :] = v
        odd = mv(state, ohi[...], olo[...]) + shift[0:1, :]
        means[0:1, :] = mv(state, b1hi[...], b1lo[...]) + off[0:1, :]
        means[1:2, :] = mv(state, bchi[...], bclo[...]) + offset[...]
        batch = jnp.concatenate(damped_rows + [jnp.zeros((1, width), F32)] * (-len(damped_rows) % 8), 0)
        batch = mm(batch, mthi[...], mtlo[...])
        for k in range(khi.shape[0]):
            t = 2 * (spans - 1 - k)
            shares[t - 1 : t, :] = batch[k : k + 1]
        shares[pl.ds(2 * span + 1, 1), :] = odd
        shares[pl.ds(2 * span, 1), :] = even
        lax.fori_loop(2 * khi.shape[0] - 2 * (spans - 1 - span), 2 * span, step, v)

    for c in range(spans):
        for q in range(chunks):
            out[c * chunks + q, 0:2, :] = shares[2 * c : 2 * c + 2, q * LANES : (q + 1) * LANES]
    for q in range(chunks):
        out[span * chunks + q, 2:4, :] = means[0:2, q * LANES : (q + 1) * LANES]


def add_kernel(parts, filt, smooth):
    ids = here()
    spans = parts.shape[0] // 4
    filt[...] = parts[ids[4], 2:4, :]
    smooth[...] = sum(parts[owner_plane(c) * spans + (place(c) | 1), 0:2, :] for c in range(spans))


def local(
    records,
    obs_values,
    block_day,
    block_count,
    propagator_matrix,
    analysis_cov,
    unattenuated_multiplier,
    damping,
    prior_mean,
):
    planes, held, peers = (lax.axis_size(a) for a in ("z", "y", "obs"))
    spans = planes * held
    blocks = block_day.shape[0]
    slots = records.shape[0] // blocks
    width = records.shape[1]
    days = damping.shape[0]
    assert planes == peers == 4 and days == 2 and slots == LANES and blocks == spans
    everyone = ("z", "y", "obs")

    def owner(span):
        return owner_plane(span) * spans + (place(span) | 1)

    tiles = len(triangle(width))
    extra_tiles = -(-(DAMP + 24 * held) // LANES)
    full, row = (width, width), ((1, width), F32)
    sent = run(
        pack_kernel,
        [((blocks, slots + EXTRA, width), BF16)],
        [
            (x, HBM)
            for x in (
                block_day,
                block_count,
                records,
                obs_values.reshape(blocks, slots),
                prior_mean.reshape(1, -1),
                damping,
            )
        ],
        [
            pltpu.SMEM((blocks,), jnp.int32),
            pltpu.SMEM((blocks,), jnp.int32),
            pltpu.VMEM((blocks, slots), BF16),
            pltpu.VMEM((1, width // peers), F32),
            pltpu.VMEM((days, width), F32),
            pltpu.VMEM((blocks, slots + EXTRA, width), BF16),
            pltpu.SemaphoreType.DMA((5 + 2 * blocks,)),
        ],
        limit=60,
        outs=HBM,
    )[0]
    got = lax.all_to_all(sent, ("y", "obs"), split_axis=0, concat_axis=0, tiled=True)
    span_slots = min(blocks, 8) * slots
    own, extra, pay, prior, gain = run(
        gram_kernel,
        [
            ((2 * tiles, LANES, LANES), F32),
            ((extra_tiles * LANES, LANES), F32),
            ((2 * tiles - width // LANES + extra_tiles, LANES, LANES), BF16),
            row,
            (unattenuated_multiplier.shape, F32),
        ],
        [got, unattenuated_multiplier],
        [pltpu.VMEM((width, span_slots), BF16), pltpu.VMEM((16, span_slots), BF16)],
        flops=4 * width * width * blocks * slots,
    )
    def swap(x, bit):
        return lax.ppermute(x, "obs", [(i, i ^ bit) for i in range(peers)])

    def plane_sum(s):
        return lax.ppermute(
            pay, everyone, [((owner_plane(p) + s) % planes * spans + place(p), owner(p)) for p in range(spans)]
        )

    fourth = lax.ppermute(
        pay, everyone, [(spans + place(p), owner(p)) for p in range(spans) if place(p) % 2 == 0]
    )
    third, first, second = plane_sum(3), plane_sum(1), plane_sum(2)
    (gains,) = run(stack_kernel, [((2,) + gain.shape, F32)], [gain, swap(gain, 2)])
    mthi, mtlo = run(gain_kernel, [(full, BF16)] * 2, [gains, swap(gains, 1)])
    pt, pthi, ptlo, chi, clo = run(
        prep_kernel, [(full, F32)] + [(full, BF16)] * 4, [propagator_matrix, analysis_cov]
    )
    smalls = pltpu.VMEM((planes + 1, extra_tiles * LANES, LANES), F32)
    omhi, omlo, info, mine, acc, y = run(
        owner_kernel,
        [((days,) + full, BF16)] * 2 + [((days, 1, width), F32), ((days, width), F32), row, row],
        [
            own, extra, fourth, third, first, second, prior, pthi, ptlo, chi, clo, (mthi, ANY)
        ],
        [smalls],
    )
    for k in range(spans - 1):
        received = lax.ppermute(y, everyone, [(owner(k), owner(k + 1))])
        if k == 0:
            maps = [(full, BF16)] * 4 + [((8, width), F32)]
            given = [omhi, omlo, info, chi, clo, pt, mine]
            flops = 24 * width**3
            days_maps = run(maps_kernel, maps, [(y, ANY), *given], flops=flops)
            acc, y = run(
                second_kernel, [row, row], [acc, received, mine, pthi, ptlo, omhi, omlo, info, chi, clo]
            )
            b1hi, b1lo, b2hi, b2lo, off = run(
                maps_kernel,
                maps,
                [(y, ANY), *given, *days_maps],
                flops=flops,
                same={8 + n: n for n in range(5)},
            )
            bchi, bclo, offset = run(
                both_kernel, [(full, BF16)] * 2 + [row], [(y, ANY), b1hi, b1lo, b2hi, b2lo, off]
            )
            (table,) = run(
                table_kernel,
                [((spans * days, width), F32)],
                [(offset, ANY), extra, first, second, third],
                [smalls],
            )
            ahead = run(
                pairs_kernel,
                [((min(spans - 1, 7),) + full, BF16)] * 2 + [(full, BF16)] * 4 + [((8, width), F32)],
                [(y, ANY), b1hi, b1lo, bchi, bclo, off, offset, table, pthi, ptlo, mthi, mtlo],
                [pltpu.VMEM(full, F32)],
            )
            side = ahead[0]
        elif k < spans - 2:
            acc, y = run(hop_kernel, [row, row], [(side, ANY), acc, received, bchi, bclo, offset])
    (answer,) = run(
        last_kernel,
        [((spans * peers, 8, LANES), F32)],
        [
            acc, received, b1hi, b1lo, b2hi, b2lo, bchi, bclo, off, offset, table, pthi, ptlo, mthi, mtlo,
            *ahead,
        ],
        [pltpu.VMEM((spans * days, width), F32), pltpu.VMEM((8, width), F32)],
    )
    parts = lax.all_to_all(answer, everyone, split_axis=0, concat_axis=0, tiled=True)
    out = ((days, LANES), F32)
    return run(add_kernel, [out, out], [parts])


def solution(mesh):
    spans, peers = mesh.devices.shape
    finer = jax.sharding.Mesh(mesh.devices.reshape(peers, spans // peers, peers), ("z", "y", "obs"))
    tm = ("z", "y")
    mapped = jax.shard_map(
        local,
        mesh=finer,
        in_specs=(
            P(("z", "y", "obs"), None),
            P(("z", "y", "obs")),
            P(("z", "y", "obs")),
            P(("z", "y", "obs")),
            P(),
            P(),
            P("obs", None),
            P(tm, None),
            P("obs"),
        ),
        out_specs=(P(tm, "obs"), P(tm, "obs")),
        check_vma=False,
    )
    return lambda *args: tuple(mapped(*args))
```

```python
import functools

import jax
import jax.numpy as jnp
from jax import lax
from jax.experimental import pallas as pl
from jax.experimental.pallas import tpu as pltpu
from jax.sharding import PartitionSpec as P

LANES = 128
F32, BF16 = jnp.float32, jnp.bfloat16
VMEM = pl.BlockSpec(memory_space=pltpu.VMEM)
SMEM = pl.BlockSpec(memory_space=pltpu.SMEM)
ANY = pl.BlockSpec(memory_space=pl.ANY)
HBM = pl.BlockSpec(memory_space=pltpu.HBM)


def run(body, out, ins, scratch=(), limit=16, flops=0, outs=VMEM, same=None):
    specs = [x[1] if isinstance(x, tuple) else VMEM for x in ins]
    arrays = [x[0] if isinstance(x, tuple) else x for x in ins]
    moved = sum(a.size * a.dtype.itemsize for a in arrays)
    return pl.pallas_call(
        body,
        out_shape=[jax.ShapeDtypeStruct(s, d) for s, d in out],
        in_specs=specs,
        out_specs=[outs] * len(out),
        scratch_shapes=list(scratch),
        input_output_aliases=same or {},
        compiler_params=pltpu.CompilerParams(vmem_limit_bytes=limit * 1024 * 1024),
        cost_estimate=pl.CostEstimate(flops=flops, bytes_accessed=moved, transcendentals=0),
    )(*arrays)


def here():
    z, y, o = (lax.axis_index(a) for a in ("z", "y", "obs"))
    held, peers = lax.axis_size("y"), lax.axis_size("obs")
    spans = held * peers
    at = y * peers + o
    seat = jnp.where(z == 1, at - lax.rem(at, 2), at)
    span = seat
    for bit in range(1, spans.bit_length()):
        span = span ^ (seat >> bit)
    c = z * held + y
    seat = c ^ (c >> 1)
    return z, span, o, c, (1 + (seat & 1)) * spans + (seat | 1), held


def triangle(width):
    parts = width // LANES
    return [(i, j) for i in range(parts) for j in range(i + 1)]


def split(x):
    hi = x.astype(BF16)
    return hi, (x - hi.astype(F32)).astype(BF16)


def mm(x, hi, lo):
    xhi, xlo = split(x)
    dot = functools.partial(jnp.dot, preferred_element_type=F32)
    return dot(xhi, hi) + (dot(xlo, hi) + dot(xhi, lo))


def mv(x, hi, lo):
    wide = jnp.broadcast_to(x, (8, x.shape[1]))
    row = lax.broadcasted_iota(jnp.int32, wide.shape, 0)
    top = wide.astype(BF16).astype(F32)
    both = jnp.where(row == 0, top, jnp.where(row == 1, wide - top, 0.0)).astype(BF16)
    first = jnp.dot(both, hi, preferred_element_type=F32)
    second = jnp.dot(both, lo, preferred_element_type=F32)
    return first[0:1] + (first[1:2] + second[0:1])


def parts3(x):
    out = []
    for _ in range(3):
        piece = x.astype(BF16).astype(F32)
        out.append(piece)
        x = x - piece
    return out


def place(span):
    return span ^ (span >> 1)


def owner_plane(span):
    return 1 + place(span) % 2


EXTRA = 8
DIAG, DAMP = 24, 48


def pack_kernel(
    day, count, rows, values, prior, damping, out, day_s, count_s, values_v, prior_v, damping_v, stage, sems
):
    blocks = out.shape[0]
    slots = out.shape[1] - EXTRA
    width = out.shape[2]
    small = [(day, day_s), (count, count_s), (values, values_v), (prior, prior_v), (damping, damping_v)]
    copies = [pltpu.make_async_copy(src, dst, sems.at[n]) for n, (src, dst) in enumerate(small)]
    large = [
        pltpu.make_async_copy(
            rows.at[pl.ds(k * slots, slots)], stage.at[place(k), pl.ds(0, slots)], sems.at[len(small) + k]
        )
        for k in range(blocks)
    ]
    for copy in copies + large:
        copy.start()
    for copy in copies:
        copy.wait()
    first, second, third = parts3(prior_v[...])
    below = jnp.concatenate(
        [jnp.concatenate([second, third, jnp.zeros((1, width - 2 * LANES), F32)], 1)] + parts3(damping_v[...]), 0
    )
    held = values_v[...].astype(F32)
    for k in range(blocks):
        line = jnp.concatenate(
            [
                held[k : k + 1, :],
                jnp.full((1, LANES), day_s[k], jnp.int32).astype(F32),
                jnp.full((1, LANES), count_s[k], jnp.int32).astype(F32),
                first,
            ],
            1,
        )
        stage[place(k), slots : slots + EXTRA, :] = jnp.concatenate([line, below], 0).astype(BF16)
    sends = [
        pltpu.make_async_copy(stage.at[place(k)], out.at[place(k)], sems.at[len(small) + blocks + k])
        for k in range(blocks)
    ]
    for k in range(blocks):
        large[k].wait()
        sends[k].start()
    for copy in sends:
        copy.wait()


def gram_kernel(got, gain, own, extra, pay, prior, gain_out, turned, marks):
    blocks = got.shape[0]
    slots = got.shape[1] - EXTRA
    width = got.shape[2]
    chunks = width // LANES
    tiles = triangle(width)
    group = min(blocks, 8)
    half = 2 * LANES
    gain_out[...] = gain[...]
    extra[...] = jnp.zeros(extra.shape, F32)

    def one(first, fresh):
        for k in range(group):
            at = slice(k * slots, (k + 1) * slots)
            line = got[first + k, slots : slots + EXTRA, :].astype(F32)
            valid = lax.broadcasted_iota(jnp.int32, (1, slots), 1).astype(F32) < line[0:1, 2 * LANES : 3 * LANES]
            day = line[0:1, LANES : 2 * LANES]
            values = line[0:1, 0:LANES]
            kept = [jnp.where(valid & (day == d), 1.0, 0.0) for d in (0.0, 1.0)]
            marks[:, at] = jnp.concatenate(
                kept + [kept[0] * values, kept[1] * values, jnp.zeros((12, slots), F32)], 0
            ).astype(BF16)
            turned[:, at] = got[first + k, 0:slots, :].T
        source = jnp.concatenate([got[first + k, 0:slots, :] for k in range(group)], 0)
        info = jnp.dot(marks[...], source, preferred_element_type=F32)
        for d in range(2):
            for top in range(0, width, half):
                left = turned[top : top + half, :] * marks[d : d + 1, :]
                block = jnp.dot(left, source[:, : top + half], preferred_element_type=F32)
                for n, (i, j) in enumerate(tiles):
                    if top <= i * LANES < top + half:
                        r = i * LANES - top
                        piece = block[r : r + LANES, j * LANES : (j + 1) * LANES]
                        at = d * len(tiles) + n
                        own[at] = piece if fresh else own[at] + piece
            for j in range(chunks):
                piece = info[2 + d : 3 + d, j * LANES : (j + 1) * LANES]
                r = 12 * d + j
                extra[r : r + 1, :] = piece if fresh else extra[r : r + 1, :] + piece

    if blocks == group:
        one(0, True)
    else:
        own[...] = jnp.zeros(own.shape, F32)

        @pl.loop(0, blocks // group)
        def _(g):
            one(g * group, False)

    row = lax.broadcasted_iota(jnp.int32, (LANES, LANES), 0)
    column = lax.broadcasted_iota(jnp.int32, (LANES, LANES), 1)
    sides = [n for n, (i, j) in enumerate(tiles) if i != j]
    middles = [n for n, (i, j) in enumerate(tiles) if i == j]
    for d in range(2):
        for part, piece in enumerate(parts3(extra[12 * d : 12 * d + chunks, :])):
            extra[12 * d + 4 * part : 12 * d + 4 * part + chunks, :] = piece
        for m, n in enumerate(sides):
            pay[d * len(sides) + m] = own[d * len(tiles) + n].astype(BF16)
    for i, n in enumerate(middles):
        squares = [own[d * len(tiles) + n] for d in range(2)]
        pay[2 * len(sides) + i] = jnp.where(row >= column, squares[0], squares[1]).astype(BF16)
        for d in range(2):
            line = jnp.sum(jnp.where(row == column, squares[d], 0.0), axis=0, keepdims=True)
            for part, piece in enumerate(parts3(line)):
                r = DIAG + 12 * d + 4 * part + i
                extra[r : r + 1, :] = piece
    for q in range(chunks):
        line = got[q, slots : slots + EXTRA, :].astype(F32)
        prior[:, q * LANES : (q + 1) * LANES] = line[0:1, 3 * LANES : 4 * LANES] + (
            line[1:2, 0:LANES] + line[1:2, LANES : 2 * LANES]
        )
    for y in range(blocks // 4):
        line = got[4 * y, slots : slots + EXTRA, :].astype(F32)
        for k in range(6):
            for j in range(chunks):
                r = DAMP + 24 * y + 4 * k + j
                extra[r : r + 1, :] = line[2 + k : 3 + k, j * LANES : (j + 1) * LANES]
    small_at = pay.shape[0] - extra.shape[0] // LANES
    for n in range(extra.shape[0] // LANES):
        pay[small_at + n] = extra[n * LANES : (n + 1) * LANES, :].astype(BF16)


def prep_kernel(trans, cov, pt, pthi, ptlo, chi, clo):
    whole = trans[...].T
    pt[...] = whole
    pthi[...], ptlo[...] = split(whole)
    chi[...], clo[...] = split(cov[...])


def stack_kernel(one, two, out):
    out[0] = one[...]
    out[1] = two[...]


def gain_kernel(held, got, mthi, mtlo):
    ids = here()
    rows = held.shape[1]
    for step, part in enumerate((held.at[0], got.at[0], held.at[1], got.at[1])):
        holder = ids[2] ^ step
        at = pl.ds(pl.multiple_of(holder * rows, rows), rows)
        hi, lo = split(part[...].T)
        mthi[:, at] = hi
        mtlo[:, at] = lo


def few(x, hi, lo):
    top = x.astype(BF16).astype(F32)
    both = jnp.concatenate([top, x - top, jnp.zeros((4, x.shape[1]), F32)], 0).astype(BF16)
    first = jnp.dot(both, hi, preferred_element_type=F32)
    second = jnp.dot(both, lo, preferred_element_type=F32)
    return first[0:2] + (first[2:4] + second[0:2])


def one_day(day, state, damping, pthi, ptlo, omhi, omlo, info, chi, clo):
    moved = mv(state, pthi[...], ptlo[...]) * damping[day : day + 1, :]
    gap = mv(moved, omhi[day], omlo[day]) - info[day]
    return moved - mv(gap, chi[...], clo[...])


def spread(extra, got, small):
    small_at = got[0].shape[0] - extra.shape[0] // LANES
    small[0] = extra[...]
    for s, part in enumerate(got):
        for n in range(extra.shape[0] // LANES):
            small[s + 1, n * LANES : (n + 1) * LANES, :] = part[small_at + n].astype(F32)


def line_of(small, s, first, gap):
    return small[s, first : first + 1, :] + (
        small[s, first + gap : first + gap + 1, :] + small[s, first + 2 * gap : first + 2 * gap + 1, :]
    )


def table_kernel(after, extra, g1, g2, g3, table, small):
    ids = here()
    planes = 4
    chunks = table.shape[1] // LANES
    held = table.shape[0] // 2 // planes
    spread(extra, (g1, g2, g3), small)
    for s in range(planes):
        plane = lax.rem(ids[0] + s, planes)
        for k in range(held):
            for day in range(2):
                table[pl.ds(2 * (plane * held + k) + day, 1), :] = jnp.concatenate(
                    [line_of(small, s, DAMP + 24 * k + 4 * day + j, 8) for j in range(chunks)], 1
                )


def owner_kernel(
    own, extra, g4, g3, g1, g2, prior, pthi, ptlo, chi, clo, after, omhi, omlo, info, mine, start, y, small
):
    ids = here()
    planes = 4
    width = pthi.shape[0]
    chunks = width // LANES
    tiles = triangle(width)
    got = (g1, g2, g3, g4)
    share = jnp.where(ids[0] == 2, 1.0, 0.0)
    row = lax.broadcasted_iota(jnp.int32, (LANES, LANES), 0)
    column = lax.broadcasted_iota(jnp.int32, (LANES, LANES), 1)
    spread(extra, got, small)

    def line(s, first, gap):
        return line_of(small, s, first, gap)

    def summed(first, gap):
        others = line(1, first, gap) + (line(2, first, gap) + (line(3, first, gap) + line(4, first, gap)))
        return line(0, first, gap) * share + others

    def added(at):
        return (g1[at].astype(F32) + g2[at].astype(F32)) + (g3[at].astype(F32) + g4[at].astype(F32))

    def put(day, i, j, piece):
        hi, lo = split(piece)
        omhi[day, i * LANES : (i + 1) * LANES, j * LANES : (j + 1) * LANES] = hi
        omlo[day, i * LANES : (i + 1) * LANES, j * LANES : (j + 1) * LANES] = lo

    sides = [n for n, (i, j) in enumerate(tiles) if i != j]
    middles = [n for n, (i, j) in enumerate(tiles) if i == j]

    def unpack(day):
        for i, n in enumerate(middles):
            both = added(2 * len(sides) + i)
            part = jnp.where(row < column if day else row > column, both, 0.0)
            others = sum(line(s, DIAG + 12 * day + i, 4) for s in range(1, 5))
            piece = own[day * len(tiles) + n] * share + (part + part.T)
            put(day, i, i, piece + jnp.where(row == column, others, 0.0))
        for m, n in enumerate(sides):
            i, j = tiles[n]
            piece = own[day * len(tiles) + n] * share + added(day * len(sides) + m)
            put(day, i, j, piece)
            put(day, j, i, piece.T)

    for day in range(2):
        info[day] = jnp.concatenate([summed(12 * day + j, 4) for j in range(chunks)], 1)
    held = ids[5]
    source = lax.rem(ids[1] // held - ids[0] + planes, planes)
    for day in range(2):
        for j in range(chunks):
            r = DAMP + 24 * lax.rem(ids[1], held) + 4 * day + j
            mine[day : day + 1, j * LANES : (j + 1) * LANES] = small[source, pl.ds(r, 1), :] + (
                small[source, pl.ds(r + 8, 1), :] + small[source, pl.ds(r + 16, 1), :]
            )
    first = (ids[1] == 0) & (ids[0] == owner_plane(0))
    start[...] = jnp.where(first, prior[...], 0.0)

    @pl.when(first)
    def _():
        state = prior[...]
        for day in range(2):
            unpack(day)
            state = one_day(day, state, mine, pthi, ptlo, omhi, omlo, info, chi, clo)
        y[...] = state

    @pl.when(jnp.logical_not(first))
    def _():
        for day in range(2):
            unpack(day)
        y[...] = jnp.zeros(y.shape, F32)


def second_kernel(acc, got, mine, pthi, ptlo, omhi, omlo, info, chi, clo, total, y):
    total[...] = acc[...] + got[...]
    y[...] = jnp.zeros(y.shape, F32)

    @pl.when(here()[1] == 1)
    def _():
        state = acc[...] + got[...]
        for day in range(2):
            state = one_day(day, state, mine, pthi, ptlo, omhi, omlo, info, chi, clo)
        y[...] = state


def maps_kernel(after, omhi, omlo, info, chi, clo, pt, damping, *rest):
    late = len(rest) == 10
    b1hi, b1lo, b2hi, b2lo, off = rest[-5:]
    parts = ((b1hi, b1lo), (b2hi, b2lo))

    @pl.when((here()[1] == 1) == late)
    def _():
        for day in range(2):
            moved = pt[...] * damping[day : day + 1, :]
            taken = mm(moved, omhi[day], omlo[day])
            step = moved - mm(taken, chi[...], clo[...])
            parts[day][0][...], parts[day][1][...] = split(step)
            off[day : day + 1, :] = mv(info[day], chi[...], clo[...])


def both_kernel(after, b1hi, b1lo, b2hi, b2lo, off, bchi, bclo, offset):
    both = jnp.dot(b1hi[...], b2hi[...], preferred_element_type=F32) + (
        jnp.dot(b1lo[...], b2hi[...], preferred_element_type=F32)
        + jnp.dot(b1hi[...], b2lo[...], preferred_element_type=F32)
    )
    bchi[...], bclo[...] = split(both)
    offset[...] = mv(off[0:1, :], b2hi[...], b2lo[...]) + off[1:2, :]


def hop_kernel(after, acc, got, bchi, bclo, offset, total, y):
    state = acc[...] + got[...]
    total[...] = state
    y[...] = mv(state, bchi[...], bclo[...]) + offset[...]


def whole_of(hi, lo):
    return hi[...].astype(F32) + lo[...].astype(F32)


def pairs_kernel(
    after, b1hi, b1lo, bchi, bclo, off, offset, table, pthi, ptlo, mthi, mtlo, khi, klo, ehi, elo, shift
):
    total = table.shape[0]
    spans = total // 2

    @pl.when(here()[1] == spans - 1)
    def _():
        @pl.loop(0, khi.shape[0])
        def _(k):
            scaled = whole_of(mthi, mtlo) * table[pl.ds(2 * (spans - 2 - k) + 1, 1), :]
            khi[k], klo[k] = split(mm(scaled, mthi[...], mtlo[...]))

        within = table[total - 1 : total, :]
        one = off[0:1, :]
        ahead = mv(one, pthi[...], ptlo[...]) * (within * within)
        shift[0:1, :] = one + mv(offset[...] * within - ahead, mthi[...], mtlo[...])
        whole = whole_of(b1hi, b1lo)
        ahead = mm(whole, pthi[...], ptlo[...]) * (within * within)
        moved = whole_of(bchi, bclo) * within - ahead
        ehi[...], elo[...] = split(whole + mm(moved, mthi[...], mtlo[...]))


def last_kernel(
    acc, got, b1hi, b1lo, b2hi, b2lo, bchi, bclo, off, offset, table, pthi, ptlo, mthi, mtlo,
    khi, klo, ehi, elo, shift, out, shares, means,
):
    span = here()[1]
    total, width = shares.shape
    spans = total // 2
    chunks = width // LANES
    shares[...] = jnp.zeros(shares.shape, F32)

    def step(k, v):
        t = 2 * span - 1 - k
        v = mv(v * table[pl.ds(t + 1, 1), :], mthi[...], mtlo[...])
        shares[pl.ds(t, 1), :] = v
        return v

    @pl.when(span < spans - 1)
    def _():
        state = acc[...] + got[...]
        one = mv(state, b1hi[...], b1lo[...]) + off[0:1, :]
        two = mv(one, b2hi[...], b2lo[...]) + off[1:2, :]
        both = jnp.concatenate([one, two], 0)
        within = table[pl.ds(2 * span + 1, 1), :]
        damped = jnp.concatenate([within, table[pl.ds(2 * span + 2, 1), :]], 0)
        const = both - few(few(both, pthi[...], ptlo[...]) * damped * damped, mthi[...], mtlo[...])
        even = const[0:1] + mv(const[1:2] * within, mthi[...], mtlo[...])
        shares[pl.ds(2 * span + 1, 1), :] = const[1:2]
        shares[pl.ds(2 * span, 1), :] = even
        means[0:2, :] = both
        lax.fori_loop(0, 2 * span, step, even)

    @pl.when(span == spans - 1)
    def _():
        state = acc[...] + got[...]
        v, damped_rows = mv(state, ehi[...], elo[...]) + shift[0:1, :], []
        shares[total - 2 : total - 1, :] = v
        for k in range(khi.shape[0]):
            t = 2 * (spans - 1 - k)
            damped_rows.append(v * table[t : t + 1, :])
            v = mv(damped_rows[-1], khi[k], klo[k])
            shares[t - 2 : t - 1, :] = v
        two = mv(state, bchi[...], bclo[...]) + offset[...]
        means[0:1, :] = mv(state, b1hi[...], b1lo[...]) + off[0:1, :]
        means[1:2, :] = two
        shares[total - 1 : total, :] = two
        batch = jnp.concatenate(damped_rows + [jnp.zeros((1, width), F32)] * (-len(damped_rows) % 8), 0)
        batch = mm(batch, mthi[...], mtlo[...])
        for k in range(khi.shape[0]):
            t = 2 * (spans - 1 - k)
            shares[t - 1 : t, :] = batch[k : k + 1]
        lax.fori_loop(2 * khi.shape[0], 2 * span, step, v)

    for c in range(spans):
        for q in range(chunks):
            out[c * chunks + q, 0:2, :] = shares[2 * c : 2 * c + 2, q * LANES : (q + 1) * LANES]
    for q in range(chunks):
        out[span * chunks + q, 2:4, :] = means[0:2, q * LANES : (q + 1) * LANES]


def add_kernel(parts, filt, smooth):
    ids = here()
    spans = parts.shape[0] // 4
    filt[...] = parts[ids[4], 2:4, :]
    smooth[...] = sum(parts[owner_plane(c) * spans + (place(c) | 1), 0:2, :] for c in range(spans))


def local(
    records,
    obs_values,
    block_day,
    block_count,
    propagator_matrix,
    analysis_cov,
    unattenuated_multiplier,
    damping,
    prior_mean,
):
    planes, held, peers = (lax.axis_size(a) for a in ("z", "y", "obs"))
    spans = planes * held
    blocks = block_day.shape[0]
    slots = records.shape[0] // blocks
    width = records.shape[1]
    days = damping.shape[0]
    assert planes == peers == 4 and days == 2 and slots == LANES and blocks == spans
    everyone = ("z", "y", "obs")

    def owner(span):
        return owner_plane(span) * spans + (place(span) | 1)

    tiles = len(triangle(width))
    extra_tiles = -(-(DAMP + 24 * held) // LANES)
    full, row = (width, width), ((1, width), F32)
    sent = run(
        pack_kernel,
        [((blocks, slots + EXTRA, width), BF16)],
        [
            (x, HBM)
            for x in (
                block_day,
                block_count,
                records,
                obs_values.reshape(blocks, slots),
                prior_mean.reshape(1, -1),
                damping,
            )
        ],
        [
            pltpu.SMEM((blocks,), jnp.int32),
            pltpu.SMEM((blocks,), jnp.int32),
            pltpu.VMEM((blocks, slots), BF16),
            pltpu.VMEM((1, width // peers), F32),
            pltpu.VMEM((days, width), F32),
            pltpu.VMEM((blocks, slots + EXTRA, width), BF16),
            pltpu.SemaphoreType.DMA((5 + 2 * blocks,)),
        ],
        limit=60,
        outs=HBM,
    )[0]
    got = lax.all_to_all(sent, ("y", "obs"), split_axis=0, concat_axis=0, tiled=True)
    span_slots = min(blocks, 8) * slots
    own, extra, pay, prior, gain = run(
        gram_kernel,
        [
            ((2 * tiles, LANES, LANES), F32),
            ((extra_tiles * LANES, LANES), F32),
            ((2 * tiles - width // LANES + extra_tiles, LANES, LANES), BF16),
            row,
            (unattenuated_multiplier.shape, F32),
        ],
        [got, unattenuated_multiplier],
        [pltpu.VMEM((width, span_slots), BF16), pltpu.VMEM((16, span_slots), BF16)],
        flops=4 * width * width * blocks * slots,
    )
    def swap(x, bit):
        return lax.ppermute(x, "obs", [(i, i ^ bit) for i in range(peers)])

    def plane_sum(s):
        return lax.ppermute(
            pay, everyone, [((owner_plane(p) + s) % planes * spans + place(p), owner(p)) for p in range(spans)]
        )

    fourth = lax.ppermute(
        pay, everyone, [(spans + place(p), owner(p)) for p in range(spans) if place(p) % 2 == 0]
    )
    third, first, second = plane_sum(3), plane_sum(1), plane_sum(2)
    (gains,) = run(stack_kernel, [((2,) + gain.shape, F32)], [gain, swap(gain, 2)])
    mthi, mtlo = run(gain_kernel, [(full, BF16)] * 2, [gains, swap(gains, 1)])
    pt, pthi, ptlo, chi, clo = run(
        prep_kernel, [(full, F32)] + [(full, BF16)] * 4, [propagator_matrix, analysis_cov]
    )
    smalls = pltpu.VMEM((planes + 1, extra_tiles * LANES, LANES), F32)
    omhi, omlo, info, mine, acc, y = run(
        owner_kernel,
        [((days,) + full, BF16)] * 2 + [((days, 1, width), F32), ((days, width), F32), row, row],
        [
            own, extra, fourth, third, first, second, prior, pthi, ptlo, chi, clo, (mthi, ANY)
        ],
        [smalls],
    )
    for k in range(spans - 1):
        received = lax.ppermute(y, everyone, [(owner(k), owner(k + 1))])
        if k == 0:
            maps = [(full, BF16)] * 4 + [((8, width), F32)]
            given = [omhi, omlo, info, chi, clo, pt, mine]
            flops = 24 * width**3
            days_maps = run(maps_kernel, maps, [(y, ANY), *given], flops=flops)
            acc, y = run(
                second_kernel, [row, row], [acc, received, mine, pthi, ptlo, omhi, omlo, info, chi, clo]
            )
            b1hi, b1lo, b2hi, b2lo, off = run(
                maps_kernel,
                maps,
                [(y, ANY), *given, *days_maps],
                flops=flops,
                same={8 + n: n for n in range(5)},
            )
            bchi, bclo, offset = run(
                both_kernel, [(full, BF16)] * 2 + [row], [(y, ANY), b1hi, b1lo, b2hi, b2lo, off]
            )
            (table,) = run(
                table_kernel,
                [((spans * days, width), F32)],
                [(offset, ANY), extra, first, second, third],
                [smalls],
            )
            ahead = run(
                pairs_kernel,
                [((min(spans - 1, 7),) + full, BF16)] * 2 + [(full, BF16)] * 2 + [((8, width), F32)],
                [(y, ANY), b1hi, b1lo, bchi, bclo, off, offset, table, pthi, ptlo, mthi, mtlo],
            )
            side = ahead[0]
        elif k < spans - 2:
            acc, y = run(hop_kernel, [row, row], [(side, ANY), acc, received, bchi, bclo, offset])
    (answer,) = run(
        last_kernel,
        [((spans * peers, 8, LANES), F32)],
        [
            acc, received, b1hi, b1lo, b2hi, b2lo, bchi, bclo, off, offset, table, pthi, ptlo, mthi, mtlo,
            *ahead,
        ],
        [pltpu.VMEM((spans * days, width), F32), pltpu.VMEM((8, width), F32)],
    )
    parts = lax.all_to_all(answer, everyone, split_axis=0, concat_axis=0, tiled=True)
    out = ((days, LANES), F32)
    return run(add_kernel, [out, out], [parts])


def solution(mesh):
    spans, peers = mesh.devices.shape
    finer = jax.sharding.Mesh(mesh.devices.reshape(peers, spans // peers, peers), ("z", "y", "obs"))
    tm = ("z", "y")
    mapped = jax.shard_map(
        local,
        mesh=finer,
        in_specs=(
            P(("z", "y", "obs"), None),
            P(("z", "y", "obs")),
            P(("z", "y", "obs")),
            P(("z", "y", "obs")),
            P(),
            P(),
            P("obs", None),
            P(tm, None),
            P("obs"),
        ),
        out_specs=(P(tm, "obs"), P(tm, "obs")),
        check_vma=False,
    )
    return lambda *args: tuple(mapped(*args))
```

```python
import functools

import jax
import jax.numpy as jnp
from jax import lax
from jax.experimental import pallas as pl
from jax.experimental.pallas import tpu as pltpu
from jax.sharding import PartitionSpec as P

LANES = 128
F32, BF16 = jnp.float32, jnp.bfloat16
VMEM = pl.BlockSpec(memory_space=pltpu.VMEM)
SMEM = pl.BlockSpec(memory_space=pltpu.SMEM)
ANY = pl.BlockSpec(memory_space=pl.ANY)
HBM = pl.BlockSpec(memory_space=pltpu.HBM)


def run(body, out, ins, scratch=(), limit=16, flops=0, outs=VMEM, same=None):
    specs = [x[1] if isinstance(x, tuple) else VMEM for x in ins]
    arrays = [x[0] if isinstance(x, tuple) else x for x in ins]
    moved = sum(a.size * a.dtype.itemsize for a in arrays)
    return pl.pallas_call(
        body,
        out_shape=[jax.ShapeDtypeStruct(s, d) for s, d in out],
        in_specs=specs,
        out_specs=[outs] * len(out),
        scratch_shapes=list(scratch),
        input_output_aliases=same or {},
        compiler_params=pltpu.CompilerParams(vmem_limit_bytes=limit * 1024 * 1024),
        cost_estimate=pl.CostEstimate(flops=flops, bytes_accessed=moved, transcendentals=0),
    )(*arrays)


def here():
    z, y, o = (lax.axis_index(a) for a in ("z", "y", "obs"))
    held, peers = lax.axis_size("y"), lax.axis_size("obs")
    spans = held * peers
    at = y * peers + o
    seat = jnp.where(z == 1, at - lax.rem(at, 2), at)
    span = seat
    for bit in range(1, spans.bit_length()):
        span = span ^ (seat >> bit)
    c = z * held + y
    seat = c ^ (c >> 1)
    return z, span, o, c, (1 + (seat & 1)) * spans + (seat | 1), held


def triangle(width):
    parts = width // LANES
    return [(i, j) for i in range(parts) for j in range(i + 1)]


def split(x):
    hi = x.astype(BF16)
    return hi, (x - hi.astype(F32)).astype(BF16)


def mm(x, hi, lo):
    xhi, xlo = split(x)
    dot = functools.partial(jnp.dot, preferred_element_type=F32)
    return dot(xhi, hi) + (dot(xlo, hi) + dot(xhi, lo))


def mv(x, hi, lo):
    wide = jnp.broadcast_to(x, (8, x.shape[1]))
    row = lax.broadcasted_iota(jnp.int32, wide.shape, 0)
    top = wide.astype(BF16).astype(F32)
    both = jnp.where(row == 0, top, jnp.where(row == 1, wide - top, 0.0)).astype(BF16)
    first = jnp.dot(both, hi, preferred_element_type=F32)
    second = jnp.dot(both, lo, preferred_element_type=F32)
    return first[0:1] + (first[1:2] + second[0:1])


def parts3(x):
    out = []
    for _ in range(3):
        piece = x.astype(BF16).astype(F32)
        out.append(piece)
        x = x - piece
    return out


def place(span):
    return span ^ (span >> 1)


def owner_plane(span):
    return 1 + place(span) % 2


EXTRA = 8
DIAG, DAMP = 24, 48


def pack_kernel(
    day, count, rows, values, prior, damping, out, day_s, count_s, values_v, prior_v, damping_v, stage, sems
):
    blocks = out.shape[0]
    slots = out.shape[1] - EXTRA
    width = out.shape[2]
    small = [(day, day_s), (count, count_s), (values, values_v), (prior, prior_v), (damping, damping_v)]
    copies = [pltpu.make_async_copy(src, dst, sems.at[n]) for n, (src, dst) in enumerate(small)]
    large = [
        pltpu.make_async_copy(
            rows.at[pl.ds(k * slots, slots)], stage.at[place(k), pl.ds(0, slots)], sems.at[len(small) + k]
        )
        for k in range(blocks)
    ]
    for copy in copies + large:
        copy.start()
    for copy in copies:
        copy.wait()
    first, second, third = parts3(prior_v[...])
    below = jnp.concatenate(
        [jnp.concatenate([second, third, jnp.zeros((1, width - 2 * LANES), F32)], 1)] + parts3(damping_v[...]), 0
    )
    held = values_v[...].astype(F32)
    for k in range(blocks):
        line = jnp.concatenate(
            [
                held[k : k + 1, :],
                jnp.full((1, LANES), day_s[k], jnp.int32).astype(F32),
                jnp.full((1, LANES), count_s[k], jnp.int32).astype(F32),
                first,
            ],
            1,
        )
        stage[place(k), slots : slots + EXTRA, :] = jnp.concatenate([line, below], 0).astype(BF16)
    sends = [
        pltpu.make_async_copy(stage.at[place(k)], out.at[place(k)], sems.at[len(small) + blocks + k])
        for k in range(blocks)
    ]
    for k in range(blocks):
        large[k].wait()
        sends[k].start()
    for copy in sends:
        copy.wait()


def gram_kernel(got, gain, own, extra, pay, prior, gain_out, turned, marks):
    blocks = got.shape[0]
    slots = got.shape[1] - EXTRA
    width = got.shape[2]
    chunks = width // LANES
    tiles = triangle(width)
    group = min(blocks, 8)
    half = 2 * LANES
    gain_out[...] = gain[...]
    extra[...] = jnp.zeros(extra.shape, F32)

    def one(first, fresh):
        for k in range(group):
            at = slice(k * slots, (k + 1) * slots)
            line = got[first + k, slots : slots + EXTRA, :].astype(F32)
            valid = lax.broadcasted_iota(jnp.int32, (1, slots), 1).astype(F32) < line[0:1, 2 * LANES : 3 * LANES]
            day = line[0:1, LANES : 2 * LANES]
            values = line[0:1, 0:LANES]
            kept = [jnp.where(valid & (day == d), 1.0, 0.0) for d in (0.0, 1.0)]
            marks[:, at] = jnp.concatenate(
                kept + [kept[0] * values, kept[1] * values, jnp.zeros((12, slots), F32)], 0
            ).astype(BF16)
            turned[:, at] = got[first + k, 0:slots, :].T
        source = jnp.concatenate([got[first + k, 0:slots, :] for k in range(group)], 0)
        info = jnp.dot(marks[...], source, preferred_element_type=F32)
        for d in range(2):
            for top in range(0, width, half):
                left = turned[top : top + half, :] * marks[d : d + 1, :]
                block = jnp.dot(left, source[:, : top + half], preferred_element_type=F32)
                for n, (i, j) in enumerate(tiles):
                    if top <= i * LANES < top + half:
                        r = i * LANES - top
                        piece = block[r : r + LANES, j * LANES : (j + 1) * LANES]
                        at = d * len(tiles) + n
                        own[at] = piece if fresh else own[at] + piece
            for j in range(chunks):
                piece = info[2 + d : 3 + d, j * LANES : (j + 1) * LANES]
                r = 12 * d + j
                extra[r : r + 1, :] = piece if fresh else extra[r : r + 1, :] + piece

    if blocks == group:
        one(0, True)
    else:
        own[...] = jnp.zeros(own.shape, F32)

        @pl.loop(0, blocks // group)
        def _(g):
            one(g * group, False)

    row = lax.broadcasted_iota(jnp.int32, (LANES, LANES), 0)
    column = lax.broadcasted_iota(jnp.int32, (LANES, LANES), 1)
    sides = [n for n, (i, j) in enumerate(tiles) if i != j]
    middles = [n for n, (i, j) in enumerate(tiles) if i == j]
    for d in range(2):
        for part, piece in enumerate(parts3(extra[12 * d : 12 * d + chunks, :])):
            extra[12 * d + 4 * part : 12 * d + 4 * part + chunks, :] = piece
        for m, n in enumerate(sides):
            pay[d * len(sides) + m] = own[d * len(tiles) + n].astype(BF16)
    for i, n in enumerate(middles):
        squares = [own[d * len(tiles) + n] for d in range(2)]
        pay[2 * len(sides) + i] = jnp.where(row >= column, squares[0], squares[1]).astype(BF16)
        for d in range(2):
            line = jnp.sum(jnp.where(row == column, squares[d], 0.0), axis=0, keepdims=True)
            for part, piece in enumerate(parts3(line)):
                r = DIAG + 12 * d + 4 * part + i
                extra[r : r + 1, :] = piece
    for q in range(chunks):
        line = got[q, slots : slots + EXTRA, :].astype(F32)
        prior[:, q * LANES : (q + 1) * LANES] = line[0:1, 3 * LANES : 4 * LANES] + (
            line[1:2, 0:LANES] + line[1:2, LANES : 2 * LANES]
        )
    for y in range(blocks // 4):
        line = got[4 * y, slots : slots + EXTRA, :].astype(F32)
        for k in range(6):
            for j in range(chunks):
                r = DAMP + 24 * y + 4 * k + j
                extra[r : r + 1, :] = line[2 + k : 3 + k, j * LANES : (j + 1) * LANES]
    small_at = pay.shape[0] - extra.shape[0] // LANES
    for n in range(extra.shape[0] // LANES):
        pay[small_at + n] = extra[n * LANES : (n + 1) * LANES, :].astype(BF16)


def prep_kernel(trans, cov, pt, pthi, ptlo, chi, clo):
    whole = trans[...].T
    pt[...] = whole
    pthi[...], ptlo[...] = split(whole)
    chi[...], clo[...] = split(cov[...])


def stack_kernel(one, two, out):
    out[0] = one[...]
    out[1] = two[...]


def gain_kernel(held, got, mthi, mtlo):
    ids = here()
    rows = held.shape[1]
    for step, part in enumerate((held.at[0], got.at[0], held.at[1], got.at[1])):
        holder = ids[2] ^ step
        at = pl.ds(pl.multiple_of(holder * rows, rows), rows)
        hi, lo = split(part[...].T)
        mthi[:, at] = hi
        mtlo[:, at] = lo


def few(x, hi, lo):
    top = x.astype(BF16).astype(F32)
    both = jnp.concatenate([top, x - top, jnp.zeros((4, x.shape[1]), F32)], 0).astype(BF16)
    first = jnp.dot(both, hi, preferred_element_type=F32)
    second = jnp.dot(both, lo, preferred_element_type=F32)
    return first[0:2] + (first[2:4] + second[0:2])


def one_day(day, state, damping, pthi, ptlo, omhi, omlo, info, chi, clo):
    moved = mv(state, pthi[...], ptlo[...]) * damping[day : day + 1, :]
    gap = mv(moved, omhi[day], omlo[day]) - info[day]
    return moved - mv(gap, chi[...], clo[...])


def spread(extra, got, small):
    small_at = got[0].shape[0] - extra.shape[0] // LANES
    small[0] = extra[...]
    for s, part in enumerate(got):
        for n in range(extra.shape[0] // LANES):
            small[s + 1, n * LANES : (n + 1) * LANES, :] = part[small_at + n].astype(F32)


def line_of(small, s, first, gap):
    return small[s, first : first + 1, :] + (
        small[s, first + gap : first + gap + 1, :] + small[s, first + 2 * gap : first + 2 * gap + 1, :]
    )


def table_kernel(after, extra, g1, g2, g3, table, small):
    ids = here()
    planes = 4
    chunks = table.shape[1] // LANES
    held = table.shape[0] // 2 // planes
    spread(extra, (g1, g2, g3), small)
    for s in range(planes):
        plane = lax.rem(ids[0] + s, planes)
        for k in range(held):
            for day in range(2):
                table[pl.ds(2 * (plane * held + k) + day, 1), :] = jnp.concatenate(
                    [line_of(small, s, DAMP + 24 * k + 4 * day + j, 8) for j in range(chunks)], 1
                )


def owner_kernel(
    own, extra, g4, g3, g1, g2, prior, pthi, ptlo, chi, clo, after, omhi, omlo, info, mine, start, y, small
):
    ids = here()
    planes = 4
    width = pthi.shape[0]
    chunks = width // LANES
    tiles = triangle(width)
    got = (g1, g2, g3, g4)
    share = jnp.where(ids[0] == 2, 1.0, 0.0)
    row = lax.broadcasted_iota(jnp.int32, (LANES, LANES), 0)
    column = lax.broadcasted_iota(jnp.int32, (LANES, LANES), 1)
    spread(extra, got, small)

    def line(s, first, gap):
        return line_of(small, s, first, gap)

    def summed(first, gap):
        others = line(1, first, gap) + (line(2, first, gap) + (line(3, first, gap) + line(4, first, gap)))
        return line(0, first, gap) * share + others

    def added(at):
        return (g1[at].astype(F32) + g2[at].astype(F32)) + (g3[at].astype(F32) + g4[at].astype(F32))

    def put(day, i, j, piece):
        hi, lo = split(piece)
        omhi[day, i * LANES : (i + 1) * LANES, j * LANES : (j + 1) * LANES] = hi
        omlo[day, i * LANES : (i + 1) * LANES, j * LANES : (j + 1) * LANES] = lo

    sides = [n for n, (i, j) in enumerate(tiles) if i != j]
    middles = [n for n, (i, j) in enumerate(tiles) if i == j]

    def unpack(day):
        for i, n in enumerate(middles):
            both = added(2 * len(sides) + i)
            part = jnp.where(row < column if day else row > column, both, 0.0)
            others = sum(line(s, DIAG + 12 * day + i, 4) for s in range(1, 5))
            piece = own[day * len(tiles) + n] * share + (part + part.T)
            put(day, i, i, piece + jnp.where(row == column, others, 0.0))
        for m, n in enumerate(sides):
            i, j = tiles[n]
            piece = own[day * len(tiles) + n] * share + added(day * len(sides) + m)
            put(day, i, j, piece)
            put(day, j, i, piece.T)

    for day in range(2):
        info[day] = jnp.concatenate([summed(12 * day + j, 4) for j in range(chunks)], 1)
    held = ids[5]
    source = lax.rem(ids[1] // held - ids[0] + planes, planes)
    for day in range(2):
        for j in range(chunks):
            r = DAMP + 24 * lax.rem(ids[1], held) + 4 * day + j
            mine[day : day + 1, j * LANES : (j + 1) * LANES] = small[source, pl.ds(r, 1), :] + (
                small[source, pl.ds(r + 8, 1), :] + small[source, pl.ds(r + 16, 1), :]
            )
    first = (ids[1] == 0) & (ids[0] == owner_plane(0))
    start[...] = jnp.where(first, prior[...], 0.0)

    @pl.when(first)
    def _():
        state = prior[...]
        for day in range(2):
            unpack(day)
            state = one_day(day, state, mine, pthi, ptlo, omhi, omlo, info, chi, clo)
        y[...] = state

    @pl.when(jnp.logical_not(first))
    def _():
        for day in range(2):
            unpack(day)
        y[...] = jnp.zeros(y.shape, F32)


def maps_kernel(after, omhi, omlo, info, chi, clo, pt, damping, b1hi, b1lo, b2hi, b2lo, off, zhi, zlo):
    for day in range(2):
        off[day : day + 1, :] = mv(info[day], chi[...], clo[...])

    def seen(day):
        return mm(omhi[day].astype(F32) + omlo[day].astype(F32), chi[...], clo[...])

    def step(day):
        moved = pt[...] * damping[day : day + 1, :]
        return moved - mm(moved, *split(seen(day)))

    b1hi[...], b1lo[...] = split(step(0))

    @pl.when(here()[1] != 1)
    def _():
        b2hi[...], b2lo[...] = split(step(1))

    @pl.when(here()[1] == 1)
    def _():
        zhi[...], zlo[...] = split(seen(1))


def second_kernel(acc, got, mine, b1hi, b1lo, off, zhi, zlo, pthi, ptlo, total, y):
    total[...] = acc[...] + got[...]
    y[...] = jnp.zeros(y.shape, F32)

    @pl.when(here()[1] == 1)
    def _():
        state = mv(acc[...] + got[...], b1hi[...], b1lo[...]) + off[0:1, :]
        moved = mv(state, pthi[...], ptlo[...]) * mine[1:2, :]
        y[...] = moved - mv(moved, zhi[...], zlo[...]) + off[1:2, :]


def rest_kernel(after, pt, damping, zhi, zlo, old_hi, old_lo, b2hi, b2lo):
    @pl.when(here()[1] == 1)
    def _():
        moved = pt[...] * damping[1:2, :]
        b2hi[...], b2lo[...] = split(moved - mm(moved, zhi[...], zlo[...]))


def both_kernel(after, b1hi, b1lo, b2hi, b2lo, off, bchi, bclo, offset):
    both = jnp.dot(b1hi[...], b2hi[...], preferred_element_type=F32) + (
        jnp.dot(b1lo[...], b2hi[...], preferred_element_type=F32)
        + jnp.dot(b1hi[...], b2lo[...], preferred_element_type=F32)
    )
    bchi[...], bclo[...] = split(both)
    offset[...] = mv(off[0:1, :], b2hi[...], b2lo[...]) + off[1:2, :]


def hop_kernel(after, acc, got, bchi, bclo, offset, total, y):
    state = acc[...] + got[...]
    total[...] = state
    y[...] = mv(state, bchi[...], bclo[...]) + offset[...]


def whole_of(hi, lo):
    return hi[...].astype(F32) + lo[...].astype(F32)


def pairs_kernel(
    after, b1hi, b1lo, bchi, bclo, off, offset, table, pthi, ptlo, mthi, mtlo, khi, klo, ehi, elo, shift
):
    total = table.shape[0]
    spans = total // 2

    span = here()[1]

    @pl.when(span >= spans - 2)
    def _():
        @pl.loop(spans - 1 - span, khi.shape[0])
        def _(k):
            scaled = whole_of(mthi, mtlo) * table[pl.ds(2 * (spans - 2 - k) + 1, 1), :]
            khi[k], klo[k] = split(mm(scaled, mthi[...], mtlo[...]))

    @pl.when(span == spans - 1)
    def _():
        within = table[total - 1 : total, :]
        one = off[0:1, :]
        ahead = mv(one, pthi[...], ptlo[...]) * (within * within)
        shift[0:1, :] = one + mv(offset[...] * within - ahead, mthi[...], mtlo[...])
        whole = whole_of(b1hi, b1lo)
        ahead = mm(whole, pthi[...], ptlo[...]) * (within * within)
        moved = whole_of(bchi, bclo) * within - ahead
        ehi[...], elo[...] = split(whole + mm(moved, mthi[...], mtlo[...]))


def last_kernel(
    acc, got, b1hi, b1lo, b2hi, b2lo, bchi, bclo, off, offset, table, pthi, ptlo, mthi, mtlo,
    khi, klo, ehi, elo, shift, out, shares, means,
):
    span = here()[1]
    total, width = shares.shape
    spans = total // 2
    chunks = width // LANES
    shares[...] = jnp.zeros(shares.shape, F32)

    def step(k, v):
        t = 2 * span - 1 - k
        v = mv(v * table[pl.ds(t + 1, 1), :], mthi[...], mtlo[...])
        shares[pl.ds(t, 1), :] = v
        return v

    @pl.when(span < spans - 1)
    def _():
        state = acc[...] + got[...]
        one = mv(state, b1hi[...], b1lo[...]) + off[0:1, :]
        two = mv(one, b2hi[...], b2lo[...]) + off[1:2, :]
        both = jnp.concatenate([one, two], 0)
        within = table[pl.ds(2 * span + 1, 1), :]
        damped = jnp.concatenate([within, table[pl.ds(2 * span + 2, 1), :]], 0)
        const = both - few(few(both, pthi[...], ptlo[...]) * damped * damped, mthi[...], mtlo[...])
        even = const[0:1] + mv(const[1:2] * within, mthi[...], mtlo[...])
        shares[pl.ds(2 * span + 1, 1), :] = const[1:2]
        shares[pl.ds(2 * span, 1), :] = even
        means[0:2, :] = both
        means[2:3, :] = even

    def descend(v, start):
        damped_rows, days = [], range(start, khi.shape[0])
        for k in days:
            t = 2 * (spans - 1 - k)
            damped_rows.append(v * table[t : t + 1, :])
            v = mv(damped_rows[-1], khi[k], klo[k])
            shares[t - 2 : t - 1, :] = v
        batch = jnp.concatenate(damped_rows + [jnp.zeros((1, width), F32)] * (-len(damped_rows) % 8), 0)
        batch = mm(batch, mthi[...], mtlo[...])
        for n, k in enumerate(days):
            t = 2 * (spans - 1 - k)
            shares[t - 1 : t, :] = batch[n : n + 1]
        lax.fori_loop(2 * len(days), 2 * span, step, v)

    @pl.when(span < spans - 2)
    def _():
        lax.fori_loop(0, 2 * span, step, means[2:3, :])

    @pl.when(span == spans - 2)
    def _():
        descend(means[2:3, :], 1)

    @pl.when(span == spans - 1)
    def _():
        state = acc[...] + got[...]
        v = mv(state, ehi[...], elo[...]) + shift[0:1, :]
        shares[total - 2 : total - 1, :] = v
        descend(v, 0)
        two = mv(state, bchi[...], bclo[...]) + offset[...]
        means[0:1, :] = mv(state, b1hi[...], b1lo[...]) + off[0:1, :]
        means[1:2, :] = two
        shares[total - 1 : total, :] = two

    for c in range(spans):
        for q in range(chunks):
            out[c * chunks + q, 0:2, :] = shares[2 * c : 2 * c + 2, q * LANES : (q + 1) * LANES]
    for q in range(chunks):
        out[span * chunks + q, 2:4, :] = means[0:2, q * LANES : (q + 1) * LANES]


def add_kernel(parts, filt, smooth):
    ids = here()
    spans = parts.shape[0] // 4
    filt[...] = parts[ids[4], 2:4, :]
    smooth[...] = sum(parts[owner_plane(c) * spans + (place(c) | 1), 0:2, :] for c in range(spans))


def local(
    records,
    obs_values,
    block_day,
    block_count,
    propagator_matrix,
    analysis_cov,
    unattenuated_multiplier,
    damping,
    prior_mean,
):
    planes, held, peers = (lax.axis_size(a) for a in ("z", "y", "obs"))
    spans = planes * held
    blocks = block_day.shape[0]
    slots = records.shape[0] // blocks
    width = records.shape[1]
    days = damping.shape[0]
    assert planes == peers == 4 and days == 2 and slots == LANES and blocks == spans
    everyone = ("z", "y", "obs")

    def owner(span):
        return owner_plane(span) * spans + (place(span) | 1)

    tiles = len(triangle(width))
    extra_tiles = -(-(DAMP + 24 * held) // LANES)
    full, row = (width, width), ((1, width), F32)
    sent = run(
        pack_kernel,
        [((blocks, slots + EXTRA, width), BF16)],
        [
            (x, HBM)
            for x in (
                block_day,
                block_count,
                records,
                obs_values.reshape(blocks, slots),
                prior_mean.reshape(1, -1),
                damping,
            )
        ],
        [
            pltpu.SMEM((blocks,), jnp.int32),
            pltpu.SMEM((blocks,), jnp.int32),
            pltpu.VMEM((blocks, slots), BF16),
            pltpu.VMEM((1, width // peers), F32),
            pltpu.VMEM((days, width), F32),
            pltpu.VMEM((blocks, slots + EXTRA, width), BF16),
            pltpu.SemaphoreType.DMA((5 + 2 * blocks,)),
        ],
        limit=60,
        outs=HBM,
    )[0]
    got = lax.all_to_all(sent, ("y", "obs"), split_axis=0, concat_axis=0, tiled=True)
    span_slots = min(blocks, 8) * slots
    own, extra, pay, prior, gain = run(
        gram_kernel,
        [
            ((2 * tiles, LANES, LANES), F32),
            ((extra_tiles * LANES, LANES), F32),
            ((2 * tiles - width // LANES + extra_tiles, LANES, LANES), BF16),
            row,
            (unattenuated_multiplier.shape, F32),
        ],
        [got, unattenuated_multiplier],
        [pltpu.VMEM((width, span_slots), BF16), pltpu.VMEM((16, span_slots), BF16)],
        flops=4 * width * width * blocks * slots,
    )
    def swap(x, bit):
        return lax.ppermute(x, "obs", [(i, i ^ bit) for i in range(peers)])

    def plane_sum(s):
        return lax.ppermute(
            pay, everyone, [((owner_plane(p) + s) % planes * spans + place(p), owner(p)) for p in range(spans)]
        )

    fourth = lax.ppermute(
        pay, everyone, [(spans + place(p), owner(p)) for p in range(spans) if place(p) % 2 == 0]
    )
    third, first, second = plane_sum(3), plane_sum(1), plane_sum(2)
    (gains,) = run(stack_kernel, [((2,) + gain.shape, F32)], [gain, swap(gain, 2)])
    mthi, mtlo = run(gain_kernel, [(full, BF16)] * 2, [gains, swap(gains, 1)])
    pt, pthi, ptlo, chi, clo = run(
        prep_kernel, [(full, F32)] + [(full, BF16)] * 4, [propagator_matrix, analysis_cov]
    )
    smalls = pltpu.VMEM((planes + 1, extra_tiles * LANES, LANES), F32)
    omhi, omlo, info, mine, acc, y = run(
        owner_kernel,
        [((days,) + full, BF16)] * 2 + [((days, 1, width), F32), ((days, width), F32), row, row],
        [
            own, extra, fourth, third, first, second, prior, pthi, ptlo, chi, clo, (mthi, ANY)
        ],
        [smalls],
    )
    for k in range(spans - 1):
        received = lax.ppermute(y, everyone, [(owner(k), owner(k + 1))])
        if k == 0:
            b1hi, b1lo, b2hi, b2lo, off, zhi, zlo = run(
                maps_kernel,
                [(full, BF16)] * 4 + [((8, width), F32)] + [(full, BF16)] * 2,
                [(y, ANY), omhi, omlo, info, chi, clo, pt, mine],
                flops=24 * width**3,
            )
            acc, y = run(
                second_kernel, [row, row], [acc, received, mine, b1hi, b1lo, off, zhi, zlo, pthi, ptlo]
            )
            b2hi, b2lo = run(
                rest_kernel,
                [(full, BF16)] * 2,
                [(y, ANY), pt, mine, zhi, zlo, b2hi, b2lo],
                flops=6 * width**3,
                same={5: 0, 6: 1},
            )
            bchi, bclo, offset = run(
                both_kernel, [(full, BF16)] * 2 + [row], [(y, ANY), b1hi, b1lo, b2hi, b2lo, off]
            )
            (table,) = run(
                table_kernel,
                [((spans * days, width), F32)],
                [(offset, ANY), extra, first, second, third],
                [smalls],
            )
            ahead = run(
                pairs_kernel,
                [((min(spans - 1, 7),) + full, BF16)] * 2 + [(full, BF16)] * 2 + [((8, width), F32)],
                [(y, ANY), b1hi, b1lo, bchi, bclo, off, offset, table, pthi, ptlo, mthi, mtlo],
            )
            side = ahead[0]
        elif k < spans - 2:
            acc, y = run(hop_kernel, [row, row], [(side, ANY), acc, received, bchi, bclo, offset])
    (answer,) = run(
        last_kernel,
        [((spans * peers, 8, LANES), F32)],
        [
            acc, received, b1hi, b1lo, b2hi, b2lo, bchi, bclo, off, offset, table, pthi, ptlo, mthi, mtlo,
            *ahead,
        ],
        [pltpu.VMEM((spans * days, width), F32), pltpu.VMEM((8, width), F32)],
    )
    parts = lax.all_to_all(answer, everyone, split_axis=0, concat_axis=0, tiled=True)
    out = ((days, LANES), F32)
    return run(add_kernel, [out, out], [parts])


def solution(mesh):
    spans, peers = mesh.devices.shape
    finer = jax.sharding.Mesh(mesh.devices.reshape(peers, spans // peers, peers), ("z", "y", "obs"))
    tm = ("z", "y")
    mapped = jax.shard_map(
        local,
        mesh=finer,
        in_specs=(
            P(("z", "y", "obs"), None),
            P(("z", "y", "obs")),
            P(("z", "y", "obs")),
            P(("z", "y", "obs")),
            P(),
            P(),
            P("obs", None),
            P(tm, None),
            P("obs"),
        ),
        out_specs=(P(tm, "obs"), P(tm, "obs")),
        check_vma=False,
    )
    return lambda *args: tuple(mapped(*args))
```

```python
import functools

import jax
import jax.numpy as jnp
from jax import lax
from jax.experimental import pallas as pl
from jax.experimental.pallas import tpu as pltpu
from jax.sharding import PartitionSpec as P

LANES = 128
F32, BF16 = jnp.float32, jnp.bfloat16
VMEM = pl.BlockSpec(memory_space=pltpu.VMEM)
SMEM = pl.BlockSpec(memory_space=pltpu.SMEM)
ANY = pl.BlockSpec(memory_space=pl.ANY)
HBM = pl.BlockSpec(memory_space=pltpu.HBM)


def run(body, out, ins, scratch=(), limit=16, flops=0, outs=VMEM, same=None):
    specs = [x[1] if isinstance(x, tuple) else VMEM for x in ins]
    arrays = [x[0] if isinstance(x, tuple) else x for x in ins]
    moved = sum(a.size * a.dtype.itemsize for a in arrays)
    return pl.pallas_call(
        body,
        out_shape=[jax.ShapeDtypeStruct(s, d) for s, d in out],
        in_specs=specs,
        out_specs=[outs] * len(out),
        scratch_shapes=list(scratch),
        input_output_aliases=same or {},
        compiler_params=pltpu.CompilerParams(vmem_limit_bytes=limit * 1024 * 1024),
        cost_estimate=pl.CostEstimate(flops=flops, bytes_accessed=moved, transcendentals=0),
    )(*arrays)


def here():
    z, y, o = (lax.axis_index(a) for a in ("z", "y", "obs"))
    held, peers = lax.axis_size("y"), lax.axis_size("obs")
    spans = held * peers
    at = y * peers + o
    seat = jnp.where(z == 1, at - lax.rem(at, 2), at)
    span = seat
    for bit in range(1, spans.bit_length()):
        span = span ^ (seat >> bit)
    c = z * held + y
    seat = c ^ (c >> 1)
    return z, span, o, c, (1 + (seat & 1)) * spans + (seat | 1), held


def triangle(width):
    parts = width // LANES
    return [(i, j) for i in range(parts) for j in range(i + 1)]


def split(x):
    hi = x.astype(BF16)
    return hi, (x - hi.astype(F32)).astype(BF16)


def mm(x, hi, lo):
    xhi, xlo = split(x)
    dot = functools.partial(jnp.dot, preferred_element_type=F32)
    return dot(xhi, hi) + (dot(xlo, hi) + dot(xhi, lo))


def mv(x, hi, lo):
    wide = jnp.broadcast_to(x, (8, x.shape[1]))
    row = lax.broadcasted_iota(jnp.int32, wide.shape, 0)
    top = wide.astype(BF16).astype(F32)
    both = jnp.where(row == 0, top, jnp.where(row == 1, wide - top, 0.0)).astype(BF16)
    first = jnp.dot(both, hi, preferred_element_type=F32)
    second = jnp.dot(both, lo, preferred_element_type=F32)
    return first[0:1] + (first[1:2] + second[0:1])


def parts3(x):
    out = []
    for _ in range(3):
        piece = x.astype(BF16).astype(F32)
        out.append(piece)
        x = x - piece
    return out


def place(span):
    return span ^ (span >> 1)


def owner_plane(span):
    return 1 + place(span) % 2


EXTRA = 8
DIAG, DAMP = 24, 48


def pack_kernel(
    day, count, rows, values, prior, damping, out, day_s, count_s, values_v, prior_v, damping_v, stage, sems
):
    blocks = out.shape[0]
    slots = out.shape[1] - EXTRA
    width = out.shape[2]
    small = [(day, day_s), (count, count_s), (values, values_v), (prior, prior_v), (damping, damping_v)]
    copies = [pltpu.make_async_copy(src, dst, sems.at[n]) for n, (src, dst) in enumerate(small)]
    large = [
        pltpu.make_async_copy(
            rows.at[pl.ds(k * slots, slots)], stage.at[place(k), pl.ds(0, slots)], sems.at[len(small) + k]
        )
        for k in range(blocks)
    ]
    for copy in copies + large:
        copy.start()
    for copy in copies:
        copy.wait()
    first, second, third = parts3(prior_v[...])
    below = jnp.concatenate(
        [jnp.concatenate([second, third, jnp.zeros((1, width - 2 * LANES), F32)], 1)] + parts3(damping_v[...]), 0
    )
    held = values_v[...].astype(F32)
    for k in range(blocks):
        line = jnp.concatenate(
            [
                held[k : k + 1, :],
                jnp.full((1, LANES), day_s[k], jnp.int32).astype(F32),
                jnp.full((1, LANES), count_s[k], jnp.int32).astype(F32),
                first,
            ],
            1,
        )
        stage[place(k), slots : slots + EXTRA, :] = jnp.concatenate([line, below], 0).astype(BF16)
    sends = [
        pltpu.make_async_copy(stage.at[place(k)], out.at[place(k)], sems.at[len(small) + blocks + k])
        for k in range(blocks)
    ]
    for k in range(blocks):
        large[k].wait()
        sends[k].start()
    for copy in sends:
        copy.wait()


def gram_kernel(got, gain, own, extra, pay, prior, gain_out, turned, marks):
    blocks = got.shape[0]
    slots = got.shape[1] - EXTRA
    width = got.shape[2]
    chunks = width // LANES
    tiles = triangle(width)
    group = min(blocks, 8)
    half = 2 * LANES
    gain_out[...] = gain[...]
    extra[...] = jnp.zeros(extra.shape, F32)

    def one(first, fresh):
        for k in range(group):
            at = slice(k * slots, (k + 1) * slots)
            line = got[first + k, slots : slots + EXTRA, :].astype(F32)
            valid = lax.broadcasted_iota(jnp.int32, (1, slots), 1).astype(F32) < line[0:1, 2 * LANES : 3 * LANES]
            day = line[0:1, LANES : 2 * LANES]
            values = line[0:1, 0:LANES]
            kept = [jnp.where(valid & (day == d), 1.0, 0.0) for d in (0.0, 1.0)]
            marks[:, at] = jnp.concatenate(
                kept + [kept[0] * values, kept[1] * values, jnp.zeros((12, slots), F32)], 0
            ).astype(BF16)
            turned[:, at] = got[first + k, 0:slots, :].T
        source = jnp.concatenate([got[first + k, 0:slots, :] for k in range(group)], 0)
        info = jnp.dot(marks[...], source, preferred_element_type=F32)
        for d in range(2):
            for top in range(0, width, half):
                left = turned[top : top + half, :] * marks[d : d + 1, :]
                block = jnp.dot(left, source[:, : top + half], preferred_element_type=F32)
                for n, (i, j) in enumerate(tiles):
                    if top <= i * LANES < top + half:
                        r = i * LANES - top
                        piece = block[r : r + LANES, j * LANES : (j + 1) * LANES]
                        at = d * len(tiles) + n
                        own[at] = piece if fresh else own[at] + piece
            for j in range(chunks):
                piece = info[2 + d : 3 + d, j * LANES : (j + 1) * LANES]
                r = 12 * d + j
                extra[r : r + 1, :] = piece if fresh else extra[r : r + 1, :] + piece

    if blocks == group:
        one(0, True)
    else:
        own[...] = jnp.zeros(own.shape, F32)

        @pl.loop(0, blocks // group)
        def _(g):
            one(g * group, False)

    row = lax.broadcasted_iota(jnp.int32, (LANES, LANES), 0)
    column = lax.broadcasted_iota(jnp.int32, (LANES, LANES), 1)
    sides = [n for n, (i, j) in enumerate(tiles) if i != j]
    middles = [n for n, (i, j) in enumerate(tiles) if i == j]
    for d in range(2):
        for part, piece in enumerate(parts3(extra[12 * d : 12 * d + chunks, :])):
            extra[12 * d + 4 * part : 12 * d + 4 * part + chunks, :] = piece
        for m, n in enumerate(sides):
            pay[d * len(sides) + m] = own[d * len(tiles) + n].astype(BF16)
    for i, n in enumerate(middles):
        squares = [own[d * len(tiles) + n] for d in range(2)]
        pay[2 * len(sides) + i] = jnp.where(row >= column, squares[0], squares[1]).astype(BF16)
        for d in range(2):
            line = jnp.sum(jnp.where(row == column, squares[d], 0.0), axis=0, keepdims=True)
            for part, piece in enumerate(parts3(line)):
                r = DIAG + 12 * d + 4 * part + i
                extra[r : r + 1, :] = piece
    for q in range(chunks):
        line = got[q, slots : slots + EXTRA, :].astype(F32)
        prior[:, q * LANES : (q + 1) * LANES] = line[0:1, 3 * LANES : 4 * LANES] + (
            line[1:2, 0:LANES] + line[1:2, LANES : 2 * LANES]
        )
    for y in range(blocks // 4):
        line = got[4 * y, slots : slots + EXTRA, :].astype(F32)
        for k in range(6):
            for j in range(chunks):
                r = DAMP + 24 * y + 4 * k + j
                extra[r : r + 1, :] = line[2 + k : 3 + k, j * LANES : (j + 1) * LANES]
    small_at = pay.shape[0] - extra.shape[0] // LANES
    for n in range(extra.shape[0] // LANES):
        pay[small_at + n] = extra[n * LANES : (n + 1) * LANES, :].astype(BF16)


def prep_kernel(trans, cov, prior, pt, pthi, ptlo, chi, clo, ahead):
    whole = trans[...].T
    pt[...] = whole
    pthi[...], ptlo[...] = split(whole)
    chi[...], clo[...] = split(cov[...])
    ahead[...] = mv(prior[...], pthi[...], ptlo[...])


def stack_kernel(one, two, out):
    out[0] = one[...]
    out[1] = two[...]


def gain_kernel(held, got, mthi, mtlo):
    ids = here()
    rows = held.shape[1]
    for step, part in enumerate((held.at[0], got.at[0], held.at[1], got.at[1])):
        holder = ids[2] ^ step
        at = pl.ds(pl.multiple_of(holder * rows, rows), rows)
        hi, lo = split(part[...].T)
        mthi[:, at] = hi
        mtlo[:, at] = lo


def few(x, hi, lo):
    top = x.astype(BF16).astype(F32)
    both = jnp.concatenate([top, x - top, jnp.zeros((4, x.shape[1]), F32)], 0).astype(BF16)
    first = jnp.dot(both, hi, preferred_element_type=F32)
    second = jnp.dot(both, lo, preferred_element_type=F32)
    return first[0:2] + (first[2:4] + second[0:2])


def one_day(day, ahead, damping, omhi, omlo, info, chi, clo):
    moved = ahead * damping[day : day + 1, :]
    gap = mv(moved, omhi[day], omlo[day]) - info[day]
    return moved - mv(gap, chi[...], clo[...])


def spread(extra, got, small):
    small_at = got[0].shape[0] - extra.shape[0] // LANES
    small[0] = extra[...]
    for s, part in enumerate(got):
        for n in range(extra.shape[0] // LANES):
            small[s + 1, n * LANES : (n + 1) * LANES, :] = part[small_at + n].astype(F32)


def line_of(small, s, first, gap):
    return small[s, first : first + 1, :] + (
        small[s, first + gap : first + gap + 1, :] + small[s, first + 2 * gap : first + 2 * gap + 1, :]
    )


def table_kernel(after, extra, g1, g2, g3, table, small):
    ids = here()
    planes = 4
    chunks = table.shape[1] // LANES
    held = table.shape[0] // 2 // planes
    spread(extra, (g1, g2, g3), small)
    for s in range(planes):
        plane = lax.rem(ids[0] + s, planes)
        for k in range(held):
            for day in range(2):
                table[pl.ds(2 * (plane * held + k) + day, 1), :] = jnp.concatenate(
                    [line_of(small, s, DAMP + 24 * k + 4 * day + j, 8) for j in range(chunks)], 1
                )


def owner_kernel(
    own, extra, g4, g3, g1, g2, prior, ahead, pthi, ptlo, chi, clo, after, omhi, omlo, info, mine, start, y, small
):
    ids = here()
    planes = 4
    width = pthi.shape[0]
    chunks = width // LANES
    tiles = triangle(width)
    got = (g1, g2, g3, g4)
    share = jnp.where(ids[0] == 2, 1.0, 0.0)
    row = lax.broadcasted_iota(jnp.int32, (LANES, LANES), 0)
    column = lax.broadcasted_iota(jnp.int32, (LANES, LANES), 1)
    spread(extra, got, small)

    def line(s, first, gap):
        return line_of(small, s, first, gap)

    def summed(first, gap):
        others = line(1, first, gap) + (line(2, first, gap) + (line(3, first, gap) + line(4, first, gap)))
        return line(0, first, gap) * share + others

    def added(at):
        return (g1[at].astype(F32) + g2[at].astype(F32)) + (g3[at].astype(F32) + g4[at].astype(F32))

    def put(day, i, j, piece):
        hi, lo = split(piece)
        omhi[day, i * LANES : (i + 1) * LANES, j * LANES : (j + 1) * LANES] = hi
        omlo[day, i * LANES : (i + 1) * LANES, j * LANES : (j + 1) * LANES] = lo

    sides = [n for n, (i, j) in enumerate(tiles) if i != j]
    middles = [n for n, (i, j) in enumerate(tiles) if i == j]

    def unpack(day):
        for i, n in enumerate(middles):
            both = added(2 * len(sides) + i)
            part = jnp.where(row < column if day else row > column, both, 0.0)
            others = sum(line(s, DIAG + 12 * day + i, 4) for s in range(1, 5))
            piece = own[day * len(tiles) + n] * share + (part + part.T)
            put(day, i, i, piece + jnp.where(row == column, others, 0.0))
        for m, n in enumerate(sides):
            i, j = tiles[n]
            piece = own[day * len(tiles) + n] * share + added(day * len(sides) + m)
            put(day, i, j, piece)
            put(day, j, i, piece.T)

    for day in range(2):
        info[day] = jnp.concatenate([summed(12 * day + j, 4) for j in range(chunks)], 1)
    held = ids[5]
    source = lax.rem(ids[1] // held - ids[0] + planes, planes)
    for day in range(2):
        for j in range(chunks):
            r = DAMP + 24 * lax.rem(ids[1], held) + 4 * day + j
            mine[day : day + 1, j * LANES : (j + 1) * LANES] = small[source, pl.ds(r, 1), :] + (
                small[source, pl.ds(r + 8, 1), :] + small[source, pl.ds(r + 16, 1), :]
            )
    first = (ids[1] == 0) & (ids[0] == owner_plane(0))
    start[...] = jnp.where(first, prior[...], 0.0)

    @pl.when(first)
    def _():
        unpack(0)
        state = one_day(0, ahead[...], mine, omhi, omlo, info, chi, clo)
        unpack(1)
        y[...] = one_day(1, mv(state, pthi[...], ptlo[...]), mine, omhi, omlo, info, chi, clo)

    @pl.when(jnp.logical_not(first))
    def _():
        for day in range(2):
            unpack(day)
        y[...] = jnp.zeros(y.shape, F32)


def seen(day, omhi, omlo, chi, clo):
    return mm(omhi[day].astype(F32) + omlo[day].astype(F32), chi[...], clo[...])


def early_kernel(after, omhi, omlo, info, chi, clo, pt, damping, b1hi, b1lo, off, zhi, zlo):
    @pl.when(here()[1] == 1)
    def _():
        for day in range(2):
            off[day : day + 1, :] = mv(info[day], chi[...], clo[...])
        moved = pt[...] * damping[0:1, :]
        b1hi[...], b1lo[...] = split(moved - mm(moved, *split(seen(0, omhi, omlo, chi, clo))))
        zhi[...], zlo[...] = split(seen(1, omhi, omlo, chi, clo))


def maps_kernel(
    after, omhi, omlo, info, chi, clo, pt, damping, zhi, zlo, old1, old2, old3, b1hi, b1lo, off, b2hi, b2lo
):
    second = here()[1] == 1

    @pl.when(jnp.logical_not(second))
    def _():
        parts = ((b1hi, b1lo), (b2hi, b2lo))
        for day in range(2):
            moved = pt[...] * damping[day : day + 1, :]
            parts[day][0][...], parts[day][1][...] = split(
                moved - mm(moved, *split(seen(day, omhi, omlo, chi, clo)))
            )
            off[day : day + 1, :] = mv(info[day], chi[...], clo[...])

    @pl.when(second)
    def _():
        moved = pt[...] * damping[1:2, :]
        b2hi[...], b2lo[...] = split(moved - mm(moved, zhi[...], zlo[...]))


def second_kernel(acc, got, mine, b1hi, b1lo, off, zhi, zlo, pthi, ptlo, total, y):
    total[...] = acc[...] + got[...]
    y[...] = jnp.zeros(y.shape, F32)

    @pl.when(here()[1] == 1)
    def _():
        state = mv(acc[...] + got[...], b1hi[...], b1lo[...]) + off[0:1, :]
        moved = mv(state, pthi[...], ptlo[...]) * mine[1:2, :]
        y[...] = moved - mv(moved, zhi[...], zlo[...]) + off[1:2, :]


def both_kernel(after, b1hi, b1lo, b2hi, b2lo, off, bchi, bclo, offset):
    both = jnp.dot(b1hi[...], b2hi[...], preferred_element_type=F32) + (
        jnp.dot(b1lo[...], b2hi[...], preferred_element_type=F32)
        + jnp.dot(b1hi[...], b2lo[...], preferred_element_type=F32)
    )
    bchi[...], bclo[...] = split(both)
    offset[...] = mv(off[0:1, :], b2hi[...], b2lo[...]) + off[1:2, :]


def hop_kernel(after, acc, got, bchi, bclo, offset, total, y):
    state = acc[...] + got[...]
    total[...] = state
    y[...] = mv(state, bchi[...], bclo[...]) + offset[...]


def whole_of(hi, lo):
    return hi[...].astype(F32) + lo[...].astype(F32)


def pairs_kernel(
    after, b1hi, b1lo, bchi, bclo, off, offset, table, pthi, ptlo, mthi, mtlo, khi, klo, ehi, elo, shift
):
    total = table.shape[0]
    spans = total // 2

    span = here()[1]

    @pl.when(span >= spans - 2)
    def _():
        @pl.loop(spans - 1 - span, khi.shape[0])
        def _(k):
            scaled = whole_of(mthi, mtlo) * table[pl.ds(2 * (spans - 2 - k) + 1, 1), :]
            khi[k], klo[k] = split(mm(scaled, mthi[...], mtlo[...]))

    @pl.when(span == spans - 1)
    def _():
        within = table[total - 1 : total, :]
        one = off[0:1, :]
        ahead = mv(one, pthi[...], ptlo[...]) * (within * within)
        shift[0:1, :] = one + mv(offset[...] * within - ahead, mthi[...], mtlo[...])
        whole = whole_of(b1hi, b1lo)
        ahead = mm(whole, pthi[...], ptlo[...]) * (within * within)
        moved = whole_of(bchi, bclo) * within - ahead
        ehi[...], elo[...] = split(whole + mm(moved, mthi[...], mtlo[...]))


def last_kernel(
    acc, got, b1hi, b1lo, b2hi, b2lo, bchi, bclo, off, offset, table, pthi, ptlo, mthi, mtlo,
    khi, klo, ehi, elo, shift, out, shares, means,
):
    span = here()[1]
    total, width = shares.shape
    spans = total // 2
    chunks = width // LANES
    shares[...] = jnp.zeros(shares.shape, F32)

    def step(k, v):
        t = 2 * span - 1 - k
        v = mv(v * table[pl.ds(t + 1, 1), :], mthi[...], mtlo[...])
        shares[pl.ds(t, 1), :] = v
        return v

    @pl.when(span < spans - 1)
    def _():
        state = acc[...] + got[...]
        one = mv(state, b1hi[...], b1lo[...]) + off[0:1, :]
        two = mv(one, b2hi[...], b2lo[...]) + off[1:2, :]
        both = jnp.concatenate([one, two], 0)
        within = table[pl.ds(2 * span + 1, 1), :]
        damped = jnp.concatenate([within, table[pl.ds(2 * span + 2, 1), :]], 0)
        const = both - few(few(both, pthi[...], ptlo[...]) * damped * damped, mthi[...], mtlo[...])
        even = const[0:1] + mv(const[1:2] * within, mthi[...], mtlo[...])
        shares[pl.ds(2 * span + 1, 1), :] = const[1:2]
        shares[pl.ds(2 * span, 1), :] = even
        means[0:2, :] = both
        means[2:3, :] = even

    def descend(v, start):
        damped_rows, days = [], range(start, khi.shape[0])
        for k in days:
            t = 2 * (spans - 1 - k)
            damped_rows.append(v * table[t : t + 1, :])
            v = mv(damped_rows[-1], khi[k], klo[k])
            shares[t - 2 : t - 1, :] = v
        batch = jnp.concatenate(damped_rows + [jnp.zeros((1, width), F32)] * (-len(damped_rows) % 8), 0)
        batch = mm(batch, mthi[...], mtlo[...])
        for n, k in enumerate(days):
            t = 2 * (spans - 1 - k)
            shares[t - 1 : t, :] = batch[n : n + 1]
        lax.fori_loop(2 * len(days), 2 * span, step, v)

    @pl.when(span < spans - 2)
    def _():
        lax.fori_loop(0, 2 * span, step, means[2:3, :])

    @pl.when(span == spans - 2)
    def _():
        descend(means[2:3, :], 1)

    @pl.when(span == spans - 1)
    def _():
        state = acc[...] + got[...]
        v = mv(state, ehi[...], elo[...]) + shift[0:1, :]
        shares[total - 2 : total - 1, :] = v
        descend(v, 0)
        two = mv(state, bchi[...], bclo[...]) + offset[...]
        means[0:1, :] = mv(state, b1hi[...], b1lo[...]) + off[0:1, :]
        means[1:2, :] = two
        shares[total - 1 : total, :] = two

    for c in range(spans):
        for q in range(chunks):
            out[c * chunks + q, 0:2, :] = shares[2 * c : 2 * c + 2, q * LANES : (q + 1) * LANES]
    for q in range(chunks):
        out[span * chunks + q, 2:4, :] = means[0:2, q * LANES : (q + 1) * LANES]


def add_kernel(parts, filt, smooth):
    ids = here()
    spans = parts.shape[0] // 4
    filt[...] = parts[ids[4], 2:4, :]
    smooth[...] = sum(parts[owner_plane(c) * spans + (place(c) | 1), 0:2, :] for c in range(spans))


def local(
    records,
    obs_values,
    block_day,
    block_count,
    propagator_matrix,
    analysis_cov,
    unattenuated_multiplier,
    damping,
    prior_mean,
):
    planes, held, peers = (lax.axis_size(a) for a in ("z", "y", "obs"))
    spans = planes * held
    blocks = block_day.shape[0]
    slots = records.shape[0] // blocks
    width = records.shape[1]
    days = damping.shape[0]
    assert planes == peers == 4 and days == 2 and slots == LANES and blocks == spans
    everyone = ("z", "y", "obs")

    def owner(span):
        return owner_plane(span) * spans + (place(span) | 1)

    tiles = len(triangle(width))
    extra_tiles = -(-(DAMP + 24 * held) // LANES)
    full, row = (width, width), ((1, width), F32)
    sent = run(
        pack_kernel,
        [((blocks, slots + EXTRA, width), BF16)],
        [
            (x, HBM)
            for x in (
                block_day,
                block_count,
                records,
                obs_values.reshape(blocks, slots),
                prior_mean.reshape(1, -1),
                damping,
            )
        ],
        [
            pltpu.SMEM((blocks,), jnp.int32),
            pltpu.SMEM((blocks,), jnp.int32),
            pltpu.VMEM((blocks, slots), BF16),
            pltpu.VMEM((1, width // peers), F32),
            pltpu.VMEM((days, width), F32),
            pltpu.VMEM((blocks, slots + EXTRA, width), BF16),
            pltpu.SemaphoreType.DMA((5 + 2 * blocks,)),
        ],
        limit=60,
        outs=HBM,
    )[0]
    got = lax.all_to_all(sent, ("y", "obs"), split_axis=0, concat_axis=0, tiled=True)
    span_slots = min(blocks, 8) * slots
    own, extra, pay, prior, gain = run(
        gram_kernel,
        [
            ((2 * tiles, LANES, LANES), F32),
            ((extra_tiles * LANES, LANES), F32),
            ((2 * tiles - width // LANES + extra_tiles, LANES, LANES), BF16),
            row,
            (unattenuated_multiplier.shape, F32),
        ],
        [got, unattenuated_multiplier],
        [pltpu.VMEM((width, span_slots), BF16), pltpu.VMEM((16, span_slots), BF16)],
        flops=4 * width * width * blocks * slots,
    )
    def swap(x, bit):
        return lax.ppermute(x, "obs", [(i, i ^ bit) for i in range(peers)])

    def plane_sum(s):
        return lax.ppermute(
            pay, everyone, [((owner_plane(p) + s) % planes * spans + place(p), owner(p)) for p in range(spans)]
        )

    fourth = lax.ppermute(
        pay, everyone, [(spans + place(p), owner(p)) for p in range(spans) if place(p) % 2 == 0]
    )
    third, first, second = plane_sum(3), plane_sum(1), plane_sum(2)
    (gains,) = run(stack_kernel, [((2,) + gain.shape, F32)], [gain, swap(gain, 2)])
    mthi, mtlo = run(gain_kernel, [(full, BF16)] * 2, [gains, swap(gains, 1)])
    pt, pthi, ptlo, chi, clo, ahead = run(
        prep_kernel, [(full, F32)] + [(full, BF16)] * 4 + [row], [propagator_matrix, analysis_cov, prior]
    )
    smalls = pltpu.VMEM((planes + 1, extra_tiles * LANES, LANES), F32)
    omhi, omlo, info, mine, acc, y = run(
        owner_kernel,
        [((days,) + full, BF16)] * 2 + [((days, 1, width), F32), ((days, width), F32), row, row],
        [
            own, extra, fourth, third, first, second, prior, ahead, pthi, ptlo, chi, clo, (mthi, ANY)
        ],
        [smalls],
    )
    for k in range(spans - 1):
        received = lax.ppermute(y, everyone, [(owner(k), owner(k + 1))])
        if k == 0:
            given = [omhi, omlo, info, chi, clo, pt, mine]
            half = [(full, BF16)] * 2
            b1hi, b1lo, off, zhi, zlo = run(
                early_kernel, half + [((8, width), F32)] + half, [(y, ANY), *given], flops=18 * width**3
            )
            acc, y = run(
                second_kernel, [row, row], [acc, received, mine, b1hi, b1lo, off, zhi, zlo, pthi, ptlo]
            )
            b1hi, b1lo, off, b2hi, b2lo = run(
                maps_kernel,
                half + [((8, width), F32)] + half,
                [(y, ANY), *given, zhi, zlo, b1hi, b1lo, off],
                flops=24 * width**3,
                same={10: 0, 11: 1, 12: 2},
            )
            bchi, bclo, offset = run(
                both_kernel, [(full, BF16)] * 2 + [row], [(y, ANY), b1hi, b1lo, b2hi, b2lo, off]
            )
            (table,) = run(
                table_kernel,
                [((spans * days, width), F32)],
                [(offset, ANY), extra, first, second, third],
                [smalls],
            )
            ahead = run(
                pairs_kernel,
                [((min(spans - 1, 7),) + full, BF16)] * 2 + [(full, BF16)] * 2 + [((8, width), F32)],
                [(y, ANY), b1hi, b1lo, bchi, bclo, off, offset, table, pthi, ptlo, mthi, mtlo],
            )
            side = ahead[0]
        elif k < spans - 2:
            acc, y = run(hop_kernel, [row, row], [(side, ANY), acc, received, bchi, bclo, offset])
    (answer,) = run(
        last_kernel,
        [((spans * peers, 8, LANES), F32)],
        [
            acc, received, b1hi, b1lo, b2hi, b2lo, bchi, bclo, off, offset, table, pthi, ptlo, mthi, mtlo,
            *ahead,
        ],
        [pltpu.VMEM((spans * days, width), F32), pltpu.VMEM((8, width), F32)],
    )
    parts = lax.all_to_all(answer, everyone, split_axis=0, concat_axis=0, tiled=True)
    out = ((days, LANES), F32)
    return run(add_kernel, [out, out], [parts])


def solution(mesh):
    spans, peers = mesh.devices.shape
    finer = jax.sharding.Mesh(mesh.devices.reshape(peers, spans // peers, peers), ("z", "y", "obs"))
    tm = ("z", "y")
    mapped = jax.shard_map(
        local,
        mesh=finer,
        in_specs=(
            P(("z", "y", "obs"), None),
            P(("z", "y", "obs")),
            P(("z", "y", "obs")),
            P(("z", "y", "obs")),
            P(),
            P(),
            P("obs", None),
            P(tm, None),
            P("obs"),
        ),
        out_specs=(P(tm, "obs"), P(tm, "obs")),
        check_vma=False,
    )
    return lambda *args: tuple(mapped(*args))
```

```python
import functools

import jax
import jax.numpy as jnp
from jax import lax
from jax.experimental import pallas as pl
from jax.experimental.pallas import tpu as pltpu
from jax.sharding import PartitionSpec as P

LANES = 128
F32, BF16 = jnp.float32, jnp.bfloat16
VMEM = pl.BlockSpec(memory_space=pltpu.VMEM)
SMEM = pl.BlockSpec(memory_space=pltpu.SMEM)
ANY = pl.BlockSpec(memory_space=pl.ANY)
HBM = pl.BlockSpec(memory_space=pltpu.HBM)


def run(body, out, ins, scratch=(), limit=16, flops=0, outs=VMEM, same=None):
    specs = [x[1] if isinstance(x, tuple) else VMEM for x in ins]
    arrays = [x[0] if isinstance(x, tuple) else x for x in ins]
    moved = sum(a.size * a.dtype.itemsize for a in arrays)
    return pl.pallas_call(
        body,
        out_shape=[jax.ShapeDtypeStruct(s, d) for s, d in out],
        in_specs=specs,
        out_specs=[outs] * len(out),
        scratch_shapes=list(scratch),
        input_output_aliases=same or {},
        compiler_params=pltpu.CompilerParams(vmem_limit_bytes=limit * 1024 * 1024),
        cost_estimate=pl.CostEstimate(flops=flops, bytes_accessed=moved, transcendentals=0),
    )(*arrays)


def here():
    z, y, o = (lax.axis_index(a) for a in ("z", "y", "obs"))
    held, peers = lax.axis_size("y"), lax.axis_size("obs")
    spans = held * peers
    at = y * peers + o
    seat = jnp.where(z == 1, at - lax.rem(at, 2), at)
    span = seat
    for bit in range(1, spans.bit_length()):
        span = span ^ (seat >> bit)
    c = z * held + y
    seat = c ^ (c >> 1)
    return z, span, o, c, (1 + (seat & 1)) * spans + (seat | 1), held


def triangle(width):
    parts = width // LANES
    return [(i, j) for i in range(parts) for j in range(i + 1)]


def split(x):
    hi = x.astype(BF16)
    return hi, (x - hi.astype(F32)).astype(BF16)


def mm(x, hi, lo):
    xhi, xlo = split(x)
    dot = functools.partial(jnp.dot, preferred_element_type=F32)
    return dot(xhi, hi) + (dot(xlo, hi) + dot(xhi, lo))


def mv(x, hi, lo):
    wide = jnp.broadcast_to(x, (8, x.shape[1]))
    row = lax.broadcasted_iota(jnp.int32, wide.shape, 0)
    top = wide.astype(BF16).astype(F32)
    both = jnp.where(row == 0, top, jnp.where(row == 1, wide - top, 0.0)).astype(BF16)
    first = jnp.dot(both, hi, preferred_element_type=F32)
    second = jnp.dot(both, lo, preferred_element_type=F32)
    return first[0:1] + (first[1:2] + second[0:1])


def parts(x):
    top = x.astype(BF16).astype(F32)
    return [top, (x - top).astype(BF16).astype(F32)]


def place(span):
    return span ^ (span >> 1)


def owner_plane(span):
    return 1 + place(span) % 2


EXTRA = 8
DIAG, DAMP = 16, 32


def pack_kernel(
    day, count, rows, values, prior, damping, out, day_s, count_s, values_v, prior_v, damping_v, rows_v, stage, sems
):
    blocks = out.shape[0]
    slots = rows_v.shape[1]
    chunks = rows_v.shape[2] // LANES
    small = [(day, day_s), (count, count_s), (values, values_v), (prior, prior_v), (damping, damping_v)]
    copies = [pltpu.make_async_copy(src, dst, sems.at[n]) for n, (src, dst) in enumerate(small)]
    large = [
        pltpu.make_async_copy(rows.at[pl.ds(k * slots, slots)], rows_v.at[k], sems.at[len(small) + k])
        for k in range(blocks)
    ]
    sends = [
        pltpu.make_async_copy(stage.at[place(k)], out.at[place(k)], sems.at[len(small) + blocks + k])
        for k in range(blocks)
    ]
    for copy in copies + large:
        copy.start()
    for copy in copies:
        copy.wait()
    mine = damping_v[:, 0:LANES]
    for q in range(1, chunks):
        mine = jnp.where(lax.axis_index("obs") == q, damping_v[:, q * LANES : (q + 1) * LANES], mine)
    below = parts(prior_v[...]) + parts(mine)
    below = jnp.concatenate(below, 0)
    held = values_v[...].astype(F32)
    lane = lax.broadcasted_iota(jnp.int32, (1, LANES), 1)
    for k in range(blocks):
        marks = jnp.where(lane < LANES // 2, day_s[k], count_s[k]).astype(F32)
        stage[place(k), chunks * slots : chunks * slots + EXTRA, :] = jnp.concatenate(
            [held[k : k + 1, :], marks, below], 0
        ).astype(BF16)
    for k in range(blocks):
        large[k].wait()
        for j in range(chunks):
            stage[place(k), j * slots : (j + 1) * slots, :] = rows_v[k, :, j * LANES : (j + 1) * LANES]
        sends[k].start()
    for copy in sends:
        copy.wait()


def gram_kernel(got, gain, own, extra, pay, prior, gain_out, turned, marks):
    blocks = got.shape[0]
    chunks = turned.shape[0] // LANES
    slots = (got.shape[1] - EXTRA) // chunks
    width = chunks * LANES
    tiles = triangle(width)
    group = min(blocks, 8)
    half = 2 * LANES
    gain_out[...] = gain[...]
    extra[...] = jnp.zeros(extra.shape, F32)

    def below(k):
        return got[k, chunks * slots : chunks * slots + EXTRA, :].astype(F32)

    def one(first, fresh):
        for k in range(group):
            at = slice(k * slots, (k + 1) * slots)
            line = below(first + k)
            slot = lax.broadcasted_iota(jnp.int32, (1, slots), 1).astype(F32)
            valid = slot < jnp.broadcast_to(line[1:2, LANES - 1 : LANES], (1, slots))
            day = jnp.broadcast_to(line[1:2, 0:1], (1, slots))
            kept = [jnp.where(valid & (day == d), 1.0, 0.0) for d in (0.0, 1.0)]
            marks[:, at] = jnp.concatenate(
                kept + [kept[0] * line[0:1], kept[1] * line[0:1], jnp.zeros((12, slots), F32)], 0
            ).astype(BF16)
            for j in range(chunks):
                turned[j * LANES : (j + 1) * LANES, at] = got[first + k, j * slots : (j + 1) * slots, :].T
        source = jnp.concatenate(
            [
                jnp.concatenate([got[first + k, j * slots : (j + 1) * slots, :] for j in range(chunks)], 1)
                for k in range(group)
            ],
            0,
        )
        info = jnp.dot(marks[...], source, preferred_element_type=F32)
        for d in range(2):
            for top in range(0, width, half):
                left = turned[top : top + half, :] * marks[d : d + 1, :]
                block = jnp.dot(left, source[:, : top + half], preferred_element_type=F32)
                for n, (i, j) in enumerate(tiles):
                    if top <= i * LANES < top + half:
                        r = i * LANES - top
                        piece = block[r : r + LANES, j * LANES : (j + 1) * LANES]
                        at = d * len(tiles) + n
                        own[at] = piece if fresh else own[at] + piece
            for j in range(chunks):
                piece = info[2 + d : 3 + d, j * LANES : (j + 1) * LANES]
                r = 8 * d + j
                extra[r : r + 1, :] = piece if fresh else extra[r : r + 1, :] + piece

    if blocks == group:
        one(0, True)
    else:
        own[...] = jnp.zeros(own.shape, F32)

        @pl.loop(0, blocks // group)
        def _(g):
            one(g * group, False)

    row = lax.broadcasted_iota(jnp.int32, (LANES, LANES), 0)
    column = lax.broadcasted_iota(jnp.int32, (LANES, LANES), 1)
    sides = [n for n, (i, j) in enumerate(tiles) if i != j]
    middles = [n for n, (i, j) in enumerate(tiles) if i == j]

    def send(n, piece):
        pay[n * LANES : (n + 1) * LANES, :] = piece.astype(BF16)

    for d in range(2):
        for part, piece in enumerate(parts(extra[8 * d : 8 * d + chunks, :])):
            extra[8 * d + 4 * part : 8 * d + 4 * part + chunks, :] = piece
        for m, n in enumerate(sides):
            send(d * len(sides) + m, own[d * len(tiles) + n])
    for i, n in enumerate(middles):
        squares = [own[d * len(tiles) + n] for d in range(2)]
        send(2 * len(sides) + i, jnp.where(row >= column, squares[0], squares[1]))
        for d in range(2):
            line = jnp.sum(jnp.where(row == column, squares[d], 0.0), axis=0, keepdims=True)
            for part, piece in enumerate(parts(line)):
                r = DIAG + 8 * d + 4 * part + i
                extra[r : r + 1, :] = piece
    for q in range(chunks):
        line = below(q)
        prior[:, q * LANES : (q + 1) * LANES] = line[2:3] + line[3:4]
    for y in range(blocks // 4):
        for q in range(chunks):
            line = below(4 * y + q)
            for part in range(2):
                for d in range(2):
                    r = DAMP + 16 * y + 8 * d + 4 * part + q
                    extra[r : r + 1, :] = line[4 + 2 * part + d : 5 + 2 * part + d]
    pay[pay.shape[0] - extra.shape[0] :, :] = extra[...].astype(BF16)


def prep_kernel(trans, cov, prior, pt, pthi, ptlo, chi, clo, ahead):
    whole = trans[...].T
    pt[...] = whole
    pthi[...], ptlo[...] = split(whole)
    chi[...], clo[...] = split(cov[...])
    ahead[...] = mv(prior[...], pthi[...], ptlo[...])


def stack_kernel(one, two, out):
    out[0] = one[...]
    out[1] = two[...]


def gain_kernel(held, got, mthi, mtlo):
    ids = here()
    rows = held.shape[1]
    for step, part in enumerate((held.at[0], got.at[0], held.at[1], got.at[1])):
        holder = ids[2] ^ step
        at = pl.ds(pl.multiple_of(holder * rows, rows), rows)
        hi, lo = split(part[...].T)
        mthi[:, at] = hi
        mtlo[:, at] = lo


def few(x, hi, lo):
    top = x.astype(BF16).astype(F32)
    both = jnp.concatenate([top, x - top, jnp.zeros((4, x.shape[1]), F32)], 0).astype(BF16)
    first = jnp.dot(both, hi, preferred_element_type=F32)
    second = jnp.dot(both, lo, preferred_element_type=F32)
    return first[0:2] + (first[2:4] + second[0:2])


def one_day(day, ahead, damping, omhi, omlo, info, chi, clo):
    moved = ahead * damping[day : day + 1, :]
    gap = mv(moved, omhi[day], omlo[day]) - info[day]
    return moved - mv(gap, chi[...], clo[...])


def spread(extra, got, small):
    small[0] = extra[...]
    for s, part in enumerate(got):
        small[s + 1] = part[part.shape[0] - extra.shape[0] :, :].astype(F32)


def line_of(small, s, first):
    return small[s, first : first + 1, :] + small[s, first + 4 : first + 5, :]


def table_kernel(after, extra, g1, g2, g3, table, small):
    ids = here()
    planes = 4
    chunks = table.shape[1] // LANES
    held = table.shape[0] // 2 // planes
    spread(extra, (g1, g2, g3), small)
    for s in range(planes):
        plane = lax.rem(ids[0] + s, planes)
        for k in range(held):
            for day in range(2):
                table[pl.ds(2 * (plane * held + k) + day, 1), :] = jnp.concatenate(
                    [line_of(small, s, DAMP + 16 * k + 8 * day + j) for j in range(chunks)], 1
                )


def owner_kernel(
    own, extra, g4, g3, g1, g2, prior, ahead, pthi, ptlo, chi, clo, after, omhi, omlo, info, mine, start, y, small
):
    ids = here()
    planes = 4
    width = pthi.shape[0]
    chunks = width // LANES
    tiles = triangle(width)
    got = (g1, g2, g3, g4)
    share = jnp.where(ids[0] == 2, 1.0, 0.0)
    row = lax.broadcasted_iota(jnp.int32, (LANES, LANES), 0)
    column = lax.broadcasted_iota(jnp.int32, (LANES, LANES), 1)
    spread(extra, got, small)

    def summed(first):
        others = line_of(small, 1, first) + line_of(small, 2, first) + (line_of(small, 3, first) + line_of(small, 4, first))
        return line_of(small, 0, first) * share + others

    def added(n):
        at = slice(n * LANES, (n + 1) * LANES)
        return (g1[at].astype(F32) + g2[at].astype(F32)) + (g3[at].astype(F32) + g4[at].astype(F32))

    def put(day, i, j, piece):
        hi, lo = split(piece)
        omhi[day, i * LANES : (i + 1) * LANES, j * LANES : (j + 1) * LANES] = hi
        omlo[day, i * LANES : (i + 1) * LANES, j * LANES : (j + 1) * LANES] = lo

    sides = [n for n, (i, j) in enumerate(tiles) if i != j]
    middles = [n for n, (i, j) in enumerate(tiles) if i == j]

    def unpack(day):
        for i, n in enumerate(middles):
            both = added(2 * len(sides) + i)
            part = jnp.where(row < column if day else row > column, both, 0.0)
            others = sum(line_of(small, s, DIAG + 8 * day + i) for s in range(1, 5))
            piece = own[day * len(tiles) + n] * share + (part + part.T)
            put(day, i, i, piece + jnp.where(row == column, others, 0.0))
        for m, n in enumerate(sides):
            i, j = tiles[n]
            piece = own[day * len(tiles) + n] * share + added(day * len(sides) + m)
            put(day, i, j, piece)
            put(day, j, i, piece.T)

    for day in range(2):
        info[day] = jnp.concatenate([summed(8 * day + j) for j in range(chunks)], 1)
    held = ids[5]
    source = lax.rem(ids[1] // held - ids[0] + planes, planes)
    for day in range(2):
        for j in range(chunks):
            r = DAMP + 16 * lax.rem(ids[1], held) + 8 * day + j
            mine[day : day + 1, j * LANES : (j + 1) * LANES] = (
                small[source, pl.ds(r, 1), :] + small[source, pl.ds(r + 4, 1), :]
            )
    first = (ids[1] == 0) & (ids[0] == owner_plane(0))
    start[...] = jnp.where(first, prior[...], 0.0)

    @pl.when(first)
    def _():
        unpack(0)
        state = one_day(0, ahead[...], mine, omhi, omlo, info, chi, clo)
        unpack(1)
        y[...] = one_day(1, mv(state, pthi[...], ptlo[...]), mine, omhi, omlo, info, chi, clo)

    @pl.when(jnp.logical_not(first))
    def _():
        for day in range(2):
            unpack(day)
        y[...] = jnp.zeros(y.shape, F32)


def seen(day, omhi, omlo, chi, clo):
    return mm(omhi[day].astype(F32) + omlo[day].astype(F32), chi[...], clo[...])


def early_kernel(after, omhi, omlo, info, chi, clo, pt, damping, b1hi, b1lo, off, zhi, zlo):
    @pl.when(here()[1] == 1)
    def _():
        for day in range(2):
            off[day : day + 1, :] = mv(info[day], chi[...], clo[...])
        moved = pt[...] * damping[0:1, :]
        b1hi[...], b1lo[...] = split(moved - mm(moved, *split(seen(0, omhi, omlo, chi, clo))))
        zhi[...], zlo[...] = split(seen(1, omhi, omlo, chi, clo))


def maps_kernel(
    after, omhi, omlo, info, chi, clo, pt, damping, zhi, zlo, old1, old2, old3, b1hi, b1lo, off, b2hi, b2lo
):
    second = here()[1] == 1

    @pl.when(jnp.logical_not(second))
    def _():
        parts = ((b1hi, b1lo), (b2hi, b2lo))
        for day in range(2):
            moved = pt[...] * damping[day : day + 1, :]
            parts[day][0][...], parts[day][1][...] = split(
                moved - mm(moved, *split(seen(day, omhi, omlo, chi, clo)))
            )
            off[day : day + 1, :] = mv(info[day], chi[...], clo[...])

    @pl.when(second)
    def _():
        moved = pt[...] * damping[1:2, :]
        b2hi[...], b2lo[...] = split(moved - mm(moved, zhi[...], zlo[...]))


def second_kernel(acc, got, mine, b1hi, b1lo, off, zhi, zlo, pthi, ptlo, total, y):
    total[...] = acc[...] + got[...]
    y[...] = jnp.zeros(y.shape, F32)

    @pl.when(here()[1] == 1)
    def _():
        state = mv(acc[...] + got[...], b1hi[...], b1lo[...]) + off[0:1, :]
        moved = mv(state, pthi[...], ptlo[...]) * mine[1:2, :]
        y[...] = moved - mv(moved, zhi[...], zlo[...]) + off[1:2, :]


def both_kernel(after, b1hi, b1lo, b2hi, b2lo, off, bchi, bclo, offset):
    both = jnp.dot(b1hi[...], b2hi[...], preferred_element_type=F32) + (
        jnp.dot(b1lo[...], b2hi[...], preferred_element_type=F32)
        + jnp.dot(b1hi[...], b2lo[...], preferred_element_type=F32)
    )
    bchi[...], bclo[...] = split(both)
    offset[...] = mv(off[0:1, :], b2hi[...], b2lo[...]) + off[1:2, :]


def hop_kernel(after, acc, got, bchi, bclo, offset, total, y):
    state = acc[...] + got[...]
    total[...] = state
    y[...] = mv(state, bchi[...], bclo[...]) + offset[...]


def whole_of(hi, lo):
    return hi[...].astype(F32) + lo[...].astype(F32)


def pairs_kernel(
    after, b1hi, b1lo, bchi, bclo, off, offset, table, pthi, ptlo, mthi, mtlo, khi, klo, ehi, elo, shift
):
    total = table.shape[0]
    spans = total // 2

    span = here()[1]

    @pl.when(span >= spans - 2)
    def _():
        @pl.loop(spans - 1 - span, khi.shape[0])
        def _(k):
            scaled = whole_of(mthi, mtlo) * table[pl.ds(2 * (spans - 2 - k) + 1, 1), :]
            khi[k], klo[k] = split(mm(scaled, mthi[...], mtlo[...]))

    @pl.when(span == spans - 1)
    def _():
        within = table[total - 1 : total, :]
        one = off[0:1, :]
        ahead = mv(one, pthi[...], ptlo[...]) * (within * within)
        shift[0:1, :] = one + mv(offset[...] * within - ahead, mthi[...], mtlo[...])
        whole = whole_of(b1hi, b1lo)
        ahead = mm(whole, pthi[...], ptlo[...]) * (within * within)
        moved = whole_of(bchi, bclo) * within - ahead
        ehi[...], elo[...] = split(whole + mm(moved, mthi[...], mtlo[...]))


def last_kernel(
    acc, got, b1hi, b1lo, b2hi, b2lo, bchi, bclo, off, offset, table, pthi, ptlo, mthi, mtlo,
    khi, klo, ehi, elo, shift, out, shares, means,
):
    span = here()[1]
    total, width = shares.shape
    spans = total // 2
    chunks = width // LANES
    shares[...] = jnp.zeros(shares.shape, F32)

    def step(k, v):
        t = 2 * span - 1 - k
        v = mv(v * table[pl.ds(t + 1, 1), :], mthi[...], mtlo[...])
        shares[pl.ds(t, 1), :] = v
        return v

    @pl.when(span < spans - 1)
    def _():
        state = acc[...] + got[...]
        one = mv(state, b1hi[...], b1lo[...]) + off[0:1, :]
        two = mv(one, b2hi[...], b2lo[...]) + off[1:2, :]
        both = jnp.concatenate([one, two], 0)
        within = table[pl.ds(2 * span + 1, 1), :]
        damped = jnp.concatenate([within, table[pl.ds(2 * span + 2, 1), :]], 0)
        const = both - few(few(both, pthi[...], ptlo[...]) * damped * damped, mthi[...], mtlo[...])
        even = const[0:1] + mv(const[1:2] * within, mthi[...], mtlo[...])
        shares[pl.ds(2 * span + 1, 1), :] = const[1:2]
        shares[pl.ds(2 * span, 1), :] = even
        means[0:2, :] = both
        means[2:3, :] = even

    def descend(v, start):
        damped_rows, days = [], range(start, khi.shape[0])
        for k in days:
            t = 2 * (spans - 1 - k)
            damped_rows.append(v * table[t : t + 1, :])
            v = mv(damped_rows[-1], khi[k], klo[k])
            shares[t - 2 : t - 1, :] = v
        batch = jnp.concatenate(damped_rows + [jnp.zeros((1, width), F32)] * (-len(damped_rows) % 8), 0)
        batch = mm(batch, mthi[...], mtlo[...])
        for n, k in enumerate(days):
            t = 2 * (spans - 1 - k)
            shares[t - 1 : t, :] = batch[n : n + 1]
        lax.fori_loop(2 * len(days), 2 * span, step, v)

    @pl.when(span < spans - 2)
    def _():
        lax.fori_loop(0, 2 * span, step, means[2:3, :])

    @pl.when(span == spans - 2)
    def _():
        descend(means[2:3, :], 1)

    @pl.when(span == spans - 1)
    def _():
        state = acc[...] + got[...]
        v = mv(state, ehi[...], elo[...]) + shift[0:1, :]
        shares[total - 2 : total - 1, :] = v
        descend(v, 0)
        two = mv(state, bchi[...], bclo[...]) + offset[...]
        means[0:1, :] = mv(state, b1hi[...], b1lo[...]) + off[0:1, :]
        means[1:2, :] = two
        shares[total - 1 : total, :] = two

    for c in range(spans):
        for q in range(chunks):
            out[c * chunks + q, 0:2, :] = shares[2 * c : 2 * c + 2, q * LANES : (q + 1) * LANES]
    for q in range(chunks):
        out[span * chunks + q, 2:4, :] = means[0:2, q * LANES : (q + 1) * LANES]


def add_kernel(parts, filt, smooth):
    ids = here()
    spans = parts.shape[0] // 4
    filt[...] = parts[ids[4], 2:4, :]
    smooth[...] = sum(parts[owner_plane(c) * spans + (place(c) | 1), 0:2, :] for c in range(spans))


def local(
    records,
    obs_values,
    block_day,
    block_count,
    propagator_matrix,
    analysis_cov,
    unattenuated_multiplier,
    damping,
    prior_mean,
):
    planes, held, peers = (lax.axis_size(a) for a in ("z", "y", "obs"))
    spans = planes * held
    blocks = block_day.shape[0]
    slots = records.shape[0] // blocks
    width = records.shape[1]
    days = damping.shape[0]
    assert planes == peers == 4 and days == 2 and slots == LANES and blocks == spans
    everyone = ("z", "y", "obs")

    def owner(span):
        return owner_plane(span) * spans + (place(span) | 1)

    tiles = len(triangle(width))
    extra_rows = DAMP + 16 * held
    chunks = width // LANES
    full, row = (width, width), ((1, width), F32)
    sent = run(
        pack_kernel,
        [((blocks, chunks * slots + EXTRA, LANES), BF16)],
        [
            (x, HBM)
            for x in (
                block_day,
                block_count,
                records,
                obs_values.reshape(blocks, slots),
                prior_mean.reshape(1, -1),
                damping,
            )
        ],
        [
            pltpu.SMEM((blocks,), jnp.int32),
            pltpu.SMEM((blocks,), jnp.int32),
            pltpu.VMEM((blocks, slots), BF16),
            pltpu.VMEM((1, width // peers), F32),
            pltpu.VMEM((days, width), F32),
            pltpu.VMEM((blocks, slots, width), BF16),
            pltpu.VMEM((blocks, chunks * slots + EXTRA, LANES), BF16),
            pltpu.SemaphoreType.DMA((5 + 2 * blocks,)),
        ],
        limit=60,
        outs=HBM,
    )[0]
    got = lax.all_to_all(sent, ("y", "obs"), split_axis=0, concat_axis=0, tiled=True)
    span_slots = min(blocks, 8) * slots
    own, extra, pay, prior, gain = run(
        gram_kernel,
        [
            ((2 * tiles, LANES, LANES), F32),
            ((extra_rows, LANES), F32),
            (((2 * tiles - chunks) * LANES + extra_rows, LANES), BF16),
            row,
            (unattenuated_multiplier.shape, F32),
        ],
        [got, unattenuated_multiplier],
        [pltpu.VMEM((width, span_slots), BF16), pltpu.VMEM((16, span_slots), BF16)],
        flops=4 * width * width * blocks * slots,
    )
    def swap(x, bit):
        return lax.ppermute(x, "obs", [(i, i ^ bit) for i in range(peers)])

    def plane_sum(s):
        return lax.ppermute(
            pay, everyone, [((owner_plane(p) + s) % planes * spans + place(p), owner(p)) for p in range(spans)]
        )

    fourth = lax.ppermute(
        pay, everyone, [(spans + place(p), owner(p)) for p in range(spans) if place(p) % 2 == 0]
    )
    third, first, second = plane_sum(3), plane_sum(1), plane_sum(2)
    (gains,) = run(stack_kernel, [((2,) + gain.shape, F32)], [gain, swap(gain, 2)])
    mthi, mtlo = run(gain_kernel, [(full, BF16)] * 2, [gains, swap(gains, 1)])
    pt, pthi, ptlo, chi, clo, ahead = run(
        prep_kernel, [(full, F32)] + [(full, BF16)] * 4 + [row], [propagator_matrix, analysis_cov, prior]
    )
    smalls = pltpu.VMEM((planes + 1, extra_rows, LANES), F32)
    omhi, omlo, info, mine, acc, y = run(
        owner_kernel,
        [((days,) + full, BF16)] * 2 + [((days, 1, width), F32), ((days, width), F32), row, row],
        [
            own, extra, fourth, third, first, second, prior, ahead, pthi, ptlo, chi, clo, (mthi, ANY)
        ],
        [smalls],
    )
    for k in range(spans - 1):
        received = lax.ppermute(y, everyone, [(owner(k), owner(k + 1))])
        if k == 0:
            given = [omhi, omlo, info, chi, clo, pt, mine]
            half = [(full, BF16)] * 2
            b1hi, b1lo, off, zhi, zlo = run(
                early_kernel, half + [((8, width), F32)] + half, [(y, ANY), *given], flops=18 * width**3
            )
            acc, y = run(
                second_kernel, [row, row], [acc, received, mine, b1hi, b1lo, off, zhi, zlo, pthi, ptlo]
            )
            b1hi, b1lo, off, b2hi, b2lo = run(
                maps_kernel,
                half + [((8, width), F32)] + half,
                [(y, ANY), *given, zhi, zlo, b1hi, b1lo, off],
                flops=24 * width**3,
                same={10: 0, 11: 1, 12: 2},
            )
            bchi, bclo, offset = run(
                both_kernel, [(full, BF16)] * 2 + [row], [(y, ANY), b1hi, b1lo, b2hi, b2lo, off]
            )
            (table,) = run(
                table_kernel,
                [((spans * days, width), F32)],
                [(offset, ANY), extra, first, second, third],
                [smalls],
            )
            ahead = run(
                pairs_kernel,
                [((min(spans - 1, 7),) + full, BF16)] * 2 + [(full, BF16)] * 2 + [((8, width), F32)],
                [(y, ANY), b1hi, b1lo, bchi, bclo, off, offset, table, pthi, ptlo, mthi, mtlo],
            )
            side = ahead[0]
        elif k < spans - 2:
            acc, y = run(hop_kernel, [row, row], [(side, ANY), acc, received, bchi, bclo, offset])
    (answer,) = run(
        last_kernel,
        [((spans * peers, 8, LANES), F32)],
        [
            acc, received, b1hi, b1lo, b2hi, b2lo, bchi, bclo, off, offset, table, pthi, ptlo, mthi, mtlo,
            *ahead,
        ],
        [pltpu.VMEM((spans * days, width), F32), pltpu.VMEM((8, width), F32)],
    )
    parts = lax.all_to_all(answer, everyone, split_axis=0, concat_axis=0, tiled=True)
    out = ((days, LANES), F32)
    return run(add_kernel, [out, out], [parts])


def solution(mesh):
    spans, peers = mesh.devices.shape
    finer = jax.sharding.Mesh(mesh.devices.reshape(peers, spans // peers, peers), ("z", "y", "obs"))
    tm = ("z", "y")
    mapped = jax.shard_map(
        local,
        mesh=finer,
        in_specs=(
            P(("z", "y", "obs"), None),
            P(("z", "y", "obs")),
            P(("z", "y", "obs")),
            P(("z", "y", "obs")),
            P(),
            P(),
            P("obs", None),
            P(tm, None),
            P("obs"),
        ),
        out_specs=(P(tm, "obs"), P(tm, "obs")),
        check_vma=False,
    )
    return lambda *args: tuple(mapped(*args))
```

```python
import functools

import jax
import jax.numpy as jnp
from jax import lax
from jax.experimental import pallas as pl
from jax.experimental.pallas import tpu as pltpu
from jax.sharding import PartitionSpec as P

LANES = 128
F32, BF16 = jnp.float32, jnp.bfloat16
VMEM = pl.BlockSpec(memory_space=pltpu.VMEM)
SMEM = pl.BlockSpec(memory_space=pltpu.SMEM)
ANY = pl.BlockSpec(memory_space=pl.ANY)
HBM = pl.BlockSpec(memory_space=pltpu.HBM)


def run(body, out, ins, scratch=(), limit=16, flops=0, outs=VMEM, same=None):
    specs = [x[1] if isinstance(x, tuple) else VMEM for x in ins]
    arrays = [x[0] if isinstance(x, tuple) else x for x in ins]
    moved = sum(a.size * a.dtype.itemsize for a in arrays)
    return pl.pallas_call(
        body,
        out_shape=[jax.ShapeDtypeStruct(s, d) for s, d in out],
        in_specs=specs,
        out_specs=[outs] * len(out),
        scratch_shapes=list(scratch),
        input_output_aliases=same or {},
        compiler_params=pltpu.CompilerParams(vmem_limit_bytes=limit * 1024 * 1024),
        cost_estimate=pl.CostEstimate(flops=flops, bytes_accessed=moved, transcendentals=0),
    )(*arrays)


def here():
    z, y, o = (lax.axis_index(a) for a in ("z", "y", "obs"))
    held, peers = lax.axis_size("y"), lax.axis_size("obs")
    spans = held * peers
    at = y * peers + o
    seat = jnp.where(z == 1, at - lax.rem(at, 2), at)
    span = seat
    for bit in range(1, spans.bit_length()):
        span = span ^ (seat >> bit)
    c = z * held + y
    kept = jnp.where((c == spans - 3) | (c == spans - 1), c - 1, c)
    seat = kept ^ (kept >> 1)
    return z, span, o, c, (1 + (seat & 1)) * spans + (seat | 1), held


def doubled(span, spans):
    return (span == spans - 4) | (span == spans - 2)


def triangle(width):
    parts = width // LANES
    return [(i, j) for i in range(parts) for j in range(i + 1)]


def split(x):
    hi = x.astype(BF16)
    return hi, (x - hi.astype(F32)).astype(BF16)


def mm(x, hi, lo):
    xhi, xlo = split(x)
    dot = functools.partial(jnp.dot, preferred_element_type=F32)
    return dot(xhi, hi) + (dot(xlo, hi) + dot(xhi, lo))


def mv(x, hi, lo):
    wide = jnp.broadcast_to(x, (8, x.shape[1]))
    row = lax.broadcasted_iota(jnp.int32, wide.shape, 0)
    top = wide.astype(BF16).astype(F32)
    both = jnp.where(row == 0, top, jnp.where(row == 1, wide - top, 0.0)).astype(BF16)
    first = jnp.dot(both, hi, preferred_element_type=F32)
    second = jnp.dot(both, lo, preferred_element_type=F32)
    return first[0:1] + (first[1:2] + second[0:1])


def parts(x):
    top = x.astype(BF16).astype(F32)
    return [top, (x - top).astype(BF16).astype(F32)]


def place(span):
    return span ^ (span >> 1)


def owner_plane(span):
    return 1 + place(span) % 2


EXTRA = 8
DIAG, DAMP = 16, 32


def pack_kernel(
    day, count, rows, values, prior, damping, out, day_s, count_s, values_v, prior_v, damping_v, rows_v, stage, sems
):
    blocks = out.shape[0]
    slots = rows_v.shape[1]
    chunks = rows_v.shape[2] // LANES
    small = [(day, day_s), (count, count_s), (values, values_v), (prior, prior_v), (damping, damping_v)]
    copies = [pltpu.make_async_copy(src, dst, sems.at[n]) for n, (src, dst) in enumerate(small)]
    large = [
        pltpu.make_async_copy(rows.at[pl.ds(k * slots, slots)], rows_v.at[k], sems.at[len(small) + k])
        for k in range(blocks)
    ]
    sends = [
        pltpu.make_async_copy(stage.at[place(k)], out.at[place(k)], sems.at[len(small) + blocks + k])
        for k in range(blocks)
    ]
    for copy in copies + large:
        copy.start()
    for copy in copies:
        copy.wait()
    mine = damping_v[:, 0:LANES]
    for q in range(1, chunks):
        mine = jnp.where(lax.axis_index("obs") == q, damping_v[:, q * LANES : (q + 1) * LANES], mine)
    below = parts(prior_v[...]) + parts(mine)
    below = jnp.concatenate(below, 0)
    held = values_v[...].astype(F32)
    lane = lax.broadcasted_iota(jnp.int32, (1, LANES), 1)
    for k in range(blocks):
        marks = jnp.where(lane < LANES // 2, day_s[k], count_s[k]).astype(F32)
        stage[place(k), chunks * slots : chunks * slots + EXTRA, :] = jnp.concatenate(
            [held[k : k + 1, :], marks, below], 0
        ).astype(BF16)
    for k in range(blocks):
        large[k].wait()
        for j in range(chunks):
            stage[place(k), j * slots : (j + 1) * slots, :] = rows_v[k, :, j * LANES : (j + 1) * LANES]
        sends[k].start()
    for copy in sends:
        copy.wait()


def gram_kernel(got, gain, own, extra, pay, prior, gain_out, turned, marks):
    blocks = got.shape[0]
    chunks = turned.shape[0] // LANES
    slots = (got.shape[1] - EXTRA) // chunks
    width = chunks * LANES
    tiles = triangle(width)
    group = min(blocks, 8)
    half = 2 * LANES
    gain_out[...] = gain[...]
    extra[...] = jnp.zeros(extra.shape, F32)

    def below(k):
        return got[k, chunks * slots : chunks * slots + EXTRA, :].astype(F32)

    def one(first, fresh):
        for k in range(group):
            at = slice(k * slots, (k + 1) * slots)
            line = below(first + k)
            slot = lax.broadcasted_iota(jnp.int32, (1, slots), 1).astype(F32)
            valid = slot < jnp.broadcast_to(line[1:2, LANES - 1 : LANES], (1, slots))
            day = jnp.broadcast_to(line[1:2, 0:1], (1, slots))
            kept = [jnp.where(valid & (day == d), 1.0, 0.0) for d in (0.0, 1.0)]
            marks[:, at] = jnp.concatenate(
                kept + [kept[0] * line[0:1], kept[1] * line[0:1], jnp.zeros((12, slots), F32)], 0
            ).astype(BF16)
            for j in range(chunks):
                turned[j * LANES : (j + 1) * LANES, at] = got[first + k, j * slots : (j + 1) * slots, :].T
        source = jnp.concatenate(
            [
                jnp.concatenate([got[first + k, j * slots : (j + 1) * slots, :] for j in range(chunks)], 1)
                for k in range(group)
            ],
            0,
        )
        info = jnp.dot(marks[...], source, preferred_element_type=F32)
        for d in range(2):
            for top in range(0, width, half):
                left = turned[top : top + half, :] * marks[d : d + 1, :]
                block = jnp.dot(left, source[:, : top + half], preferred_element_type=F32)
                for n, (i, j) in enumerate(tiles):
                    if top <= i * LANES < top + half:
                        r = i * LANES - top
                        piece = block[r : r + LANES, j * LANES : (j + 1) * LANES]
                        at = d * len(tiles) + n
                        own[at] = piece if fresh else own[at] + piece
            for j in range(chunks):
                piece = info[2 + d : 3 + d, j * LANES : (j + 1) * LANES]
                r = 8 * d + j
                extra[r : r + 1, :] = piece if fresh else extra[r : r + 1, :] + piece

    if blocks == group:
        one(0, True)
    else:
        own[...] = jnp.zeros(own.shape, F32)

        @pl.loop(0, blocks // group)
        def _(g):
            one(g * group, False)

    row = lax.broadcasted_iota(jnp.int32, (LANES, LANES), 0)
    column = lax.broadcasted_iota(jnp.int32, (LANES, LANES), 1)
    sides = [n for n, (i, j) in enumerate(tiles) if i != j]
    middles = [n for n, (i, j) in enumerate(tiles) if i == j]

    def send(n, piece):
        pay[n * LANES : (n + 1) * LANES, :] = piece.astype(BF16)

    for d in range(2):
        for part, piece in enumerate(parts(extra[8 * d : 8 * d + chunks, :])):
            extra[8 * d + 4 * part : 8 * d + 4 * part + chunks, :] = piece
        for m, n in enumerate(sides):
            send(d * len(sides) + m, own[d * len(tiles) + n])
    for i, n in enumerate(middles):
        squares = [own[d * len(tiles) + n] for d in range(2)]
        send(2 * len(sides) + i, jnp.where(row >= column, squares[0], squares[1]))
        for d in range(2):
            line = jnp.sum(jnp.where(row == column, squares[d], 0.0), axis=0, keepdims=True)
            for part, piece in enumerate(parts(line)):
                r = DIAG + 8 * d + 4 * part + i
                extra[r : r + 1, :] = piece
    for q in range(chunks):
        line = below(q)
        prior[:, q * LANES : (q + 1) * LANES] = line[2:3] + line[3:4]
    for y in range(blocks // 4):
        for q in range(chunks):
            line = below(4 * y + q)
            for part in range(2):
                for d in range(2):
                    r = DAMP + 16 * y + 8 * d + 4 * part + q
                    extra[r : r + 1, :] = line[4 + 2 * part + d : 5 + 2 * part + d]
    pay[pay.shape[0] - extra.shape[0] :, :] = extra[...].astype(BF16)


def prep_kernel(trans, cov, prior, pt, pthi, ptlo, chi, clo, ahead):
    whole = trans[...].T
    pt[...] = whole
    pthi[...], ptlo[...] = split(whole)
    chi[...], clo[...] = split(cov[...])
    ahead[...] = mv(prior[...], pthi[...], ptlo[...])


def stack_kernel(one, two, out):
    out[0] = one[...]
    out[1] = two[...]


def gain_kernel(held, got, mthi, mtlo):
    ids = here()
    rows = held.shape[1]
    for step, part in enumerate((held.at[0], got.at[0], held.at[1], got.at[1])):
        holder = ids[2] ^ step
        at = pl.ds(pl.multiple_of(holder * rows, rows), rows)
        hi, lo = split(part[...].T)
        mthi[:, at] = hi
        mtlo[:, at] = lo


def few(x, hi, lo):
    n = x.shape[0]
    top = x.astype(BF16).astype(F32)
    blank = [jnp.zeros((8 - 2 * n, x.shape[1]), F32)] if n < 4 else []
    both = jnp.concatenate([top, x - top] + blank, 0).astype(BF16)
    first = jnp.dot(both, hi, preferred_element_type=F32)
    second = jnp.dot(both, lo, preferred_element_type=F32)
    return first[0:n] + (first[n : 2 * n] + second[0:n])


def one_day(day, ahead, damping, omhi, omlo, info, chi, clo):
    moved = ahead * damping[day : day + 1, :]
    gap = mv(moved, omhi[day], omlo[day]) - info[day]
    return moved - mv(gap, chi[...], clo[...])


def spread(extra, got, small):
    small[0] = extra[...]
    for s, part in enumerate(got):
        small[s + 1] = part[part.shape[0] - extra.shape[0] :, :].astype(F32)


def line_of(small, s, first):
    return small[s, first : first + 1, :] + small[s, first + 4 : first + 5, :]


def table_kernel(after, extra, g1, g2, g3, table, small):
    ids = here()
    planes = 4
    chunks = table.shape[1] // LANES
    held = table.shape[0] // 2 // planes
    spread(extra, (g1, g2, g3), small)
    for s in range(planes):
        plane = lax.rem(ids[0] + s, planes)
        for k in range(held):
            for day in range(2):
                table[pl.ds(2 * (plane * held + k) + day, 1), :] = jnp.concatenate(
                    [line_of(small, s, DAMP + 16 * k + 8 * day + j) for j in range(chunks)], 1
                )


def sums(extra, got, small):
    share = jnp.where(here()[0] == 2, 1.0, 0.0)
    spread(extra, got, small)

    def summed(first):
        others = line_of(small, 1, first) + line_of(small, 2, first) + (line_of(small, 3, first) + line_of(small, 4, first))
        return line_of(small, 0, first) * share + others

    def added(n):
        at = slice(n * LANES, (n + 1) * LANES)
        one, two, three, four = (part[at].astype(F32) for part in got)
        return (one + two) + (three + four)

    return share, summed, added


def relay_kernel(after, own, extra, g4, g3, g1, g2, out, small, rows):
    span = here()[1]
    spans = lax.axis_size("z") * lax.axis_size("y")
    chunks = 4
    tiles = triangle(chunks * LANES)
    row = lax.broadcasted_iota(jnp.int32, (LANES, LANES), 0)
    column = lax.broadcasted_iota(jnp.int32, (LANES, LANES), 1)
    sides = [n for n, (i, j) in enumerate(tiles) if i != j]
    middles = [n for n, (i, j) in enumerate(tiles) if i == j]

    @pl.when((span == spans - 3) | (span == spans - 1))
    def _():
        share, summed, added = sums(extra, (g1, g2, g3, g4), small)

        def send(n, piece):
            out[n * LANES : (n + 1) * LANES, :] = (piece * share + added(n)).astype(BF16)

        for d in range(2):
            for m, n in enumerate(sides):
                send(d * len(sides) + m, own[d * len(tiles) + n])
        for i, n in enumerate(middles):
            send(2 * len(sides) + i, jnp.where(row >= column, own[n], own[len(tiles) + n]))
        rows[...] = jnp.zeros(rows.shape, F32)
        for first in (0, 8, DIAG, DIAG + 8):
            for j in range(chunks):
                for part, piece in enumerate(parts(summed(first + j))):
                    r = first + 4 * part + j
                    rows[r : r + 1, :] = piece
        out[out.shape[0] - rows.shape[0] :, :] = rows[...].astype(BF16)


def next_kernel(after, relay, chi, clo, zhi, zlo, off, whole, rows):
    spans = lax.axis_size("z") * lax.axis_size("y")
    width = whole.shape[0]
    chunks = width // LANES
    tiles = triangle(width)
    row = lax.broadcasted_iota(jnp.int32, (LANES, LANES), 0)
    column = lax.broadcasted_iota(jnp.int32, (LANES, LANES), 1)
    sides = [(i, j) for i, j in tiles if i != j]

    @pl.when(doubled(here()[1], spans))
    def _():
        rows[...] = relay[relay.shape[0] - rows.shape[0] :, :].astype(F32)

        def line(r):
            return rows[r : r + 1, :] + rows[r + 4 : r + 5, :]

        def tile(n):
            return relay[n * LANES : (n + 1) * LANES, :].astype(F32)

        def put(i, j, piece):
            whole[i * LANES : (i + 1) * LANES, j * LANES : (j + 1) * LANES] = piece

        for day in range(2):
            for i in range(chunks):
                both = tile(2 * len(sides) + i)
                part = jnp.where(row < column if day else row > column, both, 0.0)
                put(i, i, part + part.T + jnp.where(row == column, line(DIAG + 8 * day + i), 0.0))
            for m, (i, j) in enumerate(sides):
                piece = tile(day * len(sides) + m)
                put(i, j, piece)
                put(j, i, piece.T)
            zhi[day], zlo[day] = split(mm(whole[...], chi[...], clo[...]))
            info = jnp.concatenate([line(8 * day + j) for j in range(chunks)], 1)
            off[day : day + 1, :] = mv(info, chi[...], clo[...])


def next_day(day, state, damping, pthi, ptlo, zhi, zlo, off):
    moved = mv(state, pthi[...], ptlo[...]) * damping
    return moved - mv(moved, zhi[day], zlo[day]) + off[day : day + 1, :]


def owner_kernel(
    own, extra, g4, g3, g1, g2, prior, ahead, pthi, ptlo, chi, clo, after, omhi, omlo, info, mine, start, y, small
):
    ids = here()
    planes = 4
    width = pthi.shape[0]
    chunks = width // LANES
    tiles = triangle(width)
    got = (g1, g2, g3, g4)
    row = lax.broadcasted_iota(jnp.int32, (LANES, LANES), 0)
    column = lax.broadcasted_iota(jnp.int32, (LANES, LANES), 1)
    share, summed, added = sums(extra, got, small)

    def put(day, i, j, piece):
        hi, lo = split(piece)
        omhi[day, i * LANES : (i + 1) * LANES, j * LANES : (j + 1) * LANES] = hi
        omlo[day, i * LANES : (i + 1) * LANES, j * LANES : (j + 1) * LANES] = lo

    sides = [n for n, (i, j) in enumerate(tiles) if i != j]
    middles = [n for n, (i, j) in enumerate(tiles) if i == j]

    def unpack(day):
        for i, n in enumerate(middles):
            both = added(2 * len(sides) + i)
            part = jnp.where(row < column if day else row > column, both, 0.0)
            others = sum(line_of(small, s, DIAG + 8 * day + i) for s in range(1, 5))
            piece = own[day * len(tiles) + n] * share + (part + part.T)
            put(day, i, i, piece + jnp.where(row == column, others, 0.0))
        for m, n in enumerate(sides):
            i, j = tiles[n]
            piece = own[day * len(tiles) + n] * share + added(day * len(sides) + m)
            put(day, i, j, piece)
            put(day, j, i, piece.T)

    for day in range(2):
        info[day] = jnp.concatenate([summed(8 * day + j) for j in range(chunks)], 1)
    held = ids[5]
    source = lax.rem(ids[1] // held - ids[0] + planes, planes)
    for day in range(2):
        for j in range(chunks):
            r = DAMP + 16 * lax.rem(ids[1], held) + 8 * day + j
            mine[day : day + 1, j * LANES : (j + 1) * LANES] = (
                small[source, pl.ds(r, 1), :] + small[source, pl.ds(r + 4, 1), :]
            )
    first = (ids[1] == 0) & (ids[0] == owner_plane(0))
    start[...] = jnp.where(first, prior[...], 0.0)

    @pl.when(first)
    def _():
        unpack(0)
        state = one_day(0, ahead[...], mine, omhi, omlo, info, chi, clo)
        unpack(1)
        y[...] = one_day(1, mv(state, pthi[...], ptlo[...]), mine, omhi, omlo, info, chi, clo)

    @pl.when(jnp.logical_not(first))
    def _():
        for day in range(2):
            unpack(day)
        y[...] = jnp.zeros(y.shape, F32)


def seen(day, omhi, omlo, chi, clo):
    return mm(omhi[day].astype(F32) + omlo[day].astype(F32), chi[...], clo[...])


def early_kernel(after, omhi, omlo, info, chi, clo, pt, damping, b1hi, b1lo, off, zhi, zlo):
    @pl.when(here()[1] == 1)
    def _():
        for day in range(2):
            off[day : day + 1, :] = mv(info[day], chi[...], clo[...])
        moved = pt[...] * damping[0:1, :]
        b1hi[...], b1lo[...] = split(moved - mm(moved, *split(seen(0, omhi, omlo, chi, clo))))
        zhi[...], zlo[...] = split(seen(1, omhi, omlo, chi, clo))


def maps_kernel(
    after, omhi, omlo, info, chi, clo, pt, damping, zhi, zlo, old1, old2, old3, b1hi, b1lo, off, b2hi, b2lo
):
    span = here()[1]
    spans = lax.axis_size("z") * lax.axis_size("y")
    second = span == 1

    @pl.when(jnp.logical_not(second | (span == spans - 3) | (span == spans - 1)))
    def _():
        parts = ((b1hi, b1lo), (b2hi, b2lo))
        for day in range(2):
            moved = pt[...] * damping[day : day + 1, :]
            parts[day][0][...], parts[day][1][...] = split(
                moved - mm(moved, *split(seen(day, omhi, omlo, chi, clo)))
            )
            off[day : day + 1, :] = mv(info[day], chi[...], clo[...])

    @pl.when(second)
    def _():
        moved = pt[...] * damping[1:2, :]
        b2hi[...], b2lo[...] = split(moved - mm(moved, zhi[...], zlo[...]))


def second_kernel(acc, got, mine, b1hi, b1lo, off, zhi, zlo, pthi, ptlo, total, y):
    total[...] = acc[...] + got[...]
    y[...] = jnp.zeros(y.shape, F32)

    @pl.when(here()[1] == 1)
    def _():
        state = mv(acc[...] + got[...], b1hi[...], b1lo[...]) + off[0:1, :]
        moved = mv(state, pthi[...], ptlo[...]) * mine[1:2, :]
        y[...] = moved - mv(moved, zhi[...], zlo[...]) + off[1:2, :]


def both_kernel(after, b1hi, b1lo, b2hi, b2lo, off, bchi, bclo, offset):
    both = jnp.dot(b1hi[...], b2hi[...], preferred_element_type=F32) + (
        jnp.dot(b1lo[...], b2hi[...], preferred_element_type=F32)
        + jnp.dot(b1hi[...], b2lo[...], preferred_element_type=F32)
    )
    bchi[...], bclo[...] = split(both)
    offset[...] = mv(off[0:1, :], b2hi[...], b2lo[...]) + off[1:2, :]


def hop_kernel(after, acc, got, bchi, bclo, offset, total, y):
    state = acc[...] + got[...]
    total[...] = state
    y[...] = mv(state, bchi[...], bclo[...]) + offset[...]


def days_kernel(acc, got, b1hi, b1lo, b2hi, b2lo, off, total, y):
    state = acc[...] + got[...]
    total[...] = state
    state = mv(state, b1hi[...], b1lo[...]) + off[0:1, :]
    y[...] = mv(state, b2hi[...], b2lo[...]) + off[1:2, :]


def double_kernel(after, acc, got, bchi, bclo, offset, table, pthi, ptlo, zhi, zlo, off, total, y):
    spans = table.shape[0] // 2
    total[...] = acc[...] + got[...]
    y[...] = jnp.zeros(y.shape, F32)

    @pl.when(here()[1] == spans - 4)
    def _():
        state = mv(acc[...] + got[...], bchi[...], bclo[...]) + offset[...]
        for day in range(2):
            r = 2 * (spans - 3) + day
            state = next_day(day, state, table[r : r + 1, :], pthi, ptlo, zhi, zlo, off)
        y[...] = state


def whole_of(hi, lo):
    return hi[...].astype(F32) + lo[...].astype(F32)


def pairs_kernel(after, table, mthi, mtlo, khi, klo):
    spans = table.shape[0] // 2

    @pl.when(here()[1] == spans - 2)
    def _():
        @pl.loop(0, khi.shape[0])
        def _(k):
            scaled = whole_of(mthi, mtlo) * table[pl.ds(2 * (spans - 3 - k) + 1, 1), :]
            khi[k], klo[k] = split(mm(scaled, mthi[...], mtlo[...]))


def last_kernel(
    acc, got, b1hi, b1lo, b2hi, b2lo, bchi, bclo, off, offset, table, pthi, ptlo, mthi, mtlo,
    zhi, zlo, next_off, khi, klo, out, shares, means,
):
    span = here()[1]
    total, width = shares.shape
    spans = total // 2
    chunks = width // LANES
    twice = doubled(span, spans)
    shares[...] = jnp.zeros(shares.shape, F32)

    def step(k, v):
        t = 2 * span - 1 - k
        v = mv(v * table[pl.ds(t + 1, 1), :], mthi[...], mtlo[...])
        shares[pl.ds(t, 1), :] = v
        return v

    def own_days(rows, damped):
        both = jnp.concatenate(rows, 0)
        ahead = jnp.concatenate(damped, 0)
        const = both - few(few(both, pthi[...], ptlo[...]) * ahead * ahead, mthi[...], mtlo[...])
        n = len(rows)
        means[0:n, :] = both
        v = const[n - 1 : n]
        shares[pl.ds(2 * span + n - 1, 1), :] = v
        for i in range(n - 2, -1, -1):
            v = const[i : i + 1] + mv(v * damped[i], mthi[...], mtlo[...])
            shares[pl.ds(2 * span + i, 1), :] = v
        means[4:5, :] = v

    @pl.when(span < spans - 4)
    def _():
        state = acc[...] + got[...]
        one = mv(state, b1hi[...], b1lo[...]) + off[0:1, :]
        two = mv(one, b2hi[...], b2lo[...]) + off[1:2, :]
        own_days([one, two], [table[pl.ds(2 * span + 1 + i, 1), :] for i in range(2)])

    @pl.when(twice)
    def _():
        state = acc[...] + got[...]
        rows = [
            mv(state, b1hi[...], b1lo[...]) + off[0:1, :],
            mv(state, bchi[...], bclo[...]) + offset[...],
        ]
        for day in range(2):
            damping = table[pl.ds(2 * span + 2 + day, 1), :]
            rows.append(next_day(day, rows[-1], damping, pthi, ptlo, zhi, zlo, next_off))
        damped = [table[pl.ds(2 * span + 1 + i, 1), :] for i in range(3)]
        beyond = table[pl.ds(jnp.minimum(2 * span + 4, total - 1), 1), :]
        damped.append(beyond * jnp.where(span == spans - 2, 0.0, 1.0))
        own_days(rows, damped)

    @pl.when(span < spans - 2)
    def _():
        lax.fori_loop(0, jnp.where((span < spans - 4) | twice, 2 * span, 0), step, means[4:5, :])

    @pl.when(span == spans - 2)
    def _():
        v, damped_rows = means[4:5, :], []
        for k in range(khi.shape[0]):
            t = 2 * (spans - 2 - k)
            damped_rows.append(v * table[t : t + 1, :])
            v = mv(damped_rows[-1], khi[k], klo[k])
            shares[t - 2 : t - 1, :] = v
        batch = jnp.concatenate(damped_rows + [jnp.zeros((1, width), F32)] * (-len(damped_rows) % 8), 0)
        batch = mm(batch, mthi[...], mtlo[...])
        for k in range(khi.shape[0]):
            t = 2 * (spans - 2 - k)
            shares[t - 1 : t, :] = batch[k : k + 1]
        lax.fori_loop(2 * khi.shape[0], 2 * span, step, v)

    for c in range(spans):
        for q in range(chunks):
            out[c * chunks + q, 0:2, :] = shares[2 * c : 2 * c + 2, q * LANES : (q + 1) * LANES]
    for q in range(chunks):
        out[span * chunks + q, 2:4, :] = means[0:2, q * LANES : (q + 1) * LANES]

    @pl.when(twice)
    def _():
        for q in range(chunks):
            out[(span + 1) * chunks + q, 2:4, :] = means[2:4, q * LANES : (q + 1) * LANES]


def add_kernel(parts, filt, smooth):
    spans = parts.shape[0] // 4
    owners = [*range(spans - 4), spans - 4, spans - 2]
    filt[...] = parts[here()[4], 2:4, :]
    smooth[...] = sum(parts[owner_plane(c) * spans + (place(c) | 1), 0:2, :] for c in owners)


def local(
    records,
    obs_values,
    block_day,
    block_count,
    propagator_matrix,
    analysis_cov,
    unattenuated_multiplier,
    damping,
    prior_mean,
):
    planes, held, peers = (lax.axis_size(a) for a in ("z", "y", "obs"))
    spans = planes * held
    blocks = block_day.shape[0]
    slots = records.shape[0] // blocks
    width = records.shape[1]
    days = damping.shape[0]
    assert planes == peers == 4 and days == 2 and slots == LANES and blocks == spans
    everyone = ("z", "y", "obs")

    def owner(span):
        return owner_plane(span) * spans + (place(span) | 1)

    tiles = len(triangle(width))
    extra_rows = DAMP + 16 * held
    chunks = width // LANES
    full, row = (width, width), ((1, width), F32)
    sent = run(
        pack_kernel,
        [((blocks, chunks * slots + EXTRA, LANES), BF16)],
        [
            (x, HBM)
            for x in (
                block_day,
                block_count,
                records,
                obs_values.reshape(blocks, slots),
                prior_mean.reshape(1, -1),
                damping,
            )
        ],
        [
            pltpu.SMEM((blocks,), jnp.int32),
            pltpu.SMEM((blocks,), jnp.int32),
            pltpu.VMEM((blocks, slots), BF16),
            pltpu.VMEM((1, width // peers), F32),
            pltpu.VMEM((days, width), F32),
            pltpu.VMEM((blocks, slots, width), BF16),
            pltpu.VMEM((blocks, chunks * slots + EXTRA, LANES), BF16),
            pltpu.SemaphoreType.DMA((5 + 2 * blocks,)),
        ],
        limit=60,
        outs=HBM,
    )[0]
    got = lax.all_to_all(sent, ("y", "obs"), split_axis=0, concat_axis=0, tiled=True)
    span_slots = min(blocks, 8) * slots
    own, extra, pay, prior, gain = run(
        gram_kernel,
        [
            ((2 * tiles, LANES, LANES), F32),
            ((extra_rows, LANES), F32),
            (((2 * tiles - chunks) * LANES + extra_rows, LANES), BF16),
            row,
            (unattenuated_multiplier.shape, F32),
        ],
        [got, unattenuated_multiplier],
        [pltpu.VMEM((width, span_slots), BF16), pltpu.VMEM((16, span_slots), BF16)],
        flops=4 * width * width * blocks * slots,
    )
    def swap(x, bit):
        return lax.ppermute(x, "obs", [(i, i ^ bit) for i in range(peers)])

    def plane_sum(s):
        return lax.ppermute(
            pay, everyone, [((owner_plane(p) + s) % planes * spans + place(p), owner(p)) for p in range(spans)]
        )

    fourth = lax.ppermute(
        pay, everyone, [(spans + place(p), owner(p)) for p in range(spans) if place(p) % 2 == 0]
    )
    third, first, second = plane_sum(3), plane_sum(1), plane_sum(2)
    (gains,) = run(stack_kernel, [((2,) + gain.shape, F32)], [gain, swap(gain, 2)])
    mthi, mtlo = run(gain_kernel, [(full, BF16)] * 2, [gains, swap(gains, 1)])
    pt, pthi, ptlo, chi, clo, ahead = run(
        prep_kernel, [(full, F32)] + [(full, BF16)] * 4 + [row], [propagator_matrix, analysis_cov, prior]
    )
    smalls = pltpu.VMEM((planes + 1, extra_rows, LANES), F32)
    omhi, omlo, info, mine, acc, y = run(
        owner_kernel,
        [((days,) + full, BF16)] * 2 + [((days, 1, width), F32), ((days, width), F32), row, row],
        [
            own, extra, fourth, third, first, second, prior, ahead, pthi, ptlo, chi, clo, (mthi, ANY)
        ],
        [smalls],
    )
    (packed,) = run(
        relay_kernel,
        [(pay.shape, BF16)],
        [(y, ANY), own, extra, fourth, third, first, second],
        [smalls, pltpu.VMEM((extra_rows, LANES), F32)],
    )
    relay = lax.ppermute(
        packed, everyone, [(owner(p + 1), owner(p)) for p in (spans - 4, spans - 2)]
    )
    chain = [*range(spans - 3), spans - 2]
    half = [(full, BF16)] * 2
    for k, (source, target) in enumerate(zip(chain, chain[1:])):
        received = lax.ppermute(y, everyone, [(owner(source), owner(target))])
        if k == 0:
            given = [omhi, omlo, info, chi, clo, pt, mine]
            b1hi, b1lo, off, zhi, zlo = run(
                early_kernel, half + [((8, width), F32)] + half, [(y, ANY), *given], flops=18 * width**3
            )
            acc, y = run(
                second_kernel, [row, row], [acc, received, mine, b1hi, b1lo, off, zhi, zlo, pthi, ptlo]
            )
            b1hi, b1lo, off, b2hi, b2lo = run(
                maps_kernel,
                half + [((8, width), F32)] + half,
                [(y, ANY), *given, zhi, zlo, b1hi, b1lo, off],
                flops=24 * width**3,
                same={10: 0, 11: 1, 12: 2},
            )
        elif k == 1:
            acc, y = run(days_kernel, [row, row], [acc, received, b1hi, b1lo, b2hi, b2lo, off])
            bchi, bclo, offset = run(
                both_kernel, half + [row], [(y, ANY), b1hi, b1lo, b2hi, b2lo, off]
            )
            (table,) = run(
                table_kernel,
                [((spans * days, width), F32)],
                [(offset, ANY), extra, first, second, third],
                [smalls],
            )
            khi, klo = run(
                pairs_kernel, [((min(spans - 2, 5),) + full, BF16)] * 2, [(y, ANY), table, mthi, mtlo]
            )
            nexthi, nextlo, next_off = run(
                next_kernel,
                [((days,) + full, BF16)] * 2 + [((8, width), F32)],
                [(khi, ANY), relay, chi, clo],
                [pltpu.VMEM(full, F32), pltpu.VMEM((extra_rows, LANES), F32)],
            )
        elif target == spans - 4:
            acc, y = run(
                double_kernel,
                [row, row],
                [
                    (nexthi, ANY), acc, received, bchi, bclo, offset, table, pthi, ptlo, nexthi, nextlo, next_off
                ],
            )
        elif target != spans - 2:
            acc, y = run(hop_kernel, [row, row], [(nexthi, ANY), acc, received, bchi, bclo, offset])
    (answer,) = run(
        last_kernel,
        [((spans * peers, 8, LANES), F32)],
        [
            acc, received, b1hi, b1lo, b2hi, b2lo, bchi, bclo, off, offset, table, pthi, ptlo, mthi, mtlo,
            nexthi, nextlo, next_off, khi, klo,
        ],
        [pltpu.VMEM((spans * days, width), F32), pltpu.VMEM((8, width), F32)],
    )
    parts = lax.all_to_all(answer, everyone, split_axis=0, concat_axis=0, tiled=True)
    out = ((days, LANES), F32)
    return run(add_kernel, [out, out], [parts])


def solution(mesh):
    spans, peers = mesh.devices.shape
    finer = jax.sharding.Mesh(mesh.devices.reshape(peers, spans // peers, peers), ("z", "y", "obs"))
    tm = ("z", "y")
    mapped = jax.shard_map(
        local,
        mesh=finer,
        in_specs=(
            P(("z", "y", "obs"), None),
            P(("z", "y", "obs")),
            P(("z", "y", "obs")),
            P(("z", "y", "obs")),
            P(),
            P(),
            P("obs", None),
            P(tm, None),
            P("obs"),
        ),
        out_specs=(P(tm, "obs"), P(tm, "obs")),
        check_vma=False,
    )
    return lambda *args: tuple(mapped(*args))
```

```python
import functools

import jax
import jax.numpy as jnp
from jax import lax
from jax.experimental import pallas as pl
from jax.experimental.pallas import tpu as pltpu
from jax.sharding import PartitionSpec as P

LANES = 128
F32, BF16 = jnp.float32, jnp.bfloat16
VMEM = pl.BlockSpec(memory_space=pltpu.VMEM)
SMEM = pl.BlockSpec(memory_space=pltpu.SMEM)
ANY = pl.BlockSpec(memory_space=pl.ANY)
HBM = pl.BlockSpec(memory_space=pltpu.HBM)


def run(body, out, ins, scratch=(), limit=16, flops=0, outs=VMEM, same=None):
    specs = [x[1] if isinstance(x, tuple) else VMEM for x in ins]
    arrays = [x[0] if isinstance(x, tuple) else x for x in ins]
    moved = sum(a.size * a.dtype.itemsize for a in arrays)
    return pl.pallas_call(
        body,
        out_shape=[jax.ShapeDtypeStruct(s, d) for s, d in out],
        in_specs=specs,
        out_specs=[outs] * len(out),
        scratch_shapes=list(scratch),
        input_output_aliases=same or {},
        compiler_params=pltpu.CompilerParams(vmem_limit_bytes=limit * 1024 * 1024),
        cost_estimate=pl.CostEstimate(flops=flops, bytes_accessed=moved, transcendentals=0),
    )(*arrays)


def here():
    z, y, o = (lax.axis_index(a) for a in ("z", "y", "obs"))
    held, peers = lax.axis_size("y"), lax.axis_size("obs")
    spans = held * peers
    at = y * peers + o
    seat = jnp.where(z == 1, at - lax.rem(at, 2), at)
    span = seat
    for bit in range(1, spans.bit_length()):
        span = span ^ (seat >> bit)
    c = z * held + y
    kept = jnp.where((c == spans - 3) | (c == spans - 1), c - 1, c)
    seat = kept ^ (kept >> 1)
    return z, span, o, c, (1 + (seat & 1)) * spans + (seat | 1), held


def doubled(span, spans):
    return (span == spans - 4) | (span == spans - 2)


def triangle(width):
    parts = width // LANES
    return [(i, j) for i in range(parts) for j in range(i + 1)]


def split(x):
    hi = x.astype(BF16)
    return hi, (x - hi.astype(F32)).astype(BF16)


def mm(x, hi, lo):
    xhi, xlo = split(x)
    dot = functools.partial(jnp.dot, preferred_element_type=F32)
    return dot(xhi, hi) + (dot(xlo, hi) + dot(xhi, lo))


def mv(x, hi, lo):
    wide = jnp.broadcast_to(x, (8, x.shape[1]))
    row = lax.broadcasted_iota(jnp.int32, wide.shape, 0)
    top = wide.astype(BF16).astype(F32)
    both = jnp.where(row == 0, top, jnp.where(row == 1, wide - top, 0.0)).astype(BF16)
    first = jnp.dot(both, hi, preferred_element_type=F32)
    second = jnp.dot(both, lo, preferred_element_type=F32)
    return first[0:1] + (first[1:2] + second[0:1])


def parts(x):
    top = x.astype(BF16).astype(F32)
    return [top, (x - top).astype(BF16).astype(F32)]


def place(span):
    return span ^ (span >> 1)


def owner_plane(span):
    return 1 + place(span) % 2


EXTRA = 8
DIAG, DAMP = 16, 32


def pack_kernel(
    day, count, rows, values, prior, damping, out, day_s, count_s, values_v, prior_v, damping_v, rows_v, stage, sems
):
    blocks = out.shape[0]
    slots = rows_v.shape[1]
    chunks = rows_v.shape[2] // LANES
    small = [(day, day_s), (count, count_s), (values, values_v), (prior, prior_v), (damping, damping_v)]
    copies = [pltpu.make_async_copy(src, dst, sems.at[n]) for n, (src, dst) in enumerate(small)]
    large = [
        pltpu.make_async_copy(rows.at[pl.ds(k * slots, slots)], rows_v.at[k], sems.at[len(small) + k])
        for k in range(blocks)
    ]
    sends = [
        pltpu.make_async_copy(stage.at[place(k)], out.at[place(k)], sems.at[len(small) + blocks + k])
        for k in range(blocks)
    ]
    for copy in copies + large:
        copy.start()
    for copy in copies:
        copy.wait()
    mine = damping_v[:, 0:LANES]
    for q in range(1, chunks):
        mine = jnp.where(lax.axis_index("obs") == q, damping_v[:, q * LANES : (q + 1) * LANES], mine)
    below = parts(prior_v[...]) + parts(mine)
    below = jnp.concatenate(below, 0)
    held = values_v[...].astype(F32)
    lane = lax.broadcasted_iota(jnp.int32, (1, LANES), 1)
    for k in range(blocks):
        marks = jnp.where(lane < LANES // 2, day_s[k], count_s[k]).astype(F32)
        stage[place(k), chunks * slots : chunks * slots + EXTRA, :] = jnp.concatenate(
            [held[k : k + 1, :], marks, below], 0
        ).astype(BF16)
    for k in range(blocks):
        large[k].wait()
        for j in range(chunks):
            stage[place(k), j * slots : (j + 1) * slots, :] = rows_v[k, :, j * LANES : (j + 1) * LANES]
        sends[k].start()
    for copy in sends:
        copy.wait()


def gram_kernel(got, gain, own, extra, pay, prior, gain_out, turned, marks):
    blocks = got.shape[0]
    chunks = turned.shape[0] // LANES
    slots = (got.shape[1] - EXTRA) // chunks
    width = chunks * LANES
    tiles = triangle(width)
    group = min(blocks, 8)
    half = 2 * LANES
    gain_out[...] = gain[...]
    extra[...] = jnp.zeros(extra.shape, F32)

    def below(k):
        return got[k, chunks * slots : chunks * slots + EXTRA, :].astype(F32)

    def one(first, fresh):
        for k in range(group):
            at = slice(k * slots, (k + 1) * slots)
            line = below(first + k)
            slot = lax.broadcasted_iota(jnp.int32, (1, slots), 1).astype(F32)
            valid = slot < jnp.broadcast_to(line[1:2, LANES - 1 : LANES], (1, slots))
            day = jnp.broadcast_to(line[1:2, 0:1], (1, slots))
            kept = [jnp.where(valid & (day == d), 1.0, 0.0) for d in (0.0, 1.0)]
            marks[:, at] = jnp.concatenate(
                kept + [kept[0] * line[0:1], kept[1] * line[0:1], jnp.zeros((12, slots), F32)], 0
            ).astype(BF16)
            for j in range(chunks):
                turned[j * LANES : (j + 1) * LANES, at] = got[first + k, j * slots : (j + 1) * slots, :].T
        source = jnp.concatenate(
            [
                jnp.concatenate([got[first + k, j * slots : (j + 1) * slots, :] for j in range(chunks)], 1)
                for k in range(group)
            ],
            0,
        )
        info = jnp.dot(marks[...], source, preferred_element_type=F32)
        for d in range(2):
            for top in range(0, width, half):
                left = turned[top : top + half, :] * marks[d : d + 1, :]
                block = jnp.dot(left, source[:, : top + half], preferred_element_type=F32)
                for n, (i, j) in enumerate(tiles):
                    if top <= i * LANES < top + half:
                        r = i * LANES - top
                        piece = block[r : r + LANES, j * LANES : (j + 1) * LANES]
                        at = d * len(tiles) + n
                        own[at] = piece if fresh else own[at] + piece
            for j in range(chunks):
                piece = info[2 + d : 3 + d, j * LANES : (j + 1) * LANES]
                r = 8 * d + j
                extra[r : r + 1, :] = piece if fresh else extra[r : r + 1, :] + piece

    if blocks == group:
        one(0, True)
    else:
        own[...] = jnp.zeros(own.shape, F32)

        @pl.loop(0, blocks // group)
        def _(g):
            one(g * group, False)

    row = lax.broadcasted_iota(jnp.int32, (LANES, LANES), 0)
    column = lax.broadcasted_iota(jnp.int32, (LANES, LANES), 1)
    sides = [n for n, (i, j) in enumerate(tiles) if i != j]
    middles = [n for n, (i, j) in enumerate(tiles) if i == j]

    def send(n, piece):
        pay[n * LANES : (n + 1) * LANES, :] = piece.astype(BF16)

    for d in range(2):
        for part, piece in enumerate(parts(extra[8 * d : 8 * d + chunks, :])):
            extra[8 * d + 4 * part : 8 * d + 4 * part + chunks, :] = piece
        for m, n in enumerate(sides):
            send(d * len(sides) + m, own[d * len(tiles) + n])
    for i, n in enumerate(middles):
        squares = [own[d * len(tiles) + n] for d in range(2)]
        send(2 * len(sides) + i, jnp.where(row >= column, squares[0], squares[1]))
        for d in range(2):
            line = jnp.sum(jnp.where(row == column, squares[d], 0.0), axis=0, keepdims=True)
            for part, piece in enumerate(parts(line)):
                r = DIAG + 8 * d + 4 * part + i
                extra[r : r + 1, :] = piece
    for q in range(chunks):
        line = below(q)
        prior[:, q * LANES : (q + 1) * LANES] = line[2:3] + line[3:4]
    for y in range(blocks // 4):
        for q in range(chunks):
            line = below(4 * y + q)
            for part in range(2):
                for d in range(2):
                    r = DAMP + 16 * y + 8 * d + 4 * part + q
                    extra[r : r + 1, :] = line[4 + 2 * part + d : 5 + 2 * part + d]
    pay[pay.shape[0] - extra.shape[0] :, :] = extra[...].astype(BF16)


def prep_kernel(trans, cov, prior, pt, pthi, ptlo, chi, clo, ahead):
    whole = trans[...].T
    pt[...] = whole
    pthi[...], ptlo[...] = split(whole)
    chi[...], clo[...] = split(cov[...])
    ahead[...] = mv(prior[...], pthi[...], ptlo[...])


def stack_kernel(one, two, out):
    out[0] = one[...]
    out[1] = two[...]


def gain_kernel(held, got, mthi, mtlo):
    ids = here()
    rows = held.shape[1]
    for step, part in enumerate((held.at[0], got.at[0], held.at[1], got.at[1])):
        holder = ids[2] ^ step
        at = pl.ds(pl.multiple_of(holder * rows, rows), rows)
        hi, lo = split(part[...].T)
        mthi[:, at] = hi
        mtlo[:, at] = lo


def few(x, hi, lo):
    n = x.shape[0]
    top = x.astype(BF16).astype(F32)
    blank = [jnp.zeros((8 - 2 * n, x.shape[1]), F32)] if n < 4 else []
    both = jnp.concatenate([top, x - top] + blank, 0).astype(BF16)
    first = jnp.dot(both, hi, preferred_element_type=F32)
    second = jnp.dot(both, lo, preferred_element_type=F32)
    return first[0:n] + (first[n : 2 * n] + second[0:n])


def one_day(day, ahead, damping, omhi, omlo, info, chi, clo):
    moved = ahead * damping[day : day + 1, :]
    gap = mv(moved, omhi[day], omlo[day]) - info[day]
    return moved - mv(gap, chi[...], clo[...])


def spread(extra, got, small):
    small[0] = extra[...]
    for s, part in enumerate(got):
        small[s + 1] = part[part.shape[0] - extra.shape[0] :, :].astype(F32)


def line_of(small, s, first):
    return small[s, first : first + 1, :] + small[s, first + 4 : first + 5, :]


def table_kernel(after, extra, g1, g2, g3, table, small):
    ids = here()
    planes = 4
    chunks = table.shape[1] // LANES
    held = table.shape[0] // 2 // planes
    spread(extra, (g1, g2, g3), small)
    for s in range(planes):
        plane = lax.rem(ids[0] + s, planes)
        for k in range(held):
            for day in range(2):
                table[pl.ds(2 * (plane * held + k) + day, 1), :] = jnp.concatenate(
                    [line_of(small, s, DAMP + 16 * k + 8 * day + j) for j in range(chunks)], 1
                )


def sums(extra, got, small):
    share = jnp.where(here()[0] == 2, 1.0, 0.0)
    spread(extra, got, small)

    def summed(first):
        others = line_of(small, 1, first) + line_of(small, 2, first) + (line_of(small, 3, first) + line_of(small, 4, first))
        return line_of(small, 0, first) * share + others

    def added(n):
        at = slice(n * LANES, (n + 1) * LANES)
        one, two, three, four = (part[at].astype(F32) for part in got)
        return (one + two) + (three + four)

    return share, summed, added


def relay_kernel(after, own, extra, g4, g3, g1, g2, out, small, rows):
    span = here()[1]
    spans = lax.axis_size("z") * lax.axis_size("y")
    chunks = 4
    tiles = triangle(chunks * LANES)
    row = lax.broadcasted_iota(jnp.int32, (LANES, LANES), 0)
    column = lax.broadcasted_iota(jnp.int32, (LANES, LANES), 1)
    sides = [n for n, (i, j) in enumerate(tiles) if i != j]
    middles = [n for n, (i, j) in enumerate(tiles) if i == j]

    @pl.when((span == spans - 3) | (span == spans - 1))
    def _():
        share, summed, added = sums(extra, (g1, g2, g3, g4), small)

        def send(n, piece):
            out[n * LANES : (n + 1) * LANES, :] = (piece * share + added(n)).astype(BF16)

        for d in range(2):
            for m, n in enumerate(sides):
                send(d * len(sides) + m, own[d * len(tiles) + n])
        for i, n in enumerate(middles):
            send(2 * len(sides) + i, jnp.where(row >= column, own[n], own[len(tiles) + n]))
        rows[...] = jnp.zeros(rows.shape, F32)
        for first in (0, 8, DIAG, DIAG + 8):
            for j in range(chunks):
                for part, piece in enumerate(parts(summed(first + j))):
                    r = first + 4 * part + j
                    rows[r : r + 1, :] = piece
        out[out.shape[0] - rows.shape[0] :, :] = rows[...].astype(BF16)


def next_kernel(after, relay, chi, clo, zhi, zlo, off, whole, rows):
    spans = lax.axis_size("z") * lax.axis_size("y")
    width = whole.shape[0]
    chunks = width // LANES
    tiles = triangle(width)
    row = lax.broadcasted_iota(jnp.int32, (LANES, LANES), 0)
    column = lax.broadcasted_iota(jnp.int32, (LANES, LANES), 1)
    sides = [(i, j) for i, j in tiles if i != j]

    @pl.when(doubled(here()[1], spans))
    def _():
        rows[...] = relay[relay.shape[0] - rows.shape[0] :, :].astype(F32)

        def line(r):
            return rows[r : r + 1, :] + rows[r + 4 : r + 5, :]

        def tile(n):
            return relay[n * LANES : (n + 1) * LANES, :].astype(F32)

        def put(i, j, piece):
            whole[i * LANES : (i + 1) * LANES, j * LANES : (j + 1) * LANES] = piece

        for day in range(2):
            for i in range(chunks):
                both = tile(2 * len(sides) + i)
                part = jnp.where(row < column if day else row > column, both, 0.0)
                put(i, i, part + part.T + jnp.where(row == column, line(DIAG + 8 * day + i), 0.0))
            for m, (i, j) in enumerate(sides):
                piece = tile(day * len(sides) + m)
                put(i, j, piece)
                put(j, i, piece.T)
            zhi[day], zlo[day] = split(mm(whole[...], chi[...], clo[...]))
            info = jnp.concatenate([line(8 * day + j) for j in range(chunks)], 1)
            off[day : day + 1, :] = mv(info, chi[...], clo[...])


def next_day(day, state, damping, pthi, ptlo, zhi, zlo, off):
    moved = mv(state, pthi[...], ptlo[...]) * damping
    return moved - mv(moved, zhi[day], zlo[day]) + off[day : day + 1, :]


def owner_kernel(
    own, extra, g4, g3, g1, g2, prior, ahead, pthi, ptlo, chi, clo, after, omhi, omlo, info, mine, start, y, small
):
    ids = here()
    planes = 4
    width = pthi.shape[0]
    chunks = width // LANES
    tiles = triangle(width)
    got = (g1, g2, g3, g4)
    row = lax.broadcasted_iota(jnp.int32, (LANES, LANES), 0)
    column = lax.broadcasted_iota(jnp.int32, (LANES, LANES), 1)
    share, summed, added = sums(extra, got, small)

    def put(day, i, j, piece):
        hi, lo = split(piece)
        omhi[day, i * LANES : (i + 1) * LANES, j * LANES : (j + 1) * LANES] = hi
        omlo[day, i * LANES : (i + 1) * LANES, j * LANES : (j + 1) * LANES] = lo

    sides = [n for n, (i, j) in enumerate(tiles) if i != j]
    middles = [n for n, (i, j) in enumerate(tiles) if i == j]

    def unpack(day):
        for i, n in enumerate(middles):
            both = added(2 * len(sides) + i)
            part = jnp.where(row < column if day else row > column, both, 0.0)
            others = sum(line_of(small, s, DIAG + 8 * day + i) for s in range(1, 5))
            piece = own[day * len(tiles) + n] * share + (part + part.T)
            put(day, i, i, piece + jnp.where(row == column, others, 0.0))
        for m, n in enumerate(sides):
            i, j = tiles[n]
            piece = own[day * len(tiles) + n] * share + added(day * len(sides) + m)
            put(day, i, j, piece)
            put(day, j, i, piece.T)

    for day in range(2):
        info[day] = jnp.concatenate([summed(8 * day + j) for j in range(chunks)], 1)
    held = ids[5]
    source = lax.rem(ids[1] // held - ids[0] + planes, planes)
    for day in range(2):
        for j in range(chunks):
            r = DAMP + 16 * lax.rem(ids[1], held) + 8 * day + j
            mine[day : day + 1, j * LANES : (j + 1) * LANES] = (
                small[source, pl.ds(r, 1), :] + small[source, pl.ds(r + 4, 1), :]
            )
    first = (ids[1] == 0) & (ids[0] == owner_plane(0))
    start[...] = jnp.where(first, prior[...], 0.0)

    @pl.when(first)
    def _():
        unpack(0)
        state = one_day(0, ahead[...], mine, omhi, omlo, info, chi, clo)
        unpack(1)
        y[...] = one_day(1, mv(state, pthi[...], ptlo[...]), mine, omhi, omlo, info, chi, clo)

    @pl.when(jnp.logical_not(first))
    def _():
        for day in range(2):
            unpack(day)
        y[...] = jnp.zeros(y.shape, F32)


def seen(day, omhi, omlo, chi, clo):
    return mm(omhi[day].astype(F32) + omlo[day].astype(F32), chi[...], clo[...])


def early_kernel(after, omhi, omlo, info, chi, clo, pt, damping, b1hi, b1lo, off, zhi, zlo):
    @pl.when(here()[1] == 1)
    def _():
        for day in range(2):
            off[day : day + 1, :] = mv(info[day], chi[...], clo[...])
        moved = pt[...] * damping[0:1, :]
        b1hi[...], b1lo[...] = split(moved - mm(moved, *split(seen(0, omhi, omlo, chi, clo))))
        zhi[...], zlo[...] = split(seen(1, omhi, omlo, chi, clo))


def maps_kernel(
    after, omhi, omlo, info, chi, clo, pt, damping, zhi, zlo, old1, old2, old3, b1hi, b1lo, off, b2hi, b2lo
):
    span = here()[1]
    spans = lax.axis_size("z") * lax.axis_size("y")
    second = span == 1

    @pl.when(jnp.logical_not(second | (span == spans - 3) | (span == spans - 1)))
    def _():
        parts = ((b1hi, b1lo), (b2hi, b2lo))
        for day in range(2):
            moved = pt[...] * damping[day : day + 1, :]
            parts[day][0][...], parts[day][1][...] = split(
                moved - mm(moved, *split(seen(day, omhi, omlo, chi, clo)))
            )
            off[day : day + 1, :] = mv(info[day], chi[...], clo[...])

    @pl.when(second)
    def _():
        moved = pt[...] * damping[1:2, :]
        b2hi[...], b2lo[...] = split(moved - mm(moved, zhi[...], zlo[...]))


def second_kernel(acc, got, mine, b1hi, b1lo, off, zhi, zlo, pthi, ptlo, total, y):
    total[...] = acc[...] + got[...]
    y[...] = jnp.zeros(y.shape, F32)

    @pl.when(here()[1] == 1)
    def _():
        state = mv(acc[...] + got[...], b1hi[...], b1lo[...]) + off[0:1, :]
        moved = mv(state, pthi[...], ptlo[...]) * mine[1:2, :]
        y[...] = moved - mv(moved, zhi[...], zlo[...]) + off[1:2, :]


def both_kernel(after, b1hi, b1lo, b2hi, b2lo, off, bchi, bclo, offset):
    both = jnp.dot(b1hi[...], b2hi[...], preferred_element_type=F32) + (
        jnp.dot(b1lo[...], b2hi[...], preferred_element_type=F32)
        + jnp.dot(b1hi[...], b2lo[...], preferred_element_type=F32)
    )
    bchi[...], bclo[...] = split(both)
    offset[...] = mv(off[0:1, :], b2hi[...], b2lo[...]) + off[1:2, :]


def hop_kernel(after, acc, got, bchi, bclo, offset, total, y):
    state = acc[...] + got[...]
    total[...] = state
    y[...] = mv(state, bchi[...], bclo[...]) + offset[...]


def days_kernel(acc, got, b1hi, b1lo, b2hi, b2lo, off, total, y):
    state = acc[...] + got[...]
    total[...] = state
    state = mv(state, b1hi[...], b1lo[...]) + off[0:1, :]
    y[...] = mv(state, b2hi[...], b2lo[...]) + off[1:2, :]


def double_kernel(after, acc, got, bchi, bclo, offset, table, pthi, ptlo, zhi, zlo, off, total, y):
    spans = table.shape[0] // 2
    total[...] = acc[...] + got[...]
    y[...] = jnp.zeros(y.shape, F32)

    @pl.when(here()[1] == spans - 4)
    def _():
        state = mv(acc[...] + got[...], bchi[...], bclo[...]) + offset[...]
        for day in range(2):
            r = 2 * (spans - 3) + day
            state = next_day(day, state, table[r : r + 1, :], pthi, ptlo, zhi, zlo, off)
        y[...] = state


def whole_of(hi, lo):
    return hi[...].astype(F32) + lo[...].astype(F32)


def pairs_kernel(after, table, mthi, mtlo, khi, klo):
    spans = table.shape[0] // 2

    @pl.when(here()[1] == spans - 2)
    def _():
        @pl.loop(0, khi.shape[0])
        def _(k):
            scaled = whole_of(mthi, mtlo) * table[pl.ds(2 * (spans - 3 - k) + 1, 1), :]
            khi[k], klo[k] = split(mm(scaled, mthi[...], mtlo[...]))


def last_kernel(
    acc, got, b1hi, b1lo, b2hi, b2lo, bchi, bclo, off, offset, table, pthi, ptlo, mthi, mtlo,
    zhi, zlo, next_off, khi, klo, out, shares, means,
):
    span = here()[1]
    total, width = shares.shape
    spans = total // 2
    chunks = width // LANES
    twice = doubled(span, spans)
    shares[...] = jnp.zeros(shares.shape, F32)

    def step(k, v):
        t = 2 * span - 1 - k
        v = mv(v * table[pl.ds(t + 1, 1), :], mthi[...], mtlo[...])
        shares[pl.ds(t, 1), :] = v
        return v

    def own_days(rows, damped):
        both = jnp.concatenate(rows, 0)
        ahead = jnp.concatenate(damped, 0)
        const = both - few(few(both, pthi[...], ptlo[...]) * ahead * ahead, mthi[...], mtlo[...])
        n = len(rows)
        means[0:n, :] = both
        v = const[n - 1 : n]
        shares[pl.ds(2 * span + n - 1, 1), :] = v
        for i in range(n - 2, -1, -1):
            v = const[i : i + 1] + mv(v * damped[i], mthi[...], mtlo[...])
            shares[pl.ds(2 * span + i, 1), :] = v
        means[4:5, :] = v

    @pl.when(span < spans - 4)
    def _():
        state = acc[...] + got[...]
        one = mv(state, b1hi[...], b1lo[...]) + off[0:1, :]
        two = mv(one, b2hi[...], b2lo[...]) + off[1:2, :]
        own_days([one, two], [table[pl.ds(2 * span + 1 + i, 1), :] for i in range(2)])

    @pl.when(twice)
    def _():
        state = acc[...] + got[...]
        rows = [
            mv(state, b1hi[...], b1lo[...]) + off[0:1, :],
            mv(state, bchi[...], bclo[...]) + offset[...],
        ]
        for day in range(2):
            damping = table[pl.ds(2 * span + 2 + day, 1), :]
            rows.append(next_day(day, rows[-1], damping, pthi, ptlo, zhi, zlo, next_off))
        damped = [table[pl.ds(2 * span + 1 + i, 1), :] for i in range(3)]
        beyond = table[pl.ds(jnp.minimum(2 * span + 4, total - 1), 1), :]
        damped.append(beyond * jnp.where(span == spans - 2, 0.0, 1.0))
        own_days(rows, damped)

    @pl.when(span < spans - 2)
    def _():
        lax.fori_loop(0, jnp.where((span < spans - 4) | twice, 2 * span, 0), step, means[4:5, :])

    @pl.when(span == spans - 2)
    def _():
        v, damped_rows = means[4:5, :], []
        for k in range(khi.shape[0]):
            t = 2 * (spans - 2 - k)
            damped_rows.append(v * table[t : t + 1, :])
            v = mv(damped_rows[-1], khi[k], klo[k])
            shares[t - 2 : t - 1, :] = v
        batch = jnp.concatenate(damped_rows + [jnp.zeros((1, width), F32)] * (-len(damped_rows) % 8), 0)
        batch = mm(batch, mthi[...], mtlo[...])
        for k in range(khi.shape[0]):
            t = 2 * (spans - 2 - k)
            shares[t - 1 : t, :] = batch[k : k + 1]
        lax.fori_loop(2 * khi.shape[0], 2 * span, step, v)

    for c in range(spans):
        for q in range(chunks):
            out[c * chunks + q, 0:2, :] = shares[2 * c : 2 * c + 2, q * LANES : (q + 1) * LANES]
    for q in range(chunks):
        out[span * chunks + q, 2:4, :] = means[0:2, q * LANES : (q + 1) * LANES]

    @pl.when(twice)
    def _():
        for q in range(chunks):
            out[(span + 1) * chunks + q, 2:4, :] = means[2:4, q * LANES : (q + 1) * LANES]


def add_kernel(parts, filt, smooth):
    spans = parts.shape[0] // 4
    owners = [*range(spans - 4), spans - 4, spans - 2]
    filt[...] = parts[here()[4], 2:4, :]
    smooth[...] = sum(parts[owner_plane(c) * spans + (place(c) | 1), 0:2, :] for c in owners)


def local(
    records,
    obs_values,
    block_day,
    block_count,
    propagator_matrix,
    analysis_cov,
    unattenuated_multiplier,
    damping,
    prior_mean,
):
    planes, held, peers = (lax.axis_size(a) for a in ("z", "y", "obs"))
    spans = planes * held
    blocks = block_day.shape[0]
    slots = records.shape[0] // blocks
    width = records.shape[1]
    days = damping.shape[0]
    assert planes == peers == 4 and days == 2 and slots == LANES and blocks == spans
    everyone = ("z", "y", "obs")

    def owner(span):
        return owner_plane(span) * spans + (place(span) | 1)

    tiles = len(triangle(width))
    extra_rows = DAMP + 16 * held
    chunks = width // LANES
    full, row = (width, width), ((1, width), F32)
    sent = run(
        pack_kernel,
        [((blocks, chunks * slots + EXTRA, LANES), BF16)],
        [
            (x, HBM)
            for x in (
                block_day,
                block_count,
                records,
                obs_values.reshape(blocks, slots),
                prior_mean.reshape(1, -1),
                damping,
            )
        ],
        [
            pltpu.SMEM((blocks,), jnp.int32),
            pltpu.SMEM((blocks,), jnp.int32),
            pltpu.VMEM((blocks, slots), BF16),
            pltpu.VMEM((1, width // peers), F32),
            pltpu.VMEM((days, width), F32),
            pltpu.VMEM((blocks, slots, width), BF16),
            pltpu.VMEM((blocks, chunks * slots + EXTRA, LANES), BF16),
            pltpu.SemaphoreType.DMA((5 + 2 * blocks,)),
        ],
        limit=60,
        outs=HBM,
    )[0]
    got = lax.all_to_all(sent, ("y", "obs"), split_axis=0, concat_axis=0, tiled=True)
    span_slots = min(blocks, 8) * slots
    own, extra, pay, prior, gain = run(
        gram_kernel,
        [
            ((2 * tiles, LANES, LANES), F32),
            ((extra_rows, LANES), F32),
            (((2 * tiles - chunks) * LANES + extra_rows, LANES), BF16),
            row,
            (unattenuated_multiplier.shape, F32),
        ],
        [got, unattenuated_multiplier],
        [pltpu.VMEM((width, span_slots), BF16), pltpu.VMEM((16, span_slots), BF16)],
        flops=4 * width * width * blocks * slots,
    )
    def swap(x, bit):
        return lax.ppermute(x, "obs", [(i, i ^ bit) for i in range(peers)])

    def plane_sum(s):
        return lax.ppermute(
            pay, everyone, [((owner_plane(p) + s) % planes * spans + place(p), owner(p)) for p in range(spans)]
        )

    fourth = lax.ppermute(
        pay, everyone, [(spans + place(p), owner(p)) for p in range(spans) if place(p) % 2 == 0]
    )
    third, first, second = plane_sum(3), plane_sum(1), plane_sum(2)
    (gains,) = run(stack_kernel, [((2,) + gain.shape, F32)], [gain, swap(gain, 2)])
    mthi, mtlo = run(gain_kernel, [(full, BF16)] * 2, [gains, swap(gains, 1)])
    pt, pthi, ptlo, chi, clo, ahead = run(
        prep_kernel, [(full, F32)] + [(full, BF16)] * 4 + [row], [propagator_matrix, analysis_cov, prior]
    )
    smalls = pltpu.VMEM((planes + 1, extra_rows, LANES), F32)
    omhi, omlo, info, mine, acc, y = run(
        owner_kernel,
        [((days,) + full, BF16)] * 2 + [((days, 1, width), F32), ((days, width), F32), row, row],
        [
            own, extra, fourth, third, first, second, prior, ahead, pthi, ptlo, chi, clo, (mthi, ANY)
        ],
        [smalls],
    )
    (packed,) = run(
        relay_kernel,
        [(pay.shape, BF16)],
        [(y, ANY), own, extra, fourth, third, first, second],
        [smalls, pltpu.VMEM((extra_rows, LANES), F32)],
    )
    relay = lax.ppermute(
        packed, everyone, [(owner(p + 1), owner(p)) for p in (spans - 4, spans - 2)]
    )
    chain = [*range(spans - 3), spans - 2]
    half = [(full, BF16)] * 2
    for k, (source, target) in enumerate(zip(chain, chain[1:])):
        received = lax.ppermute(y, everyone, [(owner(source), owner(target))])
        if k == 0:
            given = [omhi, omlo, info, chi, clo, pt, mine]
            b1hi, b1lo, off, zhi, zlo = run(
                early_kernel, half + [((8, width), F32)] + half, [(y, ANY), *given], flops=18 * width**3
            )
            acc, y = run(
                second_kernel, [row, row], [acc, received, mine, b1hi, b1lo, off, zhi, zlo, pthi, ptlo]
            )
            b1hi, b1lo, off, b2hi, b2lo = run(
                maps_kernel,
                half + [((8, width), F32)] + half,
                [(y, ANY), *given, zhi, zlo, b1hi, b1lo, off],
                flops=24 * width**3,
                same={10: 0, 11: 1, 12: 2},
            )
        elif k == 1:
            acc, y = run(days_kernel, [row, row], [acc, received, b1hi, b1lo, b2hi, b2lo, off])
            bchi, bclo, offset = run(
                both_kernel, half + [row], [(y, ANY), b1hi, b1lo, b2hi, b2lo, off]
            )
            (table,) = run(
                table_kernel,
                [((spans * days, width), F32)],
                [(offset, ANY), extra, first, second, third],
                [smalls],
            )
            khi, klo = run(
                pairs_kernel, [((min(spans - 2, 4),) + full, BF16)] * 2, [(y, ANY), table, mthi, mtlo]
            )
        elif target == spans - 4:
            nexthi, nextlo, next_off = run(
                next_kernel,
                [((days,) + full, BF16)] * 2 + [((8, width), F32)],
                [(y, ANY), relay, chi, clo],
                [pltpu.VMEM(full, F32), pltpu.VMEM((extra_rows, LANES), F32)],
            )
            acc, y = run(
                double_kernel,
                [row, row],
                [
                    (nexthi, ANY), acc, received, bchi, bclo, offset, table, pthi, ptlo, nexthi, nextlo, next_off
                ],
            )
        elif target != spans - 2:
            acc, y = run(hop_kernel, [row, row], [(khi, ANY), acc, received, bchi, bclo, offset])
    (answer,) = run(
        last_kernel,
        [((spans * peers, 8, LANES), F32)],
        [
            acc, received, b1hi, b1lo, b2hi, b2lo, bchi, bclo, off, offset, table, pthi, ptlo, mthi, mtlo,
            nexthi, nextlo, next_off, khi, klo,
        ],
        [pltpu.VMEM((spans * days, width), F32), pltpu.VMEM((8, width), F32)],
    )
    parts = lax.all_to_all(answer, everyone, split_axis=0, concat_axis=0, tiled=True)
    out = ((days, LANES), F32)
    return run(add_kernel, [out, out], [parts])


def solution(mesh):
    spans, peers = mesh.devices.shape
    finer = jax.sharding.Mesh(mesh.devices.reshape(peers, spans // peers, peers), ("z", "y", "obs"))
    tm = ("z", "y")
    mapped = jax.shard_map(
        local,
        mesh=finer,
        in_specs=(
            P(("z", "y", "obs"), None),
            P(("z", "y", "obs")),
            P(("z", "y", "obs")),
            P(("z", "y", "obs")),
            P(),
            P(),
            P("obs", None),
            P(tm, None),
            P("obs"),
        ),
        out_specs=(P(tm, "obs"), P(tm, "obs")),
        check_vma=False,
    )
    return lambda *args: tuple(mapped(*args))
```

```python
import functools

import jax
import jax.numpy as jnp
from jax import lax
from jax.experimental import pallas as pl
from jax.experimental.pallas import tpu as pltpu
from jax.sharding import PartitionSpec as P

LANES = 128
F32, BF16 = jnp.float32, jnp.bfloat16
VMEM = pl.BlockSpec(memory_space=pltpu.VMEM)
SMEM = pl.BlockSpec(memory_space=pltpu.SMEM)
ANY = pl.BlockSpec(memory_space=pl.ANY)
HBM = pl.BlockSpec(memory_space=pltpu.HBM)


def run(body, out, ins, scratch=(), limit=16, flops=0, outs=VMEM, same=None):
    specs = [x[1] if isinstance(x, tuple) else VMEM for x in ins]
    arrays = [x[0] if isinstance(x, tuple) else x for x in ins]
    moved = sum(a.size * a.dtype.itemsize for a in arrays)
    return pl.pallas_call(
        body,
        out_shape=[jax.ShapeDtypeStruct(s, d) for s, d in out],
        in_specs=specs,
        out_specs=[outs] * len(out),
        scratch_shapes=list(scratch),
        input_output_aliases=same or {},
        compiler_params=pltpu.CompilerParams(vmem_limit_bytes=limit * 1024 * 1024),
        cost_estimate=pl.CostEstimate(flops=flops, bytes_accessed=moved, transcendentals=0),
    )(*arrays)


def here():
    z, y, o = (lax.axis_index(a) for a in ("z", "y", "obs"))
    held, peers = lax.axis_size("y"), lax.axis_size("obs")
    spans = held * peers
    at = y * peers + o
    seat = jnp.where(z == 1, at - lax.rem(at, 2), at)
    span = seat
    for bit in range(1, spans.bit_length()):
        span = span ^ (seat >> bit)
    c = z * held + y
    kept = jnp.where((c == spans - 3) | (c == spans - 1), c - 1, c)
    seat = kept ^ (kept >> 1)
    return z, span, o, c, (1 + (seat & 1)) * spans + (seat | 1), held


def doubled(span, spans):
    return (span == spans - 4) | (span == spans - 2)


def triangle(width):
    parts = width // LANES
    return [(i, j) for i in range(parts) for j in range(i + 1)]


def split(x):
    hi = x.astype(BF16)
    return hi, (x - hi.astype(F32)).astype(BF16)


def mm(x, hi, lo):
    xhi, xlo = split(x)
    dot = functools.partial(jnp.dot, preferred_element_type=F32)
    return dot(xhi, hi) + (dot(xlo, hi) + dot(xhi, lo))


def mv(x, hi, lo):
    wide = jnp.broadcast_to(x, (8, x.shape[1]))
    row = lax.broadcasted_iota(jnp.int32, wide.shape, 0)
    top = wide.astype(BF16).astype(F32)
    both = jnp.where(row == 0, top, jnp.where(row == 1, wide - top, 0.0)).astype(BF16)
    first = jnp.dot(both, hi, preferred_element_type=F32)
    second = jnp.dot(both, lo, preferred_element_type=F32)
    return first[0:1] + (first[1:2] + second[0:1])


def parts(x):
    top = x.astype(BF16).astype(F32)
    return [top, (x - top).astype(BF16).astype(F32)]


def place(span):
    return span ^ (span >> 1)


def owner_plane(span):
    return 1 + place(span) % 2


EXTRA = 8
DIAG, DAMP = 16, 32


def pack_kernel(
    day, count, rows, values, prior, damping, out, day_s, count_s, values_v, prior_v, damping_v, rows_v, stage, sems
):
    blocks = out.shape[0]
    slots = rows_v.shape[1]
    chunks = rows_v.shape[2] // LANES
    small = [(day, day_s), (count, count_s), (values, values_v), (prior, prior_v), (damping, damping_v)]
    copies = [pltpu.make_async_copy(src, dst, sems.at[n]) for n, (src, dst) in enumerate(small)]
    large = [
        pltpu.make_async_copy(rows.at[pl.ds(k * slots, slots)], rows_v.at[k], sems.at[len(small) + k])
        for k in range(blocks)
    ]
    sends = [
        pltpu.make_async_copy(stage.at[place(k)], out.at[place(k)], sems.at[len(small) + blocks + k])
        for k in range(blocks)
    ]
    for copy in copies + large:
        copy.start()
    for copy in copies:
        copy.wait()
    mine = damping_v[:, 0:LANES]
    for q in range(1, chunks):
        mine = jnp.where(lax.axis_index("obs") == q, damping_v[:, q * LANES : (q + 1) * LANES], mine)
    below = parts(prior_v[...]) + parts(mine)
    below = jnp.concatenate(below, 0)
    held = values_v[...].astype(F32)
    lane = lax.broadcasted_iota(jnp.int32, (1, LANES), 1)
    for k in range(blocks):
        marks = jnp.where(lane < LANES // 2, day_s[k], count_s[k]).astype(F32)
        stage[place(k), chunks * slots : chunks * slots + EXTRA, :] = jnp.concatenate(
            [held[k : k + 1, :], marks, below], 0
        ).astype(BF16)
    for k in range(blocks):
        large[k].wait()
        for j in range(chunks):
            stage[place(k), j * slots : (j + 1) * slots, :] = rows_v[k, :, j * LANES : (j + 1) * LANES]
        sends[k].start()
    for copy in sends:
        copy.wait()


def gram_kernel(got, gain, own, extra, pay, prior, gain_out, turned, marks):
    blocks = got.shape[0]
    chunks = turned.shape[0] // LANES
    slots = (got.shape[1] - EXTRA) // chunks
    width = chunks * LANES
    tiles = triangle(width)
    group = min(blocks, 8)
    half = 2 * LANES
    gain_out[...] = gain[...]
    extra[...] = jnp.zeros(extra.shape, F32)

    def below(k):
        return got[k, chunks * slots : chunks * slots + EXTRA, :].astype(F32)

    def one(first, fresh):
        for k in range(group):
            at = slice(k * slots, (k + 1) * slots)
            line = below(first + k)
            slot = lax.broadcasted_iota(jnp.int32, (1, slots), 1).astype(F32)
            valid = slot < jnp.broadcast_to(line[1:2, LANES - 1 : LANES], (1, slots))
            day = jnp.broadcast_to(line[1:2, 0:1], (1, slots))
            kept = [jnp.where(valid & (day == d), 1.0, 0.0) for d in (0.0, 1.0)]
            marks[:, at] = jnp.concatenate(
                kept + [kept[0] * line[0:1], kept[1] * line[0:1], jnp.zeros((12, slots), F32)], 0
            ).astype(BF16)
            for j in range(chunks):
                turned[j * LANES : (j + 1) * LANES, at] = got[first + k, j * slots : (j + 1) * slots, :].T
        source = jnp.concatenate(
            [
                jnp.concatenate([got[first + k, j * slots : (j + 1) * slots, :] for j in range(chunks)], 1)
                for k in range(group)
            ],
            0,
        )
        info = jnp.dot(marks[...], source, preferred_element_type=F32)
        for d in range(2):
            for top in range(0, width, half):
                left = turned[top : top + half, :] * marks[d : d + 1, :]
                block = jnp.dot(left, source[:, : top + half], preferred_element_type=F32)
                for n, (i, j) in enumerate(tiles):
                    if top <= i * LANES < top + half:
                        r = i * LANES - top
                        piece = block[r : r + LANES, j * LANES : (j + 1) * LANES]
                        at = d * len(tiles) + n
                        own[at] = piece if fresh else own[at] + piece
            for j in range(chunks):
                piece = info[2 + d : 3 + d, j * LANES : (j + 1) * LANES]
                r = 8 * d + j
                extra[r : r + 1, :] = piece if fresh else extra[r : r + 1, :] + piece

    if blocks == group:
        one(0, True)
    else:
        own[...] = jnp.zeros(own.shape, F32)

        @pl.loop(0, blocks // group)
        def _(g):
            one(g * group, False)

    row = lax.broadcasted_iota(jnp.int32, (LANES, LANES), 0)
    column = lax.broadcasted_iota(jnp.int32, (LANES, LANES), 1)
    sides = [n for n, (i, j) in enumerate(tiles) if i != j]
    middles = [n for n, (i, j) in enumerate(tiles) if i == j]

    def send(n, piece):
        pay[n * LANES : (n + 1) * LANES, :] = piece.astype(BF16)

    for d in range(2):
        for part, piece in enumerate(parts(extra[8 * d : 8 * d + chunks, :])):
            extra[8 * d + 4 * part : 8 * d + 4 * part + chunks, :] = piece
        for m, n in enumerate(sides):
            send(d * len(sides) + m, own[d * len(tiles) + n])
    for i, n in enumerate(middles):
        squares = [own[d * len(tiles) + n] for d in range(2)]
        send(2 * len(sides) + i, jnp.where(row >= column, squares[0], squares[1]))
        for d in range(2):
            line = jnp.sum(jnp.where(row == column, squares[d], 0.0), axis=0, keepdims=True)
            for part, piece in enumerate(parts(line)):
                r = DIAG + 8 * d + 4 * part + i
                extra[r : r + 1, :] = piece
    for q in range(chunks):
        line = below(q)
        prior[:, q * LANES : (q + 1) * LANES] = line[2:3] + line[3:4]
    for y in range(blocks // 4):
        for q in range(chunks):
            line = below(4 * y + q)
            for part in range(2):
                for d in range(2):
                    r = DAMP + 16 * y + 8 * d + 4 * part + q
                    extra[r : r + 1, :] = line[4 + 2 * part + d : 5 + 2 * part + d]
    pay[pay.shape[0] - extra.shape[0] :, :] = extra[...].astype(BF16)


def prep_kernel(trans, cov, prior, pt, pthi, ptlo, chi, clo, ahead):
    whole = trans[...].T
    pt[...] = whole
    pthi[...], ptlo[...] = split(whole)
    chi[...], clo[...] = split(cov[...])
    ahead[...] = mv(prior[...], pthi[...], ptlo[...])


def stack_kernel(one, two, out):
    out[0] = one[...]
    out[1] = two[...]


def gain_kernel(held, got, mthi, mtlo):
    ids = here()
    rows = held.shape[1]
    for step, part in enumerate((held.at[0], got.at[0], held.at[1], got.at[1])):
        holder = ids[2] ^ step
        at = pl.ds(pl.multiple_of(holder * rows, rows), rows)
        hi, lo = split(part[...].T)
        mthi[:, at] = hi
        mtlo[:, at] = lo


def few(x, hi, lo):
    n = x.shape[0]
    top = x.astype(BF16).astype(F32)
    blank = [jnp.zeros((8 - 2 * n, x.shape[1]), F32)] if n < 4 else []
    both = jnp.concatenate([top, x - top] + blank, 0).astype(BF16)
    first = jnp.dot(both, hi, preferred_element_type=F32)
    second = jnp.dot(both, lo, preferred_element_type=F32)
    return first[0:n] + (first[n : 2 * n] + second[0:n])


def one_day(day, ahead, damping, omhi, omlo, info, chi, clo):
    moved = ahead * damping[day : day + 1, :]
    gap = mv(moved, omhi[day], omlo[day]) - info[day]
    return moved - mv(gap, chi[...], clo[...])


def spread(extra, got, small):
    small[0] = extra[...]
    for s, part in enumerate(got):
        small[s + 1] = part[part.shape[0] - extra.shape[0] :, :].astype(F32)


def line_of(small, s, first):
    return small[s, first : first + 1, :] + small[s, first + 4 : first + 5, :]


def table_kernel(after, extra, g1, g2, g3, table, small):
    ids = here()
    planes = 4
    chunks = table.shape[1] // LANES
    held = table.shape[0] // 2 // planes
    spread(extra, (g1, g2, g3), small)
    for s in range(planes):
        plane = lax.rem(ids[0] + s, planes)
        for k in range(held):
            for day in range(2):
                table[pl.ds(2 * (plane * held + k) + day, 1), :] = jnp.concatenate(
                    [line_of(small, s, DAMP + 16 * k + 8 * day + j) for j in range(chunks)], 1
                )


def sums(extra, got, small):
    share = jnp.where(here()[0] == 2, 1.0, 0.0)
    spread(extra, got, small)

    def summed(first):
        others = line_of(small, 1, first) + line_of(small, 2, first) + (line_of(small, 3, first) + line_of(small, 4, first))
        return line_of(small, 0, first) * share + others

    def added(n):
        at = slice(n * LANES, (n + 1) * LANES)
        one, two, three, four = (part[at].astype(F32) for part in got)
        return (one + two) + (three + four)

    return share, summed, added


def relay_kernel(after, own, extra, g4, g3, g1, g2, out, small, rows):
    span = here()[1]
    spans = lax.axis_size("z") * lax.axis_size("y")
    chunks = 4
    tiles = triangle(chunks * LANES)
    row = lax.broadcasted_iota(jnp.int32, (LANES, LANES), 0)
    column = lax.broadcasted_iota(jnp.int32, (LANES, LANES), 1)
    sides = [n for n, (i, j) in enumerate(tiles) if i != j]
    middles = [n for n, (i, j) in enumerate(tiles) if i == j]

    @pl.when((span == spans - 3) | (span == spans - 1))
    def _():
        share, summed, added = sums(extra, (g1, g2, g3, g4), small)

        def send(n, piece):
            out[n * LANES : (n + 1) * LANES, :] = (piece * share + added(n)).astype(BF16)

        for d in range(2):
            for m, n in enumerate(sides):
                send(d * len(sides) + m, own[d * len(tiles) + n])
        for i, n in enumerate(middles):
            send(2 * len(sides) + i, jnp.where(row >= column, own[n], own[len(tiles) + n]))
        rows[...] = jnp.zeros(rows.shape, F32)
        for first in (0, 8, DIAG, DIAG + 8):
            for j in range(chunks):
                for part, piece in enumerate(parts(summed(first + j))):
                    r = first + 4 * part + j
                    rows[r : r + 1, :] = piece
        out[out.shape[0] - rows.shape[0] :, :] = rows[...].astype(BF16)


def next_kernel(after, relay, chi, clo, zhi, zlo, off, whole, rows):
    spans = lax.axis_size("z") * lax.axis_size("y")
    width = whole.shape[0]
    chunks = width // LANES
    tiles = triangle(width)
    row = lax.broadcasted_iota(jnp.int32, (LANES, LANES), 0)
    column = lax.broadcasted_iota(jnp.int32, (LANES, LANES), 1)
    sides = [(i, j) for i, j in tiles if i != j]

    @pl.when(doubled(here()[1], spans))
    def _():
        rows[...] = relay[relay.shape[0] - rows.shape[0] :, :].astype(F32)

        def line(r):
            return rows[r : r + 1, :] + rows[r + 4 : r + 5, :]

        def tile(n):
            return relay[n * LANES : (n + 1) * LANES, :].astype(F32)

        def put(i, j, piece):
            whole[i * LANES : (i + 1) * LANES, j * LANES : (j + 1) * LANES] = piece

        for day in range(2):
            for i in range(chunks):
                both = tile(2 * len(sides) + i)
                part = jnp.where(row < column if day else row > column, both, 0.0)
                put(i, i, part + part.T + jnp.where(row == column, line(DIAG + 8 * day + i), 0.0))
            for m, (i, j) in enumerate(sides):
                piece = tile(day * len(sides) + m)
                put(i, j, piece)
                put(j, i, piece.T)
            zhi[day], zlo[day] = split(mm(whole[...], chi[...], clo[...]))
            info = jnp.concatenate([line(8 * day + j) for j in range(chunks)], 1)
            off[day : day + 1, :] = mv(info, chi[...], clo[...])


def next_day(day, state, damping, pthi, ptlo, zhi, zlo, off):
    moved = mv(state, pthi[...], ptlo[...]) * damping
    return moved - mv(moved, zhi[day], zlo[day]) + off[day : day + 1, :]


def owner_kernel(
    own, extra, g4, g2, g1, g3, prior, ahead, pthi, ptlo, chi, clo, after, omhi, omlo, info, mine, start, y, small
):
    ids = here()
    planes = 4
    width = pthi.shape[0]
    chunks = width // LANES
    tiles = triangle(width)
    got = (g1, g2, g3, g4)
    row = lax.broadcasted_iota(jnp.int32, (LANES, LANES), 0)
    column = lax.broadcasted_iota(jnp.int32, (LANES, LANES), 1)
    share, summed, added = sums(extra, got, small)

    def put(day, i, j, piece):
        hi, lo = split(piece)
        omhi[day, i * LANES : (i + 1) * LANES, j * LANES : (j + 1) * LANES] = hi
        omlo[day, i * LANES : (i + 1) * LANES, j * LANES : (j + 1) * LANES] = lo

    sides = [n for n, (i, j) in enumerate(tiles) if i != j]
    middles = [n for n, (i, j) in enumerate(tiles) if i == j]

    def unpack(day):
        for i, n in enumerate(middles):
            both = added(2 * len(sides) + i)
            part = jnp.where(row < column if day else row > column, both, 0.0)
            others = sum(line_of(small, s, DIAG + 8 * day + i) for s in range(1, 5))
            piece = own[day * len(tiles) + n] * share + (part + part.T)
            put(day, i, i, piece + jnp.where(row == column, others, 0.0))
        for m, n in enumerate(sides):
            i, j = tiles[n]
            piece = own[day * len(tiles) + n] * share + added(day * len(sides) + m)
            put(day, i, j, piece)
            put(day, j, i, piece.T)

    for day in range(2):
        info[day] = jnp.concatenate([summed(8 * day + j) for j in range(chunks)], 1)
    held = ids[5]
    source = lax.rem(ids[1] // held - ids[0] + planes, planes)
    for day in range(2):
        for j in range(chunks):
            r = DAMP + 16 * lax.rem(ids[1], held) + 8 * day + j
            mine[day : day + 1, j * LANES : (j + 1) * LANES] = (
                small[source, pl.ds(r, 1), :] + small[source, pl.ds(r + 4, 1), :]
            )
    first = (ids[1] == 0) & (ids[0] == owner_plane(0))
    start[...] = jnp.where(first, prior[...], 0.0)

    @pl.when(first)
    def _():
        unpack(0)
        state = one_day(0, ahead[...], mine, omhi, omlo, info, chi, clo)
        unpack(1)
        y[...] = one_day(1, mv(state, pthi[...], ptlo[...]), mine, omhi, omlo, info, chi, clo)

    @pl.when(jnp.logical_not(first))
    def _():
        for day in range(2):
            unpack(day)
        y[...] = jnp.zeros(y.shape, F32)


def seen(day, omhi, omlo, chi, clo):
    return mm(omhi[day].astype(F32) + omlo[day].astype(F32), chi[...], clo[...])


def early_kernel(after, omhi, omlo, info, chi, clo, pt, damping, b1hi, b1lo, off, zhi, zlo):
    @pl.when(here()[1] == 1)
    def _():
        for day in range(2):
            off[day : day + 1, :] = mv(info[day], chi[...], clo[...])
        moved = pt[...] * damping[0:1, :]
        b1hi[...], b1lo[...] = split(moved - mm(moved, *split(seen(0, omhi, omlo, chi, clo))))
        zhi[...], zlo[...] = split(seen(1, omhi, omlo, chi, clo))


def maps_kernel(
    after, omhi, omlo, info, chi, clo, pt, damping, zhi, zlo, old1, old2, old3, b1hi, b1lo, off, b2hi, b2lo
):
    span = here()[1]
    spans = lax.axis_size("z") * lax.axis_size("y")
    second = span == 1

    @pl.when(jnp.logical_not(second | (span == spans - 3) | (span == spans - 1)))
    def _():
        parts = ((b1hi, b1lo), (b2hi, b2lo))
        for day in range(2):
            moved = pt[...] * damping[day : day + 1, :]
            parts[day][0][...], parts[day][1][...] = split(
                moved - mm(moved, *split(seen(day, omhi, omlo, chi, clo)))
            )
            off[day : day + 1, :] = mv(info[day], chi[...], clo[...])

    @pl.when(second)
    def _():
        moved = pt[...] * damping[1:2, :]
        b2hi[...], b2lo[...] = split(moved - mm(moved, zhi[...], zlo[...]))


def second_kernel(acc, got, mine, b1hi, b1lo, off, zhi, zlo, pthi, ptlo, total, y):
    total[...] = acc[...] + got[...]
    y[...] = jnp.zeros(y.shape, F32)

    @pl.when(here()[1] == 1)
    def _():
        state = mv(acc[...] + got[...], b1hi[...], b1lo[...]) + off[0:1, :]
        moved = mv(state, pthi[...], ptlo[...]) * mine[1:2, :]
        y[...] = moved - mv(moved, zhi[...], zlo[...]) + off[1:2, :]


def both_kernel(after, b1hi, b1lo, b2hi, b2lo, off, bchi, bclo, offset):
    both = jnp.dot(b1hi[...], b2hi[...], preferred_element_type=F32) + (
        jnp.dot(b1lo[...], b2hi[...], preferred_element_type=F32)
        + jnp.dot(b1hi[...], b2lo[...], preferred_element_type=F32)
    )
    bchi[...], bclo[...] = split(both)
    offset[...] = mv(off[0:1, :], b2hi[...], b2lo[...]) + off[1:2, :]


def hop_kernel(after, acc, got, bchi, bclo, offset, total, y):
    state = acc[...] + got[...]
    total[...] = state
    y[...] = mv(state, bchi[...], bclo[...]) + offset[...]


def days_kernel(acc, got, b1hi, b1lo, b2hi, b2lo, off, total, y):
    state = acc[...] + got[...]
    total[...] = state
    state = mv(state, b1hi[...], b1lo[...]) + off[0:1, :]
    y[...] = mv(state, b2hi[...], b2lo[...]) + off[1:2, :]


def double_kernel(after, acc, got, bchi, bclo, offset, table, pthi, ptlo, zhi, zlo, off, total, y):
    spans = table.shape[0] // 2
    total[...] = acc[...] + got[...]
    y[...] = jnp.zeros(y.shape, F32)

    @pl.when(here()[1] == spans - 4)
    def _():
        state = mv(acc[...] + got[...], bchi[...], bclo[...]) + offset[...]
        for day in range(2):
            r = 2 * (spans - 3) + day
            state = next_day(day, state, table[r : r + 1, :], pthi, ptlo, zhi, zlo, off)
        y[...] = state


def whole_of(hi, lo):
    return hi[...].astype(F32) + lo[...].astype(F32)


def pairs_kernel(after, table, mthi, mtlo, khi, klo):
    spans = table.shape[0] // 2

    @pl.when(here()[1] == spans - 2)
    def _():
        @pl.loop(0, khi.shape[0])
        def _(k):
            scaled = whole_of(mthi, mtlo) * table[pl.ds(2 * (spans - 3 - k) + 1, 1), :]
            khi[k], klo[k] = split(mm(scaled, mthi[...], mtlo[...]))


def last_kernel(
    acc, got, b1hi, b1lo, b2hi, b2lo, bchi, bclo, off, offset, table, pthi, ptlo, mthi, mtlo,
    zhi, zlo, next_off, khi, klo, out, shares, means,
):
    span = here()[1]
    total, width = shares.shape
    spans = total // 2
    chunks = width // LANES
    twice = doubled(span, spans)
    shares[...] = jnp.zeros(shares.shape, F32)

    def step(k, v):
        t = 2 * span - 1 - k
        v = mv(v * table[pl.ds(t + 1, 1), :], mthi[...], mtlo[...])
        shares[pl.ds(t, 1), :] = v
        return v

    def own_days(rows, damped):
        both = jnp.concatenate(rows, 0)
        ahead = jnp.concatenate(damped, 0)
        const = both - few(few(both, pthi[...], ptlo[...]) * ahead * ahead, mthi[...], mtlo[...])
        n = len(rows)
        means[0:n, :] = both
        v = const[n - 1 : n]
        shares[pl.ds(2 * span + n - 1, 1), :] = v
        for i in range(n - 2, -1, -1):
            v = const[i : i + 1] + mv(v * damped[i], mthi[...], mtlo[...])
            shares[pl.ds(2 * span + i, 1), :] = v
        means[4:5, :] = v

    @pl.when(span < spans - 4)
    def _():
        state = acc[...] + got[...]
        one = mv(state, b1hi[...], b1lo[...]) + off[0:1, :]
        two = mv(one, b2hi[...], b2lo[...]) + off[1:2, :]
        own_days([one, two], [table[pl.ds(2 * span + 1 + i, 1), :] for i in range(2)])

    @pl.when(twice)
    def _():
        state = acc[...] + got[...]
        rows = [
            mv(state, b1hi[...], b1lo[...]) + off[0:1, :],
            mv(state, bchi[...], bclo[...]) + offset[...],
        ]
        for day in range(2):
            damping = table[pl.ds(2 * span + 2 + day, 1), :]
            rows.append(next_day(day, rows[-1], damping, pthi, ptlo, zhi, zlo, next_off))
        damped = [table[pl.ds(2 * span + 1 + i, 1), :] for i in range(3)]
        beyond = table[pl.ds(jnp.minimum(2 * span + 4, total - 1), 1), :]
        damped.append(beyond * jnp.where(span == spans - 2, 0.0, 1.0))
        own_days(rows, damped)

    @pl.when(span < spans - 2)
    def _():
        lax.fori_loop(0, jnp.where((span < spans - 4) | twice, 2 * span, 0), step, means[4:5, :])

    @pl.when(span == spans - 2)
    def _():
        v, damped_rows = means[4:5, :], []
        for k in range(khi.shape[0]):
            t = 2 * (spans - 2 - k)
            damped_rows.append(v * table[t : t + 1, :])
            v = mv(damped_rows[-1], khi[k], klo[k])
            shares[t - 2 : t - 1, :] = v
        batch = jnp.concatenate(damped_rows + [jnp.zeros((1, width), F32)] * (-len(damped_rows) % 8), 0)
        batch = mm(batch, mthi[...], mtlo[...])
        for k in range(khi.shape[0]):
            t = 2 * (spans - 2 - k)
            shares[t - 1 : t, :] = batch[k : k + 1]
        lax.fori_loop(2 * khi.shape[0], 2 * span, step, v)

    for c in range(spans):
        for q in range(chunks):
            out[c * chunks + q, 0:2, :] = shares[2 * c : 2 * c + 2, q * LANES : (q + 1) * LANES]
    for q in range(chunks):
        out[span * chunks + q, 2:4, :] = means[0:2, q * LANES : (q + 1) * LANES]

    @pl.when(twice)
    def _():
        for q in range(chunks):
            out[(span + 1) * chunks + q, 2:4, :] = means[2:4, q * LANES : (q + 1) * LANES]


def add_kernel(parts, filt, smooth):
    spans = parts.shape[0] // 4
    owners = [*range(spans - 4), spans - 4, spans - 2]
    filt[...] = parts[here()[4], 2:4, :]
    smooth[...] = sum(parts[owner_plane(c) * spans + (place(c) | 1), 0:2, :] for c in owners)


def local(
    records,
    obs_values,
    block_day,
    block_count,
    propagator_matrix,
    analysis_cov,
    unattenuated_multiplier,
    damping,
    prior_mean,
):
    planes, held, peers = (lax.axis_size(a) for a in ("z", "y", "obs"))
    spans = planes * held
    blocks = block_day.shape[0]
    slots = records.shape[0] // blocks
    width = records.shape[1]
    days = damping.shape[0]
    assert planes == peers == 4 and days == 2 and slots == LANES and blocks == spans
    everyone = ("z", "y", "obs")

    def owner(span):
        return owner_plane(span) * spans + (place(span) | 1)

    tiles = len(triangle(width))
    extra_rows = DAMP + 16 * held
    chunks = width // LANES
    full, row = (width, width), ((1, width), F32)
    sent = run(
        pack_kernel,
        [((blocks, chunks * slots + EXTRA, LANES), BF16)],
        [
            (x, HBM)
            for x in (
                block_day,
                block_count,
                records,
                obs_values.reshape(blocks, slots),
                prior_mean.reshape(1, -1),
                damping,
            )
        ],
        [
            pltpu.SMEM((blocks,), jnp.int32),
            pltpu.SMEM((blocks,), jnp.int32),
            pltpu.VMEM((blocks, slots), BF16),
            pltpu.VMEM((1, width // peers), F32),
            pltpu.VMEM((days, width), F32),
            pltpu.VMEM((blocks, slots, width), BF16),
            pltpu.VMEM((blocks, chunks * slots + EXTRA, LANES), BF16),
            pltpu.SemaphoreType.DMA((5 + 2 * blocks,)),
        ],
        limit=60,
        outs=HBM,
    )[0]
    got = lax.all_to_all(sent, ("y", "obs"), split_axis=0, concat_axis=0, tiled=True)
    span_slots = min(blocks, 8) * slots
    own, extra, pay, prior, gain = run(
        gram_kernel,
        [
            ((2 * tiles, LANES, LANES), F32),
            ((extra_rows, LANES), F32),
            (((2 * tiles - chunks) * LANES + extra_rows, LANES), BF16),
            row,
            (unattenuated_multiplier.shape, F32),
        ],
        [got, unattenuated_multiplier],
        [pltpu.VMEM((width, span_slots), BF16), pltpu.VMEM((16, span_slots), BF16)],
        flops=4 * width * width * blocks * slots,
    )
    def swap(x, bit):
        return lax.ppermute(x, "obs", [(i, i ^ bit) for i in range(peers)])

    def plane_sum(s):
        return lax.ppermute(
            pay, everyone, [((owner_plane(p) + s) % planes * spans + place(p), owner(p)) for p in range(spans)]
        )

    fourth = lax.ppermute(
        pay, everyone, [(spans + place(p), owner(p)) for p in range(spans) if place(p) % 2 == 0]
    )
    second, first, third = plane_sum(2), plane_sum(1), plane_sum(3)
    (gains,) = run(stack_kernel, [((2,) + gain.shape, F32)], [gain, swap(gain, 2)])
    mthi, mtlo = run(gain_kernel, [(full, BF16)] * 2, [gains, swap(gains, 1)])
    pt, pthi, ptlo, chi, clo, ahead = run(
        prep_kernel, [(full, F32)] + [(full, BF16)] * 4 + [row], [propagator_matrix, analysis_cov, prior]
    )
    smalls = pltpu.VMEM((planes + 1, extra_rows, LANES), F32)
    omhi, omlo, info, mine, acc, y = run(
        owner_kernel,
        [((days,) + full, BF16)] * 2 + [((days, 1, width), F32), ((days, width), F32), row, row],
        [
            own, extra, fourth, second, first, third, prior, ahead, pthi, ptlo, chi, clo, (mthi, ANY)
        ],
        [smalls],
    )
    (packed,) = run(
        relay_kernel,
        [(pay.shape, BF16)],
        [(y, ANY), own, extra, fourth, third, first, second],
        [smalls, pltpu.VMEM((extra_rows, LANES), F32)],
    )
    relay = lax.ppermute(
        packed, everyone, [(owner(p + 1), owner(p)) for p in (spans - 4, spans - 2)]
    )
    chain = [*range(spans - 3), spans - 2]
    half = [(full, BF16)] * 2
    for k, (source, target) in enumerate(zip(chain, chain[1:])):
        received = lax.ppermute(y, everyone, [(owner(source), owner(target))])
        if k == 0:
            given = [omhi, omlo, info, chi, clo, pt, mine]
            b1hi, b1lo, off, zhi, zlo = run(
                early_kernel, half + [((8, width), F32)] + half, [(y, ANY), *given], flops=18 * width**3
            )
            acc, y = run(
                second_kernel, [row, row], [acc, received, mine, b1hi, b1lo, off, zhi, zlo, pthi, ptlo]
            )
            b1hi, b1lo, off, b2hi, b2lo = run(
                maps_kernel,
                half + [((8, width), F32)] + half,
                [(y, ANY), *given, zhi, zlo, b1hi, b1lo, off],
                flops=24 * width**3,
                same={10: 0, 11: 1, 12: 2},
            )
        elif k == 1:
            acc, y = run(days_kernel, [row, row], [acc, received, b1hi, b1lo, b2hi, b2lo, off])
            bchi, bclo, offset = run(
                both_kernel, half + [row], [(y, ANY), b1hi, b1lo, b2hi, b2lo, off]
            )
            (table,) = run(
                table_kernel,
                [((spans * days, width), F32)],
                [(offset, ANY), extra, first, second, third],
                [smalls],
            )
            khi, klo = run(
                pairs_kernel, [((min(spans - 2, 4),) + full, BF16)] * 2, [(y, ANY), table, mthi, mtlo]
            )
        elif target == spans - 4:
            nexthi, nextlo, next_off = run(
                next_kernel,
                [((days,) + full, BF16)] * 2 + [((8, width), F32)],
                [(y, ANY), relay, chi, clo],
                [pltpu.VMEM(full, F32), pltpu.VMEM((extra_rows, LANES), F32)],
            )
            acc, y = run(
                double_kernel,
                [row, row],
                [
                    (nexthi, ANY), acc, received, bchi, bclo, offset, table, pthi, ptlo, nexthi, nextlo, next_off
                ],
            )
        elif target != spans - 2:
            acc, y = run(hop_kernel, [row, row], [(khi, ANY), acc, received, bchi, bclo, offset])
    (answer,) = run(
        last_kernel,
        [((spans * peers, 8, LANES), F32)],
        [
            acc, received, b1hi, b1lo, b2hi, b2lo, bchi, bclo, off, offset, table, pthi, ptlo, mthi, mtlo,
            nexthi, nextlo, next_off, khi, klo,
        ],
        [pltpu.VMEM((spans * days, width), F32), pltpu.VMEM((8, width), F32)],
    )
    parts = lax.all_to_all(answer, everyone, split_axis=0, concat_axis=0, tiled=True)
    out = ((days, LANES), F32)
    return run(add_kernel, [out, out], [parts])


def solution(mesh):
    spans, peers = mesh.devices.shape
    finer = jax.sharding.Mesh(mesh.devices.reshape(peers, spans // peers, peers), ("z", "y", "obs"))
    tm = ("z", "y")
    mapped = jax.shard_map(
        local,
        mesh=finer,
        in_specs=(
            P(("z", "y", "obs"), None),
            P(("z", "y", "obs")),
            P(("z", "y", "obs")),
            P(("z", "y", "obs")),
            P(),
            P(),
            P("obs", None),
            P(tm, None),
            P("obs"),
        ),
        out_specs=(P(tm, "obs"), P(tm, "obs")),
        check_vma=False,
    )
    return lambda *args: tuple(mapped(*args))
```

```python
import functools

import jax
import jax.numpy as jnp
from jax import lax
from jax.experimental import pallas as pl
from jax.experimental.pallas import tpu as pltpu
from jax.sharding import PartitionSpec as P

LANES = 128
F32, BF16 = jnp.float32, jnp.bfloat16
VMEM = pl.BlockSpec(memory_space=pltpu.VMEM)
SMEM = pl.BlockSpec(memory_space=pltpu.SMEM)
ANY = pl.BlockSpec(memory_space=pl.ANY)
HBM = pl.BlockSpec(memory_space=pltpu.HBM)


def run(body, out, ins, scratch=(), limit=16, flops=0, outs=VMEM, same=None):
    specs = [x[1] if isinstance(x, tuple) else VMEM for x in ins]
    arrays = [x[0] if isinstance(x, tuple) else x for x in ins]
    moved = sum(a.size * a.dtype.itemsize for a in arrays)
    return pl.pallas_call(
        body,
        out_shape=[jax.ShapeDtypeStruct(s, d) for s, d in out],
        in_specs=specs,
        out_specs=[outs] * len(out),
        scratch_shapes=list(scratch),
        input_output_aliases=same or {},
        compiler_params=pltpu.CompilerParams(vmem_limit_bytes=limit * 1024 * 1024),
        cost_estimate=pl.CostEstimate(flops=flops, bytes_accessed=moved, transcendentals=0),
    )(*arrays)


def here():
    z, y, o = (lax.axis_index(a) for a in ("z", "y", "obs"))
    held, peers = lax.axis_size("y"), lax.axis_size("obs")
    spans = held * peers
    at = y * peers + o
    seat = jnp.where(z == 1, at - lax.rem(at, 2), at)
    span = seat
    for bit in range(1, spans.bit_length()):
        span = span ^ (seat >> bit)
    c = z * held + y
    kept = jnp.where((c == spans - 3) | (c == spans - 1), c - 1, c)
    seat = kept ^ (kept >> 1)
    return z, span, o, c, (1 + (seat & 1)) * spans + (seat | 1), held


def doubled(span, spans):
    return (span == spans - 4) | (span == spans - 2)


def triangle(width):
    parts = width // LANES
    return [(i, j) for i in range(parts) for j in range(i + 1)]


def split(x):
    hi = x.astype(BF16)
    return hi, (x - hi.astype(F32)).astype(BF16)


def mm(x, hi, lo):
    xhi, xlo = split(x)
    dot = functools.partial(jnp.dot, preferred_element_type=F32)
    return dot(xhi, hi) + (dot(xlo, hi) + dot(xhi, lo))


def mv(x, hi, lo):
    wide = jnp.broadcast_to(x, (8, x.shape[1]))
    row = lax.broadcasted_iota(jnp.int32, wide.shape, 0)
    top = wide.astype(BF16).astype(F32)
    both = jnp.where(row == 0, top, jnp.where(row == 1, wide - top, 0.0)).astype(BF16)
    first = jnp.dot(both, hi, preferred_element_type=F32)
    second = jnp.dot(both, lo, preferred_element_type=F32)
    return first[0:1] + (first[1:2] + second[0:1])


def parts(x):
    top = x.astype(BF16).astype(F32)
    return [top, (x - top).astype(BF16).astype(F32)]


def place(span):
    return span ^ (span >> 1)


def owner_plane(span):
    return 1 + place(span) % 2


EXTRA = 8
DIAG, DAMP = 16, 32


def pack_kernel(
    day, count, rows, values, prior, damping, out, day_s, count_s, values_v, prior_v, damping_v, rows_v, stage, sems
):
    blocks = out.shape[0]
    slots = rows_v.shape[1]
    chunks = rows_v.shape[2] // LANES
    small = [(day, day_s), (count, count_s), (values, values_v), (prior, prior_v), (damping, damping_v)]
    copies = [pltpu.make_async_copy(src, dst, sems.at[n]) for n, (src, dst) in enumerate(small)]
    large = [
        pltpu.make_async_copy(rows.at[pl.ds(k * slots, slots)], rows_v.at[k], sems.at[len(small) + k])
        for k in range(blocks)
    ]
    sends = [
        pltpu.make_async_copy(stage.at[place(k)], out.at[place(k)], sems.at[len(small) + blocks + k])
        for k in range(blocks)
    ]
    for copy in copies + large:
        copy.start()
    for copy in copies:
        copy.wait()
    mine = damping_v[:, 0:LANES]
    for q in range(1, chunks):
        mine = jnp.where(lax.axis_index("obs") == q, damping_v[:, q * LANES : (q + 1) * LANES], mine)
    below = parts(prior_v[...]) + parts(mine)
    below = jnp.concatenate(below, 0)
    held = values_v[...].astype(F32)
    lane = lax.broadcasted_iota(jnp.int32, (1, LANES), 1)
    for k in range(blocks):
        marks = jnp.where(lane < LANES // 2, day_s[k], count_s[k]).astype(F32)
        stage[place(k), chunks * slots : chunks * slots + EXTRA, :] = jnp.concatenate(
            [held[k : k + 1, :], marks, below], 0
        ).astype(BF16)
    for k in range(blocks):
        large[k].wait()
        for j in range(chunks):
            stage[place(k), j * slots : (j + 1) * slots, :] = rows_v[k, :, j * LANES : (j + 1) * LANES]
        sends[k].start()
    for copy in sends:
        copy.wait()


def gram_kernel(got, gain, own, extra, pay, prior, gain_out, turned, marks):
    blocks = got.shape[0]
    chunks = turned.shape[0] // LANES
    slots = (got.shape[1] - EXTRA) // chunks
    width = chunks * LANES
    tiles = triangle(width)
    group = min(blocks, 8)
    half = 2 * LANES
    gain_out[...] = gain[...]
    extra[...] = jnp.zeros(extra.shape, F32)

    def below(k):
        return got[k, chunks * slots : chunks * slots + EXTRA, :].astype(F32)

    def one(first, fresh):
        for k in range(group):
            at = slice(k * slots, (k + 1) * slots)
            line = below(first + k)
            slot = lax.broadcasted_iota(jnp.int32, (1, slots), 1).astype(F32)
            valid = slot < jnp.broadcast_to(line[1:2, LANES - 1 : LANES], (1, slots))
            day = jnp.broadcast_to(line[1:2, 0:1], (1, slots))
            kept = [jnp.where(valid & (day == d), 1.0, 0.0) for d in (0.0, 1.0)]
            marks[:, at] = jnp.concatenate(
                kept + [kept[0] * line[0:1], kept[1] * line[0:1], jnp.zeros((12, slots), F32)], 0
            ).astype(BF16)
            for j in range(chunks):
                turned[j * LANES : (j + 1) * LANES, at] = got[first + k, j * slots : (j + 1) * slots, :].T
        source = jnp.concatenate(
            [
                jnp.concatenate([got[first + k, j * slots : (j + 1) * slots, :] for j in range(chunks)], 1)
                for k in range(group)
            ],
            0,
        )
        info = jnp.dot(marks[...], source, preferred_element_type=F32)
        for d in range(2):
            for top in range(0, width, half):
                left = turned[top : top + half, :] * marks[d : d + 1, :]
                block = jnp.dot(left, source[:, : top + half], preferred_element_type=F32)
                for n, (i, j) in enumerate(tiles):
                    if top <= i * LANES < top + half:
                        r = i * LANES - top
                        piece = block[r : r + LANES, j * LANES : (j + 1) * LANES]
                        at = d * len(tiles) + n
                        own[at] = piece if fresh else own[at] + piece
            for j in range(chunks):
                piece = info[2 + d : 3 + d, j * LANES : (j + 1) * LANES]
                r = 8 * d + j
                extra[r : r + 1, :] = piece if fresh else extra[r : r + 1, :] + piece

    if blocks == group:
        one(0, True)
    else:
        own[...] = jnp.zeros(own.shape, F32)

        @pl.loop(0, blocks // group)
        def _(g):
            one(g * group, False)

    row = lax.broadcasted_iota(jnp.int32, (LANES, LANES), 0)
    column = lax.broadcasted_iota(jnp.int32, (LANES, LANES), 1)
    sides = [n for n, (i, j) in enumerate(tiles) if i != j]
    middles = [n for n, (i, j) in enumerate(tiles) if i == j]

    def send(n, piece):
        pay[n * LANES : (n + 1) * LANES, :] = piece.astype(BF16)

    for d in range(2):
        for part, piece in enumerate(parts(extra[8 * d : 8 * d + chunks, :])):
            extra[8 * d + 4 * part : 8 * d + 4 * part + chunks, :] = piece
        for m, n in enumerate(sides):
            send(d * len(sides) + m, own[d * len(tiles) + n])
    for i, n in enumerate(middles):
        squares = [own[d * len(tiles) + n] for d in range(2)]
        send(2 * len(sides) + i, jnp.where(row >= column, squares[0], squares[1]))
        for d in range(2):
            line = jnp.sum(jnp.where(row == column, squares[d], 0.0), axis=0, keepdims=True)
            for part, piece in enumerate(parts(line)):
                r = DIAG + 8 * d + 4 * part + i
                extra[r : r + 1, :] = piece
    for q in range(chunks):
        line = below(q)
        prior[:, q * LANES : (q + 1) * LANES] = line[2:3] + line[3:4]
    for y in range(blocks // 4):
        for q in range(chunks):
            line = below(4 * y + q)
            for part in range(2):
                for d in range(2):
                    r = DAMP + 16 * y + 8 * d + 4 * part + q
                    extra[r : r + 1, :] = line[4 + 2 * part + d : 5 + 2 * part + d]
    pay[pay.shape[0] - extra.shape[0] :, :] = extra[...].astype(BF16)


def prep_kernel(trans, cov, prior, pt, pthi, ptlo, chi, clo, ahead):
    whole = trans[...].T
    pt[...] = whole
    pthi[...], ptlo[...] = split(whole)
    chi[...], clo[...] = split(cov[...])
    ahead[...] = mv(prior[...], pthi[...], ptlo[...])


def stack_kernel(one, two, out):
    out[0] = one[...]
    out[1] = two[...]


def gain_kernel(held, got, mthi, mtlo):
    ids = here()
    rows = held.shape[1]
    for step, part in enumerate((held.at[0], got.at[0], held.at[1], got.at[1])):
        holder = ids[2] ^ step
        at = pl.ds(pl.multiple_of(holder * rows, rows), rows)
        hi, lo = split(part[...].T)
        mthi[:, at] = hi
        mtlo[:, at] = lo


def few(x, hi, lo):
    n = x.shape[0]
    top = x.astype(BF16).astype(F32)
    blank = [jnp.zeros((8 - 2 * n, x.shape[1]), F32)] if n < 4 else []
    both = jnp.concatenate([top, x - top] + blank, 0).astype(BF16)
    first = jnp.dot(both, hi, preferred_element_type=F32)
    second = jnp.dot(both, lo, preferred_element_type=F32)
    return first[0:n] + (first[n : 2 * n] + second[0:n])


def one_day(day, ahead, damping, omhi, omlo, info, chi, clo):
    moved = ahead * damping[day : day + 1, :]
    gap = mv(moved, omhi[day], omlo[day]) - info[day]
    return moved - mv(gap, chi[...], clo[...])


def spread(extra, got, small):
    small[0] = extra[...]
    for s, part in enumerate(got):
        small[s + 1] = part[part.shape[0] - extra.shape[0] :, :].astype(F32)


def line_of(small, s, first):
    return small[s, first : first + 1, :] + small[s, first + 4 : first + 5, :]


def table_kernel(after, extra, g1, g2, g3, table, small):
    ids = here()
    planes = 4
    chunks = table.shape[1] // LANES
    held = table.shape[0] // 2 // planes
    spread(extra, (g1, g2, g3), small)
    for s in range(planes):
        plane = lax.rem(ids[0] + s, planes)
        for k in range(held):
            for day in range(2):
                table[pl.ds(2 * (plane * held + k) + day, 1), :] = jnp.concatenate(
                    [line_of(small, s, DAMP + 16 * k + 8 * day + j) for j in range(chunks)], 1
                )


def sums(extra, got, small):
    share = jnp.where(here()[0] == 2, 1.0, 0.0)
    spread(extra, got, small)

    def summed(first):
        others = line_of(small, 1, first) + line_of(small, 2, first) + (line_of(small, 3, first) + line_of(small, 4, first))
        return line_of(small, 0, first) * share + others

    def added(n):
        at = slice(n * LANES, (n + 1) * LANES)
        one, two, three, four = (part[at].astype(F32) for part in got)
        return (one + two) + (three + four)

    return share, summed, added


def relay_kernel(after, own, extra, g4, g3, g1, g2, out, small, rows):
    span = here()[1]
    spans = lax.axis_size("z") * lax.axis_size("y")
    chunks = 4
    tiles = triangle(chunks * LANES)
    row = lax.broadcasted_iota(jnp.int32, (LANES, LANES), 0)
    column = lax.broadcasted_iota(jnp.int32, (LANES, LANES), 1)
    sides = [n for n, (i, j) in enumerate(tiles) if i != j]
    middles = [n for n, (i, j) in enumerate(tiles) if i == j]

    @pl.when((span == spans - 3) | (span == spans - 1))
    def _():
        share, summed, added = sums(extra, (g1, g2, g3, g4), small)

        def send(n, piece):
            out[n * LANES : (n + 1) * LANES, :] = (piece * share + added(n)).astype(BF16)

        for d in range(2):
            for m, n in enumerate(sides):
                send(d * len(sides) + m, own[d * len(tiles) + n])
        for i, n in enumerate(middles):
            send(2 * len(sides) + i, jnp.where(row >= column, own[n], own[len(tiles) + n]))
        rows[...] = jnp.zeros(rows.shape, F32)
        for first in (0, 8, DIAG, DIAG + 8):
            for j in range(chunks):
                for part, piece in enumerate(parts(summed(first + j))):
                    r = first + 4 * part + j
                    rows[r : r + 1, :] = piece
        out[out.shape[0] - rows.shape[0] :, :] = rows[...].astype(BF16)


def next_kernel(after, relay, chi, clo, zhi, zlo, off, whole, rows):
    spans = lax.axis_size("z") * lax.axis_size("y")
    width = whole.shape[0]
    chunks = width // LANES
    tiles = triangle(width)
    row = lax.broadcasted_iota(jnp.int32, (LANES, LANES), 0)
    column = lax.broadcasted_iota(jnp.int32, (LANES, LANES), 1)
    sides = [(i, j) for i, j in tiles if i != j]

    @pl.when(doubled(here()[1], spans))
    def _():
        rows[...] = relay[relay.shape[0] - rows.shape[0] :, :].astype(F32)

        def line(r):
            return rows[r : r + 1, :] + rows[r + 4 : r + 5, :]

        def tile(n):
            return relay[n * LANES : (n + 1) * LANES, :].astype(F32)

        def put(i, j, piece):
            whole[i * LANES : (i + 1) * LANES, j * LANES : (j + 1) * LANES] = piece

        for day in range(2):
            for i in range(chunks):
                both = tile(2 * len(sides) + i)
                part = jnp.where(row < column if day else row > column, both, 0.0)
                put(i, i, part + part.T + jnp.where(row == column, line(DIAG + 8 * day + i), 0.0))
            for m, (i, j) in enumerate(sides):
                piece = tile(day * len(sides) + m)
                put(i, j, piece)
                put(j, i, piece.T)
            zhi[day], zlo[day] = split(mm(whole[...], chi[...], clo[...]))
            info = jnp.concatenate([line(8 * day + j) for j in range(chunks)], 1)
            off[day : day + 1, :] = mv(info, chi[...], clo[...])


def next_day(day, state, damping, pthi, ptlo, zhi, zlo, off):
    moved = mv(state, pthi[...], ptlo[...]) * damping
    return moved - mv(moved, zhi[day], zlo[day]) + off[day : day + 1, :]


def owner_kernel(
    own, extra, g4, g3, g1, g2, prior, ahead, pthi, ptlo, chi, clo, after, omhi, omlo, info, mine, start, y, small
):
    ids = here()
    planes = 4
    width = pthi.shape[0]
    chunks = width // LANES
    tiles = triangle(width)
    got = (g1, g2, g3, g4)
    row = lax.broadcasted_iota(jnp.int32, (LANES, LANES), 0)
    column = lax.broadcasted_iota(jnp.int32, (LANES, LANES), 1)
    share, summed, added = sums(extra, got, small)

    def put(day, i, j, piece):
        hi, lo = split(piece)
        omhi[day, i * LANES : (i + 1) * LANES, j * LANES : (j + 1) * LANES] = hi
        omlo[day, i * LANES : (i + 1) * LANES, j * LANES : (j + 1) * LANES] = lo

    sides = [n for n, (i, j) in enumerate(tiles) if i != j]
    middles = [n for n, (i, j) in enumerate(tiles) if i == j]

    def unpack(day):
        for i, n in enumerate(middles):
            both = added(2 * len(sides) + i)
            part = jnp.where(row < column if day else row > column, both, 0.0)
            others = sum(line_of(small, s, DIAG + 8 * day + i) for s in range(1, 5))
            piece = own[day * len(tiles) + n] * share + (part + part.T)
            put(day, i, i, piece + jnp.where(row == column, others, 0.0))
        for m, n in enumerate(sides):
            i, j = tiles[n]
            piece = own[day * len(tiles) + n] * share + added(day * len(sides) + m)
            put(day, i, j, piece)
            put(day, j, i, piece.T)

    for day in range(2):
        info[day] = jnp.concatenate([summed(8 * day + j) for j in range(chunks)], 1)
    held = ids[5]
    source = lax.rem(ids[1] // held - ids[0] + planes, planes)
    for day in range(2):
        for j in range(chunks):
            r = DAMP + 16 * lax.rem(ids[1], held) + 8 * day + j
            mine[day : day + 1, j * LANES : (j + 1) * LANES] = (
                small[source, pl.ds(r, 1), :] + small[source, pl.ds(r + 4, 1), :]
            )
    first = (ids[1] == 0) & (ids[0] == owner_plane(0))
    start[...] = jnp.where(first, prior[...], 0.0)

    @pl.when(first)
    def _():
        unpack(0)
        state = one_day(0, ahead[...], mine, omhi, omlo, info, chi, clo)
        unpack(1)
        y[...] = one_day(1, mv(state, pthi[...], ptlo[...]), mine, omhi, omlo, info, chi, clo)

    @pl.when(jnp.logical_not(first))
    def _():
        for day in range(2):
            unpack(day)
        y[...] = jnp.zeros(y.shape, F32)


def seen(day, omhi, omlo, chi, clo):
    return mm(omhi[day].astype(F32) + omlo[day].astype(F32), chi[...], clo[...])


def early_kernel(after, omhi, omlo, info, chi, clo, pt, damping, b1hi, b1lo, off, zhi, zlo):
    @pl.when(here()[1] == 1)
    def _():
        for day in range(2):
            off[day : day + 1, :] = mv(info[day], chi[...], clo[...])
        moved = pt[...] * damping[0:1, :]
        b1hi[...], b1lo[...] = split(moved - mm(moved, *split(seen(0, omhi, omlo, chi, clo))))
        zhi[...], zlo[...] = split(seen(1, omhi, omlo, chi, clo))


def maps_kernel(
    after, omhi, omlo, info, chi, clo, pt, damping, zhi, zlo, old1, old2, old3, b1hi, b1lo, off, b2hi, b2lo
):
    span = here()[1]
    spans = lax.axis_size("z") * lax.axis_size("y")
    second = span == 1

    @pl.when(jnp.logical_not(second | (span == spans - 3) | (span == spans - 1)))
    def _():
        parts = ((b1hi, b1lo), (b2hi, b2lo))
        for day in range(2):
            moved = pt[...] * damping[day : day + 1, :]
            parts[day][0][...], parts[day][1][...] = split(
                moved - mm(moved, *split(seen(day, omhi, omlo, chi, clo)))
            )
            off[day : day + 1, :] = mv(info[day], chi[...], clo[...])

    @pl.when(second)
    def _():
        moved = pt[...] * damping[1:2, :]
        b2hi[...], b2lo[...] = split(moved - mm(moved, zhi[...], zlo[...]))


def second_kernel(acc, got, mine, b1hi, b1lo, off, zhi, zlo, pthi, ptlo, total, y):
    total[...] = acc[...] + got[...]
    y[...] = jnp.zeros(y.shape, F32)

    @pl.when(here()[1] == 1)
    def _():
        state = mv(acc[...] + got[...], b1hi[...], b1lo[...]) + off[0:1, :]
        moved = mv(state, pthi[...], ptlo[...]) * mine[1:2, :]
        y[...] = moved - mv(moved, zhi[...], zlo[...]) + off[1:2, :]


def both_kernel(after, b1hi, b1lo, b2hi, b2lo, off, bchi, bclo, offset):
    both = jnp.dot(b1hi[...], b2hi[...], preferred_element_type=F32) + (
        jnp.dot(b1lo[...], b2hi[...], preferred_element_type=F32)
        + jnp.dot(b1hi[...], b2lo[...], preferred_element_type=F32)
    )
    bchi[...], bclo[...] = split(both)
    offset[...] = mv(off[0:1, :], b2hi[...], b2lo[...]) + off[1:2, :]


def hop_kernel(after, acc, got, bchi, bclo, offset, total, y):
    state = acc[...] + got[...]
    total[...] = state
    y[...] = mv(state, bchi[...], bclo[...]) + offset[...]


def days_kernel(acc, got, b1hi, b1lo, b2hi, b2lo, off, total, y):
    state = acc[...] + got[...]
    total[...] = state
    state = mv(state, b1hi[...], b1lo[...]) + off[0:1, :]
    y[...] = mv(state, b2hi[...], b2lo[...]) + off[1:2, :]


def double_kernel(after, acc, got, bchi, bclo, offset, table, pthi, ptlo, zhi, zlo, off, total, y):
    spans = table.shape[0] // 2
    total[...] = acc[...] + got[...]
    y[...] = jnp.zeros(y.shape, F32)

    @pl.when(here()[1] == spans - 4)
    def _():
        state = mv(acc[...] + got[...], bchi[...], bclo[...]) + offset[...]
        for day in range(2):
            r = 2 * (spans - 3) + day
            state = next_day(day, state, table[r : r + 1, :], pthi, ptlo, zhi, zlo, off)
        y[...] = state


def whole_of(hi, lo):
    return hi[...].astype(F32) + lo[...].astype(F32)


def pairs_kernel(skip, after, table, mthi, mtlo, khi, klo):
    spans = table.shape[0] // 2

    @pl.when(here()[1] == spans - 2)
    def _():
        @pl.loop(0, khi.shape[0])
        def _(k):
            scaled = whole_of(mthi, mtlo) * table[pl.ds(2 * (spans - 3 - skip - k) + 1, 1), :]
            khi[k], klo[k] = split(mm(scaled, mthi[...], mtlo[...]))


def last_kernel(
    acc, got, b1hi, b1lo, b2hi, b2lo, bchi, bclo, off, offset, table, pthi, ptlo, mthi, mtlo,
    zhi, zlo, next_off, khi, klo, more_khi, more_klo, out, shares, means,
):
    span = here()[1]
    total, width = shares.shape
    spans = total // 2
    chunks = width // LANES
    twice = doubled(span, spans)
    shares[...] = jnp.zeros(shares.shape, F32)

    def step(k, v):
        t = 2 * span - 1 - k
        v = mv(v * table[pl.ds(t + 1, 1), :], mthi[...], mtlo[...])
        shares[pl.ds(t, 1), :] = v
        return v

    def own_days(rows, damped):
        both = jnp.concatenate(rows, 0)
        ahead = jnp.concatenate(damped, 0)
        const = both - few(few(both, pthi[...], ptlo[...]) * ahead * ahead, mthi[...], mtlo[...])
        n = len(rows)
        means[0:n, :] = both
        v = const[n - 1 : n]
        shares[pl.ds(2 * span + n - 1, 1), :] = v
        for i in range(n - 2, -1, -1):
            v = const[i : i + 1] + mv(v * damped[i], mthi[...], mtlo[...])
            shares[pl.ds(2 * span + i, 1), :] = v
        means[4:5, :] = v

    @pl.when(span < spans - 4)
    def _():
        state = acc[...] + got[...]
        one = mv(state, b1hi[...], b1lo[...]) + off[0:1, :]
        two = mv(one, b2hi[...], b2lo[...]) + off[1:2, :]
        own_days([one, two], [table[pl.ds(2 * span + 1 + i, 1), :] for i in range(2)])

    @pl.when(twice)
    def _():
        state = acc[...] + got[...]
        rows = [
            mv(state, b1hi[...], b1lo[...]) + off[0:1, :],
            mv(state, bchi[...], bclo[...]) + offset[...],
        ]
        for day in range(2):
            damping = table[pl.ds(2 * span + 2 + day, 1), :]
            rows.append(next_day(day, rows[-1], damping, pthi, ptlo, zhi, zlo, next_off))
        damped = [table[pl.ds(2 * span + 1 + i, 1), :] for i in range(3)]
        beyond = table[pl.ds(jnp.minimum(2 * span + 4, total - 1), 1), :]
        damped.append(beyond * jnp.where(span == spans - 2, 0.0, 1.0))
        own_days(rows, damped)

    @pl.when(span < spans - 2)
    def _():
        lax.fori_loop(0, jnp.where((span < spans - 4) | twice, 2 * span, 0), step, means[4:5, :])

    @pl.when(span == spans - 2)
    def _():
        v, damped_rows = means[4:5, :], []
        pairs = [(a, b, k) for a, b in ((khi, klo), (more_khi, more_klo)) for k in range(a.shape[0])]
        for n, (a, b, k) in enumerate(pairs):
            t = 2 * (spans - 2 - n)
            damped_rows.append(v * table[t : t + 1, :])
            v = mv(damped_rows[-1], a[k], b[k])
            shares[t - 2 : t - 1, :] = v
        batch = jnp.concatenate(damped_rows + [jnp.zeros((1, width), F32)] * (-len(damped_rows) % 8), 0)
        batch = mm(batch, mthi[...], mtlo[...])
        for n in range(len(pairs)):
            t = 2 * (spans - 2 - n)
            shares[t - 1 : t, :] = batch[n : n + 1]
        lax.fori_loop(2 * len(pairs), 2 * span, step, v)

    for c in range(spans):
        for q in range(chunks):
            out[c * chunks + q, 0:2, :] = shares[2 * c : 2 * c + 2, q * LANES : (q + 1) * LANES]
    for q in range(chunks):
        out[span * chunks + q, 2:4, :] = means[0:2, q * LANES : (q + 1) * LANES]

    @pl.when(twice)
    def _():
        for q in range(chunks):
            out[(span + 1) * chunks + q, 2:4, :] = means[2:4, q * LANES : (q + 1) * LANES]


def add_kernel(parts, filt, smooth):
    spans = parts.shape[0] // 4
    owners = [*range(spans - 4), spans - 4, spans - 2]
    filt[...] = parts[here()[4], 2:4, :]
    smooth[...] = sum(parts[owner_plane(c) * spans + (place(c) | 1), 0:2, :] for c in owners)


def local(
    records,
    obs_values,
    block_day,
    block_count,
    propagator_matrix,
    analysis_cov,
    unattenuated_multiplier,
    damping,
    prior_mean,
):
    planes, held, peers = (lax.axis_size(a) for a in ("z", "y", "obs"))
    spans = planes * held
    blocks = block_day.shape[0]
    slots = records.shape[0] // blocks
    width = records.shape[1]
    days = damping.shape[0]
    assert planes == peers == 4 and days == 2 and slots == LANES and blocks == spans
    everyone = ("z", "y", "obs")

    def owner(span):
        return owner_plane(span) * spans + (place(span) | 1)

    tiles = len(triangle(width))
    extra_rows = DAMP + 16 * held
    chunks = width // LANES
    full, row = (width, width), ((1, width), F32)
    sent = run(
        pack_kernel,
        [((blocks, chunks * slots + EXTRA, LANES), BF16)],
        [
            (x, HBM)
            for x in (
                block_day,
                block_count,
                records,
                obs_values.reshape(blocks, slots),
                prior_mean.reshape(1, -1),
                damping,
            )
        ],
        [
            pltpu.SMEM((blocks,), jnp.int32),
            pltpu.SMEM((blocks,), jnp.int32),
            pltpu.VMEM((blocks, slots), BF16),
            pltpu.VMEM((1, width // peers), F32),
            pltpu.VMEM((days, width), F32),
            pltpu.VMEM((blocks, slots, width), BF16),
            pltpu.VMEM((blocks, chunks * slots + EXTRA, LANES), BF16),
            pltpu.SemaphoreType.DMA((5 + 2 * blocks,)),
        ],
        limit=60,
        outs=HBM,
    )[0]
    got = lax.all_to_all(sent, ("y", "obs"), split_axis=0, concat_axis=0, tiled=True)
    span_slots = min(blocks, 8) * slots
    own, extra, pay, prior, gain = run(
        gram_kernel,
        [
            ((2 * tiles, LANES, LANES), F32),
            ((extra_rows, LANES), F32),
            (((2 * tiles - chunks) * LANES + extra_rows, LANES), BF16),
            row,
            (unattenuated_multiplier.shape, F32),
        ],
        [got, unattenuated_multiplier],
        [pltpu.VMEM((width, span_slots), BF16), pltpu.VMEM((16, span_slots), BF16)],
        flops=4 * width * width * blocks * slots,
    )
    def swap(x, bit):
        return lax.ppermute(x, "obs", [(i, i ^ bit) for i in range(peers)])

    def plane_sum(s):
        return lax.ppermute(
            pay, everyone, [((owner_plane(p) + s) % planes * spans + place(p), owner(p)) for p in range(spans)]
        )

    fourth = lax.ppermute(
        pay, everyone, [(spans + place(p), owner(p)) for p in range(spans) if place(p) % 2 == 0]
    )
    second, first, third = plane_sum(2), plane_sum(1), plane_sum(3)
    (gains,) = run(stack_kernel, [((2,) + gain.shape, F32)], [gain, swap(gain, 2)])
    mthi, mtlo = run(gain_kernel, [(full, BF16)] * 2, [gains, swap(gains, 1)])
    pt, pthi, ptlo, chi, clo, ahead = run(
        prep_kernel, [(full, F32)] + [(full, BF16)] * 4 + [row], [propagator_matrix, analysis_cov, prior]
    )
    smalls = pltpu.VMEM((planes + 1, extra_rows, LANES), F32)
    omhi, omlo, info, mine, acc, y = run(
        owner_kernel,
        [((days,) + full, BF16)] * 2 + [((days, 1, width), F32), ((days, width), F32), row, row],
        [
            own, extra, fourth, third, first, second, prior, ahead, pthi, ptlo, chi, clo, (mthi, ANY)
        ],
        [smalls],
    )
    (packed,) = run(
        relay_kernel,
        [(pay.shape, BF16)],
        [(y, ANY), own, extra, fourth, third, first, second],
        [smalls, pltpu.VMEM((extra_rows, LANES), F32)],
    )
    relay = lax.ppermute(
        packed, everyone, [(owner(p + 1), owner(p)) for p in (spans - 4, spans - 2)]
    )
    chain = [*range(spans - 3), spans - 2]
    half = [(full, BF16)] * 2
    for k, (source, target) in enumerate(zip(chain, chain[1:])):
        received = lax.ppermute(y, everyone, [(owner(source), owner(target))])
        if k == 0:
            given = [omhi, omlo, info, chi, clo, pt, mine]
            b1hi, b1lo, off, zhi, zlo = run(
                early_kernel, half + [((8, width), F32)] + half, [(y, ANY), *given], flops=18 * width**3
            )
            acc, y = run(
                second_kernel, [row, row], [acc, received, mine, b1hi, b1lo, off, zhi, zlo, pthi, ptlo]
            )
            b1hi, b1lo, off, b2hi, b2lo = run(
                maps_kernel,
                half + [((8, width), F32)] + half,
                [(y, ANY), *given, zhi, zlo, b1hi, b1lo, off],
                flops=24 * width**3,
                same={10: 0, 11: 1, 12: 2},
            )
        elif k == 1:
            acc, y = run(days_kernel, [row, row], [acc, received, b1hi, b1lo, b2hi, b2lo, off])
            bchi, bclo, offset = run(
                both_kernel, half + [row], [(y, ANY), b1hi, b1lo, b2hi, b2lo, off]
            )
            (table,) = run(
                table_kernel,
                [((spans * days, width), F32)],
                [(offset, ANY), extra, first, second, third],
                [smalls],
            )
            khi, klo = run(
                functools.partial(pairs_kernel, 0), [((2,) + full, BF16)] * 2, [(y, ANY), table, mthi, mtlo]
            )
        elif target == spans - 4:
            nexthi, nextlo, next_off = run(
                next_kernel,
                [((days,) + full, BF16)] * 2 + [((8, width), F32)],
                [(y, ANY), relay, chi, clo],
                [pltpu.VMEM(full, F32), pltpu.VMEM((extra_rows, LANES), F32)],
            )
            acc, y = run(
                double_kernel,
                [row, row],
                [
                    (nexthi, ANY), acc, received, bchi, bclo, offset, table, pthi, ptlo, nexthi, nextlo, next_off
                ],
            )
        elif target != spans - 2:
            acc, y = run(hop_kernel, [row, row], [(khi, ANY), acc, received, bchi, bclo, offset])
        if target == spans - 4:
            more_khi, more_klo = run(
                functools.partial(pairs_kernel, 2), [((4,) + full, BF16)] * 2, [(y, ANY), table, mthi, mtlo]
            )
    (answer,) = run(
        last_kernel,
        [((spans * peers, 8, LANES), F32)],
        [
            acc, received, b1hi, b1lo, b2hi, b2lo, bchi, bclo, off, offset, table, pthi, ptlo, mthi, mtlo,
            nexthi, nextlo, next_off, khi, klo, more_khi, more_klo,
        ],
        [pltpu.VMEM((spans * days, width), F32), pltpu.VMEM((8, width), F32)],
    )
    parts = lax.all_to_all(answer, everyone, split_axis=0, concat_axis=0, tiled=True)
    out = ((days, LANES), F32)
    return run(add_kernel, [out, out], [parts])


def solution(mesh):
    spans, peers = mesh.devices.shape
    finer = jax.sharding.Mesh(mesh.devices.reshape(peers, spans // peers, peers), ("z", "y", "obs"))
    tm = ("z", "y")
    mapped = jax.shard_map(
        local,
        mesh=finer,
        in_specs=(
            P(("z", "y", "obs"), None),
            P(("z", "y", "obs")),
            P(("z", "y", "obs")),
            P(("z", "y", "obs")),
            P(),
            P(),
            P("obs", None),
            P(tm, None),
            P("obs"),
        ),
        out_specs=(P(tm, "obs"), P(tm, "obs")),
        check_vma=False,
    )
    return lambda *args: tuple(mapped(*args))
```

```python
import functools

import jax
import jax.numpy as jnp
from jax import lax
from jax.experimental import pallas as pl
from jax.experimental.pallas import tpu as pltpu
from jax.sharding import PartitionSpec as P

LANES = 128
F32, BF16 = jnp.float32, jnp.bfloat16
VMEM = pl.BlockSpec(memory_space=pltpu.VMEM)
SMEM = pl.BlockSpec(memory_space=pltpu.SMEM)
ANY = pl.BlockSpec(memory_space=pl.ANY)
HBM = pl.BlockSpec(memory_space=pltpu.HBM)


def run(body, out, ins, scratch=(), limit=16, flops=0, outs=VMEM, same=None):
    specs = [x[1] if isinstance(x, tuple) else VMEM for x in ins]
    arrays = [x[0] if isinstance(x, tuple) else x for x in ins]
    moved = sum(a.size * a.dtype.itemsize for a in arrays)
    return pl.pallas_call(
        body,
        out_shape=[jax.ShapeDtypeStruct(s, d) for s, d in out],
        in_specs=specs,
        out_specs=[outs] * len(out),
        scratch_shapes=list(scratch),
        input_output_aliases=same or {},
        compiler_params=pltpu.CompilerParams(vmem_limit_bytes=limit * 1024 * 1024),
        cost_estimate=pl.CostEstimate(flops=flops, bytes_accessed=moved, transcendentals=0),
    )(*arrays)


def here():
    z, y, o = (lax.axis_index(a) for a in ("z", "y", "obs"))
    held, peers = lax.axis_size("y"), lax.axis_size("obs")
    spans = held * peers
    at = y * peers + o
    seat = jnp.where(z == 1, at - lax.rem(at, 2), at)
    span = seat
    for bit in range(1, spans.bit_length()):
        span = span ^ (seat >> bit)
    c = z * held + y
    kept = jnp.where((c == spans - 3) | (c == spans - 1), c - 1, c)
    seat = kept ^ (kept >> 1)
    return z, span, o, c, (1 + (seat & 1)) * spans + (seat | 1), held


def doubled(span, spans):
    return (span == spans - 4) | (span == spans - 2)


def triangle(width):
    parts = width // LANES
    return [(i, j) for i in range(parts) for j in range(i + 1)]


def split(x):
    hi = x.astype(BF16)
    return hi, (x - hi.astype(F32)).astype(BF16)


def mm(x, hi, lo):
    xhi, xlo = split(x)
    dot = functools.partial(jnp.dot, preferred_element_type=F32)
    return dot(xhi, hi) + (dot(xlo, hi) + dot(xhi, lo))


def mv(x, hi, lo):
    wide = jnp.broadcast_to(x, (8, x.shape[1]))
    row = lax.broadcasted_iota(jnp.int32, wide.shape, 0)
    top = wide.astype(BF16).astype(F32)
    both = jnp.where(row == 0, top, jnp.where(row == 1, wide - top, 0.0)).astype(BF16)
    first = jnp.dot(both, hi, preferred_element_type=F32)
    second = jnp.dot(both, lo, preferred_element_type=F32)
    return first[0:1] + (first[1:2] + second[0:1])


def parts(x):
    top = x.astype(BF16).astype(F32)
    return [top, (x - top).astype(BF16).astype(F32)]


def place(span):
    return span ^ (span >> 1)


def owner_plane(span):
    return 1 + place(span) % 2


EXTRA = 8
DIAG, DAMP = 16, 32


def pack_kernel(
    day, count, rows, values, prior, damping, out, day_s, count_s, values_v, prior_v, damping_v, rows_v, stage, sems
):
    blocks = out.shape[0]
    slots = rows_v.shape[1]
    chunks = rows_v.shape[2] // LANES
    small = [(day, day_s), (count, count_s), (values, values_v), (prior, prior_v), (damping, damping_v)]
    copies = [pltpu.make_async_copy(src, dst, sems.at[n]) for n, (src, dst) in enumerate(small)]
    large = [
        pltpu.make_async_copy(rows.at[pl.ds(k * slots, slots)], rows_v.at[k], sems.at[len(small) + k])
        for k in range(blocks)
    ]
    sends = [
        pltpu.make_async_copy(stage.at[place(k)], out.at[place(k)], sems.at[len(small) + blocks + k])
        for k in range(blocks)
    ]
    for copy in copies + large:
        copy.start()
    for copy in copies:
        copy.wait()
    mine = damping_v[:, 0:LANES]
    for q in range(1, chunks):
        mine = jnp.where(lax.axis_index("obs") == q, damping_v[:, q * LANES : (q + 1) * LANES], mine)
    below = parts(prior_v[...]) + parts(mine)
    below = jnp.concatenate(below, 0)
    held = values_v[...].astype(F32)
    lane = lax.broadcasted_iota(jnp.int32, (1, LANES), 1)
    for k in range(blocks):
        marks = jnp.where(lane < LANES // 2, day_s[k], count_s[k]).astype(F32)
        stage[place(k), chunks * slots : chunks * slots + EXTRA, :] = jnp.concatenate(
            [held[k : k + 1, :], marks, below], 0
        ).astype(BF16)
    for k in range(blocks):
        large[k].wait()
        for j in range(chunks):
            stage[place(k), j * slots : (j + 1) * slots, :] = rows_v[k, :, j * LANES : (j + 1) * LANES]
        sends[k].start()
    for copy in sends:
        copy.wait()


def gram_kernel(got, gain, own, extra, pay, prior, gain_out, turned, marks):
    blocks = got.shape[0]
    chunks = turned.shape[0] // LANES
    slots = (got.shape[1] - EXTRA) // chunks
    width = chunks * LANES
    tiles = triangle(width)
    group = min(blocks, 8)
    half = 2 * LANES
    gain_out[...] = gain[...]
    extra[...] = jnp.zeros(extra.shape, F32)

    def below(k):
        return got[k, chunks * slots : chunks * slots + EXTRA, :].astype(F32)

    def one(first, fresh):
        for k in range(group):
            at = slice(k * slots, (k + 1) * slots)
            line = below(first + k)
            slot = lax.broadcasted_iota(jnp.int32, (1, slots), 1).astype(F32)
            valid = slot < jnp.broadcast_to(line[1:2, LANES - 1 : LANES], (1, slots))
            day = jnp.broadcast_to(line[1:2, 0:1], (1, slots))
            kept = [jnp.where(valid & (day == d), 1.0, 0.0) for d in (0.0, 1.0)]
            marks[:, at] = jnp.concatenate(
                kept + [kept[0] * line[0:1], kept[1] * line[0:1], jnp.zeros((12, slots), F32)], 0
            ).astype(BF16)
            for j in range(chunks):
                turned[j * LANES : (j + 1) * LANES, at] = got[first + k, j * slots : (j + 1) * slots, :].T
        source = jnp.concatenate(
            [
                jnp.concatenate([got[first + k, j * slots : (j + 1) * slots, :] for j in range(chunks)], 1)
                for k in range(group)
            ],
            0,
        )
        info = jnp.dot(marks[...], source, preferred_element_type=F32)
        for d in range(2):
            for top in range(0, width, half):
                left = turned[top : top + half, :] * marks[d : d + 1, :]
                block = jnp.dot(left, source[:, : top + half], preferred_element_type=F32)
                for n, (i, j) in enumerate(tiles):
                    if top <= i * LANES < top + half:
                        r = i * LANES - top
                        piece = block[r : r + LANES, j * LANES : (j + 1) * LANES]
                        at = d * len(tiles) + n
                        own[at] = piece if fresh else own[at] + piece
            for j in range(chunks):
                piece = info[2 + d : 3 + d, j * LANES : (j + 1) * LANES]
                r = 8 * d + j
                extra[r : r + 1, :] = piece if fresh else extra[r : r + 1, :] + piece

    if blocks == group:
        one(0, True)
    else:
        own[...] = jnp.zeros(own.shape, F32)

        @pl.loop(0, blocks // group)
        def _(g):
            one(g * group, False)

    row = lax.broadcasted_iota(jnp.int32, (LANES, LANES), 0)
    column = lax.broadcasted_iota(jnp.int32, (LANES, LANES), 1)
    sides = [n for n, (i, j) in enumerate(tiles) if i != j]
    middles = [n for n, (i, j) in enumerate(tiles) if i == j]

    def send(n, piece):
        pay[n * LANES : (n + 1) * LANES, :] = piece.astype(BF16)

    for d in range(2):
        for part, piece in enumerate(parts(extra[8 * d : 8 * d + chunks, :])):
            extra[8 * d + 4 * part : 8 * d + 4 * part + chunks, :] = piece
        for m, n in enumerate(sides):
            send(d * len(sides) + m, own[d * len(tiles) + n])
    for i, n in enumerate(middles):
        squares = [own[d * len(tiles) + n] for d in range(2)]
        send(2 * len(sides) + i, jnp.where(row >= column, squares[0], squares[1]))
        for d in range(2):
            line = jnp.sum(jnp.where(row == column, squares[d], 0.0), axis=0, keepdims=True)
            for part, piece in enumerate(parts(line)):
                r = DIAG + 8 * d + 4 * part + i
                extra[r : r + 1, :] = piece
    for q in range(chunks):
        line = below(q)
        prior[:, q * LANES : (q + 1) * LANES] = line[2:3] + line[3:4]
    for y in range(blocks // 4):
        for q in range(chunks):
            line = below(4 * y + q)
            for part in range(2):
                for d in range(2):
                    r = DAMP + 16 * y + 8 * d + 4 * part + q
                    extra[r : r + 1, :] = line[4 + 2 * part + d : 5 + 2 * part + d]
    pay[pay.shape[0] - extra.shape[0] :, :] = extra[...].astype(BF16)


def prep_kernel(trans, cov, prior, pt, pthi, ptlo, chi, clo, ahead):
    whole = trans[...].T
    pt[...] = whole
    pthi[...], ptlo[...] = split(whole)
    chi[...], clo[...] = split(cov[...])
    ahead[...] = mv(prior[...], pthi[...], ptlo[...])


def stack_kernel(one, two, out):
    out[0] = one[...]
    out[1] = two[...]


def gain_kernel(held, got, mthi, mtlo):
    ids = here()
    rows = held.shape[1]
    for step, part in enumerate((held.at[0], got.at[0], held.at[1], got.at[1])):
        holder = ids[2] ^ step
        at = pl.ds(pl.multiple_of(holder * rows, rows), rows)
        hi, lo = split(part[...].T)
        mthi[:, at] = hi
        mtlo[:, at] = lo


def few(x, hi, lo):
    n = x.shape[0]
    top = x.astype(BF16).astype(F32)
    blank = [jnp.zeros((8 - 2 * n, x.shape[1]), F32)] if n < 4 else []
    both = jnp.concatenate([top, x - top] + blank, 0).astype(BF16)
    first = jnp.dot(both, hi, preferred_element_type=F32)
    second = jnp.dot(both, lo, preferred_element_type=F32)
    return first[0:n] + (first[n : 2 * n] + second[0:n])


def one_day(day, ahead, damping, omhi, omlo, info, chi, clo):
    moved = ahead * damping[day : day + 1, :]
    gap = mv(moved, omhi[day], omlo[day]) - info[day]
    return moved - mv(gap, chi[...], clo[...])


def spread(extra, got, small):
    small[0] = extra[...]
    for s, part in enumerate(got):
        small[s + 1] = part[part.shape[0] - extra.shape[0] :, :].astype(F32)


def line_of(small, s, first):
    return small[s, first : first + 1, :] + small[s, first + 4 : first + 5, :]


def table_kernel(after, extra, g1, g2, g3, table, small):
    ids = here()
    planes = 4
    chunks = table.shape[1] // LANES
    held = table.shape[0] // 2 // planes
    spread(extra, (g1, g2, g3), small)
    for s in range(planes):
        plane = lax.rem(ids[0] + s, planes)
        for k in range(held):
            for day in range(2):
                table[pl.ds(2 * (plane * held + k) + day, 1), :] = jnp.concatenate(
                    [line_of(small, s, DAMP + 16 * k + 8 * day + j) for j in range(chunks)], 1
                )


def sums(extra, got, small):
    share = jnp.where(here()[0] == 2, 1.0, 0.0)
    spread(extra, got, small)

    def summed(first):
        others = line_of(small, 1, first) + line_of(small, 2, first) + (line_of(small, 3, first) + line_of(small, 4, first))
        return line_of(small, 0, first) * share + others

    def added(n):
        at = slice(n * LANES, (n + 1) * LANES)
        one, two, three, four = (part[at].astype(F32) for part in got)
        return (one + two) + (three + four)

    return share, summed, added


def relay_kernel(after, own, extra, g4, g3, g1, g2, out, small, rows):
    span = here()[1]
    spans = lax.axis_size("z") * lax.axis_size("y")
    chunks = 4
    tiles = triangle(chunks * LANES)
    row = lax.broadcasted_iota(jnp.int32, (LANES, LANES), 0)
    column = lax.broadcasted_iota(jnp.int32, (LANES, LANES), 1)
    sides = [n for n, (i, j) in enumerate(tiles) if i != j]
    middles = [n for n, (i, j) in enumerate(tiles) if i == j]

    @pl.when((span == spans - 3) | (span == spans - 1))
    def _():
        share, summed, added = sums(extra, (g1, g2, g3, g4), small)

        def send(n, piece):
            out[n * LANES : (n + 1) * LANES, :] = (piece * share + added(n)).astype(BF16)

        for d in range(2):
            for m, n in enumerate(sides):
                send(d * len(sides) + m, own[d * len(tiles) + n])
        for i, n in enumerate(middles):
            send(2 * len(sides) + i, jnp.where(row >= column, own[n], own[len(tiles) + n]))
        rows[...] = jnp.zeros(rows.shape, F32)
        for first in (0, 8, DIAG, DIAG + 8):
            for j in range(chunks):
                for part, piece in enumerate(parts(summed(first + j))):
                    r = first + 4 * part + j
                    rows[r : r + 1, :] = piece
        out[out.shape[0] - rows.shape[0] :, :] = rows[...].astype(BF16)


def next_kernel(after, relay, chi, clo, zhi, zlo, off, whole, rows):
    spans = lax.axis_size("z") * lax.axis_size("y")
    width = whole.shape[0]
    chunks = width // LANES
    tiles = triangle(width)
    row = lax.broadcasted_iota(jnp.int32, (LANES, LANES), 0)
    column = lax.broadcasted_iota(jnp.int32, (LANES, LANES), 1)
    sides = [(i, j) for i, j in tiles if i != j]

    @pl.when(doubled(here()[1], spans))
    def _():
        rows[...] = relay[relay.shape[0] - rows.shape[0] :, :].astype(F32)

        def line(r):
            return rows[r : r + 1, :] + rows[r + 4 : r + 5, :]

        def tile(n):
            return relay[n * LANES : (n + 1) * LANES, :].astype(F32)

        def put(i, j, piece):
            whole[i * LANES : (i + 1) * LANES, j * LANES : (j + 1) * LANES] = piece

        for day in range(2):
            for i in range(chunks):
                both = tile(2 * len(sides) + i)
                part = jnp.where(row < column if day else row > column, both, 0.0)
                put(i, i, part + part.T + jnp.where(row == column, line(DIAG + 8 * day + i), 0.0))
            for m, (i, j) in enumerate(sides):
                piece = tile(day * len(sides) + m)
                put(i, j, piece)
                put(j, i, piece.T)
            zhi[day], zlo[day] = split(mm(whole[...], chi[...], clo[...]))
            info = jnp.concatenate([line(8 * day + j) for j in range(chunks)], 1)
            off[day : day + 1, :] = mv(info, chi[...], clo[...])


def next_day(day, state, damping, pthi, ptlo, zhi, zlo, off):
    moved = mv(state, pthi[...], ptlo[...]) * damping
    return moved, moved - mv(moved, zhi[day], zlo[day]) + off[day : day + 1, :]


def owner_kernel(
    own, extra, g4, g3, g1, g2, prior, ahead, pthi, ptlo, chi, clo, after, omhi, omlo, info, mine, start, y, small
):
    ids = here()
    planes = 4
    width = pthi.shape[0]
    chunks = width // LANES
    tiles = triangle(width)
    got = (g1, g2, g3, g4)
    row = lax.broadcasted_iota(jnp.int32, (LANES, LANES), 0)
    column = lax.broadcasted_iota(jnp.int32, (LANES, LANES), 1)
    share, summed, added = sums(extra, got, small)

    def put(day, i, j, piece):
        hi, lo = split(piece)
        omhi[day, i * LANES : (i + 1) * LANES, j * LANES : (j + 1) * LANES] = hi
        omlo[day, i * LANES : (i + 1) * LANES, j * LANES : (j + 1) * LANES] = lo

    sides = [n for n, (i, j) in enumerate(tiles) if i != j]
    middles = [n for n, (i, j) in enumerate(tiles) if i == j]

    def unpack(day):
        for i, n in enumerate(middles):
            both = added(2 * len(sides) + i)
            part = jnp.where(row < column if day else row > column, both, 0.0)
            others = sum(line_of(small, s, DIAG + 8 * day + i) for s in range(1, 5))
            piece = own[day * len(tiles) + n] * share + (part + part.T)
            put(day, i, i, piece + jnp.where(row == column, others, 0.0))
        for m, n in enumerate(sides):
            i, j = tiles[n]
            piece = own[day * len(tiles) + n] * share + added(day * len(sides) + m)
            put(day, i, j, piece)
            put(day, j, i, piece.T)

    for day in range(2):
        info[day] = jnp.concatenate([summed(8 * day + j) for j in range(chunks)], 1)
    held = ids[5]
    source = lax.rem(ids[1] // held - ids[0] + planes, planes)
    for day in range(2):
        for j in range(chunks):
            r = DAMP + 16 * lax.rem(ids[1], held) + 8 * day + j
            mine[day : day + 1, j * LANES : (j + 1) * LANES] = (
                small[source, pl.ds(r, 1), :] + small[source, pl.ds(r + 4, 1), :]
            )
    first = (ids[1] == 0) & (ids[0] == owner_plane(0))
    start[...] = jnp.where(first, prior[...], 0.0)

    @pl.when(first)
    def _():
        unpack(0)
        state = one_day(0, ahead[...], mine, omhi, omlo, info, chi, clo)
        unpack(1)
        y[...] = one_day(1, mv(state, pthi[...], ptlo[...]), mine, omhi, omlo, info, chi, clo)

    @pl.when(jnp.logical_not(first))
    def _():
        for day in range(2):
            unpack(day)
        y[...] = jnp.zeros(y.shape, F32)


def seen(day, omhi, omlo, chi, clo):
    return mm(omhi[day].astype(F32) + omlo[day].astype(F32), chi[...], clo[...])


def early_kernel(after, omhi, omlo, info, chi, clo, pt, damping, b1hi, b1lo, off):
    @pl.when(here()[1] == 1)
    def _():
        off[0:1, :] = mv(info[0], chi[...], clo[...])
        moved = pt[...] * damping[0:1, :]
        b1hi[...], b1lo[...] = split(moved - mm(moved, *split(seen(0, omhi, omlo, chi, clo))))


def maps_kernel(
    after, omhi, omlo, info, chi, clo, pt, damping, old1, old2, old3, b1hi, b1lo, off, b2hi, b2lo
):
    span = here()[1]
    spans = lax.axis_size("z") * lax.axis_size("y")
    relays = (span == spans - 3) | (span == spans - 1)
    parts = ((b1hi, b1lo), (b2hi, b2lo))

    def make(day):
        moved = pt[...] * damping[day : day + 1, :]
        parts[day][0][...], parts[day][1][...] = split(
            moved - mm(moved, *split(seen(day, omhi, omlo, chi, clo)))
        )
        off[day : day + 1, :] = mv(info[day], chi[...], clo[...])

    @pl.when(jnp.logical_not(relays | (span == 1)))
    def _():
        make(0)

    @pl.when(jnp.logical_not(relays))
    def _():
        make(1)


def second_kernel(acc, got, mine, b1hi, b1lo, off, omhi, omlo, info, chi, clo, pthi, ptlo, total, y):
    total[...] = acc[...] + got[...]
    y[...] = jnp.zeros(y.shape, F32)

    @pl.when(here()[1] == 1)
    def _():
        state = mv(acc[...] + got[...], b1hi[...], b1lo[...]) + off[0:1, :]
        ahead = mv(state, pthi[...], ptlo[...])
        y[...] = one_day(1, ahead, mine, omhi, omlo, info, chi, clo)


def both_kernel(after, b1hi, b1lo, b2hi, b2lo, off, bchi, bclo, offset):
    both = jnp.dot(b1hi[...], b2hi[...], preferred_element_type=F32) + (
        jnp.dot(b1lo[...], b2hi[...], preferred_element_type=F32)
        + jnp.dot(b1hi[...], b2lo[...], preferred_element_type=F32)
    )
    bchi[...], bclo[...] = split(both)
    offset[...] = mv(off[0:1, :], b2hi[...], b2lo[...]) + off[1:2, :]


def hop_kernel(after, acc, got, bchi, bclo, offset, total, y):
    state = acc[...] + got[...]
    total[...] = state
    y[...] = mv(state, bchi[...], bclo[...]) + offset[...]


def days_kernel(acc, got, b1hi, b1lo, b2hi, b2lo, off, total, y):
    state = acc[...] + got[...]
    total[...] = state
    state = mv(state, b1hi[...], b1lo[...]) + off[0:1, :]
    y[...] = mv(state, b2hi[...], b2lo[...]) + off[1:2, :]


def double_kernel(after, acc, got, bchi, bclo, offset, table, pthi, ptlo, zhi, zlo, off, total, y):
    spans = table.shape[0] // 2
    total[...] = acc[...] + got[...]
    y[...] = jnp.zeros(y.shape, F32)

    @pl.when(here()[1] == spans - 4)
    def _():
        state = mv(acc[...] + got[...], bchi[...], bclo[...]) + offset[...]
        for day in range(2):
            r = 2 * (spans - 3) + day
            _, state = next_day(day, state, table[r : r + 1, :], pthi, ptlo, zhi, zlo, off)
        y[...] = state


def whole_of(hi, lo):
    return hi[...].astype(F32) + lo[...].astype(F32)


def pairs_kernel(skip, after, table, mthi, mtlo, khi, klo):
    spans = table.shape[0] // 2

    @pl.when(here()[1] == spans - 2)
    def _():
        @pl.loop(0, khi.shape[0])
        def _(k):
            scaled = whole_of(mthi, mtlo) * table[pl.ds(2 * (spans - 3 - skip - k) + 1, 1), :]
            khi[k], klo[k] = split(mm(scaled, mthi[...], mtlo[...]))


def last_kernel(
    acc, got, b1hi, b1lo, b2hi, b2lo, bchi, bclo, off, offset, table, pthi, ptlo, mthi, mtlo,
    zhi, zlo, next_off, khi, klo, more_khi, more_klo, out, shares, means,
):
    span = here()[1]
    total, width = shares.shape
    spans = total // 2
    chunks = width // LANES
    twice = doubled(span, spans)
    shares[...] = jnp.zeros(shares.shape, F32)

    def step(k, v):
        t = 2 * span - 1 - k
        v = mv(v * table[pl.ds(t + 1, 1), :], mthi[...], mtlo[...])
        shares[pl.ds(t, 1), :] = v
        return v

    def own_days(const, damped):
        n = len(const)
        v = const[-1]
        shares[pl.ds(2 * span + n - 1, 1), :] = v
        for i in range(n - 2, -1, -1):
            v = const[i] + mv(v * damped[i], mthi[...], mtlo[...])
            shares[pl.ds(2 * span + i, 1), :] = v
        means[4:5, :] = v

    @pl.when(span < spans - 4)
    def _():
        state = acc[...] + got[...]
        one = mv(state, b1hi[...], b1lo[...]) + off[0:1, :]
        two = mv(one, b2hi[...], b2lo[...]) + off[1:2, :]
        both = jnp.concatenate([one, two], 0)
        damped = [table[pl.ds(2 * span + 1 + i, 1), :] for i in range(2)]
        ahead = jnp.concatenate(damped, 0)
        const = both - few(few(both, pthi[...], ptlo[...]) * ahead * ahead, mthi[...], mtlo[...])
        means[0:2, :] = both
        own_days([const[0:1], const[1:2]], damped)

    @pl.when(twice)
    def _():
        state = acc[...] + got[...]
        rows = [
            mv(state, b1hi[...], b1lo[...]) + off[0:1, :],
            mv(state, bchi[...], bclo[...]) + offset[...],
        ]
        damped = [table[pl.ds(2 * span + 1 + i, 1), :] for i in range(3)]
        ahead = [mv(rows[0], pthi[...], ptlo[...]) * damped[0]]
        for day in range(2):
            moved, after = next_day(day, rows[-1], damped[1 + day], pthi, ptlo, zhi, zlo, next_off)
            ahead.append(moved)
            rows.append(after)
        taken = [a * d for a, d in zip(ahead, damped)]
        taken = few(jnp.concatenate(taken + [jnp.zeros((1, width), F32)], 0), mthi[...], mtlo[...])
        means[0:4, :] = jnp.concatenate(rows, 0)
        means[5:8, :] = jnp.concatenate(rows[:3], 0) - taken[0:3]
        means[4:5, :] = rows[3]

    @pl.when(span == spans - 4)
    def _():
        beyond = table[pl.ds(2 * span + 4, 1), :]
        four = means[3:4, :]
        ahead = mv(four, pthi[...], ptlo[...]) * beyond * beyond
        means[4:5, :] = four - mv(ahead, mthi[...], mtlo[...])

    @pl.when(twice)
    def _():
        const = [means[5:6, :], means[6:7, :], means[7:8, :], means[4:5, :]]
        own_days(const, [table[pl.ds(2 * span + 1 + i, 1), :] for i in range(3)])

    @pl.when(span < spans - 2)
    def _():
        lax.fori_loop(0, jnp.where((span < spans - 4) | twice, 2 * span, 0), step, means[4:5, :])

    @pl.when(span == spans - 2)
    def _():
        v, damped_rows = means[4:5, :], []
        pairs = [(a, b, k) for a, b in ((khi, klo), (more_khi, more_klo)) for k in range(a.shape[0])]
        for n, (a, b, k) in enumerate(pairs):
            t = 2 * (spans - 2 - n)
            damped_rows.append(v * table[t : t + 1, :])
            v = mv(damped_rows[-1], a[k], b[k])
            shares[t - 2 : t - 1, :] = v
        batch = jnp.concatenate(damped_rows + [jnp.zeros((1, width), F32)] * (-len(damped_rows) % 8), 0)
        batch = mm(batch, mthi[...], mtlo[...])
        for n in range(len(pairs)):
            t = 2 * (spans - 2 - n)
            shares[t - 1 : t, :] = batch[n : n + 1]
        lax.fori_loop(2 * len(pairs), 2 * span, step, v)

    for c in range(spans):
        for q in range(chunks):
            out[c * chunks + q, 0:2, :] = shares[2 * c : 2 * c + 2, q * LANES : (q + 1) * LANES]
    for q in range(chunks):
        out[span * chunks + q, 2:4, :] = means[0:2, q * LANES : (q + 1) * LANES]

    @pl.when(twice)
    def _():
        for q in range(chunks):
            out[(span + 1) * chunks + q, 2:4, :] = means[2:4, q * LANES : (q + 1) * LANES]


def add_kernel(parts, filt, smooth):
    spans = parts.shape[0] // 4
    owners = [*range(spans - 4), spans - 4, spans - 2]
    filt[...] = parts[here()[4], 2:4, :]
    smooth[...] = sum(parts[owner_plane(c) * spans + (place(c) | 1), 0:2, :] for c in owners)


def local(
    records,
    obs_values,
    block_day,
    block_count,
    propagator_matrix,
    analysis_cov,
    unattenuated_multiplier,
    damping,
    prior_mean,
):
    planes, held, peers = (lax.axis_size(a) for a in ("z", "y", "obs"))
    spans = planes * held
    blocks = block_day.shape[0]
    slots = records.shape[0] // blocks
    width = records.shape[1]
    days = damping.shape[0]
    assert planes == peers == 4 and days == 2 and slots == LANES and blocks == spans
    everyone = ("z", "y", "obs")

    def owner(span):
        return owner_plane(span) * spans + (place(span) | 1)

    tiles = len(triangle(width))
    extra_rows = DAMP + 16 * held
    chunks = width // LANES
    full, row = (width, width), ((1, width), F32)
    sent = run(
        pack_kernel,
        [((blocks, chunks * slots + EXTRA, LANES), BF16)],
        [
            (x, HBM)
            for x in (
                block_day,
                block_count,
                records,
                obs_values.reshape(blocks, slots),
                prior_mean.reshape(1, -1),
                damping,
            )
        ],
        [
            pltpu.SMEM((blocks,), jnp.int32),
            pltpu.SMEM((blocks,), jnp.int32),
            pltpu.VMEM((blocks, slots), BF16),
            pltpu.VMEM((1, width // peers), F32),
            pltpu.VMEM((days, width), F32),
            pltpu.VMEM((blocks, slots, width), BF16),
            pltpu.VMEM((blocks, chunks * slots + EXTRA, LANES), BF16),
            pltpu.SemaphoreType.DMA((5 + 2 * blocks,)),
        ],
        limit=60,
        outs=HBM,
    )[0]
    got = lax.all_to_all(sent, ("y", "obs"), split_axis=0, concat_axis=0, tiled=True)
    span_slots = min(blocks, 8) * slots
    own, extra, pay, prior, gain = run(
        gram_kernel,
        [
            ((2 * tiles, LANES, LANES), F32),
            ((extra_rows, LANES), F32),
            (((2 * tiles - chunks) * LANES + extra_rows, LANES), BF16),
            row,
            (unattenuated_multiplier.shape, F32),
        ],
        [got, unattenuated_multiplier],
        [pltpu.VMEM((width, span_slots), BF16), pltpu.VMEM((16, span_slots), BF16)],
        flops=4 * width * width * blocks * slots,
    )
    def swap(x, bit):
        return lax.ppermute(x, "obs", [(i, i ^ bit) for i in range(peers)])

    def plane_sum(s):
        return lax.ppermute(
            pay, everyone, [((owner_plane(p) + s) % planes * spans + place(p), owner(p)) for p in range(spans)]
        )

    fourth = lax.ppermute(
        pay, everyone, [(spans + place(p), owner(p)) for p in range(spans) if place(p) % 2 == 0]
    )
    second, first, third = plane_sum(2), plane_sum(1), plane_sum(3)
    (gains,) = run(stack_kernel, [((2,) + gain.shape, F32)], [gain, swap(gain, 2)])
    mthi, mtlo = run(gain_kernel, [(full, BF16)] * 2, [gains, swap(gains, 1)])
    pt, pthi, ptlo, chi, clo, ahead = run(
        prep_kernel, [(full, F32)] + [(full, BF16)] * 4 + [row], [propagator_matrix, analysis_cov, prior]
    )
    smalls = pltpu.VMEM((planes + 1, extra_rows, LANES), F32)
    omhi, omlo, info, mine, acc, y = run(
        owner_kernel,
        [((days,) + full, BF16)] * 2 + [((days, 1, width), F32), ((days, width), F32), row, row],
        [
            own, extra, fourth, third, first, second, prior, ahead, pthi, ptlo, chi, clo, (mthi, ANY)
        ],
        [smalls],
    )
    (packed,) = run(
        relay_kernel,
        [(pay.shape, BF16)],
        [(y, ANY), own, extra, fourth, third, first, second],
        [smalls, pltpu.VMEM((extra_rows, LANES), F32)],
    )
    relay = lax.ppermute(
        packed, everyone, [(owner(p + 1), owner(p)) for p in (spans - 4, spans - 2)]
    )
    chain = [*range(spans - 3), spans - 2]
    half = [(full, BF16)] * 2
    for k, (source, target) in enumerate(zip(chain, chain[1:])):
        received = lax.ppermute(y, everyone, [(owner(source), owner(target))])
        if k == 0:
            given = [omhi, omlo, info, chi, clo, pt, mine]
            b1hi, b1lo, off = run(
                early_kernel, half + [((8, width), F32)], [(y, ANY), *given], flops=12 * width**3
            )
            acc, y = run(
                second_kernel,
                [row, row],
                [acc, received, mine, b1hi, b1lo, off, omhi, omlo, info, chi, clo, pthi, ptlo],
            )
            b1hi, b1lo, off, b2hi, b2lo = run(
                maps_kernel,
                half + [((8, width), F32)] + half,
                [(y, ANY), *given, b1hi, b1lo, off],
                flops=24 * width**3,
                same={8: 0, 9: 1, 10: 2},
            )
        elif k == 1:
            acc, y = run(days_kernel, [row, row], [acc, received, b1hi, b1lo, b2hi, b2lo, off])
            bchi, bclo, offset = run(
                both_kernel, half + [row], [(y, ANY), b1hi, b1lo, b2hi, b2lo, off]
            )
            (table,) = run(
                table_kernel,
                [((spans * days, width), F32)],
                [(offset, ANY), extra, first, second, third],
                [smalls],
            )
            khi, klo = run(
                functools.partial(pairs_kernel, 0), [((2,) + full, BF16)] * 2, [(y, ANY), table, mthi, mtlo]
            )
        elif target == spans - 4:
            nexthi, nextlo, next_off = run(
                next_kernel,
                [((days,) + full, BF16)] * 2 + [((8, width), F32)],
                [(y, ANY), relay, chi, clo],
                [pltpu.VMEM(full, F32), pltpu.VMEM((extra_rows, LANES), F32)],
            )
            acc, y = run(
                double_kernel,
                [row, row],
                [
                    (nexthi, ANY), acc, received, bchi, bclo, offset, table, pthi, ptlo, nexthi, nextlo, next_off
                ],
            )
        elif target != spans - 2:
            acc, y = run(hop_kernel, [row, row], [(khi, ANY), acc, received, bchi, bclo, offset])
        if target == spans - 4:
            more_khi, more_klo = run(
                functools.partial(pairs_kernel, 2), [((4,) + full, BF16)] * 2, [(y, ANY), table, mthi, mtlo]
            )
    (answer,) = run(
        last_kernel,
        [((spans * peers, 8, LANES), F32)],
        [
            acc, received, b1hi, b1lo, b2hi, b2lo, bchi, bclo, off, offset, table, pthi, ptlo, mthi, mtlo,
            nexthi, nextlo, next_off, khi, klo, more_khi, more_klo,
        ],
        [pltpu.VMEM((spans * days, width), F32), pltpu.VMEM((8, width), F32)],
    )
    parts = lax.all_to_all(answer, everyone, split_axis=0, concat_axis=0, tiled=True)
    out = ((days, LANES), F32)
    return run(add_kernel, [out, out], [parts])


def solution(mesh):
    spans, peers = mesh.devices.shape
    finer = jax.sharding.Mesh(mesh.devices.reshape(peers, spans // peers, peers), ("z", "y", "obs"))
    tm = ("z", "y")
    mapped = jax.shard_map(
        local,
        mesh=finer,
        in_specs=(
            P(("z", "y", "obs"), None),
            P(("z", "y", "obs")),
            P(("z", "y", "obs")),
            P(("z", "y", "obs")),
            P(),
            P(),
            P("obs", None),
            P(tm, None),
            P("obs"),
        ),
        out_specs=(P(tm, "obs"), P(tm, "obs")),
        check_vma=False,
    )
    return lambda *args: tuple(mapped(*args))
```

```python
import functools

import jax
import jax.numpy as jnp
from jax import lax
from jax.experimental import pallas as pl
from jax.experimental.pallas import tpu as pltpu
from jax.sharding import PartitionSpec as P

LANES = 128
F32, BF16 = jnp.float32, jnp.bfloat16
VMEM = pl.BlockSpec(memory_space=pltpu.VMEM)
SMEM = pl.BlockSpec(memory_space=pltpu.SMEM)
ANY = pl.BlockSpec(memory_space=pl.ANY)
HBM = pl.BlockSpec(memory_space=pltpu.HBM)


def run(body, out, ins, scratch=(), limit=16, flops=0, outs=VMEM, same=None):
    specs = [x[1] if isinstance(x, tuple) else VMEM for x in ins]
    arrays = [x[0] if isinstance(x, tuple) else x for x in ins]
    moved = sum(a.size * a.dtype.itemsize for a in arrays)
    return pl.pallas_call(
        body,
        out_shape=[jax.ShapeDtypeStruct(s, d) for s, d in out],
        in_specs=specs,
        out_specs=[outs] * len(out),
        scratch_shapes=list(scratch),
        input_output_aliases=same or {},
        compiler_params=pltpu.CompilerParams(vmem_limit_bytes=limit * 1024 * 1024),
        cost_estimate=pl.CostEstimate(flops=flops, bytes_accessed=moved, transcendentals=0),
    )(*arrays)


def here():
    z, y, o = (lax.axis_index(a) for a in ("z", "y", "obs"))
    held, peers = lax.axis_size("y"), lax.axis_size("obs")
    spans = held * peers
    at = y * peers + o
    seat = jnp.where(z == 2, at - lax.rem(at, 2), at) ^ (spans // 2)
    span = seat
    for bit in range(1, spans.bit_length()):
        span = span ^ (seat >> bit)
    c = z * held + y
    kept = jnp.where((c == spans - 3) | (c == spans - 1), c - 1, c)
    seat = place(kept)
    return z, span, o, c, (2 - (seat & 1)) * spans + (seat | 1), held


def doubled(span, spans):
    return (span == spans - 4) | (span == spans - 2)


def triangle(width):
    parts = width // LANES
    return [(i, j) for i in range(parts) for j in range(i + 1)]


def split(x):
    hi = x.astype(BF16)
    return hi, (x - hi.astype(F32)).astype(BF16)


def mm(x, hi, lo):
    xhi, xlo = split(x)
    dot = functools.partial(jnp.dot, preferred_element_type=F32)
    return dot(xhi, hi) + (dot(xlo, hi) + dot(xhi, lo))


def mv(x, hi, lo):
    wide = jnp.broadcast_to(x, (8, x.shape[1]))
    row = lax.broadcasted_iota(jnp.int32, wide.shape, 0)
    top = wide.astype(BF16).astype(F32)
    both = jnp.where(row == 0, top, jnp.where(row == 1, wide - top, 0.0)).astype(BF16)
    first = jnp.dot(both, hi, preferred_element_type=F32)
    second = jnp.dot(both, lo, preferred_element_type=F32)
    return first[0:1] + (first[1:2] + second[0:1])


def parts(x):
    top = x.astype(BF16).astype(F32)
    return [top, (x - top).astype(BF16).astype(F32)]


def place(span):
    return span ^ (span >> 1) ^ (lax.axis_size("z") * lax.axis_size("y") // 2)


def owner_plane(span):
    return 2 - place(span) % 2


EXTRA = 8
DIAG, DAMP = 16, 32


def pack_kernel(
    day, count, rows, values, prior, damping, out, day_s, count_s, values_v, prior_v, damping_v, rows_v, stage, sems
):
    blocks = out.shape[0]
    slots = rows_v.shape[1]
    chunks = rows_v.shape[2] // LANES
    small = [(day, day_s), (count, count_s), (values, values_v), (prior, prior_v), (damping, damping_v)]
    copies = [pltpu.make_async_copy(src, dst, sems.at[n]) for n, (src, dst) in enumerate(small)]
    large = [
        pltpu.make_async_copy(rows.at[pl.ds(k * slots, slots)], rows_v.at[k], sems.at[len(small) + k])
        for k in range(blocks)
    ]
    sends = [
        pltpu.make_async_copy(stage.at[place(k)], out.at[place(k)], sems.at[len(small) + blocks + k])
        for k in range(blocks)
    ]
    for copy in copies + large:
        copy.start()
    for copy in copies:
        copy.wait()
    mine = damping_v[:, 0:LANES]
    for q in range(1, chunks):
        mine = jnp.where(lax.axis_index("obs") == q, damping_v[:, q * LANES : (q + 1) * LANES], mine)
    below = parts(prior_v[...]) + parts(mine)
    below = jnp.concatenate(below, 0)
    held = values_v[...].astype(F32)
    lane = lax.broadcasted_iota(jnp.int32, (1, LANES), 1)
    for k in range(blocks):
        marks = jnp.where(lane < LANES // 2, day_s[k], count_s[k]).astype(F32)
        stage[place(k), chunks * slots : chunks * slots + EXTRA, :] = jnp.concatenate(
            [held[k : k + 1, :], marks, below], 0
        ).astype(BF16)
    for k in range(blocks):
        large[k].wait()
        for j in range(chunks):
            stage[place(k), j * slots : (j + 1) * slots, :] = rows_v[k, :, j * LANES : (j + 1) * LANES]
        sends[k].start()
    for copy in sends:
        copy.wait()


def gram_kernel(got, gain, own, extra, pay, prior, gain_out, turned, marks):
    blocks = got.shape[0]
    chunks = turned.shape[0] // LANES
    slots = (got.shape[1] - EXTRA) // chunks
    width = chunks * LANES
    tiles = triangle(width)
    group = min(blocks, 8)
    half = 2 * LANES
    gain_out[...] = gain[...]
    extra[...] = jnp.zeros(extra.shape, F32)

    def below(k):
        return got[k, chunks * slots : chunks * slots + EXTRA, :].astype(F32)

    def one(first, fresh):
        for k in range(group):
            at = slice(k * slots, (k + 1) * slots)
            line = below(first + k)
            slot = lax.broadcasted_iota(jnp.int32, (1, slots), 1).astype(F32)
            valid = slot < jnp.broadcast_to(line[1:2, LANES - 1 : LANES], (1, slots))
            day = jnp.broadcast_to(line[1:2, 0:1], (1, slots))
            kept = [jnp.where(valid & (day == d), 1.0, 0.0) for d in (0.0, 1.0)]
            marks[:, at] = jnp.concatenate(
                kept + [kept[0] * line[0:1], kept[1] * line[0:1], jnp.zeros((12, slots), F32)], 0
            ).astype(BF16)
            for j in range(chunks):
                turned[j * LANES : (j + 1) * LANES, at] = got[first + k, j * slots : (j + 1) * slots, :].T
        source = jnp.concatenate(
            [
                jnp.concatenate([got[first + k, j * slots : (j + 1) * slots, :] for j in range(chunks)], 1)
                for k in range(group)
            ],
            0,
        )
        info = jnp.dot(marks[...], source, preferred_element_type=F32)
        for d in range(2):
            for top in range(0, width, half):
                left = turned[top : top + half, :] * marks[d : d + 1, :]
                block = jnp.dot(left, source[:, : top + half], preferred_element_type=F32)
                for n, (i, j) in enumerate(tiles):
                    if top <= i * LANES < top + half:
                        r = i * LANES - top
                        piece = block[r : r + LANES, j * LANES : (j + 1) * LANES]
                        at = d * len(tiles) + n
                        own[at] = piece if fresh else own[at] + piece
            for j in range(chunks):
                piece = info[2 + d : 3 + d, j * LANES : (j + 1) * LANES]
                r = 8 * d + j
                extra[r : r + 1, :] = piece if fresh else extra[r : r + 1, :] + piece

    if blocks == group:
        one(0, True)
    else:
        own[...] = jnp.zeros(own.shape, F32)

        @pl.loop(0, blocks // group)
        def _(g):
            one(g * group, False)

    row = lax.broadcasted_iota(jnp.int32, (LANES, LANES), 0)
    column = lax.broadcasted_iota(jnp.int32, (LANES, LANES), 1)
    sides = [n for n, (i, j) in enumerate(tiles) if i != j]
    middles = [n for n, (i, j) in enumerate(tiles) if i == j]

    def send(n, piece):
        pay[n * LANES : (n + 1) * LANES, :] = piece.astype(BF16)

    for d in range(2):
        for part, piece in enumerate(parts(extra[8 * d : 8 * d + chunks, :])):
            extra[8 * d + 4 * part : 8 * d + 4 * part + chunks, :] = piece
        for m, n in enumerate(sides):
            send(d * len(sides) + m, own[d * len(tiles) + n])
    for i, n in enumerate(middles):
        squares = [own[d * len(tiles) + n] for d in range(2)]
        send(2 * len(sides) + i, jnp.where(row >= column, squares[0], squares[1]))
        for d in range(2):
            line = jnp.sum(jnp.where(row == column, squares[d], 0.0), axis=0, keepdims=True)
            for part, piece in enumerate(parts(line)):
                r = DIAG + 8 * d + 4 * part + i
                extra[r : r + 1, :] = piece
    for q in range(chunks):
        line = below(q)
        prior[:, q * LANES : (q + 1) * LANES] = line[2:3] + line[3:4]
    for y in range(blocks // 4):
        for q in range(chunks):
            line = below(4 * y + q)
            for part in range(2):
                for d in range(2):
                    r = DAMP + 16 * y + 8 * d + 4 * part + q
                    extra[r : r + 1, :] = line[4 + 2 * part + d : 5 + 2 * part + d]
    pay[pay.shape[0] - extra.shape[0] :, :] = extra[...].astype(BF16)


def prep_kernel(trans, cov, prior, pt, pthi, ptlo, chi, clo, ahead):
    whole = trans[...].T
    pt[...] = whole
    pthi[...], ptlo[...] = split(whole)
    chi[...], clo[...] = split(cov[...])
    ahead[...] = mv(prior[...], pthi[...], ptlo[...])


def stack_kernel(one, two, out):
    out[0] = one[...]
    out[1] = two[...]


def gain_kernel(held, got, mthi, mtlo):
    ids = here()
    rows = held.shape[1]
    for step, part in enumerate((held.at[0], got.at[0], held.at[1], got.at[1])):
        holder = ids[2] ^ step
        at = pl.ds(pl.multiple_of(holder * rows, rows), rows)
        hi, lo = split(part[...].T)
        mthi[:, at] = hi
        mtlo[:, at] = lo


def few(x, hi, lo):
    n = x.shape[0]
    top = x.astype(BF16).astype(F32)
    blank = [jnp.zeros((8 - 2 * n, x.shape[1]), F32)] if n < 4 else []
    both = jnp.concatenate([top, x - top] + blank, 0).astype(BF16)
    first = jnp.dot(both, hi, preferred_element_type=F32)
    second = jnp.dot(both, lo, preferred_element_type=F32)
    return first[0:n] + (first[n : 2 * n] + second[0:n])


def one_day(day, ahead, damping, omhi, omlo, info, chi, clo):
    moved = ahead * damping[day : day + 1, :]
    gap = mv(moved, omhi[day], omlo[day]) - info[day]
    return moved - mv(gap, chi[...], clo[...])


def spread(extra, got, small):
    small[0] = extra[...]
    for s, part in enumerate(got):
        small[s + 1] = part[part.shape[0] - extra.shape[0] :, :].astype(F32)


def line_of(small, s, first):
    return small[s, first : first + 1, :] + small[s, first + 4 : first + 5, :]


def table_kernel(after, extra, g1, g2, g3, table, small):
    ids = here()
    planes = 4
    chunks = table.shape[1] // LANES
    held = table.shape[0] // 2 // planes
    spread(extra, (g1, g2, g3), small)
    for s in range(planes):
        plane = lax.rem(ids[0] + s, planes)
        for k in range(held):
            for day in range(2):
                table[pl.ds(2 * (plane * held + k) + day, 1), :] = jnp.concatenate(
                    [line_of(small, s, DAMP + 16 * k + 8 * day + j) for j in range(chunks)], 1
                )


def sums(extra, got, small):
    share = jnp.where(here()[0] == 1, 1.0, 0.0)
    spread(extra, got, small)

    def summed(first):
        others = line_of(small, 1, first) + line_of(small, 2, first) + (line_of(small, 3, first) + line_of(small, 4, first))
        return line_of(small, 0, first) * share + others

    def added(n):
        at = slice(n * LANES, (n + 1) * LANES)
        one, two, three, four = (part[at].astype(F32) for part in got)
        return (one + two) + (three + four)

    return share, summed, added


def relay_kernel(after, own, extra, g4, g3, g1, g2, out, small, rows):
    span = here()[1]
    spans = lax.axis_size("z") * lax.axis_size("y")
    chunks = 4
    tiles = triangle(chunks * LANES)
    row = lax.broadcasted_iota(jnp.int32, (LANES, LANES), 0)
    column = lax.broadcasted_iota(jnp.int32, (LANES, LANES), 1)
    sides = [n for n, (i, j) in enumerate(tiles) if i != j]
    middles = [n for n, (i, j) in enumerate(tiles) if i == j]

    @pl.when((span == spans - 3) | (span == spans - 1))
    def _():
        share, summed, added = sums(extra, (g1, g2, g3, g4), small)

        def send(n, piece):
            out[n * LANES : (n + 1) * LANES, :] = (piece * share + added(n)).astype(BF16)

        for d in range(2):
            for m, n in enumerate(sides):
                send(d * len(sides) + m, own[d * len(tiles) + n])
        for i, n in enumerate(middles):
            send(2 * len(sides) + i, jnp.where(row >= column, own[n], own[len(tiles) + n]))
        rows[...] = jnp.zeros(rows.shape, F32)
        for first in (0, 8, DIAG, DIAG + 8):
            for j in range(chunks):
                for part, piece in enumerate(parts(summed(first + j))):
                    r = first + 4 * part + j
                    rows[r : r + 1, :] = piece
        out[out.shape[0] - rows.shape[0] :, :] = rows[...].astype(BF16)


def next_kernel(after, relay, chi, clo, zhi, zlo, off, whole, rows):
    spans = lax.axis_size("z") * lax.axis_size("y")
    width = whole.shape[0]
    chunks = width // LANES
    tiles = triangle(width)
    row = lax.broadcasted_iota(jnp.int32, (LANES, LANES), 0)
    column = lax.broadcasted_iota(jnp.int32, (LANES, LANES), 1)
    sides = [(i, j) for i, j in tiles if i != j]

    @pl.when(doubled(here()[1], spans))
    def _():
        rows[...] = relay[relay.shape[0] - rows.shape[0] :, :].astype(F32)

        def line(r):
            return rows[r : r + 1, :] + rows[r + 4 : r + 5, :]

        def tile(n):
            return relay[n * LANES : (n + 1) * LANES, :].astype(F32)

        def put(i, j, piece):
            whole[i * LANES : (i + 1) * LANES, j * LANES : (j + 1) * LANES] = piece

        for day in range(2):
            for i in range(chunks):
                both = tile(2 * len(sides) + i)
                part = jnp.where(row < column if day else row > column, both, 0.0)
                put(i, i, part + part.T + jnp.where(row == column, line(DIAG + 8 * day + i), 0.0))
            for m, (i, j) in enumerate(sides):
                piece = tile(day * len(sides) + m)
                put(i, j, piece)
                put(j, i, piece.T)
            zhi[day], zlo[day] = split(mm(whole[...], chi[...], clo[...]))
            info = jnp.concatenate([line(8 * day + j) for j in range(chunks)], 1)
            off[day : day + 1, :] = mv(info, chi[...], clo[...])


def next_day(day, state, damping, pthi, ptlo, zhi, zlo, off):
    moved = mv(state, pthi[...], ptlo[...]) * damping
    return moved, moved - mv(moved, zhi[day], zlo[day]) + off[day : day + 1, :]


def owner_kernel(
    own, extra, g4, g3, g1, g2, prior, ahead, pthi, ptlo, chi, clo, after, omhi, omlo, info, mine, start, y, small
):
    ids = here()
    planes = 4
    width = pthi.shape[0]
    chunks = width // LANES
    tiles = triangle(width)
    got = (g1, g2, g3, g4)
    row = lax.broadcasted_iota(jnp.int32, (LANES, LANES), 0)
    column = lax.broadcasted_iota(jnp.int32, (LANES, LANES), 1)
    share, summed, added = sums(extra, got, small)

    def put(day, i, j, piece):
        hi, lo = split(piece)
        omhi[day, i * LANES : (i + 1) * LANES, j * LANES : (j + 1) * LANES] = hi
        omlo[day, i * LANES : (i + 1) * LANES, j * LANES : (j + 1) * LANES] = lo

    sides = [n for n, (i, j) in enumerate(tiles) if i != j]
    middles = [n for n, (i, j) in enumerate(tiles) if i == j]

    def unpack(day):
        for i, n in enumerate(middles):
            both = added(2 * len(sides) + i)
            part = jnp.where(row < column if day else row > column, both, 0.0)
            others = sum(line_of(small, s, DIAG + 8 * day + i) for s in range(1, 5))
            piece = own[day * len(tiles) + n] * share + (part + part.T)
            put(day, i, i, piece + jnp.where(row == column, others, 0.0))
        for m, n in enumerate(sides):
            i, j = tiles[n]
            piece = own[day * len(tiles) + n] * share + added(day * len(sides) + m)
            put(day, i, j, piece)
            put(day, j, i, piece.T)

    for day in range(2):
        info[day] = jnp.concatenate([summed(8 * day + j) for j in range(chunks)], 1)
    held = ids[5]
    source = lax.rem(ids[1] // held - ids[0] + planes, planes)
    for day in range(2):
        for j in range(chunks):
            r = DAMP + 16 * lax.rem(ids[1], held) + 8 * day + j
            mine[day : day + 1, j * LANES : (j + 1) * LANES] = (
                small[source, pl.ds(r, 1), :] + small[source, pl.ds(r + 4, 1), :]
            )
    first = (ids[1] == 0) & (ids[0] == owner_plane(0))
    start[...] = jnp.where(first, prior[...], 0.0)

    @pl.when(first)
    def _():
        unpack(0)
        state = one_day(0, ahead[...], mine, omhi, omlo, info, chi, clo)
        unpack(1)
        y[...] = one_day(1, mv(state, pthi[...], ptlo[...]), mine, omhi, omlo, info, chi, clo)

    @pl.when(jnp.logical_not(first))
    def _():
        for day in range(2):
            unpack(day)
        y[...] = jnp.zeros(y.shape, F32)


def seen(day, omhi, omlo, chi, clo):
    return mm(omhi[day].astype(F32) + omlo[day].astype(F32), chi[...], clo[...])


def early_kernel(after, omhi, omlo, info, chi, clo, pt, damping, b1hi, b1lo, off):
    @pl.when(here()[1] == 1)
    def _():
        off[0:1, :] = mv(info[0], chi[...], clo[...])
        moved = pt[...] * damping[0:1, :]
        b1hi[...], b1lo[...] = split(moved - mm(moved, *split(seen(0, omhi, omlo, chi, clo))))


def maps_kernel(
    after, omhi, omlo, info, chi, clo, pt, damping, old1, old2, old3, b1hi, b1lo, off, b2hi, b2lo
):
    span = here()[1]
    spans = lax.axis_size("z") * lax.axis_size("y")
    relays = (span == spans - 3) | (span == spans - 1)
    parts = ((b1hi, b1lo), (b2hi, b2lo))

    def make(day):
        moved = pt[...] * damping[day : day + 1, :]
        parts[day][0][...], parts[day][1][...] = split(
            moved - mm(moved, *split(seen(day, omhi, omlo, chi, clo)))
        )
        off[day : day + 1, :] = mv(info[day], chi[...], clo[...])

    @pl.when(jnp.logical_not(relays | (span == 1)))
    def _():
        make(0)

    @pl.when(jnp.logical_not(relays))
    def _():
        make(1)


def second_kernel(acc, got, mine, b1hi, b1lo, off, omhi, omlo, info, chi, clo, pthi, ptlo, total, y):
    total[...] = acc[...] + got[...]
    y[...] = jnp.zeros(y.shape, F32)

    @pl.when(here()[1] == 1)
    def _():
        state = mv(acc[...] + got[...], b1hi[...], b1lo[...]) + off[0:1, :]
        ahead = mv(state, pthi[...], ptlo[...])
        y[...] = one_day(1, ahead, mine, omhi, omlo, info, chi, clo)


def both_kernel(after, b1hi, b1lo, b2hi, b2lo, off, bchi, bclo, offset):
    both = jnp.dot(b1hi[...], b2hi[...], preferred_element_type=F32) + (
        jnp.dot(b1lo[...], b2hi[...], preferred_element_type=F32)
        + jnp.dot(b1hi[...], b2lo[...], preferred_element_type=F32)
    )
    bchi[...], bclo[...] = split(both)
    offset[...] = mv(off[0:1, :], b2hi[...], b2lo[...]) + off[1:2, :]


def hop_kernel(after, acc, got, bchi, bclo, offset, total, y):
    state = acc[...] + got[...]
    total[...] = state
    y[...] = mv(state, bchi[...], bclo[...]) + offset[...]


def days_kernel(acc, got, b1hi, b1lo, b2hi, b2lo, off, total, y):
    state = acc[...] + got[...]
    total[...] = state
    state = mv(state, b1hi[...], b1lo[...]) + off[0:1, :]
    y[...] = mv(state, b2hi[...], b2lo[...]) + off[1:2, :]


def double_kernel(after, acc, got, bchi, bclo, offset, table, pthi, ptlo, zhi, zlo, off, total, y):
    spans = table.shape[0] // 2
    total[...] = acc[...] + got[...]
    y[...] = jnp.zeros(y.shape, F32)

    @pl.when(here()[1] == spans - 4)
    def _():
        state = mv(acc[...] + got[...], bchi[...], bclo[...]) + offset[...]
        for day in range(2):
            r = 2 * (spans - 3) + day
            _, state = next_day(day, state, table[r : r + 1, :], pthi, ptlo, zhi, zlo, off)
        y[...] = state


def whole_of(hi, lo):
    return hi[...].astype(F32) + lo[...].astype(F32)


def pairs_kernel(skip, after, table, mthi, mtlo, khi, klo):
    spans = table.shape[0] // 2

    @pl.when(here()[1] == spans - 2)
    def _():
        @pl.loop(0, khi.shape[0])
        def _(k):
            scaled = whole_of(mthi, mtlo) * table[pl.ds(2 * (spans - 3 - skip - k) + 1, 1), :]
            khi[k], klo[k] = split(mm(scaled, mthi[...], mtlo[...]))


def last_kernel(
    acc, got, b1hi, b1lo, b2hi, b2lo, bchi, bclo, off, offset, table, pthi, ptlo, mthi, mtlo,
    zhi, zlo, next_off, khi, klo, more_khi, more_klo, out, shares, means,
):
    span = here()[1]
    total, width = shares.shape
    spans = total // 2
    chunks = width // LANES
    twice = doubled(span, spans)
    shares[...] = jnp.zeros(shares.shape, F32)

    def step(k, v):
        t = 2 * span - 1 - k
        v = mv(v * table[pl.ds(t + 1, 1), :], mthi[...], mtlo[...])
        shares[pl.ds(t, 1), :] = v
        return v

    def own_days(const, damped):
        n = len(const)
        v = const[-1]
        shares[pl.ds(2 * span + n - 1, 1), :] = v
        for i in range(n - 2, -1, -1):
            v = const[i] + mv(v * damped[i], mthi[...], mtlo[...])
            shares[pl.ds(2 * span + i, 1), :] = v
        means[4:5, :] = v

    @pl.when(span < spans - 4)
    def _():
        state = acc[...] + got[...]
        one = mv(state, b1hi[...], b1lo[...]) + off[0:1, :]
        two = mv(one, b2hi[...], b2lo[...]) + off[1:2, :]
        both = jnp.concatenate([one, two], 0)
        damped = [table[pl.ds(2 * span + 1 + i, 1), :] for i in range(2)]
        ahead = jnp.concatenate(damped, 0)
        const = both - few(few(both, pthi[...], ptlo[...]) * ahead * ahead, mthi[...], mtlo[...])
        means[0:2, :] = both
        own_days([const[0:1], const[1:2]], damped)

    @pl.when(twice)
    def _():
        state = acc[...] + got[...]
        rows = [
            mv(state, b1hi[...], b1lo[...]) + off[0:1, :],
            mv(state, bchi[...], bclo[...]) + offset[...],
        ]
        damped = [table[pl.ds(2 * span + 1 + i, 1), :] for i in range(3)]
        ahead = [mv(rows[0], pthi[...], ptlo[...]) * damped[0]]
        for day in range(2):
            moved, after = next_day(day, rows[-1], damped[1 + day], pthi, ptlo, zhi, zlo, next_off)
            ahead.append(moved)
            rows.append(after)
        taken = [a * d for a, d in zip(ahead, damped)]
        taken = few(jnp.concatenate(taken + [jnp.zeros((1, width), F32)], 0), mthi[...], mtlo[...])
        means[0:4, :] = jnp.concatenate(rows, 0)
        means[5:8, :] = jnp.concatenate(rows[:3], 0) - taken[0:3]
        means[4:5, :] = rows[3]

    @pl.when(span == spans - 4)
    def _():
        beyond = table[pl.ds(2 * span + 4, 1), :]
        four = means[3:4, :]
        ahead = mv(four, pthi[...], ptlo[...]) * beyond * beyond
        means[4:5, :] = four - mv(ahead, mthi[...], mtlo[...])

    @pl.when(twice)
    def _():
        const = [means[5:6, :], means[6:7, :], means[7:8, :], means[4:5, :]]
        own_days(const, [table[pl.ds(2 * span + 1 + i, 1), :] for i in range(3)])

    @pl.when(span < spans - 2)
    def _():
        lax.fori_loop(0, jnp.where((span < spans - 4) | twice, 2 * span, 0), step, means[4:5, :])

    @pl.when(span == spans - 2)
    def _():
        v, damped_rows = means[4:5, :], []
        pairs = [(a, b, k) for a, b in ((khi, klo), (more_khi, more_klo)) for k in range(a.shape[0])]
        for n, (a, b, k) in enumerate(pairs):
            t = 2 * (spans - 2 - n)
            damped_rows.append(v * table[t : t + 1, :])
            v = mv(damped_rows[-1], a[k], b[k])
            shares[t - 2 : t - 1, :] = v
        batch = jnp.concatenate(damped_rows + [jnp.zeros((1, width), F32)] * (-len(damped_rows) % 8), 0)
        batch = mm(batch, mthi[...], mtlo[...])
        for n in range(len(pairs)):
            t = 2 * (spans - 2 - n)
            shares[t - 1 : t, :] = batch[n : n + 1]
        lax.fori_loop(2 * len(pairs), 2 * span, step, v)

    for c in range(spans):
        for q in range(chunks):
            out[c * chunks + q, 0:2, :] = shares[2 * c : 2 * c + 2, q * LANES : (q + 1) * LANES]
    for q in range(chunks):
        out[span * chunks + q, 2:4, :] = means[0:2, q * LANES : (q + 1) * LANES]

    @pl.when(twice)
    def _():
        for q in range(chunks):
            out[(span + 1) * chunks + q, 2:4, :] = means[2:4, q * LANES : (q + 1) * LANES]


def add_kernel(parts, filt, smooth):
    spans = parts.shape[0] // 4
    owners = [*range(spans - 4), spans - 4, spans - 2]
    filt[...] = parts[here()[4], 2:4, :]
    smooth[...] = sum(parts[owner_plane(c) * spans + (place(c) | 1), 0:2, :] for c in owners)


def local(
    records,
    obs_values,
    block_day,
    block_count,
    propagator_matrix,
    analysis_cov,
    unattenuated_multiplier,
    damping,
    prior_mean,
):
    planes, held, peers = (lax.axis_size(a) for a in ("z", "y", "obs"))
    spans = planes * held
    blocks = block_day.shape[0]
    slots = records.shape[0] // blocks
    width = records.shape[1]
    days = damping.shape[0]
    assert planes == peers == 4 and days == 2 and slots == LANES and blocks == spans
    everyone = ("z", "y", "obs")

    def owner(span):
        return owner_plane(span) * spans + (place(span) | 1)

    tiles = len(triangle(width))
    extra_rows = DAMP + 16 * held
    chunks = width // LANES
    full, row = (width, width), ((1, width), F32)
    sent = run(
        pack_kernel,
        [((blocks, chunks * slots + EXTRA, LANES), BF16)],
        [
            (x, HBM)
            for x in (
                block_day,
                block_count,
                records,
                obs_values.reshape(blocks, slots),
                prior_mean.reshape(1, -1),
                damping,
            )
        ],
        [
            pltpu.SMEM((blocks,), jnp.int32),
            pltpu.SMEM((blocks,), jnp.int32),
            pltpu.VMEM((blocks, slots), BF16),
            pltpu.VMEM((1, width // peers), F32),
            pltpu.VMEM((days, width), F32),
            pltpu.VMEM((blocks, slots, width), BF16),
            pltpu.VMEM((blocks, chunks * slots + EXTRA, LANES), BF16),
            pltpu.SemaphoreType.DMA((5 + 2 * blocks,)),
        ],
        limit=60,
        outs=HBM,
    )[0]
    got = lax.all_to_all(sent, ("y", "obs"), split_axis=0, concat_axis=0, tiled=True)
    span_slots = min(blocks, 8) * slots
    own, extra, pay, prior, gain = run(
        gram_kernel,
        [
            ((2 * tiles, LANES, LANES), F32),
            ((extra_rows, LANES), F32),
            (((2 * tiles - chunks) * LANES + extra_rows, LANES), BF16),
            row,
            (unattenuated_multiplier.shape, F32),
        ],
        [got, unattenuated_multiplier],
        [pltpu.VMEM((width, span_slots), BF16), pltpu.VMEM((16, span_slots), BF16)],
        flops=4 * width * width * blocks * slots,
    )
    def swap(x, bit):
        return lax.ppermute(x, "obs", [(i, i ^ bit) for i in range(peers)])

    def plane_sum(s):
        return lax.ppermute(
            pay, everyone, [((owner_plane(p) + s) % planes * spans + place(p), owner(p)) for p in range(spans)]
        )

    fourth = lax.ppermute(
        pay, everyone, [(2 * spans + place(p), owner(p)) for p in range(spans) if place(p) % 2 == 0]
    )
    second, first, third = plane_sum(2), plane_sum(1), plane_sum(3)
    (gains,) = run(stack_kernel, [((2,) + gain.shape, F32)], [gain, swap(gain, 2)])
    mthi, mtlo = run(gain_kernel, [(full, BF16)] * 2, [gains, swap(gains, 1)])
    pt, pthi, ptlo, chi, clo, ahead = run(
        prep_kernel, [(full, F32)] + [(full, BF16)] * 4 + [row], [propagator_matrix, analysis_cov, prior]
    )
    smalls = pltpu.VMEM((planes + 1, extra_rows, LANES), F32)
    omhi, omlo, info, mine, acc, y = run(
        owner_kernel,
        [((days,) + full, BF16)] * 2 + [((days, 1, width), F32), ((days, width), F32), row, row],
        [
            own, extra, fourth, third, first, second, prior, ahead, pthi, ptlo, chi, clo, (mthi, ANY)
        ],
        [smalls],
    )
    (packed,) = run(
        relay_kernel,
        [(pay.shape, BF16)],
        [(y, ANY), own, extra, fourth, third, first, second],
        [smalls, pltpu.VMEM((extra_rows, LANES), F32)],
    )
    relay = lax.ppermute(
        packed, everyone, [(owner(p + 1), owner(p)) for p in (spans - 4, spans - 2)]
    )
    chain = [*range(spans - 3), spans - 2]
    half = [(full, BF16)] * 2
    for k, (source, target) in enumerate(zip(chain, chain[1:])):
        received = lax.ppermute(y, everyone, [(owner(source), owner(target))])
        if k == 0:
            given = [omhi, omlo, info, chi, clo, pt, mine]
            b1hi, b1lo, off = run(
                early_kernel, half + [((8, width), F32)], [(y, ANY), *given], flops=12 * width**3
            )
            acc, y = run(
                second_kernel,
                [row, row],
                [acc, received, mine, b1hi, b1lo, off, omhi, omlo, info, chi, clo, pthi, ptlo],
            )
            b1hi, b1lo, off, b2hi, b2lo = run(
                maps_kernel,
                half + [((8, width), F32)] + half,
                [(y, ANY), *given, b1hi, b1lo, off],
                flops=24 * width**3,
                same={8: 0, 9: 1, 10: 2},
            )
        elif k == 1:
            acc, y = run(days_kernel, [row, row], [acc, received, b1hi, b1lo, b2hi, b2lo, off])
            bchi, bclo, offset = run(
                both_kernel, half + [row], [(y, ANY), b1hi, b1lo, b2hi, b2lo, off]
            )
            (table,) = run(
                table_kernel,
                [((spans * days, width), F32)],
                [(offset, ANY), extra, first, second, third],
                [smalls],
            )
            khi, klo = run(
                functools.partial(pairs_kernel, 0), [((2,) + full, BF16)] * 2, [(y, ANY), table, mthi, mtlo]
            )
        elif target == spans - 4:
            nexthi, nextlo, next_off = run(
                next_kernel,
                [((days,) + full, BF16)] * 2 + [((8, width), F32)],
                [(y, ANY), relay, chi, clo],
                [pltpu.VMEM(full, F32), pltpu.VMEM((extra_rows, LANES), F32)],
            )
            acc, y = run(
                double_kernel,
                [row, row],
                [
                    (nexthi, ANY), acc, received, bchi, bclo, offset, table, pthi, ptlo, nexthi, nextlo, next_off
                ],
            )
        elif target != spans - 2:
            acc, y = run(hop_kernel, [row, row], [(khi, ANY), acc, received, bchi, bclo, offset])
        if target == spans - 4:
            more_khi, more_klo = run(
                functools.partial(pairs_kernel, 2), [((4,) + full, BF16)] * 2, [(y, ANY), table, mthi, mtlo]
            )
    (answer,) = run(
        last_kernel,
        [((spans * peers, 8, LANES), F32)],
        [
            acc, received, b1hi, b1lo, b2hi, b2lo, bchi, bclo, off, offset, table, pthi, ptlo, mthi, mtlo,
            nexthi, nextlo, next_off, khi, klo, more_khi, more_klo,
        ],
        [pltpu.VMEM((spans * days, width), F32), pltpu.VMEM((8, width), F32)],
    )
    parts = lax.all_to_all(answer, everyone, split_axis=0, concat_axis=0, tiled=True)
    out = ((days, LANES), F32)
    return run(add_kernel, [out, out], [parts])


def solution(mesh):
    spans, peers = mesh.devices.shape
    finer = jax.sharding.Mesh(mesh.devices.reshape(peers, spans // peers, peers), ("z", "y", "obs"))
    tm = ("z", "y")
    mapped = jax.shard_map(
        local,
        mesh=finer,
        in_specs=(
            P(("z", "y", "obs"), None),
            P(("z", "y", "obs")),
            P(("z", "y", "obs")),
            P(("z", "y", "obs")),
            P(),
            P(),
            P("obs", None),
            P(tm, None),
            P("obs"),
        ),
        out_specs=(P(tm, "obs"), P(tm, "obs")),
        check_vma=False,
    )
    return lambda *args: tuple(mapped(*args))
```

```python
import functools

import jax
import jax.numpy as jnp
from jax import lax
from jax.experimental import pallas as pl
from jax.experimental.pallas import tpu as pltpu
from jax.sharding import PartitionSpec as P

LANES = 128
F32, BF16 = jnp.float32, jnp.bfloat16
VMEM = pl.BlockSpec(memory_space=pltpu.VMEM)
SMEM = pl.BlockSpec(memory_space=pltpu.SMEM)
ANY = pl.BlockSpec(memory_space=pl.ANY)
HBM = pl.BlockSpec(memory_space=pltpu.HBM)


def run(body, out, ins, scratch=(), limit=16, flops=0, outs=VMEM, same=None):
    specs = [x[1] if isinstance(x, tuple) else VMEM for x in ins]
    arrays = [x[0] if isinstance(x, tuple) else x for x in ins]
    moved = sum(a.size * a.dtype.itemsize for a in arrays)
    return pl.pallas_call(
        body,
        out_shape=[jax.ShapeDtypeStruct(s, d) for s, d in out],
        in_specs=specs,
        out_specs=[outs] * len(out),
        scratch_shapes=list(scratch),
        input_output_aliases=same or {},
        compiler_params=pltpu.CompilerParams(vmem_limit_bytes=limit * 1024 * 1024),
        cost_estimate=pl.CostEstimate(flops=flops, bytes_accessed=moved, transcendentals=0),
    )(*arrays)


def here():
    z, y, o = (lax.axis_index(a) for a in ("z", "y", "obs"))
    held, peers = lax.axis_size("y"), lax.axis_size("obs")
    spans = held * peers
    at = y * peers + o
    seat = jnp.where(z == 1, at - lax.rem(at, 2), at) ^ (spans // 2 + 1)
    span = seat
    for bit in range(1, spans.bit_length()):
        span = span ^ (seat >> bit)
    c = z * held + y
    kept = jnp.where((c == spans - 3) | (c == spans - 1), c - 1, c)
    seat = place(kept)
    return z, span, o, c, (1 + (seat & 1)) * spans + (seat | 1), held


def doubled(span, spans):
    return (span == spans - 4) | (span == spans - 2)


def triangle(width):
    parts = width // LANES
    return [(i, j) for i in range(parts) for j in range(i + 1)]


def split(x):
    hi = x.astype(BF16)
    return hi, (x - hi.astype(F32)).astype(BF16)


def mm(x, hi, lo):
    xhi, xlo = split(x)
    dot = functools.partial(jnp.dot, preferred_element_type=F32)
    return dot(xhi, hi) + (dot(xlo, hi) + dot(xhi, lo))


def mv(x, hi, lo):
    wide = jnp.broadcast_to(x, (8, x.shape[1]))
    row = lax.broadcasted_iota(jnp.int32, wide.shape, 0)
    top = wide.astype(BF16).astype(F32)
    both = jnp.where(row == 0, top, jnp.where(row == 1, wide - top, 0.0)).astype(BF16)
    first = jnp.dot(both, hi, preferred_element_type=F32)
    second = jnp.dot(both, lo, preferred_element_type=F32)
    return first[0:1] + (first[1:2] + second[0:1])


def parts(x):
    top = x.astype(BF16).astype(F32)
    return [top, (x - top).astype(BF16).astype(F32)]


def place(span):
    return span ^ (span >> 1) ^ (lax.axis_size("z") * lax.axis_size("y") // 2 + 1)


def owner_plane(span):
    return 1 + place(span) % 2


EXTRA = 8
DIAG, DAMP = 16, 32


def pack_kernel(
    day, count, rows, values, prior, damping, out, day_s, count_s, values_v, prior_v, damping_v, rows_v, stage, sems
):
    blocks = out.shape[0]
    slots = rows_v.shape[1]
    chunks = rows_v.shape[2] // LANES
    small = [(day, day_s), (count, count_s), (values, values_v), (prior, prior_v), (damping, damping_v)]
    copies = [pltpu.make_async_copy(src, dst, sems.at[n]) for n, (src, dst) in enumerate(small)]
    large = [
        pltpu.make_async_copy(rows.at[pl.ds(k * slots, slots)], rows_v.at[k], sems.at[len(small) + k])
        for k in range(blocks)
    ]
    sends = [
        pltpu.make_async_copy(stage.at[place(k)], out.at[place(k)], sems.at[len(small) + blocks + k])
        for k in range(blocks)
    ]
    for copy in copies + large:
        copy.start()
    for copy in copies:
        copy.wait()
    mine = damping_v[:, 0:LANES]
    for q in range(1, chunks):
        mine = jnp.where(lax.axis_index("obs") == q, damping_v[:, q * LANES : (q + 1) * LANES], mine)
    below = parts(prior_v[...]) + parts(mine)
    below = jnp.concatenate(below, 0)
    held = values_v[...].astype(F32)
    lane = lax.broadcasted_iota(jnp.int32, (1, LANES), 1)
    for k in range(blocks):
        marks = jnp.where(lane < LANES // 2, day_s[k], count_s[k]).astype(F32)
        stage[place(k), chunks * slots : chunks * slots + EXTRA, :] = jnp.concatenate(
            [held[k : k + 1, :], marks, below], 0
        ).astype(BF16)
    for k in range(blocks):
        large[k].wait()
        for j in range(chunks):
            stage[place(k), j * slots : (j + 1) * slots, :] = rows_v[k, :, j * LANES : (j + 1) * LANES]
        sends[k].start()
    for copy in sends:
        copy.wait()


def gram_kernel(got, gain, own, extra, pay, prior, gain_out, turned, marks):
    blocks = got.shape[0]
    chunks = turned.shape[0] // LANES
    slots = (got.shape[1] - EXTRA) // chunks
    width = chunks * LANES
    tiles = triangle(width)
    group = min(blocks, 8)
    half = 2 * LANES
    gain_out[...] = gain[...]
    extra[...] = jnp.zeros(extra.shape, F32)

    def below(k):
        return got[k, chunks * slots : chunks * slots + EXTRA, :].astype(F32)

    def one(first, fresh):
        for k in range(group):
            at = slice(k * slots, (k + 1) * slots)
            line = below(first + k)
            slot = lax.broadcasted_iota(jnp.int32, (1, slots), 1).astype(F32)
            valid = slot < jnp.broadcast_to(line[1:2, LANES - 1 : LANES], (1, slots))
            day = jnp.broadcast_to(line[1:2, 0:1], (1, slots))
            kept = [jnp.where(valid & (day == d), 1.0, 0.0) for d in (0.0, 1.0)]
            marks[:, at] = jnp.concatenate(
                kept + [kept[0] * line[0:1], kept[1] * line[0:1], jnp.zeros((12, slots), F32)], 0
            ).astype(BF16)
            for j in range(chunks):
                turned[j * LANES : (j + 1) * LANES, at] = got[first + k, j * slots : (j + 1) * slots, :].T
        source = jnp.concatenate(
            [
                jnp.concatenate([got[first + k, j * slots : (j + 1) * slots, :] for j in range(chunks)], 1)
                for k in range(group)
            ],
            0,
        )
        info = jnp.dot(marks[...], source, preferred_element_type=F32)
        for d in range(2):
            for top in range(0, width, half):
                left = turned[top : top + half, :] * marks[d : d + 1, :]
                block = jnp.dot(left, source[:, : top + half], preferred_element_type=F32)
                for n, (i, j) in enumerate(tiles):
                    if top <= i * LANES < top + half:
                        r = i * LANES - top
                        piece = block[r : r + LANES, j * LANES : (j + 1) * LANES]
                        at = d * len(tiles) + n
                        own[at] = piece if fresh else own[at] + piece
            for j in range(chunks):
                piece = info[2 + d : 3 + d, j * LANES : (j + 1) * LANES]
                r = 8 * d + j
                extra[r : r + 1, :] = piece if fresh else extra[r : r + 1, :] + piece

    if blocks == group:
        one(0, True)
    else:
        own[...] = jnp.zeros(own.shape, F32)

        @pl.loop(0, blocks // group)
        def _(g):
            one(g * group, False)

    row = lax.broadcasted_iota(jnp.int32, (LANES, LANES), 0)
    column = lax.broadcasted_iota(jnp.int32, (LANES, LANES), 1)
    sides = [n for n, (i, j) in enumerate(tiles) if i != j]
    middles = [n for n, (i, j) in enumerate(tiles) if i == j]

    def send(n, piece):
        pay[n * LANES : (n + 1) * LANES, :] = piece.astype(BF16)

    for d in range(2):
        for part, piece in enumerate(parts(extra[8 * d : 8 * d + chunks, :])):
            extra[8 * d + 4 * part : 8 * d + 4 * part + chunks, :] = piece
        for m, n in enumerate(sides):
            send(d * len(sides) + m, own[d * len(tiles) + n])
    for i, n in enumerate(middles):
        squares = [own[d * len(tiles) + n] for d in range(2)]
        send(2 * len(sides) + i, jnp.where(row >= column, squares[0], squares[1]))
        for d in range(2):
            line = jnp.sum(jnp.where(row == column, squares[d], 0.0), axis=0, keepdims=True)
            for part, piece in enumerate(parts(line)):
                r = DIAG + 8 * d + 4 * part + i
                extra[r : r + 1, :] = piece
    for q in range(chunks):
        line = below(q)
        prior[:, q * LANES : (q + 1) * LANES] = line[2:3] + line[3:4]
    for y in range(blocks // 4):
        for q in range(chunks):
            line = below(4 * y + q)
            for part in range(2):
                for d in range(2):
                    r = DAMP + 16 * y + 8 * d + 4 * part + q
                    extra[r : r + 1, :] = line[4 + 2 * part + d : 5 + 2 * part + d]
    pay[pay.shape[0] - extra.shape[0] :, :] = extra[...].astype(BF16)


def prep_kernel(trans, cov, prior, pt, pthi, ptlo, chi, clo, ahead):
    whole = trans[...].T
    pt[...] = whole
    pthi[...], ptlo[...] = split(whole)
    chi[...], clo[...] = split(cov[...])
    ahead[...] = mv(prior[...], pthi[...], ptlo[...])


def stack_kernel(one, two, out):
    out[0] = one[...]
    out[1] = two[...]


def gain_kernel(held, got, mthi, mtlo):
    ids = here()
    rows = held.shape[1]
    for step, part in enumerate((held.at[0], got.at[0], held.at[1], got.at[1])):
        holder = ids[2] ^ step
        at = pl.ds(pl.multiple_of(holder * rows, rows), rows)
        hi, lo = split(part[...].T)
        mthi[:, at] = hi
        mtlo[:, at] = lo


def few(x, hi, lo):
    n = x.shape[0]
    top = x.astype(BF16).astype(F32)
    blank = [jnp.zeros((8 - 2 * n, x.shape[1]), F32)] if n < 4 else []
    both = jnp.concatenate([top, x - top] + blank, 0).astype(BF16)
    first = jnp.dot(both, hi, preferred_element_type=F32)
    second = jnp.dot(both, lo, preferred_element_type=F32)
    return first[0:n] + (first[n : 2 * n] + second[0:n])


def one_day(day, ahead, damping, omhi, omlo, info, chi, clo):
    moved = ahead * damping[day : day + 1, :]
    gap = mv(moved, omhi[day], omlo[day]) - info[day]
    return moved - mv(gap, chi[...], clo[...])


def spread(extra, got, small):
    small[0] = extra[...]
    for s, part in enumerate(got):
        small[s + 1] = part[part.shape[0] - extra.shape[0] :, :].astype(F32)


def line_of(small, s, first):
    return small[s, first : first + 1, :] + small[s, first + 4 : first + 5, :]


def table_kernel(after, extra, g1, g2, g3, table, small):
    ids = here()
    planes = 4
    chunks = table.shape[1] // LANES
    held = table.shape[0] // 2 // planes
    spread(extra, (g1, g2, g3), small)
    for s in range(planes):
        plane = lax.rem(ids[0] + s, planes)
        for k in range(held):
            for day in range(2):
                table[pl.ds(2 * (plane * held + k) + day, 1), :] = jnp.concatenate(
                    [line_of(small, s, DAMP + 16 * k + 8 * day + j) for j in range(chunks)], 1
                )


def sums(extra, got, small):
    share = jnp.where(here()[0] == 2, 1.0, 0.0)
    spread(extra, got, small)

    def summed(first):
        others = line_of(small, 1, first) + line_of(small, 2, first) + (line_of(small, 3, first) + line_of(small, 4, first))
        return line_of(small, 0, first) * share + others

    def added(n):
        at = slice(n * LANES, (n + 1) * LANES)
        one, two, three, four = (part[at].astype(F32) for part in got)
        return (one + two) + (three + four)

    return share, summed, added


def relay_kernel(after, own, extra, g4, g3, g1, g2, out, small, rows):
    span = here()[1]
    spans = lax.axis_size("z") * lax.axis_size("y")
    chunks = 4
    tiles = triangle(chunks * LANES)
    row = lax.broadcasted_iota(jnp.int32, (LANES, LANES), 0)
    column = lax.broadcasted_iota(jnp.int32, (LANES, LANES), 1)
    sides = [n for n, (i, j) in enumerate(tiles) if i != j]
    middles = [n for n, (i, j) in enumerate(tiles) if i == j]

    @pl.when((span == spans - 3) | (span == spans - 1))
    def _():
        share, summed, added = sums(extra, (g1, g2, g3, g4), small)

        def send(n, piece):
            out[n * LANES : (n + 1) * LANES, :] = (piece * share + added(n)).astype(BF16)

        for d in range(2):
            for m, n in enumerate(sides):
                send(d * len(sides) + m, own[d * len(tiles) + n])
        for i, n in enumerate(middles):
            send(2 * len(sides) + i, jnp.where(row >= column, own[n], own[len(tiles) + n]))
        rows[...] = jnp.zeros(rows.shape, F32)
        for first in (0, 8, DIAG, DIAG + 8):
            for j in range(chunks):
                for part, piece in enumerate(parts(summed(first + j))):
                    r = first + 4 * part + j
                    rows[r : r + 1, :] = piece
        out[out.shape[0] - rows.shape[0] :, :] = rows[...].astype(BF16)


def next_kernel(after, relay, chi, clo, zhi, zlo, off, whole, rows):
    spans = lax.axis_size("z") * lax.axis_size("y")
    width = whole.shape[0]
    chunks = width // LANES
    tiles = triangle(width)
    row = lax.broadcasted_iota(jnp.int32, (LANES, LANES), 0)
    column = lax.broadcasted_iota(jnp.int32, (LANES, LANES), 1)
    sides = [(i, j) for i, j in tiles if i != j]

    @pl.when(doubled(here()[1], spans))
    def _():
        rows[...] = relay[relay.shape[0] - rows.shape[0] :, :].astype(F32)

        def line(r):
            return rows[r : r + 1, :] + rows[r + 4 : r + 5, :]

        def tile(n):
            return relay[n * LANES : (n + 1) * LANES, :].astype(F32)

        def put(i, j, piece):
            whole[i * LANES : (i + 1) * LANES, j * LANES : (j + 1) * LANES] = piece

        for day in range(2):
            for i in range(chunks):
                both = tile(2 * len(sides) + i)
                part = jnp.where(row < column if day else row > column, both, 0.0)
                put(i, i, part + part.T + jnp.where(row == column, line(DIAG + 8 * day + i), 0.0))
            for m, (i, j) in enumerate(sides):
                piece = tile(day * len(sides) + m)
                put(i, j, piece)
                put(j, i, piece.T)
            zhi[day], zlo[day] = split(mm(whole[...], chi[...], clo[...]))
            info = jnp.concatenate([line(8 * day + j) for j in range(chunks)], 1)
            off[day : day + 1, :] = mv(info, chi[...], clo[...])


def next_day(day, state, damping, pthi, ptlo, zhi, zlo, off):
    moved = mv(state, pthi[...], ptlo[...]) * damping
    return moved, moved - mv(moved, zhi[day], zlo[day]) + off[day : day + 1, :]


def owner_kernel(
    own, extra, g4, g3, g1, g2, prior, ahead, pthi, ptlo, chi, clo, after, omhi, omlo, info, mine, start, y, small
):
    ids = here()
    planes = 4
    width = pthi.shape[0]
    chunks = width // LANES
    tiles = triangle(width)
    got = (g1, g2, g3, g4)
    row = lax.broadcasted_iota(jnp.int32, (LANES, LANES), 0)
    column = lax.broadcasted_iota(jnp.int32, (LANES, LANES), 1)
    share, summed, added = sums(extra, got, small)

    def put(day, i, j, piece):
        hi, lo = split(piece)
        omhi[day, i * LANES : (i + 1) * LANES, j * LANES : (j + 1) * LANES] = hi
        omlo[day, i * LANES : (i + 1) * LANES, j * LANES : (j + 1) * LANES] = lo

    sides = [n for n, (i, j) in enumerate(tiles) if i != j]
    middles = [n for n, (i, j) in enumerate(tiles) if i == j]

    def unpack(day):
        for i, n in enumerate(middles):
            both = added(2 * len(sides) + i)
            part = jnp.where(row < column if day else row > column, both, 0.0)
            others = sum(line_of(small, s, DIAG + 8 * day + i) for s in range(1, 5))
            piece = own[day * len(tiles) + n] * share + (part + part.T)
            put(day, i, i, piece + jnp.where(row == column, others, 0.0))
        for m, n in enumerate(sides):
            i, j = tiles[n]
            piece = own[day * len(tiles) + n] * share + added(day * len(sides) + m)
            put(day, i, j, piece)
            put(day, j, i, piece.T)

    for day in range(2):
        info[day] = jnp.concatenate([summed(8 * day + j) for j in range(chunks)], 1)
    held = ids[5]
    source = lax.rem(ids[1] // held - ids[0] + planes, planes)
    for day in range(2):
        for j in range(chunks):
            r = DAMP + 16 * lax.rem(ids[1], held) + 8 * day + j
            mine[day : day + 1, j * LANES : (j + 1) * LANES] = (
                small[source, pl.ds(r, 1), :] + small[source, pl.ds(r + 4, 1), :]
            )
    first = (ids[1] == 0) & (ids[0] == owner_plane(0))
    start[...] = jnp.where(first, prior[...], 0.0)

    @pl.when(first)
    def _():
        unpack(0)
        state = one_day(0, ahead[...], mine, omhi, omlo, info, chi, clo)
        unpack(1)
        y[...] = one_day(1, mv(state, pthi[...], ptlo[...]), mine, omhi, omlo, info, chi, clo)

    @pl.when(jnp.logical_not(first))
    def _():
        for day in range(2):
            unpack(day)
        y[...] = jnp.zeros(y.shape, F32)


def seen(day, omhi, omlo, chi, clo):
    return mm(omhi[day].astype(F32) + omlo[day].astype(F32), chi[...], clo[...])


def early_kernel(after, omhi, omlo, info, chi, clo, pt, damping, b1hi, b1lo, off):
    @pl.when(here()[1] == 1)
    def _():
        off[0:1, :] = mv(info[0], chi[...], clo[...])
        moved = pt[...] * damping[0:1, :]
        b1hi[...], b1lo[...] = split(moved - mm(moved, *split(seen(0, omhi, omlo, chi, clo))))


def maps_kernel(
    after, omhi, omlo, info, chi, clo, pt, damping, old1, old2, old3, b1hi, b1lo, off, b2hi, b2lo
):
    span = here()[1]
    spans = lax.axis_size("z") * lax.axis_size("y")
    relays = (span == spans - 3) | (span == spans - 1)
    parts = ((b1hi, b1lo), (b2hi, b2lo))

    def make(day):
        moved = pt[...] * damping[day : day + 1, :]
        parts[day][0][...], parts[day][1][...] = split(
            moved - mm(moved, *split(seen(day, omhi, omlo, chi, clo)))
        )
        off[day : day + 1, :] = mv(info[day], chi[...], clo[...])

    @pl.when(jnp.logical_not(relays | (span == 1)))
    def _():
        make(0)

    @pl.when(jnp.logical_not(relays))
    def _():
        make(1)


def second_kernel(acc, got, mine, b1hi, b1lo, off, omhi, omlo, info, chi, clo, pthi, ptlo, total, y):
    total[...] = acc[...] + got[...]
    y[...] = jnp.zeros(y.shape, F32)

    @pl.when(here()[1] == 1)
    def _():
        state = mv(acc[...] + got[...], b1hi[...], b1lo[...]) + off[0:1, :]
        ahead = mv(state, pthi[...], ptlo[...])
        y[...] = one_day(1, ahead, mine, omhi, omlo, info, chi, clo)


def both_kernel(after, b1hi, b1lo, b2hi, b2lo, off, bchi, bclo, offset):
    both = jnp.dot(b1hi[...], b2hi[...], preferred_element_type=F32) + (
        jnp.dot(b1lo[...], b2hi[...], preferred_element_type=F32)
        + jnp.dot(b1hi[...], b2lo[...], preferred_element_type=F32)
    )
    bchi[...], bclo[...] = split(both)
    offset[...] = mv(off[0:1, :], b2hi[...], b2lo[...]) + off[1:2, :]


def hop_kernel(after, acc, got, bchi, bclo, offset, total, y):
    state = acc[...] + got[...]
    total[...] = state
    y[...] = mv(state, bchi[...], bclo[...]) + offset[...]


def days_kernel(acc, got, b1hi, b1lo, b2hi, b2lo, off, total, y):
    state = acc[...] + got[...]
    total[...] = state
    state = mv(state, b1hi[...], b1lo[...]) + off[0:1, :]
    y[...] = mv(state, b2hi[...], b2lo[...]) + off[1:2, :]


def double_kernel(after, acc, got, bchi, bclo, offset, table, pthi, ptlo, zhi, zlo, off, total, y):
    spans = table.shape[0] // 2
    total[...] = acc[...] + got[...]
    y[...] = jnp.zeros(y.shape, F32)

    @pl.when(here()[1] == spans - 4)
    def _():
        state = mv(acc[...] + got[...], bchi[...], bclo[...]) + offset[...]
        for day in range(2):
            r = 2 * (spans - 3) + day
            _, state = next_day(day, state, table[r : r + 1, :], pthi, ptlo, zhi, zlo, off)
        y[...] = state


def whole_of(hi, lo):
    return hi[...].astype(F32) + lo[...].astype(F32)


def pairs_kernel(skip, after, table, mthi, mtlo, khi, klo):
    spans = table.shape[0] // 2

    @pl.when(here()[1] == spans - 2)
    def _():
        @pl.loop(0, khi.shape[0])
        def _(k):
            scaled = whole_of(mthi, mtlo) * table[pl.ds(2 * (spans - 3 - skip - k) + 1, 1), :]
            khi[k], klo[k] = split(mm(scaled, mthi[...], mtlo[...]))


def last_kernel(
    acc, got, b1hi, b1lo, b2hi, b2lo, bchi, bclo, off, offset, table, pthi, ptlo, mthi, mtlo,
    zhi, zlo, next_off, khi, klo, more_khi, more_klo, out, shares, means,
):
    span = here()[1]
    total, width = shares.shape
    spans = total // 2
    chunks = width // LANES
    twice = doubled(span, spans)
    shares[...] = jnp.zeros(shares.shape, F32)

    def step(k, v):
        t = 2 * span - 1 - k
        v = mv(v * table[pl.ds(t + 1, 1), :], mthi[...], mtlo[...])
        shares[pl.ds(t, 1), :] = v
        return v

    def own_days(const, damped):
        n = len(const)
        v = const[-1]
        shares[pl.ds(2 * span + n - 1, 1), :] = v
        for i in range(n - 2, -1, -1):
            v = const[i] + mv(v * damped[i], mthi[...], mtlo[...])
            shares[pl.ds(2 * span + i, 1), :] = v
        means[4:5, :] = v

    @pl.when(span < spans - 4)
    def _():
        state = acc[...] + got[...]
        one = mv(state, b1hi[...], b1lo[...]) + off[0:1, :]
        two = mv(one, b2hi[...], b2lo[...]) + off[1:2, :]
        both = jnp.concatenate([one, two], 0)
        damped = [table[pl.ds(2 * span + 1 + i, 1), :] for i in range(2)]
        ahead = jnp.concatenate(damped, 0)
        const = both - few(few(both, pthi[...], ptlo[...]) * ahead * ahead, mthi[...], mtlo[...])
        means[0:2, :] = both
        own_days([const[0:1], const[1:2]], damped)

    @pl.when(twice)
    def _():
        state = acc[...] + got[...]
        rows = [
            mv(state, b1hi[...], b1lo[...]) + off[0:1, :],
            mv(state, bchi[...], bclo[...]) + offset[...],
        ]
        damped = [table[pl.ds(2 * span + 1 + i, 1), :] for i in range(3)]
        ahead = [mv(rows[0], pthi[...], ptlo[...]) * damped[0]]
        for day in range(2):
            moved, after = next_day(day, rows[-1], damped[1 + day], pthi, ptlo, zhi, zlo, next_off)
            ahead.append(moved)
            rows.append(after)
        taken = [a * d for a, d in zip(ahead, damped)]
        taken = few(jnp.concatenate(taken + [jnp.zeros((1, width), F32)], 0), mthi[...], mtlo[...])
        means[0:4, :] = jnp.concatenate(rows, 0)
        means[5:8, :] = jnp.concatenate(rows[:3], 0) - taken[0:3]
        means[4:5, :] = rows[3]

    @pl.when(span == spans - 4)
    def _():
        beyond = table[pl.ds(2 * span + 4, 1), :]
        four = means[3:4, :]
        ahead = mv(four, pthi[...], ptlo[...]) * beyond * beyond
        means[4:5, :] = four - mv(ahead, mthi[...], mtlo[...])

    @pl.when(twice)
    def _():
        const = [means[5:6, :], means[6:7, :], means[7:8, :], means[4:5, :]]
        own_days(const, [table[pl.ds(2 * span + 1 + i, 1), :] for i in range(3)])

    @pl.when(span < spans - 2)
    def _():
        lax.fori_loop(0, jnp.where((span < spans - 4) | twice, 2 * span, 0), step, means[4:5, :])

    @pl.when(span == spans - 2)
    def _():
        v, damped_rows = means[4:5, :], []
        pairs = [(a, b, k) for a, b in ((khi, klo), (more_khi, more_klo)) for k in range(a.shape[0])]
        for n, (a, b, k) in enumerate(pairs):
            t = 2 * (spans - 2 - n)
            damped_rows.append(v * table[t : t + 1, :])
            v = mv(damped_rows[-1], a[k], b[k])
            shares[t - 2 : t - 1, :] = v
        batch = jnp.concatenate(damped_rows + [jnp.zeros((1, width), F32)] * (-len(damped_rows) % 8), 0)
        batch = mm(batch, mthi[...], mtlo[...])
        for n in range(len(pairs)):
            t = 2 * (spans - 2 - n)
            shares[t - 1 : t, :] = batch[n : n + 1]
        lax.fori_loop(2 * len(pairs), 2 * span, step, v)

    for c in range(spans):
        for q in range(chunks):
            out[c * chunks + q, 0:2, :] = shares[2 * c : 2 * c + 2, q * LANES : (q + 1) * LANES]
    for q in range(chunks):
        out[span * chunks + q, 2:4, :] = means[0:2, q * LANES : (q + 1) * LANES]

    @pl.when(twice)
    def _():
        for q in range(chunks):
            out[(span + 1) * chunks + q, 2:4, :] = means[2:4, q * LANES : (q + 1) * LANES]


def add_kernel(parts, filt, smooth):
    spans = parts.shape[0] // 4
    owners = [*range(spans - 4), spans - 4, spans - 2]
    filt[...] = parts[here()[4], 2:4, :]
    smooth[...] = sum(parts[owner_plane(c) * spans + (place(c) | 1), 0:2, :] for c in owners)


def local(
    records,
    obs_values,
    block_day,
    block_count,
    propagator_matrix,
    analysis_cov,
    unattenuated_multiplier,
    damping,
    prior_mean,
):
    planes, held, peers = (lax.axis_size(a) for a in ("z", "y", "obs"))
    spans = planes * held
    blocks = block_day.shape[0]
    slots = records.shape[0] // blocks
    width = records.shape[1]
    days = damping.shape[0]
    assert planes == peers == 4 and days == 2 and slots == LANES and blocks == spans
    everyone = ("z", "y", "obs")

    def owner(span):
        return owner_plane(span) * spans + (place(span) | 1)

    tiles = len(triangle(width))
    extra_rows = DAMP + 16 * held
    chunks = width // LANES
    full, row = (width, width), ((1, width), F32)
    sent = run(
        pack_kernel,
        [((blocks, chunks * slots + EXTRA, LANES), BF16)],
        [
            (x, HBM)
            for x in (
                block_day,
                block_count,
                records,
                obs_values.reshape(blocks, slots),
                prior_mean.reshape(1, -1),
                damping,
            )
        ],
        [
            pltpu.SMEM((blocks,), jnp.int32),
            pltpu.SMEM((blocks,), jnp.int32),
            pltpu.VMEM((blocks, slots), BF16),
            pltpu.VMEM((1, width // peers), F32),
            pltpu.VMEM((days, width), F32),
            pltpu.VMEM((blocks, slots, width), BF16),
            pltpu.VMEM((blocks, chunks * slots + EXTRA, LANES), BF16),
            pltpu.SemaphoreType.DMA((5 + 2 * blocks,)),
        ],
        limit=60,
        outs=HBM,
    )[0]
    got = lax.all_to_all(sent, ("y", "obs"), split_axis=0, concat_axis=0, tiled=True)
    span_slots = min(blocks, 8) * slots
    own, extra, pay, prior, gain = run(
        gram_kernel,
        [
            ((2 * tiles, LANES, LANES), F32),
            ((extra_rows, LANES), F32),
            (((2 * tiles - chunks) * LANES + extra_rows, LANES), BF16),
            row,
            (unattenuated_multiplier.shape, F32),
        ],
        [got, unattenuated_multiplier],
        [pltpu.VMEM((width, span_slots), BF16), pltpu.VMEM((16, span_slots), BF16)],
        flops=4 * width * width * blocks * slots,
    )
    def swap(x, bit):
        return lax.ppermute(x, "obs", [(i, i ^ bit) for i in range(peers)])

    def plane_sum(s):
        return lax.ppermute(
            pay, everyone, [((owner_plane(p) + s) % planes * spans + place(p), owner(p)) for p in range(spans)]
        )

    fourth = lax.ppermute(
        pay, everyone, [(spans + place(p), owner(p)) for p in range(spans) if place(p) % 2 == 0]
    )
    second, first, third = plane_sum(2), plane_sum(1), plane_sum(3)
    (gains,) = run(stack_kernel, [((2,) + gain.shape, F32)], [gain, swap(gain, 2)])
    mthi, mtlo = run(gain_kernel, [(full, BF16)] * 2, [gains, swap(gains, 1)])
    pt, pthi, ptlo, chi, clo, ahead = run(
        prep_kernel, [(full, F32)] + [(full, BF16)] * 4 + [row], [propagator_matrix, analysis_cov, prior]
    )
    smalls = pltpu.VMEM((planes + 1, extra_rows, LANES), F32)
    omhi, omlo, info, mine, acc, y = run(
        owner_kernel,
        [((days,) + full, BF16)] * 2 + [((days, 1, width), F32), ((days, width), F32), row, row],
        [
            own, extra, fourth, third, first, second, prior, ahead, pthi, ptlo, chi, clo, (mthi, ANY)
        ],
        [smalls],
    )
    (packed,) = run(
        relay_kernel,
        [(pay.shape, BF16)],
        [(y, ANY), own, extra, fourth, third, first, second],
        [smalls, pltpu.VMEM((extra_rows, LANES), F32)],
    )
    relay = lax.ppermute(
        packed, everyone, [(owner(p + 1), owner(p)) for p in (spans - 4, spans - 2)]
    )
    chain = [*range(spans - 3), spans - 2]
    half = [(full, BF16)] * 2
    for k, (source, target) in enumerate(zip(chain, chain[1:])):
        received = lax.ppermute(y, everyone, [(owner(source), owner(target))])
        if k == 0:
            given = [omhi, omlo, info, chi, clo, pt, mine]
            b1hi, b1lo, off = run(
                early_kernel, half + [((8, width), F32)], [(y, ANY), *given], flops=12 * width**3
            )
            acc, y = run(
                second_kernel,
                [row, row],
                [acc, received, mine, b1hi, b1lo, off, omhi, omlo, info, chi, clo, pthi, ptlo],
            )
            b1hi, b1lo, off, b2hi, b2lo = run(
                maps_kernel,
                half + [((8, width), F32)] + half,
                [(y, ANY), *given, b1hi, b1lo, off],
                flops=24 * width**3,
                same={8: 0, 9: 1, 10: 2},
            )
        elif k == 1:
            acc, y = run(days_kernel, [row, row], [acc, received, b1hi, b1lo, b2hi, b2lo, off])
            bchi, bclo, offset = run(
                both_kernel, half + [row], [(y, ANY), b1hi, b1lo, b2hi, b2lo, off]
            )
            (table,) = run(
                table_kernel,
                [((spans * days, width), F32)],
                [(offset, ANY), extra, first, second, third],
                [smalls],
            )
            khi, klo = run(
                functools.partial(pairs_kernel, 0), [((2,) + full, BF16)] * 2, [(y, ANY), table, mthi, mtlo]
            )
        elif target == spans - 4:
            nexthi, nextlo, next_off = run(
                next_kernel,
                [((days,) + full, BF16)] * 2 + [((8, width), F32)],
                [(y, ANY), relay, chi, clo],
                [pltpu.VMEM(full, F32), pltpu.VMEM((extra_rows, LANES), F32)],
            )
            acc, y = run(
                double_kernel,
                [row, row],
                [
                    (nexthi, ANY), acc, received, bchi, bclo, offset, table, pthi, ptlo, nexthi, nextlo, next_off
                ],
            )
        elif target != spans - 2:
            acc, y = run(hop_kernel, [row, row], [(khi, ANY), acc, received, bchi, bclo, offset])
        if target == spans - 4:
            more_khi, more_klo = run(
                functools.partial(pairs_kernel, 2), [((4,) + full, BF16)] * 2, [(y, ANY), table, mthi, mtlo]
            )
    (answer,) = run(
        last_kernel,
        [((spans * peers, 8, LANES), F32)],
        [
            acc, received, b1hi, b1lo, b2hi, b2lo, bchi, bclo, off, offset, table, pthi, ptlo, mthi, mtlo,
            nexthi, nextlo, next_off, khi, klo, more_khi, more_klo,
        ],
        [pltpu.VMEM((spans * days, width), F32), pltpu.VMEM((8, width), F32)],
    )
    parts = lax.all_to_all(answer, everyone, split_axis=0, concat_axis=0, tiled=True)
    out = ((days, LANES), F32)
    return run(add_kernel, [out, out], [parts])


def solution(mesh):
    spans, peers = mesh.devices.shape
    finer = jax.sharding.Mesh(mesh.devices.reshape(peers, spans // peers, peers), ("z", "y", "obs"))
    tm = ("z", "y")
    mapped = jax.shard_map(
        local,
        mesh=finer,
        in_specs=(
            P(("z", "y", "obs"), None),
            P(("z", "y", "obs")),
            P(("z", "y", "obs")),
            P(("z", "y", "obs")),
            P(),
            P(),
            P("obs", None),
            P(tm, None),
            P("obs"),
        ),
        out_specs=(P(tm, "obs"), P(tm, "obs")),
        check_vma=False,
    )
    return lambda *args: tuple(mapped(*args))
```

```python
import functools

import jax
import jax.numpy as jnp
from jax import lax
from jax.experimental import pallas as pl
from jax.experimental.pallas import tpu as pltpu
from jax.sharding import PartitionSpec as P

LANES = 128
F32, BF16 = jnp.float32, jnp.bfloat16
VMEM = pl.BlockSpec(memory_space=pltpu.VMEM)
SMEM = pl.BlockSpec(memory_space=pltpu.SMEM)
ANY = pl.BlockSpec(memory_space=pl.ANY)
HBM = pl.BlockSpec(memory_space=pltpu.HBM)


def run(body, out, ins, scratch=(), limit=16, flops=0, outs=VMEM, same=None):
    specs = [x[1] if isinstance(x, tuple) else VMEM for x in ins]
    arrays = [x[0] if isinstance(x, tuple) else x for x in ins]
    moved = sum(a.size * a.dtype.itemsize for a in arrays)
    return pl.pallas_call(
        body,
        out_shape=[jax.ShapeDtypeStruct(s, d) for s, d in out],
        in_specs=specs,
        out_specs=[outs] * len(out),
        scratch_shapes=list(scratch),
        input_output_aliases=same or {},
        compiler_params=pltpu.CompilerParams(vmem_limit_bytes=limit * 1024 * 1024),
        cost_estimate=pl.CostEstimate(flops=flops, bytes_accessed=moved, transcendentals=0),
    )(*arrays)


def here():
    z, y, o = (lax.axis_index(a) for a in ("z", "y", "obs"))
    held, peers = lax.axis_size("y"), lax.axis_size("obs")
    spans = held * peers
    at = y * peers + o
    seat = jnp.where(z == 1, at - lax.rem(at, 2), at) ^ (spans // 2 + 1)
    span = seat
    for bit in range(1, spans.bit_length()):
        span = span ^ (seat >> bit)
    c = z * held + y
    kept = jnp.where((c == spans - 3) | (c == spans - 1), c - 1, c)
    seat = place(kept)
    return z, span, o, c, (1 + (seat & 1)) * spans + (seat | 1), held


def doubled(span, spans):
    return (span == spans - 4) | (span == spans - 2)


def triangle(width):
    parts = width // LANES
    return [(i, j) for i in range(parts) for j in range(i + 1)]


def split(x):
    hi = x.astype(BF16)
    return hi, (x - hi.astype(F32)).astype(BF16)


def mm(x, hi, lo):
    xhi, xlo = split(x)
    dot = functools.partial(jnp.dot, preferred_element_type=F32)
    return dot(xhi, hi) + (dot(xlo, hi) + dot(xhi, lo))


def mv(x, hi, lo):
    wide = jnp.broadcast_to(x, (8, x.shape[1]))
    row = lax.broadcasted_iota(jnp.int32, wide.shape, 0)
    top = wide.astype(BF16).astype(F32)
    both = jnp.where(row == 0, top, jnp.where(row == 1, wide - top, 0.0)).astype(BF16)
    first = jnp.dot(both, hi, preferred_element_type=F32)
    second = jnp.dot(both, lo, preferred_element_type=F32)
    return first[0:1] + (first[1:2] + second[0:1])


def parts(x):
    top = x.astype(BF16).astype(F32)
    return [top, (x - top).astype(BF16).astype(F32)]


def place(span):
    return span ^ (span >> 1) ^ (lax.axis_size("z") * lax.axis_size("y") // 2 + 1)


def owner_plane(span):
    return 1 + place(span) % 2


EXTRA = 8
DIAG, DAMP = 16, 32


def pack_kernel(
    day, count, rows, values, prior, damping, out, day_s, count_s, values_v, prior_v, damping_v, rows_v, stage, sems
):
    blocks = out.shape[0]
    slots = rows_v.shape[1]
    chunks = rows_v.shape[2] // LANES
    small = [(day, day_s), (count, count_s), (values, values_v), (prior, prior_v), (damping, damping_v)]
    copies = [pltpu.make_async_copy(src, dst, sems.at[n]) for n, (src, dst) in enumerate(small)]
    large = [
        pltpu.make_async_copy(rows.at[pl.ds(k * slots, slots)], rows_v.at[k], sems.at[len(small) + k])
        for k in range(blocks)
    ]
    sends = [
        pltpu.make_async_copy(stage.at[place(k)], out.at[place(k)], sems.at[len(small) + blocks + k])
        for k in range(blocks)
    ]
    for copy in copies + large:
        copy.start()
    for copy in copies:
        copy.wait()
    mine = damping_v[:, 0:LANES]
    for q in range(1, chunks):
        mine = jnp.where(lax.axis_index("obs") == q, damping_v[:, q * LANES : (q + 1) * LANES], mine)
    below = parts(prior_v[...]) + parts(mine)
    below = jnp.concatenate(below, 0)
    held = values_v[...].astype(F32)
    lane = lax.broadcasted_iota(jnp.int32, (1, LANES), 1)
    for k in range(blocks):
        marks = jnp.where(lane < LANES // 2, day_s[k], count_s[k]).astype(F32)
        stage[place(k), chunks * slots : chunks * slots + EXTRA, :] = jnp.concatenate(
            [held[k : k + 1, :], marks, below], 0
        ).astype(BF16)
    for k in range(blocks):
        large[k].wait()
        for j in range(chunks):
            stage[place(k), j * slots : (j + 1) * slots, :] = rows_v[k, :, j * LANES : (j + 1) * LANES]
        sends[k].start()
    for copy in sends:
        copy.wait()


def gram_kernel(got, gain, own, extra, pay, prior, gain_out, turned, marks):
    blocks = got.shape[0]
    chunks = turned.shape[0] // LANES
    slots = (got.shape[1] - EXTRA) // chunks
    width = chunks * LANES
    tiles = triangle(width)
    group = min(blocks, 8)
    half = 2 * LANES
    gain_out[...] = gain[...]
    extra[...] = jnp.zeros(extra.shape, F32)

    def below(k):
        return got[k, chunks * slots : chunks * slots + EXTRA, :].astype(F32)

    def one(first, fresh):
        for k in range(group):
            at = slice(k * slots, (k + 1) * slots)
            line = below(first + k)
            slot = lax.broadcasted_iota(jnp.int32, (1, slots), 1).astype(F32)
            valid = slot < jnp.broadcast_to(line[1:2, LANES - 1 : LANES], (1, slots))
            day = jnp.broadcast_to(line[1:2, 0:1], (1, slots))
            kept = [jnp.where(valid & (day == d), 1.0, 0.0) for d in (0.0, 1.0)]
            marks[:, at] = jnp.concatenate(
                kept + [kept[0] * line[0:1], kept[1] * line[0:1], jnp.zeros((12, slots), F32)], 0
            ).astype(BF16)
            for j in range(chunks):
                turned[j * LANES : (j + 1) * LANES, at] = got[first + k, j * slots : (j + 1) * slots, :].T
        source = jnp.concatenate(
            [
                jnp.concatenate([got[first + k, j * slots : (j + 1) * slots, :] for j in range(chunks)], 1)
                for k in range(group)
            ],
            0,
        )
        info = jnp.dot(marks[...], source, preferred_element_type=F32)
        for d in range(2):
            for top in range(0, width, half):
                left = turned[top : top + half, :] * marks[d : d + 1, :]
                block = jnp.dot(left, source[:, : top + half], preferred_element_type=F32)
                for n, (i, j) in enumerate(tiles):
                    if top <= i * LANES < top + half:
                        r = i * LANES - top
                        piece = block[r : r + LANES, j * LANES : (j + 1) * LANES]
                        at = d * len(tiles) + n
                        own[at] = piece if fresh else own[at] + piece
            for j in range(chunks):
                piece = info[2 + d : 3 + d, j * LANES : (j + 1) * LANES]
                r = 8 * d + j
                extra[r : r + 1, :] = piece if fresh else extra[r : r + 1, :] + piece

    if blocks == group:
        one(0, True)
    else:
        own[...] = jnp.zeros(own.shape, F32)

        @pl.loop(0, blocks // group)
        def _(g):
            one(g * group, False)

    row = lax.broadcasted_iota(jnp.int32, (LANES, LANES), 0)
    column = lax.broadcasted_iota(jnp.int32, (LANES, LANES), 1)
    sides = [n for n, (i, j) in enumerate(tiles) if i != j]
    middles = [n for n, (i, j) in enumerate(tiles) if i == j]

    def send(n, piece):
        pay[n * LANES : (n + 1) * LANES, :] = piece.astype(BF16)

    for d in range(2):
        for part, piece in enumerate(parts(extra[8 * d : 8 * d + chunks, :])):
            extra[8 * d + 4 * part : 8 * d + 4 * part + chunks, :] = piece
        for m, n in enumerate(sides):
            send(d * len(sides) + m, own[d * len(tiles) + n])
    for i, n in enumerate(middles):
        squares = [own[d * len(tiles) + n] for d in range(2)]
        send(2 * len(sides) + i, jnp.where(row >= column, squares[0], squares[1]))
        for d in range(2):
            line = jnp.sum(jnp.where(row == column, squares[d], 0.0), axis=0, keepdims=True)
            for part, piece in enumerate(parts(line)):
                r = DIAG + 8 * d + 4 * part + i
                extra[r : r + 1, :] = piece
    for q in range(chunks):
        line = below(q)
        prior[:, q * LANES : (q + 1) * LANES] = line[2:3] + line[3:4]
    for y in range(blocks // 4):
        for q in range(chunks):
            line = below(4 * y + q)
            for part in range(2):
                for d in range(2):
                    r = DAMP + 16 * y + 8 * d + 4 * part + q
                    extra[r : r + 1, :] = line[4 + 2 * part + d : 5 + 2 * part + d]
    pay[pay.shape[0] - extra.shape[0] :, :] = extra[...].astype(BF16)


def prep_kernel(trans, cov, prior, pt, pthi, ptlo, chi, clo, ahead):
    whole = trans[...].T
    pt[...] = whole
    pthi[...], ptlo[...] = split(whole)
    chi[...], clo[...] = split(cov[...])
    ahead[...] = mv(prior[...], pthi[...], ptlo[...])


def stack_kernel(one, two, out):
    out[0] = one[...]
    out[1] = two[...]


def gain_kernel(held, got, mthi, mtlo):
    ids = here()
    rows = held.shape[1]
    for step, part in enumerate((held.at[0], got.at[0], held.at[1], got.at[1])):
        holder = ids[2] ^ step
        at = pl.ds(pl.multiple_of(holder * rows, rows), rows)
        hi, lo = split(part[...].T)
        mthi[:, at] = hi
        mtlo[:, at] = lo


def few(x, hi, lo):
    n = x.shape[0]
    top = x.astype(BF16).astype(F32)
    blank = [jnp.zeros((8 - 2 * n, x.shape[1]), F32)] if n < 4 else []
    both = jnp.concatenate([top, x - top] + blank, 0).astype(BF16)
    first = jnp.dot(both, hi, preferred_element_type=F32)
    second = jnp.dot(both, lo, preferred_element_type=F32)
    return first[0:n] + (first[n : 2 * n] + second[0:n])


def one_day(day, ahead, damping, omhi, omlo, info, chi, clo):
    moved = ahead * damping[day : day + 1, :]
    gap = mv(moved, omhi[day], omlo[day]) - info[day]
    return moved - mv(gap, chi[...], clo[...])


def spread(extra, got, small):
    small[0] = extra[...]
    for s, part in enumerate(got):
        small[s + 1] = part[part.shape[0] - extra.shape[0] :, :].astype(F32)


def line_of(small, s, first):
    return small[s, first : first + 1, :] + small[s, first + 4 : first + 5, :]


def table_kernel(after, extra, g1, g2, g3, table, small):
    ids = here()
    planes = 4
    chunks = table.shape[1] // LANES
    held = table.shape[0] // 2 // planes
    spread(extra, (g1, g2, g3), small)
    for s in range(planes):
        plane = lax.rem(ids[0] + s, planes)
        for k in range(held):
            for day in range(2):
                table[pl.ds(2 * (plane * held + k) + day, 1), :] = jnp.concatenate(
                    [line_of(small, s, DAMP + 16 * k + 8 * day + j) for j in range(chunks)], 1
                )


def sums(extra, got, small):
    share = jnp.where(here()[0] == 2, 1.0, 0.0)
    spread(extra, got, small)

    def summed(first):
        others = line_of(small, 1, first) + line_of(small, 2, first) + (line_of(small, 3, first) + line_of(small, 4, first))
        return line_of(small, 0, first) * share + others

    def added(n):
        at = slice(n * LANES, (n + 1) * LANES)
        one, two, three, four = (part[at].astype(F32) for part in got)
        return (one + two) + (three + four)

    return share, summed, added


def relay_kernel(after, own, extra, g4, g3, g1, g2, out, small, rows):
    span = here()[1]
    spans = lax.axis_size("z") * lax.axis_size("y")
    chunks = 4
    tiles = triangle(chunks * LANES)
    row = lax.broadcasted_iota(jnp.int32, (LANES, LANES), 0)
    column = lax.broadcasted_iota(jnp.int32, (LANES, LANES), 1)
    sides = [n for n, (i, j) in enumerate(tiles) if i != j]
    middles = [n for n, (i, j) in enumerate(tiles) if i == j]

    @pl.when((span == spans - 3) | (span == spans - 1))
    def _():
        share, summed, added = sums(extra, (g1, g2, g3, g4), small)

        def send(n, piece):
            out[n * LANES : (n + 1) * LANES, :] = (piece * share + added(n)).astype(BF16)

        for d in range(2):
            for m, n in enumerate(sides):
                send(d * len(sides) + m, own[d * len(tiles) + n])
        for i, n in enumerate(middles):
            send(2 * len(sides) + i, jnp.where(row >= column, own[n], own[len(tiles) + n]))
        rows[...] = jnp.zeros(rows.shape, F32)
        for first in (0, 8, DIAG, DIAG + 8):
            for j in range(chunks):
                for part, piece in enumerate(parts(summed(first + j))):
                    r = first + 4 * part + j
                    rows[r : r + 1, :] = piece
        out[out.shape[0] - rows.shape[0] :, :] = rows[...].astype(BF16)


def next_kernel(after, relay, chi, clo, zhi, zlo, off, whole, rows):
    spans = lax.axis_size("z") * lax.axis_size("y")
    width = whole.shape[0]
    chunks = width // LANES
    tiles = triangle(width)
    row = lax.broadcasted_iota(jnp.int32, (LANES, LANES), 0)
    column = lax.broadcasted_iota(jnp.int32, (LANES, LANES), 1)
    sides = [(i, j) for i, j in tiles if i != j]

    @pl.when(doubled(here()[1], spans))
    def _():
        rows[...] = relay[relay.shape[0] - rows.shape[0] :, :].astype(F32)

        def line(r):
            return rows[r : r + 1, :] + rows[r + 4 : r + 5, :]

        def tile(n):
            return relay[n * LANES : (n + 1) * LANES, :].astype(F32)

        def put(i, j, piece):
            whole[i * LANES : (i + 1) * LANES, j * LANES : (j + 1) * LANES] = piece

        for day in range(2):
            for i in range(chunks):
                both = tile(2 * len(sides) + i)
                part = jnp.where(row < column if day else row > column, both, 0.0)
                put(i, i, part + part.T + jnp.where(row == column, line(DIAG + 8 * day + i), 0.0))
            for m, (i, j) in enumerate(sides):
                piece = tile(day * len(sides) + m)
                put(i, j, piece)
                put(j, i, piece.T)
            zhi[day], zlo[day] = split(mm(whole[...], chi[...], clo[...]))
            info = jnp.concatenate([line(8 * day + j) for j in range(chunks)], 1)
            off[day : day + 1, :] = mv(info, chi[...], clo[...])


def next_day(day, state, damping, pthi, ptlo, zhi, zlo, off):
    moved = mv(state, pthi[...], ptlo[...]) * damping
    return moved, moved - mv(moved, zhi[day], zlo[day]) + off[day : day + 1, :]


def owner_kernel(
    own, extra, g4, g3, g1, g2, prior, ahead, pthi, ptlo, chi, clo, after, omhi, omlo, info, mine, start, y, small
):
    ids = here()
    planes = 4
    width = pthi.shape[0]
    chunks = width // LANES
    tiles = triangle(width)
    got = (g1, g2, g3, g4)
    row = lax.broadcasted_iota(jnp.int32, (LANES, LANES), 0)
    column = lax.broadcasted_iota(jnp.int32, (LANES, LANES), 1)
    share, summed, added = sums(extra, got, small)

    def put(day, i, j, piece):
        hi, lo = split(piece)
        omhi[day, i * LANES : (i + 1) * LANES, j * LANES : (j + 1) * LANES] = hi
        omlo[day, i * LANES : (i + 1) * LANES, j * LANES : (j + 1) * LANES] = lo

    sides = [n for n, (i, j) in enumerate(tiles) if i != j]
    middles = [n for n, (i, j) in enumerate(tiles) if i == j]

    def unpack(day):
        for i, n in enumerate(middles):
            both = added(2 * len(sides) + i)
            part = jnp.where(row < column if day else row > column, both, 0.0)
            others = sum(line_of(small, s, DIAG + 8 * day + i) for s in range(1, 5))
            piece = own[day * len(tiles) + n] * share + (part + part.T)
            put(day, i, i, piece + jnp.where(row == column, others, 0.0))
        for m, n in enumerate(sides):
            i, j = tiles[n]
            piece = own[day * len(tiles) + n] * share + added(day * len(sides) + m)
            put(day, i, j, piece)
            put(day, j, i, piece.T)

    for day in range(2):
        info[day] = jnp.concatenate([summed(8 * day + j) for j in range(chunks)], 1)
    held = ids[5]
    source = lax.rem(ids[1] // held - ids[0] + planes, planes)
    for day in range(2):
        for j in range(chunks):
            r = DAMP + 16 * lax.rem(ids[1], held) + 8 * day + j
            mine[day : day + 1, j * LANES : (j + 1) * LANES] = (
                small[source, pl.ds(r, 1), :] + small[source, pl.ds(r + 4, 1), :]
            )
    first = (ids[1] == 0) & (ids[0] == owner_plane(0))
    start[...] = jnp.where(first, prior[...], 0.0)

    @pl.when(first)
    def _():
        unpack(0)
        state = one_day(0, ahead[...], mine, omhi, omlo, info, chi, clo)
        unpack(1)
        y[...] = one_day(1, mv(state, pthi[...], ptlo[...]), mine, omhi, omlo, info, chi, clo)

    @pl.when(jnp.logical_not(first))
    def _():
        for day in range(2):
            unpack(day)
        y[...] = jnp.zeros(y.shape, F32)


def seen(day, omhi, omlo, chi, clo):
    return mm(omhi[day].astype(F32) + omlo[day].astype(F32), chi[...], clo[...])


def early_kernel(after, omhi, omlo, info, chi, clo, pt, damping, b1hi, b1lo, off):
    @pl.when(here()[1] == 1)
    def _():
        off[0:1, :] = mv(info[0], chi[...], clo[...])
        moved = pt[...] * damping[0:1, :]
        b1hi[...], b1lo[...] = split(moved - mm(moved, *split(seen(0, omhi, omlo, chi, clo))))


def maps_kernel(
    after, omhi, omlo, info, chi, clo, pt, damping, old1, old2, old3, b1hi, b1lo, off, b2hi, b2lo
):
    span = here()[1]
    spans = lax.axis_size("z") * lax.axis_size("y")
    relays = (span == spans - 3) | (span == spans - 1)
    parts = ((b1hi, b1lo), (b2hi, b2lo))

    def make(day):
        moved = pt[...] * damping[day : day + 1, :]
        parts[day][0][...], parts[day][1][...] = split(
            moved - mm(moved, *split(seen(day, omhi, omlo, chi, clo)))
        )
        off[day : day + 1, :] = mv(info[day], chi[...], clo[...])

    @pl.when(jnp.logical_not(relays | (span == 1)))
    def _():
        make(0)

    @pl.when(jnp.logical_not(relays))
    def _():
        make(1)


def second_kernel(acc, got, mine, b1hi, b1lo, off, omhi, omlo, info, chi, clo, pthi, ptlo, total, y):
    total[...] = acc[...] + got[...]
    y[...] = jnp.zeros(y.shape, F32)

    @pl.when(here()[1] == 1)
    def _():
        state = mv(acc[...] + got[...], b1hi[...], b1lo[...]) + off[0:1, :]
        ahead = mv(state, pthi[...], ptlo[...])
        y[...] = one_day(1, ahead, mine, omhi, omlo, info, chi, clo)


def both_kernel(after, b1hi, b1lo, b2hi, b2lo, off, bchi, bclo, offset):
    both = jnp.dot(b1hi[...], b2hi[...], preferred_element_type=F32) + (
        jnp.dot(b1lo[...], b2hi[...], preferred_element_type=F32)
        + jnp.dot(b1hi[...], b2lo[...], preferred_element_type=F32)
    )
    bchi[...], bclo[...] = split(both)
    offset[...] = mv(off[0:1, :], b2hi[...], b2lo[...]) + off[1:2, :]


def hop_kernel(after, acc, got, bchi, bclo, offset, total, y):
    state = acc[...] + got[...]
    total[...] = state
    y[...] = mv(state, bchi[...], bclo[...]) + offset[...]


def days_kernel(acc, got, b1hi, b1lo, b2hi, b2lo, off, total, y):
    state = acc[...] + got[...]
    total[...] = state
    state = mv(state, b1hi[...], b1lo[...]) + off[0:1, :]
    y[...] = mv(state, b2hi[...], b2lo[...]) + off[1:2, :]


def double_kernel(after, acc, got, bchi, bclo, offset, table, pthi, ptlo, zhi, zlo, off, total, y):
    spans = table.shape[0] // 2
    total[...] = acc[...] + got[...]
    y[...] = jnp.zeros(y.shape, F32)

    @pl.when(here()[1] == spans - 4)
    def _():
        state = mv(acc[...] + got[...], bchi[...], bclo[...]) + offset[...]
        for day in range(2):
            r = 2 * (spans - 3) + day
            _, state = next_day(day, state, table[r : r + 1, :], pthi, ptlo, zhi, zlo, off)
        y[...] = state


def whole_of(hi, lo):
    return hi[...].astype(F32) + lo[...].astype(F32)


def pairs_kernel(skip, after, table, mthi, mtlo, khi, klo):
    spans = table.shape[0] // 2

    @pl.when(here()[1] == spans - 2)
    def _():
        @pl.loop(0, khi.shape[0])
        def _(k):
            scaled = whole_of(mthi, mtlo) * table[pl.ds(2 * (spans - 3 - skip - k) + 1, 1), :]
            khi[k], klo[k] = split(mm(scaled, mthi[...], mtlo[...]))


def last_kernel(
    acc, got, b1hi, b1lo, b2hi, b2lo, bchi, bclo, off, offset, table, pthi, ptlo, mthi, mtlo,
    zhi, zlo, next_off, khi, klo, more_khi, more_klo, out, shares, means,
):
    span = here()[1]
    total, width = shares.shape
    spans = total // 2
    chunks = width // LANES
    twice = doubled(span, spans)
    shares[...] = jnp.zeros(shares.shape, F32)

    def step(k, v):
        t = 2 * span - 1 - k
        v = mv(v * table[pl.ds(t + 1, 1), :], mthi[...], mtlo[...])
        shares[pl.ds(t, 1), :] = v
        return v

    def own_days(const, damped):
        n = len(const)
        v = const[-1]
        shares[pl.ds(2 * span + n - 1, 1), :] = v
        for i in range(n - 2, -1, -1):
            v = const[i] + mv(v * damped[i], mthi[...], mtlo[...])
            shares[pl.ds(2 * span + i, 1), :] = v
        means[4:5, :] = v

    @pl.when(span < spans - 4)
    def _():
        state = acc[...] + got[...]
        one = mv(state, b1hi[...], b1lo[...]) + off[0:1, :]
        two = mv(one, b2hi[...], b2lo[...]) + off[1:2, :]
        both = jnp.concatenate([one, two], 0)
        damped = [table[pl.ds(2 * span + 1 + i, 1), :] for i in range(2)]
        ahead = jnp.concatenate(damped, 0)
        const = both - few(few(both, pthi[...], ptlo[...]) * ahead * ahead, mthi[...], mtlo[...])
        means[0:2, :] = both
        own_days([const[0:1], const[1:2]], damped)

    @pl.when(twice)
    def _():
        state = acc[...] + got[...]
        rows = [
            mv(state, b1hi[...], b1lo[...]) + off[0:1, :],
            mv(state, bchi[...], bclo[...]) + offset[...],
        ]
        damped = [table[pl.ds(2 * span + 1 + i, 1), :] for i in range(3)]
        ahead = [mv(rows[0], pthi[...], ptlo[...]) * damped[0]]
        for day in range(2):
            moved, after = next_day(day, rows[-1], damped[1 + day], pthi, ptlo, zhi, zlo, next_off)
            ahead.append(moved)
            rows.append(after)
        taken = [a * d for a, d in zip(ahead, damped)]
        taken = few(jnp.concatenate(taken + [jnp.zeros((1, width), F32)], 0), mthi[...], mtlo[...])
        means[0:4, :] = jnp.concatenate(rows, 0)
        means[5:8, :] = jnp.concatenate(rows[:3], 0) - taken[0:3]
        means[4:5, :] = rows[3]

    @pl.when(span == spans - 4)
    def _():
        beyond = table[pl.ds(2 * span + 4, 1), :]
        four = means[3:4, :]
        ahead = mv(four, pthi[...], ptlo[...]) * beyond * beyond
        means[4:5, :] = four - mv(ahead, mthi[...], mtlo[...])

    @pl.when(twice)
    def _():
        const = [means[5:6, :], means[6:7, :], means[7:8, :], means[4:5, :]]
        own_days(const, [table[pl.ds(2 * span + 1 + i, 1), :] for i in range(3)])

    @pl.when(span < spans - 2)
    def _():
        lax.fori_loop(0, jnp.where((span < spans - 4) | twice, 2 * span, 0), step, means[4:5, :])

    @pl.when(span == spans - 2)
    def _():
        v, damped_rows = means[4:5, :], []
        pairs = [(a, b, k) for a, b in ((khi, klo), (more_khi, more_klo)) for k in range(a.shape[0])]
        for n, (a, b, k) in enumerate(pairs):
            t = 2 * (spans - 2 - n)
            damped_rows.append(v * table[t : t + 1, :])
            v = mv(damped_rows[-1], a[k], b[k])
            shares[t - 2 : t - 1, :] = v
        batch = jnp.concatenate(damped_rows + [jnp.zeros((1, width), F32)] * (-len(damped_rows) % 8), 0)
        batch = mm(batch, mthi[...], mtlo[...])
        for n in range(len(pairs)):
            t = 2 * (spans - 2 - n)
            shares[t - 1 : t, :] = batch[n : n + 1]
        lax.fori_loop(2 * len(pairs), 2 * span, step, v)

    for c in range(spans):
        for q in range(chunks):
            out[c * chunks + q, 0:2, :] = shares[2 * c : 2 * c + 2, q * LANES : (q + 1) * LANES]
    for q in range(chunks):
        out[span * chunks + q, 2:4, :] = means[0:2, q * LANES : (q + 1) * LANES]

    @pl.when(twice)
    def _():
        for q in range(chunks):
            out[(span + 1) * chunks + q, 2:4, :] = means[2:4, q * LANES : (q + 1) * LANES]


def add_kernel(parts, filt, smooth):
    spans = parts.shape[0] // 4
    owners = [*range(spans - 4), spans - 4, spans - 2]
    filt[...] = parts[here()[4], 2:4, :]
    smooth[...] = sum(parts[owner_plane(c) * spans + (place(c) | 1), 0:2, :] for c in owners)


def local(
    records,
    obs_values,
    block_day,
    block_count,
    propagator_matrix,
    analysis_cov,
    unattenuated_multiplier,
    damping,
    prior_mean,
):
    planes, held, peers = (lax.axis_size(a) for a in ("z", "y", "obs"))
    spans = planes * held
    blocks = block_day.shape[0]
    slots = records.shape[0] // blocks
    width = records.shape[1]
    days = damping.shape[0]
    assert planes == peers == 4 and days == 2 and slots == LANES and blocks == spans
    everyone = ("z", "y", "obs")

    def owner(span):
        return owner_plane(span) * spans + (place(span) | 1)

    tiles = len(triangle(width))
    extra_rows = DAMP + 16 * held
    chunks = width // LANES
    full, row = (width, width), ((1, width), F32)
    sent = run(
        pack_kernel,
        [((blocks, chunks * slots + EXTRA, LANES), BF16)],
        [
            (x, HBM)
            for x in (
                block_day,
                block_count,
                records,
                obs_values.reshape(blocks, slots),
                prior_mean.reshape(1, -1),
                damping,
            )
        ],
        [
            pltpu.SMEM((blocks,), jnp.int32),
            pltpu.SMEM((blocks,), jnp.int32),
            pltpu.VMEM((blocks, slots), BF16),
            pltpu.VMEM((1, width // peers), F32),
            pltpu.VMEM((days, width), F32),
            pltpu.VMEM((blocks, slots, width), BF16),
            pltpu.VMEM((blocks, chunks * slots + EXTRA, LANES), BF16),
            pltpu.SemaphoreType.DMA((5 + 2 * blocks,)),
        ],
        limit=60,
        outs=HBM,
    )[0]
    got = lax.all_to_all(sent, ("y", "obs"), split_axis=0, concat_axis=0, tiled=True)
    span_slots = min(blocks, 8) * slots
    own, extra, pay, prior, gain = run(
        gram_kernel,
        [
            ((2 * tiles, LANES, LANES), F32),
            ((extra_rows, LANES), F32),
            (((2 * tiles - chunks) * LANES + extra_rows, LANES), BF16),
            row,
            (unattenuated_multiplier.shape, F32),
        ],
        [got, unattenuated_multiplier],
        [pltpu.VMEM((width, span_slots), BF16), pltpu.VMEM((16, span_slots), BF16)],
        flops=4 * width * width * blocks * slots,
    )
    def swap(x, bit):
        return lax.ppermute(x, "obs", [(i, i ^ bit) for i in range(peers)])

    def plane_sum(s):
        return lax.ppermute(
            pay, everyone, [((owner_plane(p) + s) % planes * spans + place(p), owner(p)) for p in range(spans)]
        )

    fourth = lax.ppermute(
        pay, everyone, [(spans + place(p), owner(p)) for p in range(spans) if place(p) % 2 == 0]
    )
    second, first, third = plane_sum(2), plane_sum(1), plane_sum(3)
    (gains,) = run(stack_kernel, [((2,) + gain.shape, F32)], [gain, swap(gain, 2)])
    mthi, mtlo = run(gain_kernel, [(full, BF16)] * 2, [gains, swap(gains, 1)])
    pt, pthi, ptlo, chi, clo, ahead = run(
        prep_kernel, [(full, F32)] + [(full, BF16)] * 4 + [row], [propagator_matrix, analysis_cov, prior]
    )
    smalls = pltpu.VMEM((planes + 1, extra_rows, LANES), F32)
    omhi, omlo, info, mine, acc, y = run(
        owner_kernel,
        [((days,) + full, BF16)] * 2 + [((days, 1, width), F32), ((days, width), F32), row, row],
        [
            own, extra, fourth, third, first, second, prior, ahead, pthi, ptlo, chi, clo, (mthi, ANY)
        ],
        [smalls],
    )
    (packed,) = run(
        relay_kernel,
        [(pay.shape, BF16)],
        [(y, ANY), own, extra, fourth, third, first, second],
        [smalls, pltpu.VMEM((extra_rows, LANES), F32)],
    )
    relay = lax.ppermute(
        packed, everyone, [(owner(p + 1), owner(p)) for p in (spans - 4, spans - 2)]
    )
    chain = [*range(spans - 3), spans - 2]
    half = [(full, BF16)] * 2
    for k, (source, target) in enumerate(zip(chain, chain[1:])):
        received = lax.ppermute(y, everyone, [(owner(source), owner(target))])
        if k == 0:
            given = [omhi, omlo, info, chi, clo, pt, mine]
            b1hi, b1lo, off = run(
                early_kernel, half + [((8, width), F32)], [(y, ANY), *given], flops=12 * width**3
            )
            acc, y = run(
                second_kernel,
                [row, row],
                [acc, received, mine, b1hi, b1lo, off, omhi, omlo, info, chi, clo, pthi, ptlo],
            )
            b1hi, b1lo, off, b2hi, b2lo = run(
                maps_kernel,
                half + [((8, width), F32)] + half,
                [(y, ANY), *given, b1hi, b1lo, off],
                flops=24 * width**3,
                same={8: 0, 9: 1, 10: 2},
            )
        elif k == 1:
            acc, y = run(days_kernel, [row, row], [acc, received, b1hi, b1lo, b2hi, b2lo, off])
            bchi, bclo, offset = run(
                both_kernel, half + [row], [(y, ANY), b1hi, b1lo, b2hi, b2lo, off]
            )
            (table,) = run(
                table_kernel,
                [((spans * days, width), F32)],
                [(offset, ANY), extra, first, second, third],
                [smalls],
            )
            khi, klo = run(
                functools.partial(pairs_kernel, 0), [((2,) + full, BF16)] * 2, [(y, ANY), table, mthi, mtlo]
            )
        elif target == spans - 4:
            nexthi, nextlo, next_off = run(
                next_kernel,
                [((days,) + full, BF16)] * 2 + [((8, width), F32)],
                [(y, ANY), relay, chi, clo],
                [pltpu.VMEM(full, F32), pltpu.VMEM((extra_rows, LANES), F32)],
            )
            acc, y = run(
                double_kernel,
                [row, row],
                [
                    (nexthi, ANY), acc, received, bchi, bclo, offset, table, pthi, ptlo, nexthi, nextlo, next_off
                ],
            )
        elif target != spans - 2:
            acc, y = run(hop_kernel, [row, row], [(khi, ANY), acc, received, bchi, bclo, offset])
        if target == spans - 4:
            more_khi, more_klo = run(
                functools.partial(pairs_kernel, 2), [((4,) + full, BF16)] * 2, [(y, ANY), table, mthi, mtlo]
            )
    (answer,) = run(
        last_kernel,
        [((spans * peers, 4, LANES), F32)],
        [
            acc, received, b1hi, b1lo, b2hi, b2lo, bchi, bclo, off, offset, table, pthi, ptlo, mthi, mtlo,
            nexthi, nextlo, next_off, khi, klo, more_khi, more_klo,
        ],
        [pltpu.VMEM((spans * days, width), F32), pltpu.VMEM((8, width), F32)],
    )
    parts = lax.all_to_all(answer, everyone, split_axis=0, concat_axis=0, tiled=True)
    out = ((days, LANES), F32)
    return run(add_kernel, [out, out], [parts])


def solution(mesh):
    spans, peers = mesh.devices.shape
    finer = jax.sharding.Mesh(mesh.devices.reshape(peers, spans // peers, peers), ("z", "y", "obs"))
    tm = ("z", "y")
    mapped = jax.shard_map(
        local,
        mesh=finer,
        in_specs=(
            P(("z", "y", "obs"), None),
            P(("z", "y", "obs")),
            P(("z", "y", "obs")),
            P(("z", "y", "obs")),
            P(),
            P(),
            P("obs", None),
            P(tm, None),
            P("obs"),
        ),
        out_specs=(P(tm, "obs"), P(tm, "obs")),
        check_vma=False,
    )
    return lambda *args: tuple(mapped(*args))
```

```python
import functools

import jax
import jax.numpy as jnp
from jax import lax
from jax.experimental import pallas as pl
from jax.experimental.pallas import tpu as pltpu
from jax.sharding import PartitionSpec as P

LANES = 128
F32, BF16 = jnp.float32, jnp.bfloat16
VMEM = pl.BlockSpec(memory_space=pltpu.VMEM)
SMEM = pl.BlockSpec(memory_space=pltpu.SMEM)
ANY = pl.BlockSpec(memory_space=pl.ANY)
HBM = pl.BlockSpec(memory_space=pltpu.HBM)


def run(body, out, ins, scratch=(), limit=16, flops=0, outs=VMEM, same=None):
    specs = [x[1] if isinstance(x, tuple) else VMEM for x in ins]
    arrays = [x[0] if isinstance(x, tuple) else x for x in ins]
    moved = sum(a.size * a.dtype.itemsize for a in arrays)
    return pl.pallas_call(
        body,
        out_shape=[jax.ShapeDtypeStruct(s, d) for s, d in out],
        in_specs=specs,
        out_specs=[outs] * len(out),
        scratch_shapes=list(scratch),
        input_output_aliases=same or {},
        compiler_params=pltpu.CompilerParams(vmem_limit_bytes=limit * 1024 * 1024),
        cost_estimate=pl.CostEstimate(flops=flops, bytes_accessed=moved, transcendentals=0),
    )(*arrays)


def here():
    z, y, o = (lax.axis_index(a) for a in ("z", "y", "obs"))
    held, peers = lax.axis_size("y"), lax.axis_size("obs")
    spans = held * peers
    at = y * peers + o
    seat = jnp.where(z == 1, at - lax.rem(at, 2), at) ^ (spans // 2 + 1)
    span = seat
    for bit in range(1, spans.bit_length()):
        span = span ^ (seat >> bit)
    c = z * held + y
    kept = jnp.where((c == spans - 3) | (c == spans - 1), c - 1, c)
    seat = place(kept)
    return z, span, o, c, (1 + (seat & 1)) * spans + (seat | 1), held


def doubled(span, spans):
    return (span == spans - 4) | (span == spans - 2)


def triangle(width):
    parts = width // LANES
    return [(i, j) for i in range(parts) for j in range(i + 1)]


def split(x):
    hi = x.astype(BF16)
    return hi, (x - hi.astype(F32)).astype(BF16)


def mm(x, hi, lo):
    xhi, xlo = split(x)
    dot = functools.partial(jnp.dot, preferred_element_type=F32)
    return dot(xhi, hi) + (dot(xlo, hi) + dot(xhi, lo))


def mv(x, hi, lo):
    wide = jnp.broadcast_to(x, (8, x.shape[1]))
    row = lax.broadcasted_iota(jnp.int32, wide.shape, 0)
    top = wide.astype(BF16).astype(F32)
    both = jnp.where(row == 0, top, jnp.where(row == 1, wide - top, 0.0)).astype(BF16)
    first = jnp.dot(both, hi, preferred_element_type=F32)
    second = jnp.dot(both, lo, preferred_element_type=F32)
    return first[0:1] + (first[1:2] + second[0:1])


def parts(x):
    top = x.astype(BF16).astype(F32)
    return [top, (x - top).astype(BF16).astype(F32)]


def place(span):
    return span ^ (span >> 1) ^ (lax.axis_size("z") * lax.axis_size("y") // 2 + 1)


def owner_plane(span):
    return 1 + place(span) % 2


EXTRA = 8
DIAG, DAMP = 16, 32


def pack_kernel(
    day, count, rows, values, prior, damping, out, day_s, count_s, values_v, prior_v, damping_v, rows_v, stage, sems
):
    blocks = out.shape[0]
    slots = rows_v.shape[1]
    chunks = rows_v.shape[2] // LANES
    small = [(day, day_s), (count, count_s), (values, values_v), (prior, prior_v), (damping, damping_v)]
    copies = [pltpu.make_async_copy(src, dst, sems.at[n]) for n, (src, dst) in enumerate(small)]
    large = [
        pltpu.make_async_copy(rows.at[pl.ds(k * slots, slots)], rows_v.at[k], sems.at[len(small) + k])
        for k in range(blocks)
    ]
    sends = [
        pltpu.make_async_copy(stage.at[place(k)], out.at[place(k)], sems.at[len(small) + blocks + k])
        for k in range(blocks)
    ]
    for copy in copies + large:
        copy.start()
    for copy in copies:
        copy.wait()
    mine = damping_v[:, 0:LANES]
    for q in range(1, chunks):
        mine = jnp.where(lax.axis_index("obs") == q, damping_v[:, q * LANES : (q + 1) * LANES], mine)
    below = parts(prior_v[...]) + parts(mine)
    below = jnp.concatenate(below, 0)
    held = values_v[...].astype(F32)
    lane = lax.broadcasted_iota(jnp.int32, (1, LANES), 1)
    for k in range(blocks):
        marks = jnp.where(lane < LANES // 2, day_s[k], count_s[k]).astype(F32)
        stage[place(k), chunks * slots : chunks * slots + EXTRA, :] = jnp.concatenate(
            [held[k : k + 1, :], marks, below], 0
        ).astype(BF16)
    for k in range(blocks):
        large[k].wait()
        for j in range(chunks):
            stage[place(k), j * slots : (j + 1) * slots, :] = rows_v[k, :, j * LANES : (j + 1) * LANES]
        sends[k].start()
    for copy in sends:
        copy.wait()


def gram_kernel(got, gain, own, extra, pay, prior, gain_out, turned, marks):
    blocks = got.shape[0]
    chunks = turned.shape[0] // LANES
    slots = (got.shape[1] - EXTRA) // chunks
    width = chunks * LANES
    tiles = triangle(width)
    group = min(blocks, 8)
    half = 2 * LANES
    gain_out[...] = gain[...]
    extra[...] = jnp.zeros(extra.shape, F32)

    def below(k):
        return got[k, chunks * slots : chunks * slots + EXTRA, :].astype(F32)

    def one(first, fresh):
        for k in range(group):
            at = slice(k * slots, (k + 1) * slots)
            line = below(first + k)
            slot = lax.broadcasted_iota(jnp.int32, (1, slots), 1).astype(F32)
            valid = slot < jnp.broadcast_to(line[1:2, LANES - 1 : LANES], (1, slots))
            day = jnp.broadcast_to(line[1:2, 0:1], (1, slots))
            kept = [jnp.where(valid & (day == d), 1.0, 0.0) for d in (0.0, 1.0)]
            marks[:, at] = jnp.concatenate(
                kept + [kept[0] * line[0:1], kept[1] * line[0:1], jnp.zeros((12, slots), F32)], 0
            ).astype(BF16)
            for j in range(chunks):
                turned[j * LANES : (j + 1) * LANES, at] = got[first + k, j * slots : (j + 1) * slots, :].T
        source = jnp.concatenate(
            [
                jnp.concatenate([got[first + k, j * slots : (j + 1) * slots, :] for j in range(chunks)], 1)
                for k in range(group)
            ],
            0,
        )
        info = jnp.dot(marks[...], source, preferred_element_type=F32)
        for d in range(2):
            for top in range(0, width, half):
                left = turned[top : top + half, :] * marks[d : d + 1, :]
                block = jnp.dot(left, source[:, : top + half], preferred_element_type=F32)
                for n, (i, j) in enumerate(tiles):
                    if top <= i * LANES < top + half:
                        r = i * LANES - top
                        piece = block[r : r + LANES, j * LANES : (j + 1) * LANES]
                        at = d * len(tiles) + n
                        own[at] = piece if fresh else own[at] + piece
            for j in range(chunks):
                piece = info[2 + d : 3 + d, j * LANES : (j + 1) * LANES]
                r = 8 * d + j
                extra[r : r + 1, :] = piece if fresh else extra[r : r + 1, :] + piece

    if blocks == group:
        one(0, True)
    else:
        own[...] = jnp.zeros(own.shape, F32)

        @pl.loop(0, blocks // group)
        def _(g):
            one(g * group, False)

    row = lax.broadcasted_iota(jnp.int32, (LANES, LANES), 0)
    column = lax.broadcasted_iota(jnp.int32, (LANES, LANES), 1)
    sides = [n for n, (i, j) in enumerate(tiles) if i != j]
    middles = [n for n, (i, j) in enumerate(tiles) if i == j]

    def send(n, piece):
        pay[n * LANES : (n + 1) * LANES, :] = piece.astype(BF16)

    for d in range(2):
        for part, piece in enumerate(parts(extra[8 * d : 8 * d + chunks, :])):
            extra[8 * d + 4 * part : 8 * d + 4 * part + chunks, :] = piece
        for m, n in enumerate(sides):
            send(d * len(sides) + m, own[d * len(tiles) + n])
    for i, n in enumerate(middles):
        squares = [own[d * len(tiles) + n] for d in range(2)]
        send(2 * len(sides) + i, jnp.where(row >= column, squares[0], squares[1]))
        for d in range(2):
            line = jnp.sum(jnp.where(row == column, squares[d], 0.0), axis=0, keepdims=True)
            for part, piece in enumerate(parts(line)):
                r = DIAG + 8 * d + 4 * part + i
                extra[r : r + 1, :] = piece
    for q in range(chunks):
        line = below(q)
        prior[:, q * LANES : (q + 1) * LANES] = line[2:3] + line[3:4]
    for y in range(blocks // 4):
        for q in range(chunks):
            line = below(4 * y + q)
            for part in range(2):
                for d in range(2):
                    r = DAMP + 16 * y + 8 * d + 4 * part + q
                    extra[r : r + 1, :] = line[4 + 2 * part + d : 5 + 2 * part + d]
    pay[pay.shape[0] - extra.shape[0] :, :] = extra[...].astype(BF16)


def prep_kernel(trans, cov, prior, pt, pthi, ptlo, chi, clo, ahead):
    whole = trans[...].T
    pt[...] = whole
    pthi[...], ptlo[...] = split(whole)
    chi[...], clo[...] = split(cov[...])
    ahead[...] = mv(prior[...], pthi[...], ptlo[...])


def stack_kernel(one, two, out):
    out[0] = one[...]
    out[1] = two[...]


def gain_kernel(held, got, mthi, mtlo):
    ids = here()
    rows = held.shape[1]
    for step, part in enumerate((held.at[0], got.at[0], held.at[1], got.at[1])):
        holder = ids[2] ^ step
        at = pl.ds(pl.multiple_of(holder * rows, rows), rows)
        hi, lo = split(part[...].T)
        mthi[:, at] = hi
        mtlo[:, at] = lo


def few(x, hi, lo):
    n = x.shape[0]
    top = x.astype(BF16).astype(F32)
    blank = [jnp.zeros((8 - 2 * n, x.shape[1]), F32)] if n < 4 else []
    both = jnp.concatenate([top, x - top] + blank, 0).astype(BF16)
    first = jnp.dot(both, hi, preferred_element_type=F32)
    second = jnp.dot(both, lo, preferred_element_type=F32)
    return first[0:n] + (first[n : 2 * n] + second[0:n])


def one_day(day, ahead, damping, omhi, omlo, info, chi, clo):
    moved = ahead * damping[day : day + 1, :]
    gap = mv(moved, omhi[day], omlo[day]) - info[day]
    return moved - mv(gap, chi[...], clo[...])


def spread(extra, got, small):
    small[0] = extra[...]
    for s, part in enumerate(got):
        small[s + 1] = part[part.shape[0] - extra.shape[0] :, :].astype(F32)


def line_of(small, s, first):
    return small[s, first : first + 1, :] + small[s, first + 4 : first + 5, :]


def table_kernel(after, extra, g1, g2, g3, table, small):
    ids = here()
    planes = 4
    chunks = table.shape[1] // LANES
    held = table.shape[0] // 2 // planes
    spread(extra, (g1, g2, g3), small)
    for s in range(planes):
        plane = lax.rem(ids[0] + s, planes)
        for k in range(held):
            for day in range(2):
                table[pl.ds(2 * (plane * held + k) + day, 1), :] = jnp.concatenate(
                    [line_of(small, s, DAMP + 16 * k + 8 * day + j) for j in range(chunks)], 1
                )


def sums(extra, got, small):
    share = jnp.where(here()[0] == 2, 1.0, 0.0)
    spread(extra, got, small)

    def summed(first):
        others = line_of(small, 1, first) + line_of(small, 2, first) + (line_of(small, 3, first) + line_of(small, 4, first))
        return line_of(small, 0, first) * share + others

    def added(n):
        at = slice(n * LANES, (n + 1) * LANES)
        one, two, three, four = (part[at].astype(F32) for part in got)
        return (one + two) + (three + four)

    return share, summed, added


def relay_kernel(after, own, extra, g4, g3, g1, g2, out, small, rows):
    span = here()[1]
    spans = lax.axis_size("z") * lax.axis_size("y")
    chunks = 4
    tiles = triangle(chunks * LANES)
    row = lax.broadcasted_iota(jnp.int32, (LANES, LANES), 0)
    column = lax.broadcasted_iota(jnp.int32, (LANES, LANES), 1)
    sides = [n for n, (i, j) in enumerate(tiles) if i != j]
    middles = [n for n, (i, j) in enumerate(tiles) if i == j]

    @pl.when((span == spans - 3) | (span == spans - 1))
    def _():
        share, summed, added = sums(extra, (g1, g2, g3, g4), small)

        def send(n, piece):
            out[n * LANES : (n + 1) * LANES, :] = (piece * share + added(n)).astype(BF16)

        for d in range(2):
            for m, n in enumerate(sides):
                send(d * len(sides) + m, own[d * len(tiles) + n])
        for i, n in enumerate(middles):
            send(2 * len(sides) + i, jnp.where(row >= column, own[n], own[len(tiles) + n]))
        rows[...] = jnp.zeros(rows.shape, F32)
        for first in (0, 8, DIAG, DIAG + 8):
            for j in range(chunks):
                for part, piece in enumerate(parts(summed(first + j))):
                    r = first + 4 * part + j
                    rows[r : r + 1, :] = piece
        out[out.shape[0] - rows.shape[0] :, :] = rows[...].astype(BF16)


def next_kernel(after, relay, chi, clo, zhi, zlo, off, whole, rows):
    spans = lax.axis_size("z") * lax.axis_size("y")
    width = whole.shape[0]
    chunks = width // LANES
    tiles = triangle(width)
    row = lax.broadcasted_iota(jnp.int32, (LANES, LANES), 0)
    column = lax.broadcasted_iota(jnp.int32, (LANES, LANES), 1)
    sides = [(i, j) for i, j in tiles if i != j]

    @pl.when(doubled(here()[1], spans))
    def _():
        rows[...] = relay[relay.shape[0] - rows.shape[0] :, :].astype(F32)

        def line(r):
            return rows[r : r + 1, :] + rows[r + 4 : r + 5, :]

        def tile(n):
            return relay[n * LANES : (n + 1) * LANES, :].astype(F32)

        def put(i, j, piece):
            whole[i * LANES : (i + 1) * LANES, j * LANES : (j + 1) * LANES] = piece

        for day in range(2):
            for i in range(chunks):
                both = tile(2 * len(sides) + i)
                part = jnp.where(row < column if day else row > column, both, 0.0)
                put(i, i, part + part.T + jnp.where(row == column, line(DIAG + 8 * day + i), 0.0))
            for m, (i, j) in enumerate(sides):
                piece = tile(day * len(sides) + m)
                put(i, j, piece)
                put(j, i, piece.T)
            zhi[day], zlo[day] = split(mm(whole[...], chi[...], clo[...]))
            info = jnp.concatenate([line(8 * day + j) for j in range(chunks)], 1)
            off[day : day + 1, :] = mv(info, chi[...], clo[...])


def next_day(day, state, damping, pthi, ptlo, zhi, zlo, off):
    moved = mv(state, pthi[...], ptlo[...]) * damping
    return moved, moved - mv(moved, zhi[day], zlo[day]) + off[day : day + 1, :]


def owner_kernel(
    own, extra, g4, g3, g1, g2, prior, ahead, pthi, ptlo, chi, clo, after, omhi, omlo, info, mine, start, y, small
):
    ids = here()
    planes = 4
    width = pthi.shape[0]
    chunks = width // LANES
    tiles = triangle(width)
    got = (g1, g2, g3, g4)
    row = lax.broadcasted_iota(jnp.int32, (LANES, LANES), 0)
    column = lax.broadcasted_iota(jnp.int32, (LANES, LANES), 1)
    share, summed, added = sums(extra, got, small)

    def put(day, i, j, piece):
        hi, lo = split(piece)
        omhi[day, i * LANES : (i + 1) * LANES, j * LANES : (j + 1) * LANES] = hi
        omlo[day, i * LANES : (i + 1) * LANES, j * LANES : (j + 1) * LANES] = lo

    sides = [n for n, (i, j) in enumerate(tiles) if i != j]
    middles = [n for n, (i, j) in enumerate(tiles) if i == j]

    def unpack(day):
        for i, n in enumerate(middles):
            both = added(2 * len(sides) + i)
            part = jnp.where(row < column if day else row > column, both, 0.0)
            others = sum(line_of(small, s, DIAG + 8 * day + i) for s in range(1, 5))
            piece = own[day * len(tiles) + n] * share + (part + part.T)
            put(day, i, i, piece + jnp.where(row == column, others, 0.0))
        for m, n in enumerate(sides):
            i, j = tiles[n]
            piece = own[day * len(tiles) + n] * share + added(day * len(sides) + m)
            put(day, i, j, piece)
            put(day, j, i, piece.T)

    for day in range(2):
        info[day] = jnp.concatenate([summed(8 * day + j) for j in range(chunks)], 1)
    held = ids[5]
    source = lax.rem(ids[1] // held - ids[0] + planes, planes)
    for day in range(2):
        for j in range(chunks):
            r = DAMP + 16 * lax.rem(ids[1], held) + 8 * day + j
            mine[day : day + 1, j * LANES : (j + 1) * LANES] = (
                small[source, pl.ds(r, 1), :] + small[source, pl.ds(r + 4, 1), :]
            )
    first = (ids[1] == 0) & (ids[0] == owner_plane(0))
    start[...] = jnp.where(first, prior[...], 0.0)

    @pl.when(first)
    def _():
        unpack(0)
        state = one_day(0, ahead[...], mine, omhi, omlo, info, chi, clo)
        unpack(1)
        y[...] = one_day(1, mv(state, pthi[...], ptlo[...]), mine, omhi, omlo, info, chi, clo)

    @pl.when(jnp.logical_not(first))
    def _():
        for day in range(2):
            unpack(day)
        y[...] = jnp.zeros(y.shape, F32)


def seen(day, omhi, omlo, chi, clo):
    return mm(omhi[day].astype(F32) + omlo[day].astype(F32), chi[...], clo[...])


def early_kernel(after, omhi, omlo, info, chi, clo, pt, damping, b1hi, b1lo, off):
    @pl.when(here()[1] == 1)
    def _():
        off[0:1, :] = mv(info[0], chi[...], clo[...])
        moved = pt[...] * damping[0:1, :]
        b1hi[...], b1lo[...] = split(moved - mm(moved, *split(seen(0, omhi, omlo, chi, clo))))


def maps_kernel(
    after, omhi, omlo, info, chi, clo, pt, damping, old1, old2, old3, b1hi, b1lo, off, b2hi, b2lo
):
    span = here()[1]
    spans = lax.axis_size("z") * lax.axis_size("y")
    relays = (span == spans - 3) | (span == spans - 1)
    parts = ((b1hi, b1lo), (b2hi, b2lo))

    def make(day):
        moved = pt[...] * damping[day : day + 1, :]
        parts[day][0][...], parts[day][1][...] = split(
            moved - mm(moved, *split(seen(day, omhi, omlo, chi, clo)))
        )
        off[day : day + 1, :] = mv(info[day], chi[...], clo[...])

    @pl.when(jnp.logical_not(relays | (span == 1)))
    def _():
        make(0)

    @pl.when(jnp.logical_not(relays))
    def _():
        make(1)


def second_kernel(acc, got, mine, b1hi, b1lo, off, omhi, omlo, info, chi, clo, pthi, ptlo, total, y):
    total[...] = acc[...] + got[...]
    y[...] = jnp.zeros(y.shape, F32)

    @pl.when(here()[1] == 1)
    def _():
        state = mv(acc[...] + got[...], b1hi[...], b1lo[...]) + off[0:1, :]
        ahead = mv(state, pthi[...], ptlo[...])
        y[...] = one_day(1, ahead, mine, omhi, omlo, info, chi, clo)


def both_kernel(after, b1hi, b1lo, b2hi, b2lo, off, bchi, bclo, offset):
    both = jnp.dot(b1hi[...], b2hi[...], preferred_element_type=F32) + (
        jnp.dot(b1lo[...], b2hi[...], preferred_element_type=F32)
        + jnp.dot(b1hi[...], b2lo[...], preferred_element_type=F32)
    )
    bchi[...], bclo[...] = split(both)
    offset[...] = mv(off[0:1, :], b2hi[...], b2lo[...]) + off[1:2, :]


def hop_kernel(after, acc, got, bchi, bclo, offset, total, y):
    state = acc[...] + got[...]
    total[...] = state
    y[...] = mv(state, bchi[...], bclo[...]) + offset[...]


def days_kernel(acc, got, b1hi, b1lo, b2hi, b2lo, off, total, y):
    state = acc[...] + got[...]
    total[...] = state
    state = mv(state, b1hi[...], b1lo[...]) + off[0:1, :]
    y[...] = mv(state, b2hi[...], b2lo[...]) + off[1:2, :]


def double_kernel(after, acc, got, bchi, bclo, offset, table, pthi, ptlo, zhi, zlo, off, total, y):
    spans = table.shape[0] // 2
    total[...] = acc[...] + got[...]
    y[...] = jnp.zeros(y.shape, F32)

    @pl.when(here()[1] == spans - 4)
    def _():
        state = mv(acc[...] + got[...], bchi[...], bclo[...]) + offset[...]
        for day in range(2):
            r = 2 * (spans - 3) + day
            _, state = next_day(day, state, table[r : r + 1, :], pthi, ptlo, zhi, zlo, off)
        y[...] = state


def whole_of(hi, lo):
    return hi[...].astype(F32) + lo[...].astype(F32)


def pairs_kernel(skip, after, table, mthi, mtlo, khi, klo):
    spans = table.shape[0] // 2

    @pl.when(here()[1] == spans - 2)
    def _():
        @pl.loop(0, khi.shape[0])
        def _(k):
            scaled = whole_of(mthi, mtlo) * table[pl.ds(2 * (spans - 3 - skip - k) + 1, 1), :]
            khi[k], klo[k] = split(mm(scaled, mthi[...], mtlo[...]))


def last_kernel(
    acc, got, b1hi, b1lo, b2hi, b2lo, bchi, bclo, off, offset, table, pthi, ptlo, mthi, mtlo,
    zhi, zlo, next_off, khi, klo, more_khi, more_klo, out, shares, means,
):
    span = here()[1]
    total, width = shares.shape
    spans = total // 2
    chunks = width // LANES
    twice = doubled(span, spans)
    shares[...] = jnp.zeros(shares.shape, F32)

    def step(k, v):
        t = 2 * span - 1 - k
        v = mv(v * table[pl.ds(t + 1, 1), :], mthi[...], mtlo[...])
        shares[pl.ds(t, 1), :] = v
        return v

    def own_days(const, damped):
        n = len(const)
        v = const[-1]
        shares[pl.ds(2 * span + n - 1, 1), :] = v
        for i in range(n - 2, -1, -1):
            v = const[i] + mv(v * damped[i], mthi[...], mtlo[...])
            shares[pl.ds(2 * span + i, 1), :] = v
        means[4:5, :] = v

    @pl.when(span < spans - 4)
    def _():
        state = acc[...] + got[...]
        one = mv(state, b1hi[...], b1lo[...]) + off[0:1, :]
        two = mv(one, b2hi[...], b2lo[...]) + off[1:2, :]
        both = jnp.concatenate([one, two], 0)
        damped = [table[pl.ds(2 * span + 1 + i, 1), :] for i in range(2)]
        ahead = jnp.concatenate(damped, 0)
        const = both - few(few(both, pthi[...], ptlo[...]) * ahead * ahead, mthi[...], mtlo[...])
        means[0:2, :] = both
        own_days([const[0:1], const[1:2]], damped)

    @pl.when(twice)
    def _():
        state = acc[...] + got[...]
        rows = [
            mv(state, b1hi[...], b1lo[...]) + off[0:1, :],
            mv(state, bchi[...], bclo[...]) + offset[...],
        ]
        damped = [table[pl.ds(2 * span + 1 + i, 1), :] for i in range(3)]
        ahead = [mv(rows[0], pthi[...], ptlo[...]) * damped[0]]
        for day in range(2):
            moved, after = next_day(day, rows[-1], damped[1 + day], pthi, ptlo, zhi, zlo, next_off)
            ahead.append(moved)
            rows.append(after)
        taken = [a * d for a, d in zip(ahead, damped)]
        taken = few(jnp.concatenate(taken + [jnp.zeros((1, width), F32)], 0), mthi[...], mtlo[...])
        means[0:4, :] = jnp.concatenate(rows, 0)
        means[5:8, :] = jnp.concatenate(rows[:3], 0) - taken[0:3]
        means[4:5, :] = rows[3]

    @pl.when(span == spans - 4)
    def _():
        beyond = table[pl.ds(2 * span + 4, 1), :]
        four = means[3:4, :]
        ahead = mv(four, pthi[...], ptlo[...]) * beyond * beyond
        means[4:5, :] = four - mv(ahead, mthi[...], mtlo[...])

    @pl.when(twice)
    def _():
        const = [means[5:6, :], means[6:7, :], means[7:8, :], means[4:5, :]]
        own_days(const, [table[pl.ds(2 * span + 1 + i, 1), :] for i in range(3)])

    @pl.when(span < spans - 2)
    def _():
        lax.fori_loop(0, jnp.where((span < spans - 4) | twice, 2 * span, 0), step, means[4:5, :])

    @pl.when(span == spans - 2)
    def _():
        v, damped_rows = means[4:5, :], []
        pairs = [(a, b, k) for a, b in ((khi, klo), (more_khi, more_klo)) for k in range(a.shape[0])]
        for n, (a, b, k) in enumerate(pairs):
            t = 2 * (spans - 2 - n)
            damped_rows.append(v * table[t : t + 1, :])
            v = mv(damped_rows[-1], a[k], b[k])
            shares[t - 2 : t - 1, :] = v
        batch = jnp.concatenate(damped_rows + [jnp.zeros((1, width), F32)] * (-len(damped_rows) % 8), 0)
        batch = mm(batch, mthi[...], mtlo[...])
        for n in range(len(pairs)):
            t = 2 * (spans - 2 - n)
            shares[t - 1 : t, :] = batch[n : n + 1]
        lax.fori_loop(2 * len(pairs), 2 * span, step, v)

    for c in range(spans):
        for q in range(chunks):
            out[c * chunks + q, 0:2, :] = shares[2 * c : 2 * c + 2, q * LANES : (q + 1) * LANES]
    for q in range(chunks):
        out[span * chunks + q, 2:4, :] = means[0:2, q * LANES : (q + 1) * LANES]

    @pl.when(twice)
    def _():
        for q in range(chunks):
            out[(span + 1) * chunks + q, 2:4, :] = means[2:4, q * LANES : (q + 1) * LANES]


def add_kernel(parts, filt, smooth):
    spans = parts.shape[0] // 4
    owners = [*range(spans - 4), spans - 4, spans - 2]
    filt[...] = parts[here()[4], 2:4, :]
    smooth[...] = sum(parts[owner_plane(c) * spans + (place(c) | 1), 0:2, :] for c in owners)


def local(
    records,
    obs_values,
    block_day,
    block_count,
    propagator_matrix,
    analysis_cov,
    unattenuated_multiplier,
    damping,
    prior_mean,
):
    planes, held, peers = (lax.axis_size(a) for a in ("z", "y", "obs"))
    spans = planes * held
    blocks = block_day.shape[0]
    slots = records.shape[0] // blocks
    width = records.shape[1]
    days = damping.shape[0]
    assert planes == peers == 4 and days == 2 and slots == LANES and blocks == spans
    everyone = ("z", "y", "obs")

    def owner(span):
        return owner_plane(span) * spans + (place(span) | 1)

    tiles = len(triangle(width))
    extra_rows = DAMP + 16 * held
    chunks = width // LANES
    full, row = (width, width), ((1, width), F32)
    sent = run(
        pack_kernel,
        [((blocks, chunks * slots + EXTRA, LANES), BF16)],
        [
            (x, HBM)
            for x in (
                block_day,
                block_count,
                records,
                obs_values.reshape(blocks, slots),
                prior_mean.reshape(1, -1),
                damping,
            )
        ],
        [
            pltpu.SMEM((blocks,), jnp.int32),
            pltpu.SMEM((blocks,), jnp.int32),
            pltpu.VMEM((blocks, slots), BF16),
            pltpu.VMEM((1, width // peers), F32),
            pltpu.VMEM((days, width), F32),
            pltpu.VMEM((blocks, slots, width), BF16),
            pltpu.VMEM((blocks, chunks * slots + EXTRA, LANES), BF16),
            pltpu.SemaphoreType.DMA((5 + 2 * blocks,)),
        ],
        limit=60,
        outs=HBM,
    )[0]
    got = lax.all_to_all(sent, ("y", "obs"), split_axis=0, concat_axis=0, tiled=True)
    span_slots = min(blocks, 8) * slots
    own, extra, pay, prior, gain = run(
        gram_kernel,
        [
            ((2 * tiles, LANES, LANES), F32),
            ((extra_rows, LANES), F32),
            (((2 * tiles - chunks) * LANES + extra_rows, LANES), BF16),
            row,
            (unattenuated_multiplier.shape, F32),
        ],
        [got, unattenuated_multiplier],
        [pltpu.VMEM((width, span_slots), BF16), pltpu.VMEM((16, span_slots), BF16)],
        flops=4 * width * width * blocks * slots,
    )
    def swap(x, bit):
        return lax.ppermute(x, "obs", [(i, i ^ bit) for i in range(peers)])

    def plane_sum(s):
        return lax.ppermute(
            pay, everyone, [((owner_plane(p) + s) % planes * spans + place(p), owner(p)) for p in range(spans)]
        )

    fourth = lax.ppermute(
        pay, everyone, [(spans + place(p), owner(p)) for p in range(spans) if place(p) % 2 == 0]
    )
    second, first, third = plane_sum(2), plane_sum(1), plane_sum(3)
    (gains,) = run(stack_kernel, [((2,) + gain.shape, F32)], [gain, swap(gain, 2)])
    mthi, mtlo = run(gain_kernel, [(full, BF16)] * 2, [gains, swap(gains, 1)])
    pt, pthi, ptlo, chi, clo, ahead = run(
        prep_kernel, [(full, F32)] + [(full, BF16)] * 4 + [row], [propagator_matrix, analysis_cov, prior]
    )
    smalls = pltpu.VMEM((planes + 1, extra_rows, LANES), F32)
    omhi, omlo, info, mine, acc, y = run(
        owner_kernel,
        [((days,) + full, BF16)] * 2 + [((days, 1, width), F32), ((days, width), F32), row, row],
        [
            own, extra, fourth, third, first, second, prior, ahead, pthi, ptlo, chi, clo, (mthi, ANY)
        ],
        [smalls],
    )
    (packed,) = run(
        relay_kernel,
        [(pay.shape, BF16)],
        [(y, ANY), own, extra, fourth, third, first, second],
        [smalls, pltpu.VMEM((extra_rows, LANES), F32)],
    )
    relay = lax.ppermute(
        packed, everyone, [(owner(p + 1), owner(p)) for p in (spans - 4, spans - 2)]
    )
    chain = [*range(spans - 3), spans - 2]
    half = [(full, BF16)] * 2
    for k, (source, target) in enumerate(zip(chain, chain[1:])):
        received = lax.ppermute(y, everyone, [(owner(source), owner(target))])
        if k == 0:
            given = [omhi, omlo, info, chi, clo, pt, mine]
            b1hi, b1lo, off = run(
                early_kernel, half + [((8, width), F32)], [(y, ANY), *given], flops=12 * width**3
            )
            acc, y = run(
                second_kernel,
                [row, row],
                [acc, received, mine, b1hi, b1lo, off, omhi, omlo, info, chi, clo, pthi, ptlo],
            )
            b1hi, b1lo, off, b2hi, b2lo = run(
                maps_kernel,
                half + [((8, width), F32)] + half,
                [(y, ANY), *given, b1hi, b1lo, off],
                flops=24 * width**3,
                same={8: 0, 9: 1, 10: 2},
            )
        elif k == 1:
            acc, y = run(days_kernel, [row, row], [acc, received, b1hi, b1lo, b2hi, b2lo, off])
            bchi, bclo, offset = run(
                both_kernel, half + [row], [(y, ANY), b1hi, b1lo, b2hi, b2lo, off]
            )
            (table,) = run(
                table_kernel,
                [((spans * days, width), F32)],
                [(offset, ANY), extra, first, second, third],
                [smalls],
            )
            khi, klo = run(
                functools.partial(pairs_kernel, 0), [((2,) + full, BF16)] * 2, [(y, ANY), table, mthi, mtlo]
            )
        elif target == spans - 4:
            nexthi, nextlo, next_off = run(
                next_kernel,
                [((days,) + full, BF16)] * 2 + [((8, width), F32)],
                [(y, ANY), relay, chi, clo],
                [pltpu.VMEM(full, F32), pltpu.VMEM((extra_rows, LANES), F32)],
            )
            acc, y = run(
                double_kernel,
                [row, row],
                [
                    (nexthi, ANY), acc, received, bchi, bclo, offset, table, pthi, ptlo, nexthi, nextlo, next_off
                ],
            )
        elif target != spans - 2:
            acc, y = run(hop_kernel, [row, row], [(khi, ANY), acc, received, bchi, bclo, offset])
        if target == spans - 4:
            more_khi, more_klo = run(
                functools.partial(pairs_kernel, 2), [((3,) + full, BF16)] * 2, [(y, ANY), table, mthi, mtlo]
            )
    (answer,) = run(
        last_kernel,
        [((spans * peers, 4, LANES), F32)],
        [
            acc, received, b1hi, b1lo, b2hi, b2lo, bchi, bclo, off, offset, table, pthi, ptlo, mthi, mtlo,
            nexthi, nextlo, next_off, khi, klo, more_khi, more_klo,
        ],
        [pltpu.VMEM((spans * days, width), F32), pltpu.VMEM((8, width), F32)],
    )
    parts = lax.all_to_all(answer, everyone, split_axis=0, concat_axis=0, tiled=True)
    out = ((days, LANES), F32)
    return run(add_kernel, [out, out], [parts])


def solution(mesh):
    spans, peers = mesh.devices.shape
    finer = jax.sharding.Mesh(mesh.devices.reshape(peers, spans // peers, peers), ("z", "y", "obs"))
    tm = ("z", "y")
    mapped = jax.shard_map(
        local,
        mesh=finer,
        in_specs=(
            P(("z", "y", "obs"), None),
            P(("z", "y", "obs")),
            P(("z", "y", "obs")),
            P(("z", "y", "obs")),
            P(),
            P(),
            P("obs", None),
            P(tm, None),
            P("obs"),
        ),
        out_specs=(P(tm, "obs"), P(tm, "obs")),
        check_vma=False,
    )
    return lambda *args: tuple(mapped(*args))
```
